32 devices in a mesh: grp: 8 (over z, x), seq: 4 (over y, core).
Axes of the slice: x: 2, y: 2, z: 4, core: 2. Of those that a mesh axis runs over, the one named last changes fastest.
Arguments:
- tokens: bfloat16 [4096, 768], P(('grp', 'seq')), may hold values from -6 to 6
- global_tokens: bfloat16 [512, 768], P('grp'), may hold values from -6 to 6
- neighbours: int32 [4096, 8], P(('grp', 'seq')), may hold values from 0 to 383
- token_ranks: int32 [2, 4096], P(None, ('grp', 'seq')), may hold values from 0 to 511
- membership: int32 [4096], P(('grp', 'seq')), may hold values from 0 to 63
- w_graph: bfloat16 [768, 768], replicated, may hold values from -0.625 to 0.625
- gain_one: float32 [768], replicated, may hold values from 0.5 to 1.5
- shift_one: float32 [768], replicated, may hold values from -1.75 to 1.75
- w_query: bfloat16 [768, 768], replicated, may hold values from -0.21875 to 0.21875
- w_key: bfloat16 [768, 768], replicated, may hold values from -0.21875 to 0.21875
- w_value: bfloat16 [768, 768], replicated, may hold values from -0.21875 to 0.21875
- rich_query: bfloat16 [64, 48], replicated, may hold values from -0.75 to 0.75
- rich_key: bfloat16 [64, 48], replicated, may hold values from -0.75 to 0.75
- w_out: bfloat16 [768, 768], replicated, may hold values from -1.25 to 1.25
- gain_two: float32 [768], replicated, may hold values from 0.5 to 1.5
- shift_two: float32 [768], replicated, may hold values from -1.75 to 1.75
- w_up: bfloat16 [768, 3072], replicated, may hold values from -0.21875 to 0.21875
- bias_up: float32 [3072], replicated, may hold values from -1.75 to 1.75
- w_down: bfloat16 [3072, 768], replicated, may hold values from -0.109375 to 0.109375
- bias_down: float32 [768], replicated, may hold values from -1.75 to 1.75
- cot_tokens: bfloat16 [4096, 768], P(('grp', 'seq')), may hold values from -6 to 6
- cot_global: bfloat16 [512, 768], P('grp'), may hold values from -6 to 6
Outputs:
- out_tokens: bfloat16 [4096, 768], P(('grp', 'seq'))
- out_global: bfloat16 [512, 768], P('grp')
- grad_tokens: float32 [4096, 768], P(('grp', 'seq'))
- grad_global: float32 [512, 768], P('grp')
- grad_w_graph: float32 [768, 768], P('seq')
- grad_gain_one: float32 [768], P('seq')
- grad_shift_one: float32 [768], P('seq')
- grad_w_query: float32 [768, 768], P('seq')
- grad_w_key: float32 [768, 768], P('seq')
- grad_w_value: float32 [768, 768], P('seq')
- grad_rich_query: float32 [64, 48], P('seq')
- grad_rich_key: float32 [64, 48], P('seq')
- grad_w_out: float32 [768, 768], P('seq')
- grad_gain_two: float32 [768], P('seq')
- grad_shift_two: float32 [768], P('seq')
- grad_w_up: float32 [768, 3072], P('seq')
- grad_bias_up: float32 [3072], P('seq')
- grad_w_down: float32 [3072, 768], P('seq')
- grad_bias_down: float32 [768], P('seq')
The draws below stay inside these ranges and needn't reach their ends.
Inputs may be any that keep to these rules, and one draw needn't show every extreme that they name: neighbours[i, k] = n names position (i // 128) * 128 - 128 + n of i's sequence.
All inputs are finite; a program needn't handle non-finite values.
Results may differ from the reference program's by a relative error of at most 0.019.
Values may be sent and summed in bfloat16 or wider, within the bound.
No kernel may reach another device: no remote copies, remote signals or barrier semaphores. Data moves between devices by JAX's collectives and lax.ppermute only.
A program may use at most 192 MiB of HBM per device.

```python
import math
import jax
import jax.numpy as jnp
from jax import lax

D = 768
HEADS = 12
HEAD_DIM = 64
FF = 3072
RADIUS = 128
GLOBALS = 64
NEIGH = 8
TOK_DEV = 128
SEQ_LEN = 512
TOKENS = 4096
GLOBAL_ROWS = 512


def plant(entries, own_key, least, high):
    extent = entries.shape
    spot = [jax.random.randint(jax.random.fold_in(own_key, axis), (), 0, extent[axis]) for axis in range(len(extent))]
    entries = entries.at[tuple(spot)].set(least)
    longest = extent.index(max(extent))
    spot[longest] = (spot[longest] + 1) % extent[longest]
    return entries.at[tuple(spot)].set(high)


def block_scale(key, shape, shards, least, largest):
    loudness = 1.0
    for dim, shards_of in shards:
        heights = jax.random.uniform(jax.random.fold_in(jax.random.fold_in(key, 6), dim), (shards_of,), jnp.float32, least / len(shards), largest / len(shards))
        loudness = loudness * jnp.repeat(jnp.exp(heights), shape[dim] // shards_of).reshape((-1,) + (1,) * (len(shape) - 1 - dim))
    return loudness


def normal_values(key, shape, width, bound, pieces=(), kind=jnp.bfloat16):
    drawn = jax.random.normal(key, shape, jnp.float32) * width
    if len(pieces) > 0:
        drawn = block_scale(key, shape, pieces, -0.22, 0.18) * drawn
    return jnp.clip(drawn, min=-bound, max=bound).astype(kind)


def setup_inputs(seed: int = 0) -> dict:
    seeds = jax.random.split(jax.random.key(seed), 23)
    tokens = normal_values(seeds[0], (TOKENS, D), 1.0, 6.0, ((0, 32),))
    global_tokens = normal_values(seeds[1], (GLOBAL_ROWS, D), 1.0, 6.0, ((0, 8),))
    neighbours = plant(jax.random.randint(seeds[2], (TOKENS, NEIGH), 0, TOK_DEV + 2 * RADIUS), jax.random.fold_in(seeds[2], 1), 0, (TOK_DEV + 2 * RADIUS) - 1).astype(jnp.int32)
    token_ranks = plant(jax.random.randint(seeds[3], (2, TOKENS), 0, SEQ_LEN), jax.random.fold_in(seeds[3], 1), 0, SEQ_LEN - 1).astype(jnp.int32)
    membership = plant(jax.random.randint(seeds[4], (TOKENS,), 0, GLOBALS), jax.random.fold_in(seeds[4], 1), 0, GLOBALS - 1).astype(jnp.int32)
    w_graph = normal_values(seeds[5], (D, D), (D // 8) ** -0.5, 0.625)
    gain_one = jnp.clip(1.0 + 0.1 * jax.random.normal(seeds[6], (D,), jnp.float32), 0.5, 1.5)
    shift_one = normal_values(seeds[7], (D,), 0.3, 1.75, (), jnp.float32)
    w_query = normal_values(seeds[8], (D, D), D ** -0.5, 0.21875)
    w_key = normal_values(seeds[9], (D, D), D ** -0.5, 0.21875)
    w_value = normal_values(seeds[10], (D, D), D ** -0.5, 0.21875)
    rich_query = normal_values(seeds[11], (HEAD_DIM, 4 * HEADS), HEAD_DIM ** -0.5, 0.75)
    rich_key = normal_values(seeds[12], (HEAD_DIM, 4 * HEADS), HEAD_DIM ** -0.5, 0.75)
    w_out = normal_values(seeds[13], (D, D), (D // 32) ** -0.5, 1.25)
    gain_two = jnp.clip(1.0 + 0.1 * jax.random.normal(seeds[14], (D,), jnp.float32), 0.5, 1.5)
    shift_two = normal_values(seeds[15], (D,), 0.3, 1.75, (), jnp.float32)
    w_up = normal_values(seeds[16], (D, FF), D ** -0.5, 0.21875)
    bias_up = normal_values(seeds[17], (FF,), 0.3, 1.75, (), jnp.float32)
    w_down = normal_values(seeds[18], (FF, D), FF ** -0.5, 0.109375)
    bias_down = normal_values(seeds[19], (D,), 0.3, 1.75, (), jnp.float32)
    cot_tokens = normal_values(seeds[20], (TOKENS, D), 1.0, 6.0, ((0, 32),))
    cot_global = normal_values(seeds[21], (GLOBAL_ROWS, D), 1.0, 6.0, ((0, 8),))
    return {"tokens": tokens, "global_tokens": global_tokens, "neighbours": neighbours, "token_ranks": token_ranks, "membership": membership, "w_graph": w_graph, "gain_one": gain_one, "shift_one": shift_one, "w_query": w_query, "w_key": w_key, "w_value": w_value, "rich_query": rich_query, "rich_key": rich_key, "w_out": w_out, "gain_two": gain_two, "shift_two": shift_two, "w_up": w_up, "bias_up": bias_up, "w_down": w_down, "bias_down": bias_down, "cot_tokens": cot_tokens, "cot_global": cot_global}


@jax.custom_vjp
def low(v):
    return lax.optimization_barrier(v.astype(jnp.bfloat16)).astype(jnp.float32)

@jax.custom_vjp
def low_back(v):
    return v

def low_keep(v):
    return (low(v), None)

def low_pass(kept, grad):
    return (grad,)

def back_keep(v):
    return (v, None)

def back_low(kept, grad):
    return (low(grad),)
low.defvjp(low_keep, low_pass)
low_back.defvjp(back_keep, back_low)
EPSILON = 1e-05
PRECISE = lax.Precision.HIGHEST
MASKED = -1e+30

def layer_norm(rows_in, gain_in, shift_in):
    row_mean = lax.optimization_barrier(jnp.mean(rows_in, axis=-1, keepdims=True))
    centred = rows_in - row_mean
    variance = lax.optimization_barrier(jnp.mean(centred * centred, axis=-1, keepdims=True))
    return centred * lax.rsqrt(variance + EPSILON) * gain_in + shift_in

def rich_part(a_block, b_window, rank_query, rank_key, log_norm):
    combined = None
    for coordinate in range(2):
        order_flag = (rank_query[coordinate][:, None] < rank_key[coordinate][None, :]).astype(jnp.float32)
        distance = jnp.log1p(jnp.abs(rank_query[coordinate][:, None] - rank_key[coordinate][None, :]).astype(jnp.float32)) / log_norm
        order_logit = a_block[:, :, None, coordinate] + b_window[:, None, :, coordinate]
        centre = a_block[:, :, None, 2 + coordinate] + b_window[:, None, :, 2 + coordinate]
        pair_term = order_flag * jax.nn.log_sigmoid(order_logit) + (1.0 - order_flag) * jax.nn.log_sigmoid(-order_logit) - 0.5 * (distance - centre) ** 2
        combined = pair_term if combined is None else combined + pair_term
    return combined

def product(left, right):
    return jnp.dot(left, right, precision=PRECISE)

def group_forward(tok_rows, glob_rows, params, neigh_rows, rank_rows, member_rows):
    w_graph, gain_one, shift_one, w_query, w_key, w_value, rich_query, rich_key, w_out, gain_two, shift_two, w_up, bias_up, w_down, bias_down = params
    seq_len = tok_rows.shape[0]
    score_scale = 1.0 / math.sqrt(HEAD_DIM)
    log_norm = math.log(1.0 + seq_len)
    padded = jnp.pad(tok_rows, ((RADIUS, RADIUS), (0, 0)))
    base_rows = jnp.arange(seq_len, dtype=jnp.int32) // TOK_DEV * TOK_DEV
    gathered = padded[base_rows[:, None] + neigh_rows]
    agg_mean = lax.optimization_barrier(jnp.mean(gathered, axis=1))
    graph_pre = low_back(product(low(agg_mean), w_graph))
    super_rows = tok_rows + jax.nn.gelu(graph_pre)
    normed = low(layer_norm(super_rows, gain_one, shift_one))
    glob_normed = low(layer_norm(glob_rows, gain_one, shift_one))

    def project(rows_in, weight):
        return low_back(low(product(rows_in, weight))).reshape(rows_in.shape[0], HEADS, HEAD_DIM)
    query, key_rows, value_rows = (project(normed, w_query), project(normed, w_key), project(normed, w_value))
    glob_query, glob_key, glob_value = (project(glob_normed, w_query), project(glob_normed, w_key), project(glob_normed, w_value))
    rich_q3 = rich_query.reshape(HEAD_DIM, HEADS, 4)
    rich_k3 = rich_key.reshape(HEAD_DIM, HEADS, 4)
    a_rows = jnp.einsum('the,ehc->htc', query, rich_q3, precision=PRECISE)
    b_rows = jnp.einsum('the,ehc->htc', key_rows, rich_k3, precision=PRECISE)
    block_rows = min(512, TOK_DEV)
    window = block_rows + 2 * RADIUS
    key_pad = jnp.pad(key_rows, ((RADIUS, RADIUS), (0, 0), (0, 0)))
    value_pad = jnp.pad(value_rows, ((RADIUS, RADIUS), (0, 0), (0, 0)))
    b_pad = jnp.pad(b_rows, ((0, 0), (RADIUS, RADIUS), (0, 0)))
    rank_pad = jnp.pad(rank_rows, ((0, 0), (RADIUS, RADIUS)))

    def long_block(block_index):
        row_start = block_index * block_rows
        q_part = lax.dynamic_slice_in_dim(query, row_start, block_rows, 0)
        a_part = lax.dynamic_slice_in_dim(a_rows, row_start, block_rows, 1)
        key_win = lax.dynamic_slice_in_dim(key_pad, row_start, window, 0)
        value_win = lax.dynamic_slice_in_dim(value_pad, row_start, window, 0)
        b_win = lax.dynamic_slice_in_dim(b_pad, row_start, window, 1)
        rank_q = lax.dynamic_slice_in_dim(rank_rows, row_start, block_rows, 1)
        rank_k = lax.dynamic_slice_in_dim(rank_pad, row_start, window, 1)
        q_pos = row_start + jnp.arange(block_rows, dtype=jnp.int32)
        k_pos = row_start - RADIUS + jnp.arange(window, dtype=jnp.int32)
        key_mask = (jnp.abs(q_pos[:, None] - k_pos[None, :]) <= RADIUS) & ((k_pos >= 0) & (k_pos < seq_len))[None, :]
        raw_scores = jnp.einsum('qhe,khe->hqk', q_part, key_win, precision=PRECISE) * score_scale
        scores = low_back(raw_scores + rich_part(a_part, b_win, rank_q, rank_k, log_norm))
        scores = jnp.where(key_mask[None], scores, MASKED)
        glob_scores = low_back(jnp.einsum('qhe,ghe->hqg', q_part, glob_key, precision=PRECISE) * score_scale)
        row_top = jnp.maximum(lax.optimization_barrier(jnp.max(scores, axis=-1)), lax.optimization_barrier(jnp.max(glob_scores, axis=-1)))
        row_denom = lax.optimization_barrier(jnp.sum(jnp.exp(scores - row_top[..., None]), axis=-1)) + lax.optimization_barrier(jnp.sum(jnp.exp(glob_scores - row_top[..., None]), axis=-1))
        log_total = row_top + jnp.log(row_denom)
        prob_rows = low(jnp.exp(scores - log_total[..., None]))
        glob_probs = low(jnp.exp(glob_scores - log_total[..., None]))
        return jnp.einsum('hqk,khe->qhe', prob_rows, value_win, precision=PRECISE) + jnp.einsum('hqg,ghe->qhe', glob_probs, glob_value, precision=PRECISE)
    attn_rows = lax.map(jax.checkpoint(long_block), jnp.arange(seq_len // block_rows, dtype=jnp.int32))
    attn_rows = low_back(low(attn_rows.reshape(seq_len, D)))
    member_mask = member_rows[None, :] == jnp.arange(GLOBALS, dtype=jnp.int32)[:, None]
    member_scores = low_back(jnp.einsum('ghe,the->ght', glob_query, key_rows, precision=PRECISE) * score_scale)
    member_scores = jnp.where(member_mask[:, None, :], member_scores, MASKED)
    self_scores = low_back(jnp.einsum('ghe,khe->ghk', glob_query, glob_key, precision=PRECISE) * score_scale)
    glob_top = jnp.maximum(lax.optimization_barrier(jnp.max(member_scores, axis=-1)), lax.optimization_barrier(jnp.max(self_scores, axis=-1)))
    glob_denom = lax.optimization_barrier(jnp.sum(jnp.exp(member_scores - glob_top[..., None]), axis=-1)) + lax.optimization_barrier(jnp.sum(jnp.exp(self_scores - glob_top[..., None]), axis=-1))
    glob_lse = glob_top + jnp.log(glob_denom)
    glob_attn = jnp.einsum('ght,the->ghe', jnp.exp(member_scores - glob_lse[..., None]), value_rows, precision=PRECISE) + jnp.einsum('ghk,khe->ghe', jnp.exp(self_scores - glob_lse[..., None]), glob_value, precision=PRECISE)
    glob_attn = low_back(low(glob_attn.reshape(GLOBALS, D)))
    y_one = super_rows + low_back(product(attn_rows, w_out))
    glob_y_one = glob_rows + low_back(product(glob_attn, w_out))

    def feed_forward(rows_in):
        normed_two = low(layer_norm(rows_in, gain_two, shift_two))
        hidden_pre = low_back(product(normed_two, w_up) + bias_up)
        hidden = low(jax.nn.gelu(hidden_pre))
        return rows_in + product(hidden, w_down) + bias_down
    return (feed_forward(y_one), feed_forward(glob_y_one))

def reference(tokens, global_tokens, neighbours, token_ranks, membership, w_graph, gain_one, shift_one, w_query, w_key, w_value, rich_query, rich_key, w_out, gain_two, shift_two, w_up, bias_up, w_down, bias_down, cot_tokens, cot_global):
    seq_len = SEQ_LEN
    n_seqs = tokens.shape[0] // seq_len
    params = tuple((weight.astype(jnp.float32) for weight in (w_graph, gain_one, shift_one, w_query, w_key, w_value, rich_query, rich_key, w_out, gain_two, shift_two, w_up, bias_up, w_down, bias_down)))
    tok_groups = tokens.astype(jnp.float32).reshape(n_seqs, seq_len, D)
    glob_groups = global_tokens.astype(jnp.float32).reshape(n_seqs, GLOBALS, D)
    neigh_groups = neighbours.reshape(n_seqs, seq_len, NEIGH)
    rank_groups = token_ranks.reshape(2, n_seqs, seq_len).transpose(1, 0, 2)
    member_groups = membership.reshape(n_seqs, seq_len)
    cot_tok_groups = cot_tokens.astype(jnp.float32).reshape(n_seqs, seq_len, D)
    cot_glob_groups = cot_global.astype(jnp.float32).reshape(n_seqs, GLOBALS, D)

    def group_step(carry, inputs):
        tok_rows, glob_rows, neigh_rows, rank_rows, member_rows, cot_tok, cot_glob = inputs

        def run(tok_in, glob_in, params_in):
            return group_forward(tok_in, glob_in, params_in, neigh_rows, rank_rows, member_rows)
        outputs, back_fn = jax.vjp(run, tok_rows, glob_rows, params)
        grad_tok, grad_glob, grad_params = back_fn((cot_tok, cot_glob))
        carry = tuple((total + part for total, part in zip(carry, grad_params)))
        return (carry, (outputs[0].astype(jnp.bfloat16), outputs[1].astype(jnp.bfloat16), grad_tok, grad_glob))
    zeros = tuple((jnp.zeros_like(weight) for weight in params))
    totals, stacked = lax.scan(group_step, zeros, (tok_groups, glob_groups, neigh_groups, rank_groups, member_groups, cot_tok_groups, cot_glob_groups))
    out_tokens = stacked[0].reshape(n_seqs * seq_len, D)
    out_global = stacked[1].reshape(n_seqs * GLOBALS, D)
    grad_tokens = stacked[2].reshape(n_seqs * seq_len, D)
    grad_global = stacked[3].reshape(n_seqs * GLOBALS, D)
    return (out_tokens, out_global, grad_tokens, grad_global, totals[0], totals[1], totals[2], totals[3], totals[4], totals[5], totals[6], totals[7], totals[8], totals[9], totals[10], totals[11], totals[12], totals[13], totals[14])
```

```python
import math

import jax
import jax.numpy as jnp
from jax import lax
from jax.experimental import pallas as pl
from jax.experimental.pallas import tpu as pltpu
from jax.sharding import PartitionSpec as P

D = 768
HEADS = 12
HEAD_DIM = 64
RADIUS = 128
GLOBALS = 64
NEIGH = 8
SEQ_TOKENS = 2048


EPSILON = 1e-05
PRECISE = lax.Precision.HIGHEST
MASKED = -1e30


def with_halo(cells, sides, width):
    for axis, dim in sides:
        count = lax.axis_size(axis)
        ends = count - 1
        head = lax.slice_in_dim(cells, 0, width, axis=dim)
        tail = lax.slice_in_dim(cells, cells.shape[dim] - width, cells.shape[dim], axis=dim)
        cells = jnp.concatenate(
            [
                lax.ppermute(tail, axis, [(i, (i + 1) % count) for i in range(ends)]),
                cells,
                lax.ppermute(head, axis, [((i + 1) % count, i) for i in range(ends)]),
            ],
            axis=dim,
        )
    return cells


def joined(array, axis, combine):
    everything = jax.tree.map(
        lambda part, kind: lax.all_gather(part.astype(kind), axis),
        array,
        (jnp.bfloat16, jnp.bfloat16, jnp.bfloat16),
    )

    def take(k):
        return jax.tree.map(lambda part, own: part[k].astype(own.dtype), everything, array)

    return lax.fori_loop(
        1, lax.axis_size(axis), lambda k, so_far: combine(so_far, take(k)), take(0)
    )


def shifted(block, axis, distance):
    devices = range(lax.axis_size(axis))
    route = [(i - distance, i) for i in devices if i - distance in devices]
    return lax.ppermute(block, axis, route)


def layer_norm(rows_in, gain_in, shift_in):
    row_mean = jnp.mean(rows_in, axis=-1, keepdims=True)
    centred = rows_in - row_mean
    variance = jnp.mean(centred * centred, axis=-1, keepdims=True)
    return centred * lax.rsqrt(variance + EPSILON) * gain_in + shift_in


def rich_part(a_block, b_window, rank_query, rank_key, log_norm):
    combined = None
    for coordinate in range(2):
        order_flag = (rank_query[coordinate][:, None] < rank_key[coordinate][None, :]).astype(
            jnp.float32
        )
        distance = (
            jnp.log1p(
                jnp.abs(rank_query[coordinate][:, None] - rank_key[coordinate][None, :]).astype(
                    jnp.float32
                )
            )
            / log_norm
        )
        order_logit = a_block[:, :, None, coordinate] + b_window[:, None, :, coordinate]
        centre = a_block[:, :, None, 2 + coordinate] + b_window[:, None, :, 2 + coordinate]
        pair_term = (
            order_flag * jax.nn.log_sigmoid(order_logit)
            + (1.0 - order_flag) * jax.nn.log_sigmoid(-order_logit)
            - 0.5 * (distance - centre) ** 2
        )
        combined = pair_term if combined is None else combined + pair_term
    return combined


def product(left, right):
    return jnp.dot(left, right, preferred_element_type=jnp.float32)


def product_left(left, right):
    return jnp.einsum("ta,tb->ab", left, right, preferred_element_type=jnp.float32)


def product_right(left, right):
    return jnp.einsum("tb,ab->ta", left, right, preferred_element_type=jnp.float32)


def local(
    tokens,
    global_tokens,
    neighbours,
    token_ranks,
    membership,
    w_graph,
    gain_one,
    shift_one,
    w_query,
    w_key,
    w_value,
    rich_query,
    rich_key,
    w_out,
    gain_two,
    shift_two,
    w_up,
    bias_up,
    w_down,
    bias_down,
    cot_tokens,
    cot_global,
):
    tok_count = tokens.shape[0]
    seq_count = lax.axis_size("seq")
    seq_index = lax.axis_index("seq")
    seq_len = min(SEQ_TOKENS, tok_count * seq_count)
    span = seq_len // tok_count
    group_seqs = global_tokens.shape[0] // GLOBALS
    seq_slot = seq_index // span
    seq_local = seq_index % span
    slot_flag = (jnp.arange(group_seqs, dtype=jnp.int32) == seq_slot).astype(jnp.float32)
    log_norm = math.log(1.0 + seq_len)
    score_scale = 1.0 / math.sqrt(HEAD_DIM)
    block_rows = min(512, tok_count)
    window = block_rows + 2 * RADIUS
    ext_count = tok_count + 2 * RADIUS
    first_flag = (seq_index == 0).astype(jnp.float32)
    own_pos = seq_local * tok_count + jnp.arange(tok_count, dtype=jnp.int32)
    ext_pos = seq_local * tok_count - RADIUS + jnp.arange(ext_count, dtype=jnp.int32)
    key_valid = (ext_pos >= 0) & (ext_pos < seq_len)

    def own_slot(array_in):
        return lax.dynamic_index_in_dim(array_in, seq_slot, 0, keepdims=False)

    def to_slots(array_in):
        return slot_flag.reshape((group_seqs,) + (1,) * array_in.ndim) * array_in[None]

    token_ext = with_halo(tokens, (("seq", 0),), RADIUS)
    token_ext = jnp.where(key_valid[:, None], token_ext, jnp.zeros_like(token_ext))
    flat_index = neighbours.reshape(-1)
    gathered = (
        jnp.take(token_ext, flat_index, axis=0).astype(jnp.float32).reshape(tok_count, NEIGH, D)
    )
    agg_low = jnp.mean(gathered, axis=1).astype(jnp.bfloat16)
    graph_pre = product(agg_low, w_graph)
    graph_out, graph_back = jax.vjp(jax.nn.gelu, graph_pre)
    super_rows = tokens.astype(jnp.float32) + graph_out
    normed_full, norm_back = jax.vjp(layer_norm, super_rows, gain_one, shift_one)
    normed = normed_full.astype(jnp.bfloat16)
    glob_in = global_tokens.astype(jnp.float32)
    glob_normed_full, glob_norm_back = jax.vjp(layer_norm, glob_in, gain_one, shift_one)
    glob_normed = glob_normed_full.astype(jnp.bfloat16)
    query = product(normed, w_query).astype(jnp.bfloat16)
    key_own = product(normed, w_key).astype(jnp.bfloat16)
    value_own = product(normed, w_value).astype(jnp.bfloat16)
    glob_query = (
        product(glob_normed, w_query)
        .astype(jnp.bfloat16)
        .reshape(group_seqs, GLOBALS, HEADS, HEAD_DIM)
    )
    glob_key = (
        product(glob_normed, w_key)
        .astype(jnp.bfloat16)
        .reshape(group_seqs, GLOBALS, HEADS, HEAD_DIM)
    )
    glob_value = (
        product(glob_normed, w_value)
        .astype(jnp.bfloat16)
        .reshape(group_seqs, GLOBALS, HEADS, HEAD_DIM)
    )
    glob_query_own = own_slot(glob_query)
    glob_key_own = own_slot(glob_key)
    glob_value_own = own_slot(glob_value)
    kv_ext = with_halo(jnp.concatenate([key_own, value_own], axis=1), (("seq", 0),), RADIUS)
    key_ext = kv_ext[:, :D].reshape(ext_count, HEADS, HEAD_DIM)
    value_ext = kv_ext[:, D:].reshape(ext_count, HEADS, HEAD_DIM)
    rank_ext = with_halo(token_ranks, (("seq", 1),), RADIUS)
    rich_q3 = rich_query.reshape(HEAD_DIM, HEADS, 4)
    rich_k3 = rich_key.reshape(HEAD_DIM, HEADS, 4)
    query_heads = query.reshape(tok_count, HEADS, HEAD_DIM)
    a_rows = jnp.einsum("the,ehc->htc", query_heads, rich_q3, preferred_element_type=jnp.float32)
    b_ext = jnp.einsum("the,ehc->htc", key_ext, rich_k3, preferred_element_type=jnp.float32)

    def block_scores():

        def rich_scores(left_rows, right_rows):
            return rich_part(left_rows, right_rows, token_ranks, rank_ext, log_norm)

        rich_vals, rich_back = jax.vjp(rich_scores, a_rows, b_ext)
        raw_scores = (
            jnp.einsum("qhe,khe->hqk", query_heads, key_ext, preferred_element_type=jnp.float32)
            * score_scale
        )
        pos_gap = own_pos[:, None] - ext_pos[None, :]
        key_mask = (jnp.abs(pos_gap) <= RADIUS) & key_valid[None, :]
        scores = jnp.where(key_mask[None], raw_scores + rich_vals, MASKED)
        glob_scores = (
            jnp.einsum(
                "qhe,ghe->hqg", query_heads, glob_key_own, preferred_element_type=jnp.float32
            )
            * score_scale
        )
        return (scores, glob_scores, rich_back, query_heads, key_ext)

    scored = block_scores()
    scores = scored[0]
    glob_scores = scored[1]
    row_top = jnp.maximum(jnp.max(scores, axis=-1), jnp.max(glob_scores, axis=-1))
    row_denom = jnp.sum(jnp.exp(scores - row_top[..., None]), axis=-1) + jnp.sum(
        jnp.exp(glob_scores - row_top[..., None]), axis=-1
    )
    log_total = row_top + jnp.log(row_denom)
    prob_rows = jnp.exp(scores - log_total[..., None]).astype(jnp.bfloat16)
    glob_probs = jnp.exp(glob_scores - log_total[..., None]).astype(jnp.bfloat16)
    attn_block = jnp.einsum(
        "hqk,khe->qhe", prob_rows, value_ext, preferred_element_type=jnp.float32
    ) + jnp.einsum("hqg,ghe->qhe", glob_probs, glob_value_own, preferred_element_type=jnp.float32)
    attn_parts = attn_block.reshape(block_rows, D)
    attn_rows = attn_parts.astype(jnp.bfloat16)
    member_mask = membership[None, :] == jnp.arange(GLOBALS, dtype=jnp.int32)[:, None]
    key_heads = key_ext[RADIUS : RADIUS + tok_count]
    value_heads = value_ext[RADIUS : RADIUS + tok_count]
    member_raw = (
        jnp.einsum("ghe,the->ght", glob_query_own, key_heads, preferred_element_type=jnp.float32)
        * score_scale
    )
    member_scores = jnp.where(member_mask[:, None, :], member_raw, MASKED)
    local_top = jnp.max(member_scores, axis=-1)
    member_exp = jnp.where(
        member_mask[:, None, :], jnp.exp(member_scores - local_top[..., None]), 0.0
    )
    local_sum = jnp.sum(member_exp, axis=-1)
    local_acc = jnp.einsum(
        "ght,the->ghe", member_exp, value_heads.astype(jnp.float32), precision=PRECISE
    )
    slot_top = jnp.where(slot_flag[:, None, None] > 0.5, local_top[None], MASKED)
    slot_sum = to_slots(local_sum)
    slot_acc = to_slots(local_acc)

    def combine_softmax(first_part, second_part):
        top_one, sum_one, acc_one = first_part
        top_two, sum_two, acc_two = second_part
        top_both = jnp.maximum(top_one, top_two)
        scale_one = jnp.exp(top_one - top_both)
        scale_two = jnp.exp(top_two - top_both)
        return (
            top_both,
            sum_one * scale_one + sum_two * scale_two,
            acc_one * scale_one[..., None] + acc_two * scale_two[..., None],
        )

    merged_top, merged_sum, merged_acc = joined(
        (slot_top, slot_sum, slot_acc), "seq", combine_softmax
    )
    self_scores = (
        jnp.einsum("sghe,skhe->sghk", glob_query, glob_key, preferred_element_type=jnp.float32)
        * score_scale
    )
    glob_top = jnp.maximum(merged_top, jnp.max(self_scores, axis=-1))
    self_exp = jnp.exp(self_scores - glob_top[..., None])
    merged_scale = jnp.exp(merged_top - glob_top)
    glob_denom = merged_sum * merged_scale + jnp.sum(self_exp, axis=-1)
    glob_lse = glob_top + jnp.log(glob_denom)
    glob_att_f = (
        merged_acc * merged_scale[..., None]
        + jnp.einsum("sghk,skhe->sghe", self_exp, glob_value.astype(jnp.float32), precision=PRECISE)
    ) / glob_denom[..., None]
    glob_attn = glob_att_f.reshape(group_seqs * GLOBALS, D).astype(jnp.bfloat16)
    y_one = super_rows + product(attn_rows, w_out)
    glob_y_one = glob_in + product(glob_attn, w_out)

    def feed_forward(rows_in):
        normed_two_full, back_two = jax.vjp(layer_norm, rows_in, gain_two, shift_two)
        normed_two = normed_two_full.astype(jnp.bfloat16)
        hidden_pre = product(normed_two, w_up) + bias_up
        hidden_full, gelu_back = jax.vjp(jax.nn.gelu, hidden_pre)
        hidden = hidden_full.astype(jnp.bfloat16)
        result = rows_in + product(hidden, w_down) + bias_down
        return (result, normed_two, hidden, back_two, gelu_back)

    def feed_back(cotangent, normed_two, hidden, back_two, gelu_back):
        cot_full = cotangent.astype(jnp.float32)
        grad_down = product_left(hidden, cotangent)
        grad_bias_d = jnp.sum(cot_full, axis=0)
        d_hidden = product_right(cotangent, w_down)
        d_pre = gelu_back(d_hidden)[0].astype(jnp.bfloat16)
        grad_up = product_left(normed_two, d_pre)
        grad_bias_u = jnp.sum(d_pre.astype(jnp.float32), axis=0)
        d_normed_two = product_right(d_pre, w_up)
        d_rows, grad_gain, grad_shift = back_two(d_normed_two)
        return (
            cot_full + d_rows,
            (grad_gain, grad_shift, grad_up, grad_bias_u, grad_down, grad_bias_d),
        )

    long_ff = feed_forward(y_one)
    glob_ff = feed_forward(glob_y_one)
    out_tokens = long_ff[0].astype(jnp.bfloat16)
    out_global = glob_ff[0].astype(jnp.bfloat16)
    d_y_one, long_mlp = feed_back(cot_tokens, long_ff[1], long_ff[2], long_ff[3], long_ff[4])
    glob_d_y_one, glob_mlp = feed_back(cot_global, glob_ff[1], glob_ff[2], glob_ff[3], glob_ff[4])
    mlp_grads = [
        local_part + first_flag * glob_part for local_part, glob_part in zip(long_mlp, glob_mlp)
    ]
    d_proj = d_y_one.astype(jnp.bfloat16)
    glob_d_proj = glob_d_y_one.astype(jnp.bfloat16)
    grad_out = product_left(attn_rows, d_proj) + first_flag * product_left(glob_attn, glob_d_proj)
    d_attn = product_right(d_proj, w_out).astype(jnp.bfloat16).reshape(tok_count, HEADS, HEAD_DIM)
    glob_d_attn = (
        product_right(glob_d_proj, w_out)
        .astype(jnp.bfloat16)
        .reshape(group_seqs, GLOBALS, HEADS, HEAD_DIM)
    )
    glob_d_attn_own = own_slot(glob_d_attn)
    rich_q3_full = rich_q3.astype(jnp.float32)
    rich_k3_full = rich_k3.astype(jnp.float32)
    d_key_ext = jnp.zeros((ext_count, HEADS, HEAD_DIM), jnp.float32)
    d_value_ext = jnp.zeros((ext_count, HEADS, HEAD_DIM), jnp.float32)
    scores, glob_scores, rich_back, q_part, key_win = block_scores()
    prob_full = jnp.exp(scores - log_total[..., None])
    glob_prob_full = jnp.exp(glob_scores - log_total[..., None])
    d_probs = jnp.einsum("qhe,khe->hqk", d_attn, value_ext, preferred_element_type=jnp.float32)
    glob_d_probs = jnp.einsum(
        "qhe,ghe->hqg", d_attn, glob_value_own, preferred_element_type=jnp.float32
    )
    row_delta = jnp.sum(prob_full * d_probs, axis=-1) + jnp.sum(
        glob_prob_full * glob_d_probs, axis=-1
    )
    d_scores = (prob_full * (d_probs - row_delta[..., None])).astype(jnp.bfloat16)
    glob_d_scores = (glob_prob_full * (glob_d_probs - row_delta[..., None])).astype(jnp.bfloat16)
    query_rich_grad, key_rich_grad = rich_back(d_scores.astype(jnp.float32))
    query_grad = (
        jnp.einsum("hqk,khe->qhe", d_scores, key_win, preferred_element_type=jnp.float32)
        + jnp.einsum(
            "hqg,ghe->qhe", glob_d_scores, glob_key_own, preferred_element_type=jnp.float32
        )
    ) * score_scale + jnp.einsum("hqc,ehc->qhe", query_rich_grad, rich_q3_full, precision=PRECISE)
    key_win_grad = jnp.einsum(
        "hqk,qhe->khe", d_scores, q_part, preferred_element_type=jnp.float32
    ) * score_scale + jnp.einsum("hkc,ehc->khe", key_rich_grad, rich_k3_full, precision=PRECISE)
    value_win_grad = jnp.einsum(
        "hqk,qhe->khe", prob_full.astype(jnp.bfloat16), d_attn, preferred_element_type=jnp.float32
    )
    d_key_ext = d_key_ext.at[0:window].add(key_win_grad)
    d_value_ext = d_value_ext.at[0:window].add(value_win_grad)
    glob_key_grad = (
        jnp.einsum("hqg,qhe->ghe", glob_d_scores, q_part, preferred_element_type=jnp.float32)
        * score_scale
    )
    glob_value_grad = jnp.einsum(
        "hqg,qhe->ghe",
        glob_prob_full.astype(jnp.bfloat16),
        d_attn,
        preferred_element_type=jnp.float32,
    )
    grad_rich_q = jnp.einsum(
        "qhe,hqc->ehc", q_part.astype(jnp.float32), query_rich_grad, precision=PRECISE
    )
    grad_rich_k = jnp.einsum(
        "khe,hkc->ehc", key_win.astype(jnp.float32), key_rich_grad, precision=PRECISE
    )
    query_grads = query_grad.reshape(block_rows, D)
    glob_delta = jnp.sum(glob_d_attn.astype(jnp.float32) * glob_att_f, axis=-1)
    glob_delta_own = own_slot(glob_delta)
    glob_lse_own = own_slot(glob_lse)
    member_probs = jnp.where(
        member_mask[:, None, :], jnp.exp(member_scores - glob_lse_own[..., None]), 0.0
    )
    member_d_probs = jnp.einsum(
        "ghe,the->ght", glob_d_attn_own, value_heads, preferred_element_type=jnp.float32
    )
    member_d_scores = (member_probs * (member_d_probs - glob_delta_own[..., None])).astype(
        jnp.bfloat16
    )
    glob_query_part = (
        jnp.einsum("ght,the->ghe", member_d_scores, key_heads, preferred_element_type=jnp.float32)
        * score_scale
    )
    own_key_extra = (
        jnp.einsum(
            "ght,ghe->the", member_d_scores, glob_query_own, preferred_element_type=jnp.float32
        )
        * score_scale
    )
    own_value_extra = jnp.einsum(
        "ght,ghe->the", member_probs, glob_d_attn_own.astype(jnp.float32), precision=PRECISE
    )
    d_key_ext = d_key_ext.at[RADIUS : RADIUS + tok_count].add(own_key_extra)
    d_value_ext = d_value_ext.at[RADIUS : RADIUS + tok_count].add(own_value_extra)
    grad_rims = jnp.concatenate(
        [d_key_ext.reshape(ext_count, D), d_value_ext.reshape(ext_count, D)], axis=1
    )
    from_above = shifted(grad_rims[:RADIUS].astype(jnp.bfloat16), "seq", -1).astype(jnp.float32)
    from_below = shifted(grad_rims[tok_count + RADIUS :].astype(jnp.bfloat16), "seq", 1).astype(
        jnp.float32
    )
    kv_grad = grad_rims[RADIUS : RADIUS + tok_count]
    kv_grad = kv_grad.at[:RADIUS].add(from_below).at[tok_count - RADIUS :].add(from_above)
    summed_query, summed_key, summed_value = (
        lax.psum(to_slots(glob_query_part).astype(jnp.bfloat16), "seq").astype(jnp.float32),
        lax.psum(to_slots(glob_key_grad).astype(jnp.bfloat16), "seq").astype(jnp.float32),
        lax.psum(to_slots(glob_value_grad).astype(jnp.bfloat16), "seq").astype(jnp.float32),
    )
    self_probs = jnp.exp(self_scores - glob_lse[..., None])
    self_d_probs = jnp.einsum(
        "sghe,skhe->sghk", glob_d_attn, glob_value, preferred_element_type=jnp.float32
    )
    self_d_scores = (self_probs * (self_d_probs - glob_delta[..., None])).astype(jnp.bfloat16)
    glob_rows_total = group_seqs * GLOBALS
    glob_d_query = (
        (
            summed_query
            + jnp.einsum(
                "sghk,skhe->sghe", self_d_scores, glob_key, preferred_element_type=jnp.float32
            )
            * score_scale
        )
        .astype(jnp.bfloat16)
        .reshape(glob_rows_total, D)
    )
    glob_d_key = (
        (
            summed_key
            + jnp.einsum(
                "sghk,sghe->skhe", self_d_scores, glob_query, preferred_element_type=jnp.float32
            )
            * score_scale
        )
        .astype(jnp.bfloat16)
        .reshape(glob_rows_total, D)
    )
    glob_d_value = (
        (
            summed_value
            + jnp.einsum(
                "sghk,sghe->skhe", self_probs, glob_d_attn.astype(jnp.float32), precision=PRECISE
            )
        )
        .astype(jnp.bfloat16)
        .reshape(glob_rows_total, D)
    )
    d_query = query_grads.astype(jnp.bfloat16)
    d_key = kv_grad[:, :D].astype(jnp.bfloat16)
    d_value = kv_grad[:, D:].astype(jnp.bfloat16)
    grad_query = product_left(normed, d_query) + first_flag * product_left(
        glob_normed, glob_d_query
    )
    grad_key = product_left(normed, d_key) + first_flag * product_left(glob_normed, glob_d_key)
    grad_value = product_left(normed, d_value) + first_flag * product_left(
        glob_normed, glob_d_value
    )
    d_normed = (
        product_right(d_query, w_query)
        + product_right(d_key, w_key)
        + product_right(d_value, w_value)
    )
    glob_d_normed = (
        product_right(glob_d_query, w_query)
        + product_right(glob_d_key, w_key)
        + product_right(glob_d_value, w_value)
    )
    d_super_norm, grad_gain_one, grad_shift_one = norm_back(d_normed)
    d_super = d_y_one + d_super_norm
    glob_d_norm, glob_gain_one, glob_shift_one = glob_norm_back(glob_d_normed)
    grad_global = glob_d_y_one + glob_d_norm
    grad_gain_one = grad_gain_one + first_flag * glob_gain_one
    grad_shift_one = grad_shift_one + first_flag * glob_shift_one
    d_graph_pre = graph_back(d_super)[0].astype(jnp.bfloat16)
    grad_graph = product_left(agg_low, d_graph_pre)
    d_agg = product_right(d_graph_pre, w_graph) / NEIGH
    d_token_ext = (
        jnp.zeros((ext_count, D), jnp.float32).at[flat_index].add(jnp.repeat(d_agg, NEIGH, axis=0))
    )
    d_token_ext = jnp.where(key_valid[:, None], d_token_ext, 0.0)
    token_above = shifted(d_token_ext[:RADIUS].astype(jnp.bfloat16), "seq", -1).astype(jnp.float32)
    token_below = shifted(d_token_ext[tok_count + RADIUS :].astype(jnp.bfloat16), "seq", 1).astype(
        jnp.float32
    )
    own_grad = (
        d_token_ext[RADIUS : RADIUS + tok_count]
        .at[:RADIUS]
        .add(token_below)
        .at[tok_count - RADIUS :]
        .add(token_above)
    )
    grad_tokens = d_super + own_grad
    weight_grads = (
        grad_graph,
        grad_gain_one,
        grad_shift_one,
        grad_query,
        grad_key,
        grad_value,
        grad_rich_q.reshape(HEAD_DIM, 4 * HEADS),
        grad_rich_k.reshape(HEAD_DIM, 4 * HEADS),
        grad_out,
        mlp_grads[0],
        mlp_grads[1],
        mlp_grads[2],
        mlp_grads[3],
        mlp_grads[4],
        mlp_grads[5],
    )
    pieces = [weight_grad.reshape(seq_count, -1) for weight_grad in weight_grads]
    packed = jnp.concatenate(pieces, axis=1)
    group_count = lax.axis_size("grp")
    received = lax.all_to_all(
        packed.astype(jnp.bfloat16), "seq", split_axis=0, concat_axis=0, tiled=True
    ).astype(packed.dtype)
    group_total = jnp.sum(received, axis=0).reshape(group_count, -1)
    crossed = lax.all_to_all(
        group_total.astype(jnp.bfloat16), "grp", split_axis=0, concat_axis=0, tiled=True
    ).astype(group_total.dtype)
    final_part = jnp.sum(crossed, axis=0)
    flat_sum = lax.all_gather(final_part.astype(jnp.bfloat16), "grp", axis=0, tiled=True).astype(
        final_part.dtype
    )
    results = []
    offset = 0
    for weight_grad in weight_grads:
        part_len = weight_grad.size // seq_count
        results.append(
            flat_sum[offset : offset + part_len].reshape(
                (weight_grad.shape[0] // seq_count,) + weight_grad.shape[1:]
            )
        )
        offset = offset + part_len
    return (
        out_tokens,
        out_global,
        grad_tokens,
        grad_global,
        results[0],
        results[1],
        results[2],
        results[3],
        results[4],
        results[5],
        results[6],
        results[7],
        results[8],
        results[9],
        results[10],
        results[11],
        results[12],
        results[13],
        results[14],
    )


SEQ_WAYS = 4
GRP_WAYS = 8
OWN_HEADS = HEADS // SEQ_WAYS
OWN = D // SEQ_WAYS
FF = 3072
FF_OWN = FF // SEQ_WAYS
TOK = 128
ROWS = SEQ_WAYS * TOK
ALL = ROWS + GLOBALS
GLOB_OWN = GLOBALS // SEQ_WAYS
CHUNK = TOK + GLOB_OWN
WIN = TOK + 2 * RADIUS
PAD = ROWS + 2 * RADIUS
BF = jnp.bfloat16
F32 = jnp.float32
GELU_SCALE = math.sqrt(2.0 / math.pi)
GELU_CUBE = 0.044715
LOG_NORM = math.log(1.0 + ROWS)
SCORE_SCALE = 1.0 / math.sqrt(HEAD_DIM)
CORE_SWAP = [(0, 1), (1, 0), (2, 3), (3, 2)]
Y_SWAP = [(0, 2), (2, 0), (1, 3), (3, 1)]
X_SWAP = [(g, g ^ 1) for g in range(GRP_WAYS)]
Z_NEAR = [(g, g ^ 2) for g in range(GRP_WAYS)]
Z_FAR = [(g, g ^ 4) for g in range(GRP_WAYS)]


def nn(left, right):
    return lax.dot_general(left, right, (((1,), (0,)), ((), ())), preferred_element_type=F32)


def nt(left, right):
    return lax.dot_general(left, right, (((1,), (1,)), ((), ())), preferred_element_type=F32)


def tn(left, right):
    return lax.dot_general(left, right, (((0,), (0,)), ((), ())), preferred_element_type=F32)


def pick(stacked, index):
    return lax.dynamic_index_in_dim(stacked, index, 0, keepdims=False)


def gather_seq(block):
    across = lax.ppermute(block, "seq", Y_SWAP)
    beside = lax.ppermute(block, "seq", CORE_SWAP)
    diagonal = lax.ppermute(across, "seq", CORE_SWAP)
    return [block, beside, across, diagonal]


def scatter_seq(chunks):
    me = lax.axis_index("seq")
    core, y = me % 2, me // 2
    grid = chunks.reshape((2, 2) + chunks.shape[1:])
    sent = lax.dynamic_index_in_dim(grid, 1 - core, 1, keepdims=False)
    kept = lax.dynamic_index_in_dim(grid, core, 1, keepdims=False)
    half = kept.astype(F32) + lax.ppermute(sent, "seq", CORE_SWAP).astype(F32)
    far = lax.ppermute(pick(half, 1 - y).astype(BF), "seq", Y_SWAP)
    return pick(half, y) + far.astype(F32)


def turn_seq(chunks):
    me = lax.axis_index("seq")
    core, y = me % 2, me // 2
    grid = chunks.reshape((2, 2) + chunks.shape[1:])
    kept = lax.dynamic_index_in_dim(grid, core, 1, keepdims=False)
    sent = lax.dynamic_index_in_dim(grid, 1 - core, 1, keepdims=False)
    came = lax.ppermute(sent, "seq", CORE_SWAP)
    low = jnp.where(core == 0, kept, came)
    high = jnp.where(core == 0, came, kept)
    pair = jnp.stack([low, high], axis=1)
    far = lax.ppermute(pick(pair, 1 - y), "seq", Y_SWAP)
    near = pick(pair, y)
    return jnp.concatenate([jnp.where(y == 0, near, far), jnp.where(y == 0, far, near)], axis=0)


def reduce_grp(chunks):
    me = lax.axis_index("grp")
    x, z_low, z_high = me % 2, (me // 2) % 2, me // 4
    grid = chunks.reshape((4, 2) + chunks.shape[1:])
    sent = lax.dynamic_index_in_dim(grid, 1 - x, 1, keepdims=False)
    kept = lax.dynamic_index_in_dim(grid, x, 1, keepdims=False)
    part = (kept.astype(F32) + lax.ppermute(sent, "grp", X_SWAP).astype(F32)).astype(BF)
    part = part.reshape((2, 2) + part.shape[1:])
    sent = lax.dynamic_index_in_dim(part, 1 - z_low, 1, keepdims=False)
    kept = lax.dynamic_index_in_dim(part, z_low, 1, keepdims=False)
    part = (kept.astype(F32) + lax.ppermute(sent, "grp", Z_NEAR).astype(F32)).astype(BF)
    came = lax.ppermute(pick(part, 1 - z_high), "grp", Z_FAR)
    return pick(part, z_high).astype(F32) + came.astype(F32)


def gather_grp(block):
    me = lax.axis_index("grp")
    x, z_low, z_high = me % 2, (me // 2) % 2, me // 4

    def both(flag, mine, other, axis):
        low = jnp.where(flag == 0, mine, other)
        high = jnp.where(flag == 0, other, mine)
        return jnp.stack([low, high], axis=axis)

    block = block.astype(BF)
    held = both(z_high, block, lax.ppermute(block, "grp", Z_FAR), 0)
    held = both(z_low, held, lax.ppermute(held, "grp", Z_NEAR), 1)
    held = both(x, held, lax.ppermute(held, "grp", X_SWAP), 2)
    return held.reshape((GRP_WAYS,) + block.shape)


def row_stats(rows_in):
    centred = rows_in - jnp.mean(rows_in, axis=-1, keepdims=True)
    scale = lax.rsqrt(jnp.mean(centred * centred, axis=-1, keepdims=True) + EPSILON)
    return centred * scale, scale


def norm_back(cotangent, gain, rows_in):
    hat, scale = row_stats(rows_in)
    scaled = cotangent * gain
    back = scale * (
        scaled
        - jnp.mean(scaled, axis=-1, keepdims=True)
        - hat * jnp.mean(scaled * hat, axis=-1, keepdims=True)
    )
    return (
        back,
        jnp.sum(cotangent * hat, axis=0, keepdims=True),
        jnp.sum(cotangent, axis=0, keepdims=True),
    )


def gelu_parts(pre):
    square = pre * pre
    bent = jnp.tanh(GELU_SCALE * pre * (1.0 + GELU_CUBE * square))
    half = 0.5 * (1.0 + bent)
    slope = half + 0.5 * pre * (1.0 - bent * bent) * (
        GELU_SCALE * (1.0 + 3.0 * GELU_CUBE * square)
    )
    return pre * half, slope


def counts_of(neigh, first, width):
    spots = lax.broadcasted_iota(jnp.int32, (neigh.shape[0], width), 1) + first
    total = jnp.zeros((neigh.shape[0], width), F32)
    for k in range(NEIGH):
        total = total + jnp.where(neigh[:, k : k + 1] == spots, 1.0, 0.0)
    return total.astype(BF)


def graph_kernel(
    me_ref, tok_a, tok_b, tok_c, tok_d, int_a, int_b, int_c, int_d, glob_ref, w_graph_ref,
    w_qkv_ref, gain_ref, shift_ref,
    agg_ref, pre_ref, super_ref, normed_ref, qkv_ref, meta_col_ref, meta_row_ref, padded,
):
    me = me_ref[0]
    padded[:RADIUS] = jnp.zeros((RADIUS, D), BF)
    padded[RADIUS + ROWS :] = jnp.zeros((RADIUS, D), BF)
    starts = [pl.multiple_of((me ^ k) * TOK, TOK) for k in range(SEQ_WAYS)]
    for start, tok in zip(starts, (tok_a, tok_b, tok_c, tok_d)):
        padded[pl.ds(start + RADIUS, TOK)] = tok[...]
    for start, ints in zip(starts, (int_a, int_b, int_c, int_d)):
        values = ints[...]
        floats = values.astype(F32)
        meta_col_ref[pl.ds(start, TOK)] = floats
        meta_row_ref[:, pl.ds(start, TOK)] = floats.T[:16]
        counts = counts_of(values, 0, WIN)
        mean = nn(counts, padded[pl.ds(start, WIN)]) * (1.0 / NEIGH)
        agg_ref[pl.ds(start, TOK)] = mean.astype(BF)
    gain, shift = gain_ref[...], shift_ref[...]
    for low in range(0, ROWS, 256):
        rows = slice(low, low + 256)
        pre = nn(agg_ref[rows], w_graph_ref[...])
        pre_ref[rows] = pre
        tokens = padded[RADIUS + low : RADIUS + low + 256].astype(F32)
        super_rows = tokens + gelu_parts(pre)[0]
        super_ref[rows] = super_rows
        normed_ref[rows] = (row_stats(super_rows)[0] * gain + shift).astype(BF)
    glob_hat = row_stats(glob_ref[...].astype(F32))[0]
    normed_ref[ROWS:] = (glob_hat * gain + shift).astype(BF)
    projected = nn(normed_ref[...], w_qkv_ref[...]).astype(BF)
    for part in range(3 * OWN_HEADS):
        qkv_ref[part] = projected[:, part * HEAD_DIM : (part + 1) * HEAD_DIM]


def pair_terms(meta_col, meta_row):
    terms = []
    for c in range(2):
        gap = meta_col[:, 8 + c : 9 + c] - meta_row[8 + c : 9 + c]
        distance = jnp.log(1.0 + jnp.abs(gap)) * (1.0 / LOG_NORM)
        terms.append((gap < 0.0, distance))
    return terms


def attend_kernel(
    qkv_ref, meta_col_ref, meta_row_ref, rich_q_ref, rich_k_ref,
    attn_ref, prob_ref, glob_prob_ref, member_ref, self_ref, glob_att_ref,
    keys, values, key_rich, meta_pad,
):
    edge = jnp.zeros((OWN_HEADS, RADIUS, HEAD_DIM), BF)
    for held, first in ((keys, OWN_HEADS), (values, 2 * OWN_HEADS)):
        held[:, :RADIUS] = edge
        held[:, RADIUS + ROWS :] = edge
        held[:, RADIUS : RADIUS + ROWS] = qkv_ref[first : first + OWN_HEADS, :ROWS]
    meta_pad[...] = jnp.zeros((16, PAD), F32)
    meta_pad[:, RADIUS : RADIUS + ROWS] = meta_row_ref[...]
    for h in range(OWN_HEADS):
        key_rich[h] = nt(rich_k_ref[h], keys[h])

    def block(b, carry):
        start = pl.multiple_of(b * TOK, TOK)
        rows = pl.ds(start, TOK)
        window = pl.ds(start, WIN)
        terms = pair_terms(meta_col_ref[rows], meta_pad[:, window])
        q_spot = lax.broadcasted_iota(jnp.int32, (TOK, WIN), 0)
        k_spot = lax.broadcasted_iota(jnp.int32, (TOK, WIN), 1)
        ahead = k_spot - q_spot
        place = k_spot + (start - RADIUS)
        mask = (ahead >= 0) & (ahead <= 2 * RADIUS) & (place >= 0) & (place < ROWS)
        for h in range(OWN_HEADS):
            query = qkv_ref[h, rows]
            query_rich = nn(query, rich_q_ref[h])
            right = key_rich[h, :, window]
            scores = nt(query, keys[h, window]) * SCORE_SCALE
            spread = None
            for c, (before, distance) in enumerate(terms):
                logit = query_rich[:, c : c + 1] + right[c : c + 1]
                logit = jnp.where(before, logit, -logit)
                off = distance - (query_rich[:, 2 + c : 3 + c] + right[2 + c : 3 + c])
                scores = scores + (jnp.minimum(logit, 0.0) - 0.5 * off * off)
                grown = 1.0 + jnp.exp(-jnp.abs(logit))
                spread = grown if spread is None else spread * grown
            scores = jnp.where(mask, scores - jnp.log(spread), MASKED)
            glob_scores = nt(query, qkv_ref[OWN_HEADS + h, ROWS:]) * SCORE_SCALE
            top = jnp.maximum(
                jnp.max(scores, axis=-1, keepdims=True), jnp.max(glob_scores, axis=-1, keepdims=True)
            )
            prob = jnp.exp(scores - top)
            glob_prob = jnp.exp(glob_scores - top)
            total = jnp.sum(prob, axis=-1, keepdims=True) + jnp.sum(
                glob_prob, axis=-1, keepdims=True
            )
            inverse = 1.0 / total
            prob = prob * inverse
            glob_prob = glob_prob * inverse
            prob_ref[h, rows] = prob
            glob_prob_ref[h, rows] = glob_prob
            mixed = nn(prob.astype(BF), values[h, window]) + nn(
                glob_prob.astype(BF), qkv_ref[2 * OWN_HEADS + h, ROWS:]
            )
            attn_ref[rows, h * HEAD_DIM : (h + 1) * HEAD_DIM] = mixed.astype(BF)
        return carry

    lax.fori_loop(0, SEQ_WAYS, block, 0)
    slot = lax.broadcasted_iota(jnp.int32, (GLOBALS, ROWS), 0).astype(F32)
    member = meta_row_ref[10:11] == slot
    for h in range(OWN_HEADS):
        query = qkv_ref[h, ROWS:]
        scores = nt(query, qkv_ref[OWN_HEADS + h, :ROWS]) * SCORE_SCALE
        scores = jnp.where(member, scores, MASKED)
        own = nt(query, qkv_ref[OWN_HEADS + h, ROWS:]) * SCORE_SCALE
        top = jnp.maximum(
            jnp.max(scores, axis=-1, keepdims=True), jnp.max(own, axis=-1, keepdims=True)
        )
        prob = jnp.exp(scores - top)
        own_prob = jnp.exp(own - top)
        total = jnp.sum(prob, axis=-1, keepdims=True) + jnp.sum(own_prob, axis=-1, keepdims=True)
        inverse = 1.0 / total
        prob = prob * inverse
        own_prob = own_prob * inverse
        member_ref[h] = prob
        self_ref[h] = own_prob
        mixed = nn(prob.astype(BF), qkv_ref[2 * OWN_HEADS + h, :ROWS]) + nn(
            own_prob.astype(BF), qkv_ref[2 * OWN_HEADS + h, ROWS:]
        )
        glob_att_ref[h] = mixed
        attn_ref[ROWS:, h * HEAD_DIM : (h + 1) * HEAD_DIM] = mixed.astype(BF)


def feed_kernel(
    me_ref, att_a, att_b, att_c, att_d, cot_a, cot_b, cot_c, cot_d, cot_glob_ref, super_ref,
    glob_ref, w_out_ref, w_up_ref, w_down_ref, bias_ref, gain_ref, shift_ref,
    y_ref, normed_ref, hidden_ref, d_pre_ref, cot_ref, out_ref, back_ref, d_bias_ref, cot_sum_ref,
):
    me = me_ref[0]
    for k, cot in enumerate((cot_a, cot_b, cot_c, cot_d)):
        cot_ref[pl.ds(pl.multiple_of((me ^ k) * TOK, TOK), TOK)] = cot[...]
    cot_ref[ROWS:] = cot_glob_ref[...]
    gain, shift, bias = gain_ref[...], shift_ref[...], bias_ref[...]
    d_bias = jnp.zeros((1, FF_OWN), F32)
    cot_sum = jnp.zeros((1, D), F32)
    tile = 192
    for low in range(0, ALL, tile):
        rows = slice(low, low + tile)
        if low + tile <= ROWS:
            y_rows = super_ref[rows]
        else:
            y_rows = jnp.concatenate([super_ref[low:], glob_ref[...].astype(F32)], axis=0)
        for k, att in enumerate((att_a, att_b, att_c, att_d)):
            y_rows = y_rows + nn(att[rows], w_out_ref[pl.ds(pl.multiple_of((me ^ k) * OWN, OWN), OWN)])
        y_ref[rows] = y_rows
        normed = (row_stats(y_rows)[0] * gain + shift).astype(BF)
        normed_ref[rows] = normed
        hidden, slope = gelu_parts(nn(normed, w_up_ref[...]) + bias)
        hidden = hidden.astype(BF)
        hidden_ref[rows] = hidden
        cot = cot_ref[rows]
        cot_sum = cot_sum + jnp.sum(cot.astype(F32), axis=0, keepdims=True)
        d_pre = (nt(cot, w_down_ref[...]) * slope).astype(BF)
        d_pre_ref[rows] = d_pre
        d_bias = d_bias + jnp.sum(d_pre.astype(F32), axis=0, keepdims=True)
        out_part = nn(hidden, w_down_ref[...]).astype(BF)
        back_part = nt(d_pre, w_up_ref[...]).astype(BF)
        for ref, part in ((out_ref, out_part), (back_ref, back_part)):
            spot = low
            while spot < low + tile:
                if spot < ROWS:
                    b, inner = spot // TOK, spot % TOK
                    count = min(TOK - inner, low + tile - spot)
                    ref[b, inner : inner + count] = part[spot - low : spot - low + count]
                else:
                    b, count = (spot - ROWS) // GLOB_OWN, GLOB_OWN
                    ref[b, TOK:] = part[spot - low : spot - low + count]
                spot = spot + count
    d_bias_ref[...] = d_bias
    cot_sum_ref[...] = cot_sum


def back_kernel(
    me_ref, back_a, back_b, back_c, back_d, y_ref, cot_ref, w_out_ref, gain_ref,
    qkv_ref, meta_col_ref, meta_row_ref, rich_q_ref, rich_k_ref, prob_ref, glob_prob_ref,
    member_ref, self_ref, glob_att_ref, rich_qt_ref, rich_kt_ref,
    d_y_ref, d_proj_ref, d_qkv_ref, vec_ref, grad_rich_ref,
    keys, values, key_rich, meta_pad, d_norm, d_att, d_keys, d_values, d_key_rich, d_query_rich,
):
    me = me_ref[0]
    for k, back in enumerate((back_a, back_b, back_c, back_d)):
        at = me ^ k
        d_norm[pl.ds(pl.multiple_of(at * TOK, TOK), TOK)] = back[:TOK]
        d_norm[pl.ds(pl.multiple_of(ROWS + at * GLOB_OWN, GLOB_OWN), GLOB_OWN)] = back[TOK:]
    gain = gain_ref[...]
    d_gain = jnp.zeros((1, D), F32)
    d_shift = jnp.zeros((1, D), F32)
    for low in range(0, ALL, 192):
        rows = slice(low, low + 192)
        d_rows, gain_part, shift_part = norm_back(d_norm[rows].astype(F32), gain, y_ref[rows])
        d_rows = cot_ref[rows].astype(F32) + d_rows
        d_y_ref[rows] = d_rows
        d_proj = d_rows.astype(BF)
        d_proj_ref[rows] = d_proj
        d_gain = d_gain + gain_part
        d_shift = d_shift + shift_part
        projected = nt(d_proj, w_out_ref[...]).astype(BF)
        for h in range(OWN_HEADS):
            d_att[h, rows] = projected[:, h * HEAD_DIM : (h + 1) * HEAD_DIM]
    vec_ref[...] = jnp.zeros((8, D), F32)
    vec_ref[0:1] = d_gain
    vec_ref[1:2] = d_shift

    edge = jnp.zeros((OWN_HEADS, RADIUS, HEAD_DIM), BF)
    for held, first in ((keys, OWN_HEADS), (values, 2 * OWN_HEADS)):
        held[:, :RADIUS] = edge
        held[:, RADIUS + ROWS :] = edge
        held[:, RADIUS : RADIUS + ROWS] = qkv_ref[first : first + OWN_HEADS, :ROWS]
    meta_pad[...] = jnp.zeros((16, PAD), F32)
    meta_pad[:, RADIUS : RADIUS + ROWS] = meta_row_ref[...]
    for h in range(OWN_HEADS):
        key_rich[h] = nt(rich_k_ref[h], keys[h])
    d_keys[...] = jnp.zeros((OWN_HEADS, PAD, HEAD_DIM), F32)
    d_values[...] = jnp.zeros((OWN_HEADS, PAD, HEAD_DIM), F32)
    d_key_rich[...] = jnp.zeros((OWN_HEADS, 8, PAD), F32)
    glob_key = [qkv_ref[OWN_HEADS + h, ROWS:] for h in range(OWN_HEADS)]
    glob_value = [qkv_ref[2 * OWN_HEADS + h, ROWS:] for h in range(OWN_HEADS)]

    def block(b, carry):
        start = pl.multiple_of(b * TOK, TOK)
        rows = pl.ds(start, TOK)
        window = pl.ds(start, WIN)
        terms = pair_terms(meta_col_ref[rows], meta_pad[:, window])
        carry = list(carry)
        for h in range(OWN_HEADS):
            query = qkv_ref[h, rows]
            d_out = d_att[h, rows]
            prob = prob_ref[h, rows]
            glob_prob = glob_prob_ref[h, rows]
            d_prob = nt(d_out, values[h, window])
            d_glob_prob = nt(d_out, glob_value[h])
            delta = jnp.sum(prob * d_prob, axis=-1, keepdims=True) + jnp.sum(
                glob_prob * d_glob_prob, axis=-1, keepdims=True
            )
            d_scores = prob * (d_prob - delta)
            d_low = d_scores.astype(BF)
            d_glob_low = (glob_prob * (d_glob_prob - delta)).astype(BF)
            query_rich = nn(query, rich_q_ref[h])
            right = key_rich[h, :, window]
            lefts = []
            for c, (before, distance) in enumerate(terms):
                logit = query_rich[:, c : c + 1] + right[c : c + 1]
                pulled = jnp.where(before, 0.5, -0.5) - 0.5 * jnp.tanh(0.5 * logit)
                pulled = d_scores * pulled
                off = distance - (query_rich[:, 2 + c : 3 + c] + right[2 + c : 3 + c])
                off = d_scores * off
                lefts.append((c, jnp.sum(pulled, axis=-1, keepdims=True)))
                lefts.append((2 + c, jnp.sum(off, axis=-1, keepdims=True)))
                d_key_rich[h, c : c + 1, window] += jnp.sum(pulled, axis=0, keepdims=True)
                d_key_rich[h, 2 + c : 3 + c, window] += jnp.sum(off, axis=0, keepdims=True)
            lane = lax.broadcasted_iota(jnp.int32, (TOK, 8), 1)
            d_left = jnp.zeros((TOK, 8), F32)
            d_query = (nn(d_low, keys[h, window]) + nn(d_glob_low, glob_key[h])) * SCORE_SCALE
            for c, column in lefts:
                d_left = jnp.where(lane == c, column, d_left)
                d_query = d_query + column * rich_qt_ref[h, c : c + 1]
            d_query_rich[h, rows] = d_left
            d_qkv_ref[rows, h * HEAD_DIM : (h + 1) * HEAD_DIM] = d_query.astype(BF)
            d_keys[h, window] += tn(d_low, query) * SCORE_SCALE
            d_values[h, window] += tn(prob.astype(BF), d_out)
            carry[2 * h] = carry[2 * h] + tn(d_glob_low, query) * SCORE_SCALE
            carry[2 * h + 1] = carry[2 * h + 1] + tn(glob_prob.astype(BF), d_out)
        return tuple(carry)

    zero = jnp.zeros((GLOBALS, HEAD_DIM), F32)
    sums = lax.fori_loop(0, SEQ_WAYS, block, (zero,) * (2 * OWN_HEADS))
    for h in range(OWN_HEADS):
        span = slice(h * HEAD_DIM, (h + 1) * HEAD_DIM)
        key_span = slice(OWN + h * HEAD_DIM, OWN + (h + 1) * HEAD_DIM)
        value_span = slice(2 * OWN + h * HEAD_DIM, 2 * OWN + (h + 1) * HEAD_DIM)
        query = qkv_ref[h, ROWS:]
        key_rows = qkv_ref[OWN_HEADS + h, :ROWS]
        value_rows = qkv_ref[2 * OWN_HEADS + h, :ROWS]
        d_out = d_att[h, ROWS:]
        delta = jnp.sum(d_out.astype(F32) * glob_att_ref[h], axis=-1, keepdims=True)
        prob, own_prob = member_ref[h], self_ref[h]
        d_low = (prob * (nt(d_out, value_rows) - delta)).astype(BF)
        d_own = (own_prob * (nt(d_out, glob_value[h]) - delta)).astype(BF)
        d_query = (nn(d_low, key_rows) + nn(d_own, glob_key[h])) * SCORE_SCALE
        d_qkv_ref[ROWS:, span] = d_query.astype(BF)
        d_qkv_ref[ROWS:, key_span] = (sums[2 * h] + tn(d_own, query) * SCORE_SCALE).astype(BF)
        d_qkv_ref[ROWS:, value_span] = (sums[2 * h + 1] + tn(own_prob.astype(BF), d_out)).astype(BF)
        d_right = d_key_rich[h, :, RADIUS : RADIUS + ROWS]
        d_key = d_keys[h, RADIUS : RADIUS + ROWS] + tn(d_low, query) * SCORE_SCALE
        d_key = d_key + lax.dot_general(
            d_right, rich_kt_ref[h], (((0,), (0,)), ((), ())), precision=PRECISE,
            preferred_element_type=F32,
        )
        d_value = d_values[h, RADIUS : RADIUS + ROWS] + tn(prob.astype(BF), d_out)
        d_qkv_ref[:ROWS, key_span] = d_key.astype(BF)
        d_qkv_ref[:ROWS, value_span] = d_value.astype(BF)
        grad_rich_ref[h] = tn(d_query_rich[h].astype(BF), qkv_ref[h, :ROWS])
        grad_rich_ref[OWN_HEADS + h] = nn(d_right.astype(BF), key_rows)


def last_kernel(
    me_ref, dqkv_a, dqkv_b, dqkv_c, dqkv_d, w_qkv_ref, super_ref, glob_ref, d_y_ref, pre_ref,
    w_graph_ref, meta_col_ref, gain_ref,
    grad_tok_ref, grad_glob_ref, d_pre_ref, vec_ref, d_super,
):
    me = me_ref[0]
    gain = gain_ref[...]
    d_gain = jnp.zeros((1, D), F32)
    d_shift = jnp.zeros((1, D), F32)
    for low in range(0, ALL, 192):
        rows = slice(low, low + 192)
        inner = min(192, ROWS - low)
        d_norm = None
        for k, part in enumerate((dqkv_a, dqkv_b, dqkv_c, dqkv_d)):
            term = nt(part[rows], w_qkv_ref[me ^ k])
            d_norm = term if d_norm is None else d_norm + term
        if inner == 192:
            rows_in = super_ref[rows]
        else:
            rows_in = jnp.concatenate([super_ref[low:], glob_ref[...].astype(F32)], axis=0)
        back, gain_part, shift_part = norm_back(d_norm, gain, rows_in)
        d_gain = d_gain + gain_part
        d_shift = d_shift + shift_part
        back = back + d_y_ref[rows]
        d_super[rows] = back
        long = slice(low, low + inner)
        slope = gelu_parts(pre_ref[long])[1]
        d_pre_ref[long] = (back[:inner] * slope).astype(BF)
    grad_glob_ref[...] = d_super[ROWS:]
    vec_ref[...] = jnp.zeros((8, D), F32)
    vec_ref[0:1] = d_gain
    vec_ref[1:2] = d_shift
    total = d_super[pl.ds(pl.multiple_of(me * TOK, TOK), TOK)]
    for shift in (-1, 0, 1):
        b = me - shift
        fits = (b >= 0) & (b < SEQ_WAYS)
        rows = pl.ds(pl.multiple_of(jnp.clip(b, 0, SEQ_WAYS - 1) * TOK, TOK), TOK)
        d_agg = (nt(d_pre_ref[rows], w_graph_ref[...]) * (1.0 / NEIGH)).astype(BF)
        neigh = meta_col_ref[rows].astype(jnp.int32)
        counts = counts_of(neigh, (shift + 1) * TOK, TOK)
        total = total + jnp.where(fits, tn(counts, d_agg), 0.0)
    grad_tok_ref[...] = total


def call(kernel, ins, outs, scratch=(), flops=0, moved=0, scalars=1):
    specs = [pl.BlockSpec(memory_space=pltpu.SMEM)] * scalars
    specs += [pl.BlockSpec(memory_space=pltpu.VMEM)] * (len(ins) - scalars)
    return pl.pallas_call(
        kernel,
        out_shape=[jax.ShapeDtypeStruct(shape, kind) for shape, kind in outs],
        in_specs=specs,
        out_specs=[pl.BlockSpec(memory_space=pltpu.VMEM)] * len(outs),
        scratch_shapes=[pltpu.VMEM(shape, kind) for shape, kind in scratch],
        compiler_params=pltpu.CompilerParams(vmem_limit_bytes=48 * 1024 * 1024),
        cost_estimate=pl.CostEstimate(flops=flops, bytes_accessed=moved, transcendentals=0),
    )(*ins)


def split_heads(
    tokens, global_tokens, neighbours, token_ranks, membership, w_graph, gain_one, shift_one,
    w_query, w_key, w_value, rich_query, rich_key, w_out, gain_two, shift_two, w_up, bias_up,
    w_down, bias_down, cot_tokens, cot_global,
):
    me = lax.axis_index("seq")
    me_arr = me.reshape(1).astype(jnp.int32)
    ints = jnp.concatenate([neighbours, token_ranks.T, membership[:, None]], axis=1)
    ints = jnp.pad(ints, ((0, 0), (0, 128 - ints.shape[1])))
    tok_blocks = gather_seq(tokens)
    int_blocks = gather_seq(ints)
    cot_blocks = gather_seq(cot_tokens)

    def own_columns(weight, width):
        return lax.dynamic_slice_in_dim(weight, me * width, width, axis=1)

    def row(vector):
        return vector.reshape(1, -1)

    w_all = jnp.stack([w.reshape(D, SEQ_WAYS, OWN) for w in (w_query, w_key, w_value)], axis=2)
    w_all = w_all.transpose(1, 0, 2, 3).reshape(SEQ_WAYS, D, 3 * OWN)
    w_qkv = pick(w_all, me)
    w_up_own = own_columns(w_up, FF_OWN)
    w_down_own = lax.dynamic_slice_in_dim(w_down, me * FF_OWN, FF_OWN, axis=0)
    w_out_own = lax.dynamic_slice_in_dim(w_out, me * OWN, OWN, axis=0)
    bias_own = row(lax.dynamic_slice_in_dim(bias_up, me * FF_OWN, FF_OWN, axis=0))

    def own_rich(rich):
        rich = own_columns(rich, 4 * OWN_HEADS).reshape(HEAD_DIM, OWN_HEADS, 4)
        return rich.transpose(1, 0, 2)

    rich_q_own, rich_k_own = own_rich(rich_query), own_rich(rich_key)
    rich_q_in = jnp.pad(rich_q_own, ((0, 0), (0, 0), (0, 124)))
    rich_kt = jnp.pad(rich_k_own.transpose(0, 2, 1), ((0, 0), (0, 4), (0, 0)))
    rich_qt = jnp.pad(rich_q_own.transpose(0, 2, 1), ((0, 0), (0, 4), (0, 0)))

    agg, graph_pre, super_rows, normed, qkv, meta_col, meta_row = call(
        graph_kernel,
        [me_arr, *tok_blocks, *int_blocks, global_tokens, w_graph, w_qkv, row(gain_one), row(shift_one)],
        [((ROWS, D), BF), ((ROWS, D), F32), ((ROWS, D), F32), ((ALL, D), BF),
         ((3 * OWN_HEADS, ALL, HEAD_DIM), BF), ((ROWS, 128), F32), ((16, ROWS), F32)],
        [((PAD, D), BF)],
        flops=1_500_000_000, moved=9_000_000,
    )
    heads_scratch = [
        ((OWN_HEADS, PAD, HEAD_DIM), BF), ((OWN_HEADS, PAD, HEAD_DIM), BF),
        ((OWN_HEADS, 8, PAD), F32), ((16, PAD), F32),
    ]
    attn, prob, glob_prob, member_prob, self_prob, glob_att = call(
        attend_kernel,
        [qkv, meta_col, meta_row, rich_q_in, rich_kt],
        [((ALL, OWN), BF), ((OWN_HEADS, ROWS, WIN), F32), ((OWN_HEADS, ROWS, GLOBALS), F32),
         ((OWN_HEADS, GLOBALS, ROWS), F32), ((OWN_HEADS, GLOBALS, GLOBALS), F32),
         ((OWN_HEADS, GLOBALS, HEAD_DIM), F32)],
        heads_scratch,
        flops=4_000_000_000, moved=6_000_000, scalars=0,
    )
    att_blocks = gather_seq(attn)
    y_rows, normed_two, hidden, d_pre, cot_all, out_parts, back_parts, d_bias_up, cot_sum = call(
        feed_kernel,
        [me_arr, *att_blocks, *cot_blocks, cot_global, super_rows, global_tokens, w_out, w_up_own,
         w_down_own, bias_own, row(gain_two), row(shift_two)],
        [((ALL, D), F32), ((ALL, D), BF), ((ALL, FF_OWN), BF), ((ALL, FF_OWN), BF), ((ALL, D), BF),
         ((SEQ_WAYS, CHUNK, D), BF), ((SEQ_WAYS, CHUNK, D), BF), ((1, FF_OWN), F32), ((1, D), F32)],
        flops=4_000_000_000, moved=12_000_000,
    )
    back_blocks = gather_seq(scatter_seq(back_parts).astype(BF))
    grad_down = tn(hidden, cot_all).astype(BF).reshape(GRP_WAYS, FF_OWN // GRP_WAYS, D)
    grad_up = rows_to_chunks(tn(normed_two, d_pre).astype(BF))
    down_sum = gather_grp(reduce_grp(grad_down))
    up_sum = gather_grp(turned_reduce(grad_up))
    out_own = scatter_seq(out_parts)
    own_start = me * TOK
    glob_start = ROWS + me * GLOB_OWN
    out_tokens = (
        lax.dynamic_slice_in_dim(y_rows, own_start, TOK, 0) + out_own[:TOK] + bias_down
    ).astype(BF)
    out_glob = (
        lax.dynamic_slice_in_dim(y_rows, glob_start, GLOB_OWN, 0) + out_own[TOK:] + bias_down
    ).astype(BF)
    out_global = jnp.stack(gather_seq(out_glob))[jnp.arange(SEQ_WAYS) ^ me].reshape(GLOBALS, D)

    d_y, d_proj, d_qkv, vec_two, grad_rich = call(
        back_kernel,
        [me_arr, *back_blocks, y_rows, cot_all, w_out_own, row(gain_two), qkv, meta_col, meta_row,
         rich_q_in, rich_kt, prob, glob_prob, member_prob, self_prob, glob_att,
         rich_qt.astype(F32), rich_kt.astype(F32)],
        [((ALL, D), F32), ((ALL, D), BF), ((ALL, 3 * OWN), BF), ((8, D), F32),
         ((2 * OWN_HEADS, 8, HEAD_DIM), F32)],
        heads_scratch + [
            ((ALL, D), BF), ((OWN_HEADS, ALL, HEAD_DIM), BF), ((OWN_HEADS, PAD, HEAD_DIM), F32),
            ((OWN_HEADS, PAD, HEAD_DIM), F32), ((OWN_HEADS, 8, PAD), F32),
            ((OWN_HEADS, ROWS, 8), F32),
        ],
        flops=6_000_000_000, moved=14_000_000,
    )
    d_qkv_blocks = gather_seq(d_qkv)
    grad_qkv = rows_to_chunks(tn(normed, d_qkv).astype(BF))
    qkv_sum = gather_grp(turned_reduce(grad_qkv))
    grad_out = tn(attn, d_proj)
    own_bits = [
        lax.dynamic_slice_in_dim(vector, me * OWN, OWN, 0)
        for vector in (vec_two[0], vec_two[1], cot_sum[0])
    ]
    small = jnp.concatenate([*own_bits, d_bias_up[0], grad_rich[:, :4].reshape(-1)])
    out_sum = gather_grp(reduce_grp(with_small(grad_out, small)))

    grad_tokens, grad_global, d_graph_pre, vec_one = call(
        last_kernel,
        [me_arr, *d_qkv_blocks, w_all, super_rows, global_tokens, d_y, graph_pre, w_graph, meta_col,
         row(gain_one)],
        [((TOK, D), F32), ((GLOBALS, D), F32), ((ROWS, D), BF), ((8, D), F32)],
        [((ALL, D), F32)],
        flops=4_000_000_000, moved=12_000_000,
    )
    grad_graph = tn(own_columns(agg, OWN), d_graph_pre)
    small_last = jnp.concatenate(
        [lax.dynamic_slice_in_dim(vector, me * OWN, OWN, 0) for vector in (vec_one[0], vec_one[1])]
    )
    graph_sum = gather_grp(reduce_grp(with_small(grad_graph, small_last)))

    g_down = down_sum.astype(F32).reshape(FF_OWN, D)
    g_up = chunks_to_rows(up_sum, FF_OWN)
    g_qkv = chunks_to_rows(qkv_sum, 3 * OWN).reshape(OWN, SEQ_WAYS, 3, OWN)
    g_query, g_key, g_value = (g_qkv[:, :, i].reshape(OWN, D) for i in range(3))
    g_out = out_sum[:, :24].astype(F32).reshape(OWN, D)
    g_graph = graph_sum[:, :24].astype(F32).reshape(OWN, D)
    bits = out_sum[0, 24:].astype(F32).reshape(-1)
    last_bits = graph_sum[0, 24:].astype(F32).reshape(-1)
    g_gain_two, g_shift_two, g_bias_down = (bits[i * OWN : (i + 1) * OWN] for i in range(3))
    g_bias_up = bits[3 * OWN : 3 * OWN + FF_OWN]
    rich = bits[3 * OWN + FF_OWN :][: 2 * OWN_HEADS * 4 * HEAD_DIM]
    rich = rich.reshape(8, -1).astype(BF)
    rich = jnp.stack(gather_seq(rich))[jnp.arange(SEQ_WAYS) ^ me]
    rich = rich.reshape(SEQ_WAYS, 2, OWN_HEADS, 4, HEAD_DIM).transpose(1, 4, 0, 2, 3)
    rich = rich.reshape(2, HEAD_DIM, 4 * HEADS).astype(F32)
    rich = lax.dynamic_slice_in_dim(rich, me * (HEAD_DIM // SEQ_WAYS), HEAD_DIM // SEQ_WAYS, 1)
    return (
        out_tokens, out_global, grad_tokens, grad_global,
        g_graph, last_bits[:OWN], last_bits[OWN : 2 * OWN], g_query, g_key, g_value, rich[0], rich[1],
        g_out, g_gain_two, g_shift_two, g_up, g_bias_up, g_down, g_bias_down,
    )


def rows_to_chunks(grad):
    part = D // SEQ_WAYS // GRP_WAYS
    grad = grad.reshape(SEQ_WAYS, GRP_WAYS, part, grad.shape[1]).transpose(1, 0, 2, 3)
    return grad.reshape(GRP_WAYS, SEQ_WAYS * part, grad.shape[3])


def turned_reduce(chunks):
    mine = reduce_grp(chunks).astype(BF)
    part = D // SEQ_WAYS // GRP_WAYS
    return turn_seq(mine.reshape(SEQ_WAYS, part, mine.shape[1])).reshape(mine.shape)


def chunks_to_rows(chunks, width):
    part = D // SEQ_WAYS // GRP_WAYS
    chunks = chunks.reshape(GRP_WAYS, SEQ_WAYS, part, width).transpose(0, 2, 1, 3)
    return chunks.reshape(GRP_WAYS * part, SEQ_WAYS * width).astype(F32)


def with_small(grad, small):
    part = D // SEQ_WAYS // GRP_WAYS
    grad = grad.astype(BF).reshape(GRP_WAYS, part, D)
    small = jnp.pad(small.astype(BF), (0, 8 * D - small.shape[0])).reshape(1, 8, D)
    return jnp.concatenate([grad, jnp.broadcast_to(small, (GRP_WAYS, 8, D))], axis=1)


def layer(*arrays):
    tokens, global_tokens = arrays[:2]
    ways = (lax.axis_size("seq"), lax.axis_size("grp"))
    if ways == (SEQ_WAYS, GRP_WAYS) and tokens.shape[0] == TOK and global_tokens.shape[0] == GLOBALS:
        return split_heads(*arrays)
    return local(*arrays)


def solution(mesh):
    return jax.shard_map(
        layer,
        mesh=mesh,
        in_specs=(
            P(("grp", "seq"), None),
            P("grp", None),
            P(("grp", "seq"), None),
            P(None, ("grp", "seq")),
            P(("grp", "seq")),
            P(),
            P(),
            P(),
            P(),
            P(),
            P(),
            P(),
            P(),
            P(),
            P(),
            P(),
            P(),
            P(),
            P(),
            P(),
            P(("grp", "seq"), None),
            P("grp", None),
        ),
        out_specs=(
            P(("grp", "seq"), None),
            P("grp", None),
            P(("grp", "seq"), None),
            P("grp", None),
            P("seq", None),
            P("seq"),
            P("seq"),
            P("seq", None),
            P("seq", None),
            P("seq", None),
            P("seq", None),
            P("seq", None),
            P("seq", None),
            P("seq"),
            P("seq"),
            P("seq", None),
            P("seq"),
            P("seq", None),
            P("seq"),
        ),
        check_vma=False,
    )
```

```python
import functools
import math

import jax
import jax.numpy as jnp
from jax import lax
from jax.experimental import pallas as pl
from jax.experimental.pallas import tpu as pltpu
from jax.sharding import PartitionSpec as P

D = 768
HEADS = 12
HEAD_DIM = 64
RADIUS = 128
GLOBALS = 64
NEIGH = 8
SEQ_TOKENS = 2048


EPSILON = 1e-05
PRECISE = lax.Precision.HIGHEST
MASKED = -1e30


def with_halo(cells, sides, width):
    for axis, dim in sides:
        count = lax.axis_size(axis)
        ends = count - 1
        head = lax.slice_in_dim(cells, 0, width, axis=dim)
        tail = lax.slice_in_dim(cells, cells.shape[dim] - width, cells.shape[dim], axis=dim)
        cells = jnp.concatenate(
            [
                lax.ppermute(tail, axis, [(i, (i + 1) % count) for i in range(ends)]),
                cells,
                lax.ppermute(head, axis, [((i + 1) % count, i) for i in range(ends)]),
            ],
            axis=dim,
        )
    return cells


def joined(array, axis, combine):
    everything = jax.tree.map(
        lambda part, kind: lax.all_gather(part.astype(kind), axis),
        array,
        (jnp.bfloat16, jnp.bfloat16, jnp.bfloat16),
    )

    def take(k):
        return jax.tree.map(lambda part, own: part[k].astype(own.dtype), everything, array)

    return lax.fori_loop(
        1, lax.axis_size(axis), lambda k, so_far: combine(so_far, take(k)), take(0)
    )


def shifted(block, axis, distance):
    devices = range(lax.axis_size(axis))
    route = [(i - distance, i) for i in devices if i - distance in devices]
    return lax.ppermute(block, axis, route)


def layer_norm(rows_in, gain_in, shift_in):
    row_mean = jnp.mean(rows_in, axis=-1, keepdims=True)
    centred = rows_in - row_mean
    variance = jnp.mean(centred * centred, axis=-1, keepdims=True)
    return centred * lax.rsqrt(variance + EPSILON) * gain_in + shift_in


def rich_part(a_block, b_window, rank_query, rank_key, log_norm):
    combined = None
    for coordinate in range(2):
        order_flag = (rank_query[coordinate][:, None] < rank_key[coordinate][None, :]).astype(
            jnp.float32
        )
        distance = (
            jnp.log1p(
                jnp.abs(rank_query[coordinate][:, None] - rank_key[coordinate][None, :]).astype(
                    jnp.float32
                )
            )
            / log_norm
        )
        order_logit = a_block[:, :, None, coordinate] + b_window[:, None, :, coordinate]
        centre = a_block[:, :, None, 2 + coordinate] + b_window[:, None, :, 2 + coordinate]
        pair_term = (
            order_flag * jax.nn.log_sigmoid(order_logit)
            + (1.0 - order_flag) * jax.nn.log_sigmoid(-order_logit)
            - 0.5 * (distance - centre) ** 2
        )
        combined = pair_term if combined is None else combined + pair_term
    return combined


def product(left, right):
    return jnp.dot(left, right, preferred_element_type=jnp.float32)


def product_left(left, right):
    return jnp.einsum("ta,tb->ab", left, right, preferred_element_type=jnp.float32)


def product_right(left, right):
    return jnp.einsum("tb,ab->ta", left, right, preferred_element_type=jnp.float32)


def local(
    tokens,
    global_tokens,
    neighbours,
    token_ranks,
    membership,
    w_graph,
    gain_one,
    shift_one,
    w_query,
    w_key,
    w_value,
    rich_query,
    rich_key,
    w_out,
    gain_two,
    shift_two,
    w_up,
    bias_up,
    w_down,
    bias_down,
    cot_tokens,
    cot_global,
):
    tok_count = tokens.shape[0]
    seq_count = lax.axis_size("seq")
    seq_index = lax.axis_index("seq")
    seq_len = min(SEQ_TOKENS, tok_count * seq_count)
    span = seq_len // tok_count
    group_seqs = global_tokens.shape[0] // GLOBALS
    seq_slot = seq_index // span
    seq_local = seq_index % span
    slot_flag = (jnp.arange(group_seqs, dtype=jnp.int32) == seq_slot).astype(jnp.float32)
    log_norm = math.log(1.0 + seq_len)
    score_scale = 1.0 / math.sqrt(HEAD_DIM)
    block_rows = min(512, tok_count)
    window = block_rows + 2 * RADIUS
    ext_count = tok_count + 2 * RADIUS
    first_flag = (seq_index == 0).astype(jnp.float32)
    own_pos = seq_local * tok_count + jnp.arange(tok_count, dtype=jnp.int32)
    ext_pos = seq_local * tok_count - RADIUS + jnp.arange(ext_count, dtype=jnp.int32)
    key_valid = (ext_pos >= 0) & (ext_pos < seq_len)

    def own_slot(array_in):
        return lax.dynamic_index_in_dim(array_in, seq_slot, 0, keepdims=False)

    def to_slots(array_in):
        return slot_flag.reshape((group_seqs,) + (1,) * array_in.ndim) * array_in[None]

    token_ext = with_halo(tokens, (("seq", 0),), RADIUS)
    token_ext = jnp.where(key_valid[:, None], token_ext, jnp.zeros_like(token_ext))
    flat_index = neighbours.reshape(-1)
    gathered = (
        jnp.take(token_ext, flat_index, axis=0).astype(jnp.float32).reshape(tok_count, NEIGH, D)
    )
    agg_low = jnp.mean(gathered, axis=1).astype(jnp.bfloat16)
    graph_pre = product(agg_low, w_graph)
    graph_out, graph_back = jax.vjp(jax.nn.gelu, graph_pre)
    super_rows = tokens.astype(jnp.float32) + graph_out
    normed_full, norm_back = jax.vjp(layer_norm, super_rows, gain_one, shift_one)
    normed = normed_full.astype(jnp.bfloat16)
    glob_in = global_tokens.astype(jnp.float32)
    glob_normed_full, glob_norm_back = jax.vjp(layer_norm, glob_in, gain_one, shift_one)
    glob_normed = glob_normed_full.astype(jnp.bfloat16)
    query = product(normed, w_query).astype(jnp.bfloat16)
    key_own = product(normed, w_key).astype(jnp.bfloat16)
    value_own = product(normed, w_value).astype(jnp.bfloat16)
    glob_query = (
        product(glob_normed, w_query)
        .astype(jnp.bfloat16)
        .reshape(group_seqs, GLOBALS, HEADS, HEAD_DIM)
    )
    glob_key = (
        product(glob_normed, w_key)
        .astype(jnp.bfloat16)
        .reshape(group_seqs, GLOBALS, HEADS, HEAD_DIM)
    )
    glob_value = (
        product(glob_normed, w_value)
        .astype(jnp.bfloat16)
        .reshape(group_seqs, GLOBALS, HEADS, HEAD_DIM)
    )
    glob_query_own = own_slot(glob_query)
    glob_key_own = own_slot(glob_key)
    glob_value_own = own_slot(glob_value)
    kv_ext = with_halo(jnp.concatenate([key_own, value_own], axis=1), (("seq", 0),), RADIUS)
    key_ext = kv_ext[:, :D].reshape(ext_count, HEADS, HEAD_DIM)
    value_ext = kv_ext[:, D:].reshape(ext_count, HEADS, HEAD_DIM)
    rank_ext = with_halo(token_ranks, (("seq", 1),), RADIUS)
    rich_q3 = rich_query.reshape(HEAD_DIM, HEADS, 4)
    rich_k3 = rich_key.reshape(HEAD_DIM, HEADS, 4)
    query_heads = query.reshape(tok_count, HEADS, HEAD_DIM)
    a_rows = jnp.einsum("the,ehc->htc", query_heads, rich_q3, preferred_element_type=jnp.float32)
    b_ext = jnp.einsum("the,ehc->htc", key_ext, rich_k3, preferred_element_type=jnp.float32)

    def block_scores():

        def rich_scores(left_rows, right_rows):
            return rich_part(left_rows, right_rows, token_ranks, rank_ext, log_norm)

        rich_vals, rich_back = jax.vjp(rich_scores, a_rows, b_ext)
        raw_scores = (
            jnp.einsum("qhe,khe->hqk", query_heads, key_ext, preferred_element_type=jnp.float32)
            * score_scale
        )
        pos_gap = own_pos[:, None] - ext_pos[None, :]
        key_mask = (jnp.abs(pos_gap) <= RADIUS) & key_valid[None, :]
        scores = jnp.where(key_mask[None], raw_scores + rich_vals, MASKED)
        glob_scores = (
            jnp.einsum(
                "qhe,ghe->hqg", query_heads, glob_key_own, preferred_element_type=jnp.float32
            )
            * score_scale
        )
        return (scores, glob_scores, rich_back, query_heads, key_ext)

    scored = block_scores()
    scores = scored[0]
    glob_scores = scored[1]
    row_top = jnp.maximum(jnp.max(scores, axis=-1), jnp.max(glob_scores, axis=-1))
    row_denom = jnp.sum(jnp.exp(scores - row_top[..., None]), axis=-1) + jnp.sum(
        jnp.exp(glob_scores - row_top[..., None]), axis=-1
    )
    log_total = row_top + jnp.log(row_denom)
    prob_rows = jnp.exp(scores - log_total[..., None]).astype(jnp.bfloat16)
    glob_probs = jnp.exp(glob_scores - log_total[..., None]).astype(jnp.bfloat16)
    attn_block = jnp.einsum(
        "hqk,khe->qhe", prob_rows, value_ext, preferred_element_type=jnp.float32
    ) + jnp.einsum("hqg,ghe->qhe", glob_probs, glob_value_own, preferred_element_type=jnp.float32)
    attn_parts = attn_block.reshape(block_rows, D)
    attn_rows = attn_parts.astype(jnp.bfloat16)
    member_mask = membership[None, :] == jnp.arange(GLOBALS, dtype=jnp.int32)[:, None]
    key_heads = key_ext[RADIUS : RADIUS + tok_count]
    value_heads = value_ext[RADIUS : RADIUS + tok_count]
    member_raw = (
        jnp.einsum("ghe,the->ght", glob_query_own, key_heads, preferred_element_type=jnp.float32)
        * score_scale
    )
    member_scores = jnp.where(member_mask[:, None, :], member_raw, MASKED)
    local_top = jnp.max(member_scores, axis=-1)
    member_exp = jnp.where(
        member_mask[:, None, :], jnp.exp(member_scores - local_top[..., None]), 0.0
    )
    local_sum = jnp.sum(member_exp, axis=-1)
    local_acc = jnp.einsum(
        "ght,the->ghe", member_exp, value_heads.astype(jnp.float32), precision=PRECISE
    )
    slot_top = jnp.where(slot_flag[:, None, None] > 0.5, local_top[None], MASKED)
    slot_sum = to_slots(local_sum)
    slot_acc = to_slots(local_acc)

    def combine_softmax(first_part, second_part):
        top_one, sum_one, acc_one = first_part
        top_two, sum_two, acc_two = second_part
        top_both = jnp.maximum(top_one, top_two)
        scale_one = jnp.exp(top_one - top_both)
        scale_two = jnp.exp(top_two - top_both)
        return (
            top_both,
            sum_one * scale_one + sum_two * scale_two,
            acc_one * scale_one[..., None] + acc_two * scale_two[..., None],
        )

    merged_top, merged_sum, merged_acc = joined(
        (slot_top, slot_sum, slot_acc), "seq", combine_softmax
    )
    self_scores = (
        jnp.einsum("sghe,skhe->sghk", glob_query, glob_key, preferred_element_type=jnp.float32)
        * score_scale
    )
    glob_top = jnp.maximum(merged_top, jnp.max(self_scores, axis=-1))
    self_exp = jnp.exp(self_scores - glob_top[..., None])
    merged_scale = jnp.exp(merged_top - glob_top)
    glob_denom = merged_sum * merged_scale + jnp.sum(self_exp, axis=-1)
    glob_lse = glob_top + jnp.log(glob_denom)
    glob_att_f = (
        merged_acc * merged_scale[..., None]
        + jnp.einsum("sghk,skhe->sghe", self_exp, glob_value.astype(jnp.float32), precision=PRECISE)
    ) / glob_denom[..., None]
    glob_attn = glob_att_f.reshape(group_seqs * GLOBALS, D).astype(jnp.bfloat16)
    y_one = super_rows + product(attn_rows, w_out)
    glob_y_one = glob_in + product(glob_attn, w_out)

    def feed_forward(rows_in):
        normed_two_full, back_two = jax.vjp(layer_norm, rows_in, gain_two, shift_two)
        normed_two = normed_two_full.astype(jnp.bfloat16)
        hidden_pre = product(normed_two, w_up) + bias_up
        hidden_full, gelu_back = jax.vjp(jax.nn.gelu, hidden_pre)
        hidden = hidden_full.astype(jnp.bfloat16)
        result = rows_in + product(hidden, w_down) + bias_down
        return (result, normed_two, hidden, back_two, gelu_back)

    def feed_back(cotangent, normed_two, hidden, back_two, gelu_back):
        cot_full = cotangent.astype(jnp.float32)
        grad_down = product_left(hidden, cotangent)
        grad_bias_d = jnp.sum(cot_full, axis=0)
        d_hidden = product_right(cotangent, w_down)
        d_pre = gelu_back(d_hidden)[0].astype(jnp.bfloat16)
        grad_up = product_left(normed_two, d_pre)
        grad_bias_u = jnp.sum(d_pre.astype(jnp.float32), axis=0)
        d_normed_two = product_right(d_pre, w_up)
        d_rows, grad_gain, grad_shift = back_two(d_normed_two)
        return (
            cot_full + d_rows,
            (grad_gain, grad_shift, grad_up, grad_bias_u, grad_down, grad_bias_d),
        )

    long_ff = feed_forward(y_one)
    glob_ff = feed_forward(glob_y_one)
    out_tokens = long_ff[0].astype(jnp.bfloat16)
    out_global = glob_ff[0].astype(jnp.bfloat16)
    d_y_one, long_mlp = feed_back(cot_tokens, long_ff[1], long_ff[2], long_ff[3], long_ff[4])
    glob_d_y_one, glob_mlp = feed_back(cot_global, glob_ff[1], glob_ff[2], glob_ff[3], glob_ff[4])
    mlp_grads = [
        local_part + first_flag * glob_part for local_part, glob_part in zip(long_mlp, glob_mlp)
    ]
    d_proj = d_y_one.astype(jnp.bfloat16)
    glob_d_proj = glob_d_y_one.astype(jnp.bfloat16)
    grad_out = product_left(attn_rows, d_proj) + first_flag * product_left(glob_attn, glob_d_proj)
    d_attn = product_right(d_proj, w_out).astype(jnp.bfloat16).reshape(tok_count, HEADS, HEAD_DIM)
    glob_d_attn = (
        product_right(glob_d_proj, w_out)
        .astype(jnp.bfloat16)
        .reshape(group_seqs, GLOBALS, HEADS, HEAD_DIM)
    )
    glob_d_attn_own = own_slot(glob_d_attn)
    rich_q3_full = rich_q3.astype(jnp.float32)
    rich_k3_full = rich_k3.astype(jnp.float32)
    d_key_ext = jnp.zeros((ext_count, HEADS, HEAD_DIM), jnp.float32)
    d_value_ext = jnp.zeros((ext_count, HEADS, HEAD_DIM), jnp.float32)
    scores, glob_scores, rich_back, q_part, key_win = block_scores()
    prob_full = jnp.exp(scores - log_total[..., None])
    glob_prob_full = jnp.exp(glob_scores - log_total[..., None])
    d_probs = jnp.einsum("qhe,khe->hqk", d_attn, value_ext, preferred_element_type=jnp.float32)
    glob_d_probs = jnp.einsum(
        "qhe,ghe->hqg", d_attn, glob_value_own, preferred_element_type=jnp.float32
    )
    row_delta = jnp.sum(prob_full * d_probs, axis=-1) + jnp.sum(
        glob_prob_full * glob_d_probs, axis=-1
    )
    d_scores = (prob_full * (d_probs - row_delta[..., None])).astype(jnp.bfloat16)
    glob_d_scores = (glob_prob_full * (glob_d_probs - row_delta[..., None])).astype(jnp.bfloat16)
    query_rich_grad, key_rich_grad = rich_back(d_scores.astype(jnp.float32))
    query_grad = (
        jnp.einsum("hqk,khe->qhe", d_scores, key_win, preferred_element_type=jnp.float32)
        + jnp.einsum(
            "hqg,ghe->qhe", glob_d_scores, glob_key_own, preferred_element_type=jnp.float32
        )
    ) * score_scale + jnp.einsum("hqc,ehc->qhe", query_rich_grad, rich_q3_full, precision=PRECISE)
    key_win_grad = jnp.einsum(
        "hqk,qhe->khe", d_scores, q_part, preferred_element_type=jnp.float32
    ) * score_scale + jnp.einsum("hkc,ehc->khe", key_rich_grad, rich_k3_full, precision=PRECISE)
    value_win_grad = jnp.einsum(
        "hqk,qhe->khe", prob_full.astype(jnp.bfloat16), d_attn, preferred_element_type=jnp.float32
    )
    d_key_ext = d_key_ext.at[0:window].add(key_win_grad)
    d_value_ext = d_value_ext.at[0:window].add(value_win_grad)
    glob_key_grad = (
        jnp.einsum("hqg,qhe->ghe", glob_d_scores, q_part, preferred_element_type=jnp.float32)
        * score_scale
    )
    glob_value_grad = jnp.einsum(
        "hqg,qhe->ghe",
        glob_prob_full.astype(jnp.bfloat16),
        d_attn,
        preferred_element_type=jnp.float32,
    )
    grad_rich_q = jnp.einsum(
        "qhe,hqc->ehc", q_part.astype(jnp.float32), query_rich_grad, precision=PRECISE
    )
    grad_rich_k = jnp.einsum(
        "khe,hkc->ehc", key_win.astype(jnp.float32), key_rich_grad, precision=PRECISE
    )
    query_grads = query_grad.reshape(block_rows, D)
    glob_delta = jnp.sum(glob_d_attn.astype(jnp.float32) * glob_att_f, axis=-1)
    glob_delta_own = own_slot(glob_delta)
    glob_lse_own = own_slot(glob_lse)
    member_probs = jnp.where(
        member_mask[:, None, :], jnp.exp(member_scores - glob_lse_own[..., None]), 0.0
    )
    member_d_probs = jnp.einsum(
        "ghe,the->ght", glob_d_attn_own, value_heads, preferred_element_type=jnp.float32
    )
    member_d_scores = (member_probs * (member_d_probs - glob_delta_own[..., None])).astype(
        jnp.bfloat16
    )
    glob_query_part = (
        jnp.einsum("ght,the->ghe", member_d_scores, key_heads, preferred_element_type=jnp.float32)
        * score_scale
    )
    own_key_extra = (
        jnp.einsum(
            "ght,ghe->the", member_d_scores, glob_query_own, preferred_element_type=jnp.float32
        )
        * score_scale
    )
    own_value_extra = jnp.einsum(
        "ght,ghe->the", member_probs, glob_d_attn_own.astype(jnp.float32), precision=PRECISE
    )
    d_key_ext = d_key_ext.at[RADIUS : RADIUS + tok_count].add(own_key_extra)
    d_value_ext = d_value_ext.at[RADIUS : RADIUS + tok_count].add(own_value_extra)
    grad_rims = jnp.concatenate(
        [d_key_ext.reshape(ext_count, D), d_value_ext.reshape(ext_count, D)], axis=1
    )
    from_above = shifted(grad_rims[:RADIUS].astype(jnp.bfloat16), "seq", -1).astype(jnp.float32)
    from_below = shifted(grad_rims[tok_count + RADIUS :].astype(jnp.bfloat16), "seq", 1).astype(
        jnp.float32
    )
    kv_grad = grad_rims[RADIUS : RADIUS + tok_count]
    kv_grad = kv_grad.at[:RADIUS].add(from_below).at[tok_count - RADIUS :].add(from_above)
    summed_query, summed_key, summed_value = (
        lax.psum(to_slots(glob_query_part).astype(jnp.bfloat16), "seq").astype(jnp.float32),
        lax.psum(to_slots(glob_key_grad).astype(jnp.bfloat16), "seq").astype(jnp.float32),
        lax.psum(to_slots(glob_value_grad).astype(jnp.bfloat16), "seq").astype(jnp.float32),
    )
    self_probs = jnp.exp(self_scores - glob_lse[..., None])
    self_d_probs = jnp.einsum(
        "sghe,skhe->sghk", glob_d_attn, glob_value, preferred_element_type=jnp.float32
    )
    self_d_scores = (self_probs * (self_d_probs - glob_delta[..., None])).astype(jnp.bfloat16)
    glob_rows_total = group_seqs * GLOBALS
    glob_d_query = (
        (
            summed_query
            + jnp.einsum(
                "sghk,skhe->sghe", self_d_scores, glob_key, preferred_element_type=jnp.float32
            )
            * score_scale
        )
        .astype(jnp.bfloat16)
        .reshape(glob_rows_total, D)
    )
    glob_d_key = (
        (
            summed_key
            + jnp.einsum(
                "sghk,sghe->skhe", self_d_scores, glob_query, preferred_element_type=jnp.float32
            )
            * score_scale
        )
        .astype(jnp.bfloat16)
        .reshape(glob_rows_total, D)
    )
    glob_d_value = (
        (
            summed_value
            + jnp.einsum(
                "sghk,sghe->skhe", self_probs, glob_d_attn.astype(jnp.float32), precision=PRECISE
            )
        )
        .astype(jnp.bfloat16)
        .reshape(glob_rows_total, D)
    )
    d_query = query_grads.astype(jnp.bfloat16)
    d_key = kv_grad[:, :D].astype(jnp.bfloat16)
    d_value = kv_grad[:, D:].astype(jnp.bfloat16)
    grad_query = product_left(normed, d_query) + first_flag * product_left(
        glob_normed, glob_d_query
    )
    grad_key = product_left(normed, d_key) + first_flag * product_left(glob_normed, glob_d_key)
    grad_value = product_left(normed, d_value) + first_flag * product_left(
        glob_normed, glob_d_value
    )
    d_normed = (
        product_right(d_query, w_query)
        + product_right(d_key, w_key)
        + product_right(d_value, w_value)
    )
    glob_d_normed = (
        product_right(glob_d_query, w_query)
        + product_right(glob_d_key, w_key)
        + product_right(glob_d_value, w_value)
    )
    d_super_norm, grad_gain_one, grad_shift_one = norm_back(d_normed)
    d_super = d_y_one + d_super_norm
    glob_d_norm, glob_gain_one, glob_shift_one = glob_norm_back(glob_d_normed)
    grad_global = glob_d_y_one + glob_d_norm
    grad_gain_one = grad_gain_one + first_flag * glob_gain_one
    grad_shift_one = grad_shift_one + first_flag * glob_shift_one
    d_graph_pre = graph_back(d_super)[0].astype(jnp.bfloat16)
    grad_graph = product_left(agg_low, d_graph_pre)
    d_agg = product_right(d_graph_pre, w_graph) / NEIGH
    d_token_ext = (
        jnp.zeros((ext_count, D), jnp.float32).at[flat_index].add(jnp.repeat(d_agg, NEIGH, axis=0))
    )
    d_token_ext = jnp.where(key_valid[:, None], d_token_ext, 0.0)
    token_above = shifted(d_token_ext[:RADIUS].astype(jnp.bfloat16), "seq", -1).astype(jnp.float32)
    token_below = shifted(d_token_ext[tok_count + RADIUS :].astype(jnp.bfloat16), "seq", 1).astype(
        jnp.float32
    )
    own_grad = (
        d_token_ext[RADIUS : RADIUS + tok_count]
        .at[:RADIUS]
        .add(token_below)
        .at[tok_count - RADIUS :]
        .add(token_above)
    )
    grad_tokens = d_super + own_grad
    weight_grads = (
        grad_graph,
        grad_gain_one,
        grad_shift_one,
        grad_query,
        grad_key,
        grad_value,
        grad_rich_q.reshape(HEAD_DIM, 4 * HEADS),
        grad_rich_k.reshape(HEAD_DIM, 4 * HEADS),
        grad_out,
        mlp_grads[0],
        mlp_grads[1],
        mlp_grads[2],
        mlp_grads[3],
        mlp_grads[4],
        mlp_grads[5],
    )
    pieces = [weight_grad.reshape(seq_count, -1) for weight_grad in weight_grads]
    packed = jnp.concatenate(pieces, axis=1)
    group_count = lax.axis_size("grp")
    received = lax.all_to_all(
        packed.astype(jnp.bfloat16), "seq", split_axis=0, concat_axis=0, tiled=True
    ).astype(packed.dtype)
    group_total = jnp.sum(received, axis=0).reshape(group_count, -1)
    crossed = lax.all_to_all(
        group_total.astype(jnp.bfloat16), "grp", split_axis=0, concat_axis=0, tiled=True
    ).astype(group_total.dtype)
    final_part = jnp.sum(crossed, axis=0)
    flat_sum = lax.all_gather(final_part.astype(jnp.bfloat16), "grp", axis=0, tiled=True).astype(
        final_part.dtype
    )
    results = []
    offset = 0
    for weight_grad in weight_grads:
        part_len = weight_grad.size // seq_count
        results.append(
            flat_sum[offset : offset + part_len].reshape(
                (weight_grad.shape[0] // seq_count,) + weight_grad.shape[1:]
            )
        )
        offset = offset + part_len
    return (
        out_tokens,
        out_global,
        grad_tokens,
        grad_global,
        results[0],
        results[1],
        results[2],
        results[3],
        results[4],
        results[5],
        results[6],
        results[7],
        results[8],
        results[9],
        results[10],
        results[11],
        results[12],
        results[13],
        results[14],
    )


SEQ_WAYS = 4
GRP_WAYS = 8
OWN_HEADS = HEADS // SEQ_WAYS
OWN = D // SEQ_WAYS
FF = 3072
FF_OWN = FF // SEQ_WAYS
TOK = 128
ROWS = SEQ_WAYS * TOK
ALL = ROWS + GLOBALS
GLOB_OWN = GLOBALS // SEQ_WAYS
CHUNK = TOK + GLOB_OWN
PIECE = OWN // GRP_WAYS
BAND = SEQ_WAYS * PIECE
WIN = TOK + 2 * RADIUS
PAD = ROWS + 2 * RADIUS
BF = jnp.bfloat16
F32 = jnp.float32
GELU_SCALE = math.sqrt(2.0 / math.pi)
GELU_CUBE = 0.044715
LOG_NORM = math.log(1.0 + ROWS)
SCORE_SCALE = 1.0 / math.sqrt(HEAD_DIM)
CORE_SWAP = [(0, 1), (1, 0), (2, 3), (3, 2)]
Y_SWAP = [(0, 2), (2, 0), (1, 3), (3, 1)]
X_SWAP = [(g, g ^ 1) for g in range(GRP_WAYS)]
Z_NEAR = [(g, g ^ 2) for g in range(GRP_WAYS)]
Z_FAR = [(g, g ^ 4) for g in range(GRP_WAYS)]
HALF_TOK = ROWS // 2
HALF_GLOB = GLOBALS // 2
HALF = HALF_TOK + HALF_GLOB
SEND = CHUNK + 32
CODED = D + 128
WIDE = 640
GRAPH_ROWS = 64
KERNEL_COST = 60_000_000_000
RICH = OWN_HEADS * 2 * 4


def nn(left, right):
    return lax.dot_general(left, right, (((1,), (0,)), ((), ())), preferred_element_type=F32)


def nt(left, right):
    return lax.dot_general(left, right, (((1,), (1,)), ((), ())), preferred_element_type=F32)


def tn(left, right):
    return lax.dot_general(left, right, (((0,), (0,)), ((), ())), preferred_element_type=F32)


def load(source, target, sem):
    copy = pltpu.make_async_copy(source, target, sem)
    copy.start()
    return copy


def pick(stacked, index):
    return lax.dynamic_index_in_dim(stacked, index, 0, keepdims=False)


def after(value, *marks):
    return lax.optimization_barrier((value, *marks))[0]


def reach_seq(block):
    return lax.ppermute(block, "seq", CORE_SWAP), lax.ppermute(block, "seq", Y_SWAP)


def gather_seq(block, *marks):
    beside, across = reach_seq(block)
    return [block, beside, across, lax.ppermute(after(across, *marks), "seq", CORE_SWAP)]


def turn_core(chunks):
    me = lax.axis_index("seq")
    return lax.ppermute(jnp.stack([pick(chunks, me ^ 1), pick(chunks, me ^ 3)]), "seq", CORE_SWAP)


def turn_y(chunks, came):
    return jnp.stack([pick(chunks, lax.axis_index("seq") ^ 2), came[1]])


def turned(chunks, came, far):
    mine = pick(chunks, lax.axis_index("seq"))
    return jnp.concatenate([mine, came[0], far[0], far[1]], axis=0)


def added(kept, came):
    return (kept.astype(F32) + came.astype(F32)).astype(BF)


def swap_x(sent):
    return lax.ppermute(sent, "grp", X_SWAP)


def swap_near(sent):
    return lax.ppermute(sent, "grp", Z_NEAR)


def swap_far(sent):
    return lax.ppermute(sent, "grp", Z_FAR)


def halves(kept, came, bit):
    grid = added(kept, came).reshape((-1, 2) + kept.shape[1:])
    mine = lax.dynamic_index_in_dim(grid, bit, 1, keepdims=False)
    return mine, lax.dynamic_index_in_dim(grid, 1 - bit, 1, keepdims=False)


def row_stats(rows_in):
    centred = rows_in - jnp.mean(rows_in, axis=-1, keepdims=True)
    scale = lax.rsqrt(jnp.mean(centred * centred, axis=-1, keepdims=True) + EPSILON)
    return centred * scale, scale


def norm_back(cotangent, gain, rows_in):
    hat, scale = row_stats(rows_in)
    scaled = cotangent * gain
    back = scale * (
        scaled
        - jnp.mean(scaled, axis=-1, keepdims=True)
        - hat * jnp.mean(scaled * hat, axis=-1, keepdims=True)
    )
    return (
        back,
        jnp.sum(cotangent * hat, axis=0, keepdims=True),
        jnp.sum(cotangent, axis=0, keepdims=True),
    )


def gelu_parts(pre):
    square = pre * pre
    bent = jnp.tanh(GELU_SCALE * pre * (1.0 + GELU_CUBE * square))
    half = 0.5 * (1.0 + bent)
    slope = half + 0.5 * pre * (1.0 - bent * bent) * (
        GELU_SCALE * (1.0 + 3.0 * GELU_CUBE * square)
    )
    return pre * half, slope


def counts_of(neigh, first, width):
    spots = (lax.broadcasted_iota(jnp.int32, (neigh.shape[0], width), 1) + first).astype(F32)
    total = jnp.zeros((neigh.shape[0], width), F32)
    for k in range(NEIGH):
        total = total + jnp.where(neigh[:, k : k + 1] == spots, 1.0, 0.0)
    return total.astype(BF)


def as_row(ref):
    return ref[...].reshape(1, ref.shape[0])


def own_window(me):
    return pl.ds(pl.multiple_of(lax.div(3 * me, 2) * 128, 128), 256)


def own_part(wide, me):
    return jnp.where(me % 2 == 0, wide[:, :OWN], wide[:, 256 - OWN :])


def rich_rows(rich, me, h):
    lane = lax.broadcasted_iota(jnp.int32, (8, 4 * HEADS), 1)
    term = lax.broadcasted_iota(jnp.int32, (8, 4 * HEADS), 0)
    chosen = (lane == 4 * (OWN_HEADS * me + h) + term) & (term < 4)
    return nn(jnp.where(chosen, 1.0, 0.0).astype(BF), rich)


def rich_columns(rich, me, h):
    row = lax.broadcasted_iota(jnp.int32, (4 * HEADS, 128), 0)
    term = lax.broadcasted_iota(jnp.int32, (4 * HEADS, 128), 1)
    chosen = (row == 4 * (OWN_HEADS * me + h) + term) & (term < 4)
    return tn(rich, jnp.where(chosen, 1.0, 0.0).astype(BF))


def code_kernel(tok_ref, neigh_ref, rank_ref, member_ref, out_ref):
    out_ref[:, :D] = tok_ref[...]
    ints = jnp.concatenate(
        [neigh_ref[...], rank_ref[...], member_ref[...], jnp.zeros((TOK - 11, TOK), jnp.int32)], axis=0
    )
    ints = ints.astype(F32).T
    high = jnp.floor(ints * (1.0 / 256.0))
    low = ints - 256.0 * high
    out_ref[:, D:] = jnp.concatenate([low[:, :16], high[:, :16], low[:, 32:]], axis=1).astype(BF)


def decoded(coded):
    coded = coded.astype(F32)
    return coded + 256.0 * jnp.concatenate([coded[:, 16:], coded[:, :16]], axis=1)


def share_out(chunk_of, x, kept_ref, sent_ref):
    for z in range(GRP_WAYS // 2):
        even, odd = chunk_of(2 * z), chunk_of(2 * z + 1)
        kept_ref[z] = jnp.where(x == 0, even, odd)
        sent_ref[z] = jnp.where(x == 0, odd, even)


def row_pieces(ref, g):
    return [ref[OWN * p + PIECE * g : OWN * p + PIECE * (g + 1)] for p in range(SEQ_WAYS)]


def pair_terms(meta_col, meta_row):
    terms = []
    for c in range(2):
        gap = meta_col[:, 8 + c : 9 + c] - meta_row[8 + c : 9 + c]
        distance = jnp.log(1.0 + jnp.abs(gap)) * (1.0 / LOG_NORM)
        terms.append((gap < 0.0, distance))
    return terms


def attend_kernel(
    tok_a, tok_b, tok_c, tok_d, glob_ref, gain_ref, shift_ref, rich_q_ref, rich_k_ref,
    w_graph_any, w_query_any, w_key_any, w_value_any,
    attn_ref, both_ref, member_ref, glob_att_ref, meta_col_ref, meta_row_ref,
    agg_any, pre_any, super_any, normed_any, qkv_any, prob_any,
    agg_ref, pre_ref, super_ref, normed_ref, qkv_ref, prob_ref,
    padded, w_graph_ref, w_project_ref, keys, values, key_rich, meta_pad, sems, prob_sems,
):
    me = lax.axis_index("seq")
    graph_copy = load(w_graph_any, w_graph_ref, sems.at[0])
    project_copies = [
        load(weight.at[:, own_window(me)], w_project_ref.at[i], sems.at[1 + i])
        for i, weight in enumerate((w_query_any, w_key_any, w_value_any))
    ]
    padded[:RADIUS] = jnp.zeros((RADIUS, D), BF)
    padded[RADIUS + ROWS :] = jnp.zeros((RADIUS, D), BF)
    starts = [pl.multiple_of((me ^ k) * TOK, TOK) for k in range(SEQ_WAYS)]
    for start, tok in zip(starts, (tok_a, tok_b, tok_c, tok_d)):
        padded[pl.ds(start + RADIUS, TOK)] = tok[:, :D]
    for start, tok in zip(starts, (tok_a, tok_b, tok_c, tok_d)):
        floats = decoded(tok[:, D:])
        meta_col_ref[pl.ds(start, TOK)] = floats
        meta_row_ref[:, pl.ds(start, TOK)] = floats.T[:16]
        counts = counts_of(floats, 0, WIN)
        mean = nn(counts, padded[pl.ds(start, WIN)]) * (1.0 / NEIGH)
        agg_ref[pl.ds(start, TOK)] = mean.astype(BF)
    gain, shift = as_row(gain_ref), as_row(shift_ref)
    graph_copy.wait()
    for low in range(0, ROWS, 256):
        rows = slice(low, low + 256)
        pre = nn(agg_ref[rows], w_graph_ref[...])
        pre_ref[rows] = pre
        tokens = padded[RADIUS + low : RADIUS + low + 256].astype(F32)
        super_rows = tokens + gelu_parts(pre)[0]
        super_ref[rows] = super_rows
        normed_ref[rows] = (row_stats(super_rows)[0] * gain + shift).astype(BF)
    glob_hat = row_stats(glob_ref[...].astype(F32))[0]
    normed_ref[ROWS:] = (glob_hat * gain + shift).astype(BF)
    kept = [
        load(source, target, sems.at[4 + i])
        for i, (source, target) in enumerate((
            (agg_ref, agg_any), (pre_ref, pre_any), (super_ref, super_any), (normed_ref, normed_any),
        ))
    ]
    normed = normed_ref[...]
    for part in range(3):
        project_copies[part].wait()
        projected = nn(normed, own_part(w_project_ref[part], me)).astype(BF)
        for h in range(OWN_HEADS):
            qkv_ref[part * OWN_HEADS + h] = projected[:, h * HEAD_DIM : (h + 1) * HEAD_DIM]
    kept.append(load(qkv_ref, qkv_any, sems.at[8]))
    rich_q, rich_k = rich_q_ref[...], rich_k_ref[...]
    spread_keys(qkv_ref, keys, values)
    meta_pad[...] = jnp.zeros((16, PAD), F32)
    meta_pad[:, RADIUS : RADIUS + ROWS] = meta_row_ref[...]
    rich_left = []
    for h in range(OWN_HEADS):
        key_rich[h] = nt(rich_rows(rich_k, me, h).astype(BF), keys[h])
        rich_left.append(rich_columns(rich_q, me, h).astype(BF))

    def prob_copy(b):
        rows = pl.ds(pl.multiple_of(b * TOK, TOK), TOK)
        return pltpu.make_async_copy(prob_ref.at[:, rows], prob_any.at[:, rows], prob_sems.at[b])

    def block(b, carry):
        start = pl.multiple_of(b * TOK, TOK)
        rows = pl.ds(start, TOK)
        window = pl.ds(start, WIN)
        terms = pair_terms(meta_col_ref[rows], meta_pad[:, window])
        q_spot = lax.broadcasted_iota(jnp.int32, (TOK, WIN), 0)
        k_spot = lax.broadcasted_iota(jnp.int32, (TOK, WIN), 1)
        ahead = k_spot - q_spot
        place = k_spot + (start - RADIUS)
        mask = (ahead >= 0) & (ahead <= 2 * RADIUS) & (place >= 0) & (place < ROWS)
        for h in range(OWN_HEADS):
            query = qkv_ref[h, rows]
            query_rich = nn(query, rich_left[h])
            right = key_rich[h, :, window]
            scores = nt(query, keys[h, window]) * SCORE_SCALE
            spread = None
            for c, (before, distance) in enumerate(terms):
                logit = query_rich[:, c : c + 1] + right[c : c + 1]
                logit = jnp.where(before, logit, -logit)
                off = distance - (query_rich[:, 2 + c : 3 + c] + right[2 + c : 3 + c])
                scores = scores + (jnp.minimum(logit, 0.0) - 0.5 * off * off)
                grown = 1.0 + jnp.exp(-jnp.abs(logit))
                spread = grown if spread is None else spread * grown
            scores = jnp.where(mask, scores - jnp.log(spread), MASKED)
            glob_scores = nt(query, qkv_ref[OWN_HEADS + h, ROWS:]) * SCORE_SCALE
            top = jnp.maximum(
                jnp.max(scores, axis=-1, keepdims=True), jnp.max(glob_scores, axis=-1, keepdims=True)
            )
            prob = jnp.exp(scores - top)
            glob_prob = jnp.exp(glob_scores - top)
            total = jnp.sum(prob, axis=-1, keepdims=True) + jnp.sum(
                glob_prob, axis=-1, keepdims=True
            )
            inverse = 1.0 / total
            prob = prob * inverse
            glob_prob = glob_prob * inverse
            prob_ref[h, rows, :WIN] = prob
            prob_ref[h, rows, WIN : WIN + GLOBALS] = glob_prob
            mixed = nn(prob.astype(BF), values[h, window]) + nn(
                glob_prob.astype(BF), qkv_ref[2 * OWN_HEADS + h, ROWS:]
            )
            attn_ref[rows, h * HEAD_DIM : (h + 1) * HEAD_DIM] = mixed.astype(BF)
        prob_copy(b).start()
        return carry

    lax.fori_loop(0, SEQ_WAYS, block, 0)
    slot = lax.broadcasted_iota(jnp.int32, (GLOBALS, ROWS), 0).astype(F32)
    member = meta_row_ref[10:11] == slot
    for h in range(OWN_HEADS):
        query = qkv_ref[h, ROWS:]
        scores = nt(query, qkv_ref[OWN_HEADS + h, :ROWS]) * SCORE_SCALE
        scores = jnp.where(member, scores, MASKED)
        own = nt(query, qkv_ref[OWN_HEADS + h, ROWS:]) * SCORE_SCALE
        top = jnp.maximum(
            jnp.max(scores, axis=-1, keepdims=True), jnp.max(own, axis=-1, keepdims=True)
        )
        prob = jnp.exp(scores - top)
        own_prob = jnp.exp(own - top)
        total = jnp.sum(prob, axis=-1, keepdims=True) + jnp.sum(own_prob, axis=-1, keepdims=True)
        inverse = 1.0 / total
        prob = prob * inverse
        own_prob = own_prob * inverse
        member_ref[h, :, :ROWS] = prob
        member_ref[h, :, ROWS : ROWS + GLOBALS] = own_prob
        mixed = nn(prob.astype(BF), qkv_ref[2 * OWN_HEADS + h, :ROWS]) + nn(
            own_prob.astype(BF), qkv_ref[2 * OWN_HEADS + h, ROWS:]
        )
        glob_att_ref[h] = mixed
        attn_ref[ROWS:, h * HEAD_DIM : (h + 1) * HEAD_DIM] = mixed.astype(BF)
    for half in range(2):
        span = slice(OWN * half, OWN * (half + 1))
        low, glob_low = HALF_TOK * half, ROWS + HALF_GLOB * half
        both_ref[:HALF_TOK, span] = attn_ref[low : low + HALF_TOK]
        both_ref[HALF_TOK:, span] = attn_ref[glob_low : glob_low + HALF_GLOB]
    for copy in kept:
        copy.wait()
    for b in range(SEQ_WAYS):
        prob_copy(b).wait()


def spread_keys(qkv_ref, keys, values):
    edge = jnp.zeros((OWN_HEADS, RADIUS, HEAD_DIM), BF)
    for held, first in ((keys, OWN_HEADS), (values, 2 * OWN_HEADS)):
        held[:, :RADIUS] = edge
        held[:, RADIUS + ROWS :] = edge
        held[:, RADIUS : RADIUS + ROWS] = qkv_ref[first : first + OWN_HEADS, :ROWS]


def own_feed_kernel(
    att_a, att_b, att_c, att_d, gain_ref, shift_ref, bias_up_ref, bias_down_ref, cot_ref,
    super_any, glob_any, cot_glob_any, w_out_any, w_up_any, w_down_any,
    out_ref, send_ref,
    att_refs, glob_att_refs, super_ref, glob_ref, cot_glob_ref, w_out_ref, w_up_ref, w_down_ref, sems,
):
    me = lax.axis_index("seq")
    half = lax.div(me, 2)
    inner = lax.rem(me, 2)
    tok_rows = pl.ds(pl.multiple_of(inner * TOK, TOK), TOK)
    glob_rows = pl.ds(pl.multiple_of(HALF_TOK + inner * GLOB_OWN, GLOB_OWN), GLOB_OWN)
    own_tok = pl.ds(pl.multiple_of(me * TOK, TOK), TOK)
    own_glob = pl.ds(pl.multiple_of(me * GLOB_OWN, GLOB_OWN), GLOB_OWN)
    first = []
    for k, att in enumerate((att_a, att_b, att_c, att_d)):
        first.append(load(att.at[tok_rows], att_refs.at[k], sems.at[k]))
        first.append(load(att.at[glob_rows], glob_att_refs.at[k], sems.at[4 + k]))
    first.append(load(super_any.at[own_tok], super_ref, sems.at[8]))
    first.append(load(glob_any.at[own_glob], glob_ref, sems.at[9]))
    first.append(load(cot_glob_any.at[own_glob], cot_glob_ref, sems.at[10]))
    first.append(load(w_out_any, w_out_ref, sems.at[11]))
    ups, downs = [], []
    for j in range(SEQ_WAYS):
        span = slice(FF_OWN * j, FF_OWN * (j + 1))
        ups.append(load(w_up_any.at[:, span], w_up_ref.at[j], sems.at[12 + j]))
        downs.append(load(w_down_any.at[span], w_down_ref.at[j], sems.at[16 + j]))
    for copy in first:
        copy.wait()
    y_rows = jnp.concatenate([super_ref[...], glob_ref[...].astype(F32)], axis=0)
    for k in range(SEQ_WAYS):
        wide = jnp.concatenate([att_refs[k], glob_att_refs[k]], axis=0)
        mixed = jnp.where(half == 0, wide[:, :OWN], wide[:, OWN:])
        y_rows = y_rows + nn(mixed, w_out_ref[pl.ds(pl.multiple_of((me ^ k) * OWN, OWN), OWN)])
    gain = as_row(gain_ref)
    hat, scale = row_stats(y_rows)
    normed = (hat * gain + as_row(shift_ref)).astype(BF)
    cot = jnp.concatenate([cot_ref[...], cot_glob_ref[...]], axis=0)
    out = y_rows + as_row(bias_down_ref)
    bias = as_row(bias_up_ref)
    back = None
    for j in range(SEQ_WAYS):
        ups[j].wait()
        hidden, slope = gelu_parts(nn(normed, w_up_ref[j]) + bias[:, FF_OWN * j : FF_OWN * (j + 1)])
        downs[j].wait()
        d_pre = (nt(cot, w_down_ref[j]) * slope).astype(BF)
        term = nt(d_pre, w_up_ref[j])
        back = term if back is None else back + term
        out = out + nn(hidden.astype(BF), w_down_ref[j])
    out_ref[...] = out[:TOK].astype(BF)
    scaled = back * gain
    cot = cot.astype(F32)
    d_rows = cot + scale * (
        scaled
        - jnp.mean(scaled, axis=-1, keepdims=True)
        - hat * jnp.mean(scaled * hat, axis=-1, keepdims=True)
    )
    sums = [back * hat, back, cot]
    sums = [jnp.sum(rows, axis=0, keepdims=True) for rows in sums]
    send_ref[:CHUNK] = d_rows.astype(BF)
    send_ref[CHUNK : CHUNK + GLOB_OWN] = out[TOK:].astype(BF)
    sums = jnp.concatenate(sums + [jnp.zeros((13, D), F32)], axis=0)
    send_ref[CHUNK + GLOB_OWN :] = sums.astype(BF)


def feed_rows_kernel(
    att_a, att_b, att_c, att_d, cot_a, cot_b, cot_c, cot_d, cot_glob_ref, glob_ref, gain_ref,
    shift_ref, bias_ref, super_any, w_out_any, w_up_any,
    kept_ref, sent_ref, normed_ref, slope_ref, cot_ref,
    super_ref, w_out_ref, w_up_ref, hidden_ref, grad, sems,
):
    me, x = lax.axis_index("seq"), lax.rem(lax.axis_index("grp"), 2)
    mine = pl.multiple_of(me * FF_OWN, FF_OWN)
    copies = [
        load(super_any, super_ref, sems.at[0]),
        load(w_out_any, w_out_ref, sems.at[1]),
        load(w_up_any.at[:, pl.ds(mine, FF_OWN)], w_up_ref, sems.at[2]),
    ]
    for k, cot in enumerate((cot_a, cot_b, cot_c, cot_d)):
        b = me ^ k
        at = lax.div(b, 2) * HALF + lax.rem(b, 2) * TOK
        cot_ref[pl.ds(pl.multiple_of(at, 32), TOK)] = cot[...]
    for half in range(2):
        cot_ref[HALF * half + HALF_TOK : HALF * (half + 1)] = cot_glob_ref[
            HALF_GLOB * half : HALF_GLOB * (half + 1)
        ]
    gain, shift = as_row(gain_ref), as_row(shift_ref)
    bias = as_row(bias_ref)
    bias = [bias[:, FF_OWN * j : FF_OWN * (j + 1)] for j in range(SEQ_WAYS)]
    bias = jnp.where(me < 2, jnp.where(me == 0, bias[0], bias[1]), jnp.where(me == 2, bias[2], bias[3]))
    for copy in copies:
        copy.wait()
    for half in range(2):
        rows = slice(HALF * half, HALF * (half + 1))
        glob_rows = glob_ref[HALF_GLOB * half : HALF_GLOB * (half + 1)].astype(F32)
        y_rows = jnp.concatenate([super_ref[HALF_TOK * half : HALF_TOK * (half + 1)], glob_rows], axis=0)
        for k, att in enumerate((att_a, att_b, att_c, att_d)):
            w_rows = w_out_ref[pl.ds(pl.multiple_of((me ^ k) * OWN, OWN), OWN)]
            y_rows = y_rows + nn(att[:, OWN * half : OWN * (half + 1)], w_rows)
        normed = (row_stats(y_rows)[0] * gain + shift).astype(BF)
        normed_ref[rows] = normed
        hidden, slope = gelu_parts(nn(normed, w_up_ref[...]) + bias)
        hidden_ref[rows] = hidden.astype(BF)
        slope_ref[rows] = slope
    grad[...] = tn(hidden_ref[...], cot_ref[...])
    share_out(lambda g: grad[BAND * g : BAND * (g + 1)].astype(BF), x, kept_ref, sent_ref)


def feed_back_kernel(
    normed_ref, slope_ref, cot_ref, w_down_any,
    kept_ref, sent_ref, d_bias_ref, w_down_ref, d_pre_ref, grad, sems,
):
    me, x = lax.axis_index("seq"), lax.rem(lax.axis_index("grp"), 2)
    mine = pl.ds(pl.multiple_of(me * FF_OWN, FF_OWN), FF_OWN)
    load(w_down_any.at[mine], w_down_ref, sems.at[0]).wait()
    d_bias = jnp.zeros((1, FF_OWN), F32)
    for half in range(2):
        rows = slice(HALF * half, HALF * (half + 1))
        d_pre = (nt(cot_ref[rows], w_down_ref[...]) * slope_ref[rows]).astype(BF)
        d_pre_ref[rows] = d_pre
        d_bias = d_bias + jnp.sum(d_pre.astype(F32), axis=0, keepdims=True)
    d_bias_ref[...] = d_bias
    grad[...] = tn(normed_ref[...], d_pre_ref[...])
    share_out(lambda g: jnp.concatenate(row_pieces(grad, g), axis=0).astype(BF), x, kept_ref, sent_ref)


def project_grad_kernel(normed_ref, d_qkv_ref, kept_ref, sent_ref, grad):
    x = lax.rem(lax.axis_index("grp"), 2)
    grad[...] = tn(normed_ref[...], d_qkv_ref[:, : 3 * OWN])
    share_out(lambda g: jnp.concatenate(row_pieces(grad, g), axis=0).astype(BF), x, kept_ref, sent_ref)


def back_kernel(
    back_a, back_b, back_c, back_d, glob_att_ref, meta_col_ref, meta_row_ref, rich_q_ref,
    rich_k_ref, w_out_any, qkv_any, prob_any, member_any,
    d_proj_ref, d_qkv_ref, vec_ref, out_global_ref,
    w_out_ref, qkv_ref, prob_ref, member_ref, keys, values, key_rich, meta_pad, d_att, d_keys, d_values,
    d_key_rich, d_query_rich, sems, prob_sems,
):
    me = lax.axis_index("seq")
    own_rows = pl.ds(pl.multiple_of(me * OWN, OWN), OWN)
    w_copy = load(w_out_any.at[own_rows], w_out_ref, sems.at[0])
    qkv_copy = load(qkv_any, qkv_ref, sems.at[1])

    def prob_copy(b):
        rows = pl.ds(pl.multiple_of(b * TOK, TOK), TOK)
        return pltpu.make_async_copy(prob_any.at[:, rows], prob_ref.at[:, rows], prob_sems.at[b])

    for b in range(SEQ_WAYS):
        prob_copy(b).start()
    member_copy = load(member_any, member_ref, sems.at[2])
    sums = None
    for k, back in enumerate((back_a, back_b, back_c, back_d)):
        at = me ^ k
        d_proj_ref[pl.ds(pl.multiple_of(at * TOK, TOK), TOK)] = back[:TOK]
        d_proj_ref[pl.ds(pl.multiple_of(ROWS + at * GLOB_OWN, GLOB_OWN), GLOB_OWN)] = back[TOK:CHUNK]
        out_global_ref[pl.ds(pl.multiple_of(at * GLOB_OWN, GLOB_OWN), GLOB_OWN)] = back[
            CHUNK : CHUNK + GLOB_OWN
        ]
        part = back[CHUNK + GLOB_OWN :].astype(F32)
        sums = part if sums is None else sums + part
    vec_ref[...] = sums[:8]
    w_copy.wait()
    projected = nt(d_proj_ref[...], w_out_ref[...]).astype(BF)
    for h in range(OWN_HEADS):
        d_att[h] = projected[:, h * HEAD_DIM : (h + 1) * HEAD_DIM]
    meta_pad[...] = jnp.zeros((16, PAD), F32)
    meta_pad[:, RADIUS : RADIUS + ROWS] = meta_row_ref[...]
    qkv_copy.wait()
    spread_keys(qkv_ref, keys, values)
    rich_q, rich_k = rich_q_ref[...], rich_k_ref[...]
    rich_left, rich_qt, rich_kt = [], [], []
    for h in range(OWN_HEADS):
        rich_left.append(rich_columns(rich_q, me, h).astype(BF))
        rich_qt.append(rich_rows(rich_q, me, h))
        rich_kt.append(rich_rows(rich_k, me, h))
        key_rich[h] = nt(rich_kt[h].astype(BF), keys[h])
    d_keys[...] = jnp.zeros((OWN_HEADS, PAD, HEAD_DIM), F32)
    d_values[...] = jnp.zeros((OWN_HEADS, PAD, HEAD_DIM), F32)
    d_key_rich[...] = jnp.zeros((OWN_HEADS, 8, PAD), F32)
    glob_key = [qkv_ref[OWN_HEADS + h, ROWS:] for h in range(OWN_HEADS)]
    glob_value = [qkv_ref[2 * OWN_HEADS + h, ROWS:] for h in range(OWN_HEADS)]

    def block(b, carry):
        start = pl.multiple_of(b * TOK, TOK)
        rows = pl.ds(start, TOK)
        window = pl.ds(start, WIN)
        terms = pair_terms(meta_col_ref[rows], meta_pad[:, window])
        carry = list(carry)
        prob_copy(b).wait()
        for h in range(OWN_HEADS):
            query = qkv_ref[h, rows]
            d_out = d_att[h, rows]
            prob = prob_ref[h, rows, :WIN]
            glob_prob = prob_ref[h, rows, WIN : WIN + GLOBALS]
            d_prob = nt(d_out, values[h, window])
            d_glob_prob = nt(d_out, glob_value[h])
            delta = jnp.sum(prob * d_prob, axis=-1, keepdims=True) + jnp.sum(
                glob_prob * d_glob_prob, axis=-1, keepdims=True
            )
            d_scores = prob * (d_prob - delta)
            d_low = d_scores.astype(BF)
            d_glob_low = (glob_prob * (d_glob_prob - delta)).astype(BF)
            query_rich = nn(query, rich_left[h])
            right = key_rich[h, :, window]
            lefts = []
            for c, (before, distance) in enumerate(terms):
                logit = query_rich[:, c : c + 1] + right[c : c + 1]
                pulled = jnp.where(before, 0.5, -0.5) - 0.5 * jnp.tanh(0.5 * logit)
                pulled = d_scores * pulled
                off = distance - (query_rich[:, 2 + c : 3 + c] + right[2 + c : 3 + c])
                off = d_scores * off
                lefts.append((c, jnp.sum(pulled, axis=-1, keepdims=True)))
                lefts.append((2 + c, jnp.sum(off, axis=-1, keepdims=True)))
                d_key_rich[h, c : c + 1, window] += jnp.sum(pulled, axis=0, keepdims=True)
                d_key_rich[h, 2 + c : 3 + c, window] += jnp.sum(off, axis=0, keepdims=True)
            lane = lax.broadcasted_iota(jnp.int32, (TOK, 8), 1)
            d_left = jnp.zeros((TOK, 8), F32)
            d_query = (nn(d_low, keys[h, window]) + nn(d_glob_low, glob_key[h])) * SCORE_SCALE
            for c, column in lefts:
                d_left = jnp.where(lane == c, column, d_left)
                d_query = d_query + column * rich_qt[h][c : c + 1]
            d_query_rich[h, rows] = d_left
            d_qkv_ref[rows, h * HEAD_DIM : (h + 1) * HEAD_DIM] = d_query.astype(BF)
            d_keys[h, window] += tn(d_low, query) * SCORE_SCALE
            d_values[h, window] += tn(prob.astype(BF), d_out)
            carry[2 * h] = carry[2 * h] + tn(d_glob_low, query) * SCORE_SCALE
            carry[2 * h + 1] = carry[2 * h + 1] + tn(glob_prob.astype(BF), d_out)
        return tuple(carry)

    zero = jnp.zeros((GLOBALS, HEAD_DIM), F32)
    sums = lax.fori_loop(0, SEQ_WAYS, block, (zero,) * (2 * OWN_HEADS))
    member_copy.wait()
    rich = []
    for h in range(OWN_HEADS):
        span = slice(h * HEAD_DIM, (h + 1) * HEAD_DIM)
        key_span = slice(OWN + h * HEAD_DIM, OWN + (h + 1) * HEAD_DIM)
        value_span = slice(2 * OWN + h * HEAD_DIM, 2 * OWN + (h + 1) * HEAD_DIM)
        query = qkv_ref[h, ROWS:]
        key_rows = qkv_ref[OWN_HEADS + h, :ROWS]
        value_rows = qkv_ref[2 * OWN_HEADS + h, :ROWS]
        d_out = d_att[h, ROWS:]
        delta = jnp.sum(d_out.astype(F32) * glob_att_ref[h], axis=-1, keepdims=True)
        prob = member_ref[h, :, :ROWS]
        own_prob = member_ref[h, :, ROWS : ROWS + GLOBALS]
        d_low = (prob * (nt(d_out, value_rows) - delta)).astype(BF)
        d_own = (own_prob * (nt(d_out, glob_value[h]) - delta)).astype(BF)
        d_query = (nn(d_low, key_rows) + nn(d_own, glob_key[h])) * SCORE_SCALE
        d_qkv_ref[ROWS:, span] = d_query.astype(BF)
        d_qkv_ref[ROWS:, key_span] = (sums[2 * h] + tn(d_own, query) * SCORE_SCALE).astype(BF)
        d_qkv_ref[ROWS:, value_span] = (sums[2 * h + 1] + tn(own_prob.astype(BF), d_out)).astype(BF)
        d_right = d_key_rich[h, :, RADIUS : RADIUS + ROWS]
        d_key = d_keys[h, RADIUS : RADIUS + ROWS] + tn(d_low, query) * SCORE_SCALE
        d_key = d_key + lax.dot_general(
            d_right, rich_kt[h], (((0,), (0,)), ((), ())), precision=PRECISE,
            preferred_element_type=F32,
        )
        d_value = d_values[h, RADIUS : RADIUS + ROWS] + tn(prob.astype(BF), d_out)
        d_qkv_ref[:ROWS, key_span] = d_key.astype(BF)
        d_qkv_ref[:ROWS, value_span] = d_value.astype(BF)
        rich.append(tn(d_query_rich[h].astype(BF), qkv_ref[h, :ROWS])[:4])
        rich.append(nn(d_right.astype(BF), key_rows)[:4])
    rich = jnp.concatenate(rich, axis=0)
    d_qkv_ref[:, 3 * OWN :] = jnp.zeros((ALL, WIDE - 3 * OWN), BF)
    rich = jnp.concatenate([rich, jnp.zeros((32 - RICH, HEAD_DIM), F32)], axis=0)
    d_qkv_ref[:32, 3 * OWN :] = rich.astype(BF)


def norm_kernel(
    dqkv_a, dqkv_b, dqkv_c, dqkv_d, glob_ref, d_proj_ref, gain_ref, vec_two_ref, d_bias_up_ref, attn_ref,
    w_query_any, w_key_any, w_value_any, super_any, pre_any, agg_any,
    grad_glob_ref, kept_ref, sent_ref, d_own_ref, d_pre,
    w_query_ref, w_key_ref, w_value_ref, super_ref, pre_ref, agg_ref, d_super, d_qkv, d_norm, rich, sems,
):
    me, x = lax.axis_index("seq"), lax.rem(lax.axis_index("grp"), 2)
    weight_copies = [
        load(source, target, sems.at[i])
        for i, (source, target) in enumerate((
            (w_query_any, w_query_ref), (w_key_any, w_key_ref), (w_value_any, w_value_ref),
        ))
    ]
    row_copies = [load(super_any, super_ref, sems.at[3]), load(pre_any, pre_ref, sems.at[4])]
    agg_copy = load(agg_any.at[:, own_window(me)], agg_ref, sems.at[5])
    for k, part in enumerate((dqkv_a, dqkv_b, dqkv_c, dqkv_d)):
        d_qkv[me ^ k] = part[...]
        rich[me ^ k] = part[:32, 3 * OWN :].astype(F32)
    for copy in weight_copies:
        copy.wait()
    total = None
    for p in range(SEQ_WAYS):
        for i, weight in enumerate((w_query_ref, w_key_ref, w_value_ref)):
            term = nt(d_qkv[p, :, OWN * i : OWN * (i + 1)], weight[:, OWN * p : OWN * (p + 1)])
            total = term if total is None else total + term
    d_norm[...] = total
    for copy in row_copies:
        copy.wait()
    gain = as_row(gain_ref)
    d_gain = jnp.zeros((1, D), F32)
    d_shift = jnp.zeros((1, D), F32)
    for low in range(0, ALL, 192):
        rows = slice(low, low + 192)
        inner = min(192, ROWS - low)
        if inner == 192:
            rows_in = super_ref[rows]
        else:
            rows_in = jnp.concatenate([super_ref[low:], glob_ref[...].astype(F32)], axis=0)
        back, gain_part, shift_part = norm_back(d_norm[rows], gain, rows_in)
        d_gain = d_gain + gain_part
        d_shift = d_shift + shift_part
        back = back + d_proj_ref[rows].astype(F32)
        d_super[rows] = back
        long = slice(low, low + inner)
        slope = gelu_parts(pre_ref[long])[1]
        d_pre[long] = (back[:inner] * slope).astype(BF)
    grad_glob_ref[...] = d_super[ROWS:]
    d_own_ref[...] = d_super[pl.ds(pl.multiple_of(me * TOK, TOK), TOK)]
    grad_out = tn(attn_ref[...], d_proj_ref[...])
    agg_copy.wait()
    grad = tn(own_part(agg_ref[...], me), d_pre[...])
    extra = jnp.concatenate(
        [vec_two_ref[0:3], d_bias_up_ref[...], d_gain, d_shift, jnp.zeros((1, D), F32)], axis=0
    )

    def chunk(g):
        pieces = [rich[g // 2, 12 * (g % 2) + i : 12 * (g % 2) + i + 1] for i in range(12)]
        rows = [grad[PIECE * g : PIECE * (g + 1)], jnp.concatenate(pieces, axis=1), extra]
        rows += [grad_out[PIECE * g : PIECE * (g + 1)], jnp.zeros((8, D), F32)]
        return jnp.concatenate(rows, axis=0).astype(BF)

    share_out(chunk, x, kept_ref, sent_ref)


def tokens_kernel(d_own_ref, d_pre, meta_col_ref, w_graph_ref, grad_tok_ref):
    me = lax.axis_index("seq")
    total = d_own_ref[...]
    for shift in (-1, 0, 1):
        b = me - shift
        fits = (b >= 0) & (b < SEQ_WAYS)
        rows = pl.ds(pl.multiple_of(jnp.clip(b, 0, SEQ_WAYS - 1) * TOK, TOK), TOK)
        d_agg = (nt(d_pre[rows], w_graph_ref[...]) * (1.0 / NEIGH)).astype(BF)
        counts = counts_of(meta_col_ref[rows], (shift + 1) * TOK, TOK)
        total = total + jnp.where(fits, tn(counts, d_agg), 0.0)
    grad_tok_ref[...] = total


DISTANCES = (0, 4, 2, 6)


def down_out_kernel(held, came, out_ref):
    for i, distance in enumerate(DISTANCES):
        for flip, pieces in enumerate((held, came)):
            g = lax.axis_index("grp") ^ (distance + flip)
            out_ref[pl.ds(pl.multiple_of(BAND * g, BAND), BAND)] = pieces[i].astype(F32)


def up_out_kernel(held, came, out_ref):
    for i, distance in enumerate(DISTANCES):
        for flip, pieces in enumerate((held, came)):
            g = lax.axis_index("grp") ^ (distance + flip)
            piece = pieces[i].astype(F32)
            rows = pl.ds(pl.multiple_of(PIECE * g, 8), PIECE)
            for k in range(SEQ_WAYS):
                columns = pl.ds(pl.multiple_of((lax.axis_index("seq") ^ k) * D, D), D)
                out_ref[rows, columns] = piece[PIECE * k : PIECE * (k + 1)]


def project_out_kernel(held, came, query_ref, key_ref, value_ref, pieces):
    for i, distance in enumerate(DISTANCES):
        for flip, blocks in enumerate((held, came)):
            g = lax.axis_index("grp") ^ (distance + flip)
            rows = pl.ds(pl.multiple_of(PIECE * g, 8), PIECE)
            piece = blocks[i].astype(F32)
            for k in range(SEQ_WAYS):
                pieces[lax.axis_index("seq") ^ k] = piece[PIECE * k : PIECE * (k + 1)]
            for j, ref in enumerate((query_ref, key_ref, value_ref)):
                parts = [pieces[p, :, OWN * j : OWN * (j + 1)] for p in range(SEQ_WAYS)]
                ref[rows] = jnp.concatenate(parts, axis=1)


def graph_out_kernel(held, came, out_ref, graph_ref, vec_ref, rich_ref):
    for i, distance in enumerate(DISTANCES):
        for flip, blocks in enumerate((held, came)):
            g = lax.axis_index("grp") ^ (distance + flip)
            rows = pl.ds(pl.multiple_of(PIECE * g, 8), PIECE)
            piece = blocks[i].astype(F32)
            graph_ref[rows] = piece[:PIECE]
            out_ref[rows] = piece[PIECE + 8 : 2 * PIECE + 8]
            rich_ref[pl.ds(g, 1)] = piece[PIECE : PIECE + 1]
    vec_ref[...] = held[0, PIECE : PIECE + 8].astype(F32)


def call(kernel, ins, outs, scratch=(), apart=0, outs_apart=0):
    vmem, any_space = pl.BlockSpec(memory_space=pltpu.VMEM), pl.BlockSpec(memory_space=pl.ANY)
    return pl.pallas_call(
        kernel,
        out_shape=[jax.ShapeDtypeStruct(shape, kind) for shape, kind in outs],
        in_specs=[vmem] * (len(ins) - apart) + [any_space] * apart,
        out_specs=[vmem] * (len(outs) - outs_apart) + [any_space] * outs_apart,
        scratch_shapes=[pltpu.VMEM(*s) if isinstance(s, tuple) else s for s in scratch],
        compiler_params=pltpu.CompilerParams(vmem_limit_bytes=60 * 1024 * 1024),
        cost_estimate=pl.CostEstimate(flops=KERNEL_COST, bytes_accessed=0, transcendentals=0),
    )(*ins)


def split_heads(
    tokens, global_tokens, neighbours, token_ranks, membership, w_graph, gain_one, shift_one,
    w_query, w_key, w_value, rich_query, rich_key, w_out, gain_two, shift_two, w_up, bias_up,
    w_down, bias_down, cot_tokens, cot_global,
):
    me = lax.axis_index("seq")
    grp = lax.axis_index("grp")
    x, z_low, z_high = grp % 2, (grp // 2) % 2, grp // 4
    (coded,) = call(
        code_kernel,
        [tokens, neighbours.T, token_ranks, membership.reshape(1, TOK)],
        [((TOK, CODED), BF)],
    )
    tok_blocks = gather_seq(coded)
    cot_beside, cot_across = reach_seq(after(cot_tokens, tok_blocks[2]))
    rich_query, rich_key = rich_query.T, rich_key.T

    weights_shape = (D, D), BF
    stored = [
        ((ROWS, D), BF), ((ROWS, D), F32), ((ROWS, D), F32), ((ALL, D), BF),
        ((3 * OWN_HEADS, ALL, HEAD_DIM), BF), ((OWN_HEADS, ROWS, 512), F32),
    ]
    heads_scratch = [
        ((OWN_HEADS, PAD, HEAD_DIM), BF), ((OWN_HEADS, PAD, HEAD_DIM), BF),
        ((OWN_HEADS, 8, PAD), F32), ((16, PAD), F32),
    ]
    (
        attn, both, member_prob, glob_att, meta_col, meta_row, agg, graph_pre, super_rows, normed, qkv,
        prob,
    ) = call(
        attend_kernel,
        [*tok_blocks, global_tokens, gain_one, shift_one, rich_query, rich_key, w_graph, w_query,
         w_key, w_value],
        [((ALL, OWN), BF), ((HALF, 2 * OWN), BF), ((OWN_HEADS, GLOBALS, 640), F32),
         ((OWN_HEADS, GLOBALS, HEAD_DIM), F32), ((ROWS, 128), F32), ((16, ROWS), F32), *stored],
        [*stored, ((PAD, D), BF), weights_shape, ((3, D, 256), BF), *heads_scratch,
         pltpu.SemaphoreType.DMA((9,)), pltpu.SemaphoreType.DMA((SEQ_WAYS,))],
        apart=4, outs_apart=6,
    )
    att_blocks = gather_seq(after(both, cot_beside, cot_across))
    cot_diagonal = lax.ppermute(after(cot_across, both), "seq", CORE_SWAP)
    cot_blocks = [cot_tokens, cot_beside, cot_across, cot_diagonal]
    out_tokens, back = call(
        own_feed_kernel,
        [*att_blocks, gain_two, shift_two, bias_up, bias_down, cot_tokens, super_rows,
         global_tokens, cot_global, w_out, w_up, w_down],
        [((TOK, D), BF), ((SEND, D), BF)],
        [((SEQ_WAYS, TOK, 2 * OWN), BF), ((SEQ_WAYS, GLOB_OWN, 2 * OWN), BF), ((TOK, D), F32),
         ((GLOB_OWN, D), BF), ((GLOB_OWN, D), BF), weights_shape, ((SEQ_WAYS, D, FF_OWN), BF),
         ((SEQ_WAYS, FF_OWN, D), BF), pltpu.SemaphoreType.DMA((20,))],
        apart=6,
    )
    down_kept, down_sent, normed_two, slope, cot_all = call(
        feed_rows_kernel,
        [*att_blocks, *cot_blocks, cot_global, global_tokens, after(gain_two, back), shift_two,
         bias_up, super_rows, w_out, w_up],
        [((4, BAND, D), BF), ((4, BAND, D), BF), ((ALL, D), BF), ((ALL, FF_OWN), F32), ((ALL, D), BF)],
        [((ROWS, D), F32), weights_shape, ((D, FF_OWN), BF), ((ALL, FF_OWN), BF), ((D, D), F32),
         pltpu.SemaphoreType.DMA((3,))],
        apart=3,
    )
    down_came = swap_x(down_sent)
    back_blocks = gather_seq(back, down_sent)
    up_kept, up_sent, d_bias_up = call(
        feed_back_kernel,
        [after(normed_two, back_blocks[2]), slope, cot_all, w_down],
        [((4, BAND, D), BF), ((4, BAND, D), BF), ((1, FF_OWN), F32)],
        [((FF_OWN, D), BF), ((ALL, FF_OWN), BF), ((D, D), F32), pltpu.SemaphoreType.DMA((1,))],
        apart=1,
    )
    up_came = swap_x(up_sent)

    d_proj, d_qkv, vec_two, out_global = call(
        back_kernel,
        [*back_blocks, glob_att, meta_col, after(meta_row, up_sent), rich_query, rich_key,
         w_out, qkv, prob, member_prob],
        [((ALL, D), BF), ((ALL, WIDE), BF), ((8, D), F32), ((GLOBALS, D), BF)],
        [((OWN, D), BF), stored[4], stored[5], ((OWN_HEADS, GLOBALS, 640), F32), *heads_scratch,
         ((OWN_HEADS, ALL, HEAD_DIM), BF), ((OWN_HEADS, PAD, HEAD_DIM), F32),
         ((OWN_HEADS, PAD, HEAD_DIM), F32), ((OWN_HEADS, 8, PAD), F32), ((OWN_HEADS, ROWS, 8), F32),
         pltpu.SemaphoreType.DMA((3,)), pltpu.SemaphoreType.DMA((SEQ_WAYS,))],
        apart=4,
    )
    beside, across = reach_seq(d_qkv)
    clock = [d_qkv]

    def due(value):
        return after(value, *clock)

    def step(value):
        clock[:] = [value]
        return value

    down_kept, down_sent = halves(down_kept, due(down_came), z_low)
    down_came = swap_near(step(down_sent))
    proj_kept, proj_sent = call(
        project_grad_kernel,
        [due(normed), d_qkv],
        [((4, BAND, 3 * OWN), BF)] * 2,
        [((D, 3 * OWN), F32)],
    )
    proj_came = swap_x(step(proj_sent))
    up_kept, up_sent = halves(up_kept, due(up_came), z_low)
    up_came = swap_near(step(up_sent))
    down_kept, down_sent = halves(down_kept, due(down_came), z_high)
    down_came = swap_far(step(down_sent))
    across = step(due(across))
    d_qkv_blocks = [d_qkv, beside, across, lax.ppermute(across, "seq", CORE_SWAP)]
    up_kept, up_sent = halves(up_kept, due(up_came), z_high)
    up_came = swap_far(step(up_sent))
    proj_kept, proj_sent = halves(proj_kept, due(proj_came), z_low)
    proj_came = swap_near(step(proj_sent))

    grad_global, graph_kept, graph_sent, d_own, d_pre = call(
        norm_kernel,
        [*d_qkv_blocks, global_tokens, d_proj, gain_one, due(vec_two), d_bias_up,
         attn, w_query, w_key, w_value, super_rows, graph_pre, agg],
        [((GLOBALS, D), F32), ((4, GRAPH_ROWS, D), BF), ((4, GRAPH_ROWS, D), BF), ((TOK, D), F32),
         ((ROWS, D), BF)],
        [*[weights_shape] * 3, ((ROWS, D), F32), ((ROWS, D), F32), ((ROWS, 256), BF), ((ALL, D), F32),
         ((SEQ_WAYS, ALL, WIDE), BF), ((ALL, D), F32), ((SEQ_WAYS, 32, HEAD_DIM), F32),
         pltpu.SemaphoreType.DMA((6,))],
        apart=6,
    )
    graph_came = swap_x(step(graph_sent))
    down_held = step(added(down_kept, due(down_came)))
    down_came = swap_far(down_held)
    up_mine = step(added(up_kept, due(up_came))).reshape(SEQ_WAYS, PIECE, D)
    up_core = turn_core(up_mine)
    proj_kept, proj_sent = halves(proj_kept, due(proj_came), z_high)
    proj_came = swap_far(step(proj_sent))
    up_sent = step(turn_y(up_mine, due(up_core)))
    up_far = lax.ppermute(up_sent, "seq", Y_SWAP)
    (grad_tokens,) = call(
        tokens_kernel, [due(d_own), d_pre, meta_col, w_graph], [((TOK, D), F32)]
    )
    step(grad_tokens)
    down_held = step(jnp.concatenate([down_held, due(down_came)], axis=0))
    down_came = swap_near(down_held)
    up_held = step(turned(up_mine, up_core, due(up_far)))[None]
    up_came = swap_far(up_held)
    graph_kept, graph_sent = halves(graph_kept, due(graph_came), z_low)
    graph_came = swap_near(step(graph_sent))
    proj_mine = step(added(proj_kept, due(proj_came))).reshape(SEQ_WAYS, PIECE, 3 * OWN)
    proj_core = turn_core(proj_mine)
    down_held = step(jnp.concatenate([down_held, due(down_came)], axis=0))
    down_came = swap_x(down_held)
    proj_sent = step(turn_y(proj_mine, due(proj_core)))
    proj_far = lax.ppermute(proj_sent, "seq", Y_SWAP)
    up_held = step(jnp.concatenate([up_held, due(up_came)], axis=0))
    up_came = swap_near(up_held)
    graph_kept, graph_sent = halves(graph_kept, due(graph_came), z_high)
    graph_came = swap_far(step(graph_sent))
    proj_held = step(turned(proj_mine, proj_core, due(proj_far)))[None]
    proj_came = swap_far(proj_held)
    up_held = step(jnp.concatenate([up_held, due(up_came)], axis=0))
    up_came = swap_x(up_held)
    graph_held = step(added(graph_kept, due(graph_came)))
    graph_came = swap_far(graph_held)
    proj_held = step(jnp.concatenate([proj_held, due(proj_came)], axis=0))
    proj_came = swap_near(proj_held)
    (g_down,) = call(down_out_kernel, [due(down_held), down_came], [((FF_OWN, D), F32)])
    step(g_down)
    graph_held = step(jnp.concatenate([graph_held, due(graph_came)], axis=0))
    graph_came = swap_near(graph_held)
    proj_held = step(jnp.concatenate([proj_held, due(proj_came)], axis=0))
    proj_came = swap_x(proj_held)
    (g_up,) = call(up_out_kernel, [due(up_held), up_came], [((OWN, FF), F32)])
    step(g_up)
    graph_held = step(jnp.concatenate([graph_held, due(graph_came)], axis=0))
    graph_came = swap_x(graph_held)
    g_query, g_key, g_value = call(
        project_out_kernel,
        [due(proj_held), proj_came],
        [((OWN, D), F32)] * 3,
        [((SEQ_WAYS, PIECE, 3 * OWN), F32)],
    )
    step(g_query)
    g_out, g_graph, vectors, rich = call(
        graph_out_kernel,
        [due(graph_held), graph_came],
        [((OWN, D), F32)] * 2 + [((8, D), F32), ((8, D), F32)],
    )
    vectors, d_bias_up = lax.dynamic_slice_in_dim(vectors[1:], me * OWN, OWN, axis=1), vectors[4]
    rich = rich.reshape(SEQ_WAYS, OWN_HEADS, 2, 4, HEAD_DIM).transpose(2, 4, 0, 1, 3)
    rich = rich.reshape(2, HEAD_DIM, 4 * HEADS)
    rich = lax.dynamic_slice_in_dim(rich, me * (HEAD_DIM // SEQ_WAYS), HEAD_DIM // SEQ_WAYS, 1)
    return (
        out_tokens, out_global, grad_tokens, grad_global,
        g_graph, vectors[4], vectors[5], g_query, g_key, g_value, rich[0], rich[1],
        g_out, vectors[0], vectors[1], g_up, d_bias_up, g_down, vectors[2],
    )


def layer(*arrays):
    tokens, global_tokens = arrays[:2]
    ways = (lax.axis_size("seq"), lax.axis_size("grp"))
    if ways == (SEQ_WAYS, GRP_WAYS) and tokens.shape[0] == TOK and global_tokens.shape[0] == GLOBALS:
        return split_heads(*arrays)
    return local(*arrays)


def solution(mesh):
    return jax.shard_map(
        layer,
        mesh=mesh,
        in_specs=(
            P(("grp", "seq"), None),
            P("grp", None),
            P(("grp", "seq"), None),
            P(None, ("grp", "seq")),
            P(("grp", "seq")),
            P(),
            P(),
            P(),
            P(),
            P(),
            P(),
            P(),
            P(),
            P(),
            P(),
            P(),
            P(),
            P(),
            P(),
            P(),
            P(("grp", "seq"), None),
            P("grp", None),
        ),
        out_specs=(
            P(("grp", "seq"), None),
            P("grp", None),
            P(("grp", "seq"), None),
            P("grp", None),
            P("seq", None),
            P("seq"),
            P("seq"),
            P("seq", None),
            P("seq", None),
            P("seq", None),
            P("seq", None),
            P("seq", None),
            P("seq", None),
            P("seq"),
            P("seq"),
            P("seq", None),
            P("seq"),
            P("seq", None),
            P("seq"),
        ),
        check_vma=False,
    )
```

```python
import functools
import math

import jax
import jax.numpy as jnp
from jax import lax
from jax.experimental import pallas as pl
from jax.experimental.pallas import tpu as pltpu
from jax.sharding import PartitionSpec as P

D = 768
HEADS = 12
HEAD_DIM = 64
RADIUS = 128
GLOBALS = 64
NEIGH = 8
SEQ_TOKENS = 2048


EPSILON = 1e-05
PRECISE = lax.Precision.HIGHEST
MASKED = -1e30


def with_halo(cells, sides, width):
    for axis, dim in sides:
        count = lax.axis_size(axis)
        ends = count - 1
        head = lax.slice_in_dim(cells, 0, width, axis=dim)
        tail = lax.slice_in_dim(cells, cells.shape[dim] - width, cells.shape[dim], axis=dim)
        cells = jnp.concatenate(
            [
                lax.ppermute(tail, axis, [(i, (i + 1) % count) for i in range(ends)]),
                cells,
                lax.ppermute(head, axis, [((i + 1) % count, i) for i in range(ends)]),
            ],
            axis=dim,
        )
    return cells


def joined(array, axis, combine):
    everything = jax.tree.map(
        lambda part, kind: lax.all_gather(part.astype(kind), axis),
        array,
        (jnp.bfloat16, jnp.bfloat16, jnp.bfloat16),
    )

    def take(k):
        return jax.tree.map(lambda part, own: part[k].astype(own.dtype), everything, array)

    return lax.fori_loop(
        1, lax.axis_size(axis), lambda k, so_far: combine(so_far, take(k)), take(0)
    )


def shifted(block, axis, distance):
    devices = range(lax.axis_size(axis))
    route = [(i - distance, i) for i in devices if i - distance in devices]
    return lax.ppermute(block, axis, route)


def layer_norm(rows_in, gain_in, shift_in):
    row_mean = jnp.mean(rows_in, axis=-1, keepdims=True)
    centred = rows_in - row_mean
    variance = jnp.mean(centred * centred, axis=-1, keepdims=True)
    return centred * lax.rsqrt(variance + EPSILON) * gain_in + shift_in


def rich_part(a_block, b_window, rank_query, rank_key, log_norm):
    combined = None
    for coordinate in range(2):
        order_flag = (rank_query[coordinate][:, None] < rank_key[coordinate][None, :]).astype(
            jnp.float32
        )
        distance = (
            jnp.log1p(
                jnp.abs(rank_query[coordinate][:, None] - rank_key[coordinate][None, :]).astype(
                    jnp.float32
                )
            )
            / log_norm
        )
        order_logit = a_block[:, :, None, coordinate] + b_window[:, None, :, coordinate]
        centre = a_block[:, :, None, 2 + coordinate] + b_window[:, None, :, 2 + coordinate]
        pair_term = (
            order_flag * jax.nn.log_sigmoid(order_logit)
            + (1.0 - order_flag) * jax.nn.log_sigmoid(-order_logit)
            - 0.5 * (distance - centre) ** 2
        )
        combined = pair_term if combined is None else combined + pair_term
    return combined


def product(left, right):
    return jnp.dot(left, right, preferred_element_type=jnp.float32)


def product_left(left, right):
    return jnp.einsum("ta,tb->ab", left, right, preferred_element_type=jnp.float32)


def product_right(left, right):
    return jnp.einsum("tb,ab->ta", left, right, preferred_element_type=jnp.float32)


def local(
    tokens,
    global_tokens,
    neighbours,
    token_ranks,
    membership,
    w_graph,
    gain_one,
    shift_one,
    w_query,
    w_key,
    w_value,
    rich_query,
    rich_key,
    w_out,
    gain_two,
    shift_two,
    w_up,
    bias_up,
    w_down,
    bias_down,
    cot_tokens,
    cot_global,
):
    tok_count = tokens.shape[0]
    seq_count = lax.axis_size("seq")
    seq_index = lax.axis_index("seq")
    seq_len = min(SEQ_TOKENS, tok_count * seq_count)
    span = seq_len // tok_count
    group_seqs = global_tokens.shape[0] // GLOBALS
    seq_slot = seq_index // span
    seq_local = seq_index % span
    slot_flag = (jnp.arange(group_seqs, dtype=jnp.int32) == seq_slot).astype(jnp.float32)
    log_norm = math.log(1.0 + seq_len)
    score_scale = 1.0 / math.sqrt(HEAD_DIM)
    block_rows = min(512, tok_count)
    window = block_rows + 2 * RADIUS
    ext_count = tok_count + 2 * RADIUS
    first_flag = (seq_index == 0).astype(jnp.float32)
    own_pos = seq_local * tok_count + jnp.arange(tok_count, dtype=jnp.int32)
    ext_pos = seq_local * tok_count - RADIUS + jnp.arange(ext_count, dtype=jnp.int32)
    key_valid = (ext_pos >= 0) & (ext_pos < seq_len)

    def own_slot(array_in):
        return lax.dynamic_index_in_dim(array_in, seq_slot, 0, keepdims=False)

    def to_slots(array_in):
        return slot_flag.reshape((group_seqs,) + (1,) * array_in.ndim) * array_in[None]

    token_ext = with_halo(tokens, (("seq", 0),), RADIUS)
    token_ext = jnp.where(key_valid[:, None], token_ext, jnp.zeros_like(token_ext))
    flat_index = neighbours.reshape(-1)
    gathered = (
        jnp.take(token_ext, flat_index, axis=0).astype(jnp.float32).reshape(tok_count, NEIGH, D)
    )
    agg_low = jnp.mean(gathered, axis=1).astype(jnp.bfloat16)
    graph_pre = product(agg_low, w_graph)
    graph_out, graph_back = jax.vjp(jax.nn.gelu, graph_pre)
    super_rows = tokens.astype(jnp.float32) + graph_out
    normed_full, norm_back = jax.vjp(layer_norm, super_rows, gain_one, shift_one)
    normed = normed_full.astype(jnp.bfloat16)
    glob_in = global_tokens.astype(jnp.float32)
    glob_normed_full, glob_norm_back = jax.vjp(layer_norm, glob_in, gain_one, shift_one)
    glob_normed = glob_normed_full.astype(jnp.bfloat16)
    query = product(normed, w_query).astype(jnp.bfloat16)
    key_own = product(normed, w_key).astype(jnp.bfloat16)
    value_own = product(normed, w_value).astype(jnp.bfloat16)
    glob_query = (
        product(glob_normed, w_query)
        .astype(jnp.bfloat16)
        .reshape(group_seqs, GLOBALS, HEADS, HEAD_DIM)
    )
    glob_key = (
        product(glob_normed, w_key)
        .astype(jnp.bfloat16)
        .reshape(group_seqs, GLOBALS, HEADS, HEAD_DIM)
    )
    glob_value = (
        product(glob_normed, w_value)
        .astype(jnp.bfloat16)
        .reshape(group_seqs, GLOBALS, HEADS, HEAD_DIM)
    )
    glob_query_own = own_slot(glob_query)
    glob_key_own = own_slot(glob_key)
    glob_value_own = own_slot(glob_value)
    kv_ext = with_halo(jnp.concatenate([key_own, value_own], axis=1), (("seq", 0),), RADIUS)
    key_ext = kv_ext[:, :D].reshape(ext_count, HEADS, HEAD_DIM)
    value_ext = kv_ext[:, D:].reshape(ext_count, HEADS, HEAD_DIM)
    rank_ext = with_halo(token_ranks, (("seq", 1),), RADIUS)
    rich_q3 = rich_query.reshape(HEAD_DIM, HEADS, 4)
    rich_k3 = rich_key.reshape(HEAD_DIM, HEADS, 4)
    query_heads = query.reshape(tok_count, HEADS, HEAD_DIM)
    a_rows = jnp.einsum("the,ehc->htc", query_heads, rich_q3, preferred_element_type=jnp.float32)
    b_ext = jnp.einsum("the,ehc->htc", key_ext, rich_k3, preferred_element_type=jnp.float32)

    def block_scores():

        def rich_scores(left_rows, right_rows):
            return rich_part(left_rows, right_rows, token_ranks, rank_ext, log_norm)

        rich_vals, rich_back = jax.vjp(rich_scores, a_rows, b_ext)
        raw_scores = (
            jnp.einsum("qhe,khe->hqk", query_heads, key_ext, preferred_element_type=jnp.float32)
            * score_scale
        )
        pos_gap = own_pos[:, None] - ext_pos[None, :]
        key_mask = (jnp.abs(pos_gap) <= RADIUS) & key_valid[None, :]
        scores = jnp.where(key_mask[None], raw_scores + rich_vals, MASKED)
        glob_scores = (
            jnp.einsum(
                "qhe,ghe->hqg", query_heads, glob_key_own, preferred_element_type=jnp.float32
            )
            * score_scale
        )
        return (scores, glob_scores, rich_back, query_heads, key_ext)

    scored = block_scores()
    scores = scored[0]
    glob_scores = scored[1]
    row_top = jnp.maximum(jnp.max(scores, axis=-1), jnp.max(glob_scores, axis=-1))
    row_denom = jnp.sum(jnp.exp(scores - row_top[..., None]), axis=-1) + jnp.sum(
        jnp.exp(glob_scores - row_top[..., None]), axis=-1
    )
    log_total = row_top + jnp.log(row_denom)
    prob_rows = jnp.exp(scores - log_total[..., None]).astype(jnp.bfloat16)
    glob_probs = jnp.exp(glob_scores - log_total[..., None]).astype(jnp.bfloat16)
    attn_block = jnp.einsum(
        "hqk,khe->qhe", prob_rows, value_ext, preferred_element_type=jnp.float32
    ) + jnp.einsum("hqg,ghe->qhe", glob_probs, glob_value_own, preferred_element_type=jnp.float32)
    attn_parts = attn_block.reshape(block_rows, D)
    attn_rows = attn_parts.astype(jnp.bfloat16)
    member_mask = membership[None, :] == jnp.arange(GLOBALS, dtype=jnp.int32)[:, None]
    key_heads = key_ext[RADIUS : RADIUS + tok_count]
    value_heads = value_ext[RADIUS : RADIUS + tok_count]
    member_raw = (
        jnp.einsum("ghe,the->ght", glob_query_own, key_heads, preferred_element_type=jnp.float32)
        * score_scale
    )
    member_scores = jnp.where(member_mask[:, None, :], member_raw, MASKED)
    local_top = jnp.max(member_scores, axis=-1)
    member_exp = jnp.where(
        member_mask[:, None, :], jnp.exp(member_scores - local_top[..., None]), 0.0
    )
    local_sum = jnp.sum(member_exp, axis=-1)
    local_acc = jnp.einsum(
        "ght,the->ghe", member_exp, value_heads.astype(jnp.float32), precision=PRECISE
    )
    slot_top = jnp.where(slot_flag[:, None, None] > 0.5, local_top[None], MASKED)
    slot_sum = to_slots(local_sum)
    slot_acc = to_slots(local_acc)

    def combine_softmax(first_part, second_part):
        top_one, sum_one, acc_one = first_part
        top_two, sum_two, acc_two = second_part
        top_both = jnp.maximum(top_one, top_two)
        scale_one = jnp.exp(top_one - top_both)
        scale_two = jnp.exp(top_two - top_both)
        return (
            top_both,
            sum_one * scale_one + sum_two * scale_two,
            acc_one * scale_one[..., None] + acc_two * scale_two[..., None],
        )

    merged_top, merged_sum, merged_acc = joined(
        (slot_top, slot_sum, slot_acc), "seq", combine_softmax
    )
    self_scores = (
        jnp.einsum("sghe,skhe->sghk", glob_query, glob_key, preferred_element_type=jnp.float32)
        * score_scale
    )
    glob_top = jnp.maximum(merged_top, jnp.max(self_scores, axis=-1))
    self_exp = jnp.exp(self_scores - glob_top[..., None])
    merged_scale = jnp.exp(merged_top - glob_top)
    glob_denom = merged_sum * merged_scale + jnp.sum(self_exp, axis=-1)
    glob_lse = glob_top + jnp.log(glob_denom)
    glob_att_f = (
        merged_acc * merged_scale[..., None]
        + jnp.einsum("sghk,skhe->sghe", self_exp, glob_value.astype(jnp.float32), precision=PRECISE)
    ) / glob_denom[..., None]
    glob_attn = glob_att_f.reshape(group_seqs * GLOBALS, D).astype(jnp.bfloat16)
    y_one = super_rows + product(attn_rows, w_out)
    glob_y_one = glob_in + product(glob_attn, w_out)

    def feed_forward(rows_in):
        normed_two_full, back_two = jax.vjp(layer_norm, rows_in, gain_two, shift_two)
        normed_two = normed_two_full.astype(jnp.bfloat16)
        hidden_pre = product(normed_two, w_up) + bias_up
        hidden_full, gelu_back = jax.vjp(jax.nn.gelu, hidden_pre)
        hidden = hidden_full.astype(jnp.bfloat16)
        result = rows_in + product(hidden, w_down) + bias_down
        return (result, normed_two, hidden, back_two, gelu_back)

    def feed_back(cotangent, normed_two, hidden, back_two, gelu_back):
        cot_full = cotangent.astype(jnp.float32)
        grad_down = product_left(hidden, cotangent)
        grad_bias_d = jnp.sum(cot_full, axis=0)
        d_hidden = product_right(cotangent, w_down)
        d_pre = gelu_back(d_hidden)[0].astype(jnp.bfloat16)
        grad_up = product_left(normed_two, d_pre)
        grad_bias_u = jnp.sum(d_pre.astype(jnp.float32), axis=0)
        d_normed_two = product_right(d_pre, w_up)
        d_rows, grad_gain, grad_shift = back_two(d_normed_two)
        return (
            cot_full + d_rows,
            (grad_gain, grad_shift, grad_up, grad_bias_u, grad_down, grad_bias_d),
        )

    long_ff = feed_forward(y_one)
    glob_ff = feed_forward(glob_y_one)
    out_tokens = long_ff[0].astype(jnp.bfloat16)
    out_global = glob_ff[0].astype(jnp.bfloat16)
    d_y_one, long_mlp = feed_back(cot_tokens, long_ff[1], long_ff[2], long_ff[3], long_ff[4])
    glob_d_y_one, glob_mlp = feed_back(cot_global, glob_ff[1], glob_ff[2], glob_ff[3], glob_ff[4])
    mlp_grads = [
        local_part + first_flag * glob_part for local_part, glob_part in zip(long_mlp, glob_mlp)
    ]
    d_proj = d_y_one.astype(jnp.bfloat16)
    glob_d_proj = glob_d_y_one.astype(jnp.bfloat16)
    grad_out = product_left(attn_rows, d_proj) + first_flag * product_left(glob_attn, glob_d_proj)
    d_attn = product_right(d_proj, w_out).astype(jnp.bfloat16).reshape(tok_count, HEADS, HEAD_DIM)
    glob_d_attn = (
        product_right(glob_d_proj, w_out)
        .astype(jnp.bfloat16)
        .reshape(group_seqs, GLOBALS, HEADS, HEAD_DIM)
    )
    glob_d_attn_own = own_slot(glob_d_attn)
    rich_q3_full = rich_q3.astype(jnp.float32)
    rich_k3_full = rich_k3.astype(jnp.float32)
    d_key_ext = jnp.zeros((ext_count, HEADS, HEAD_DIM), jnp.float32)
    d_value_ext = jnp.zeros((ext_count, HEADS, HEAD_DIM), jnp.float32)
    scores, glob_scores, rich_back, q_part, key_win = block_scores()
    prob_full = jnp.exp(scores - log_total[..., None])
    glob_prob_full = jnp.exp(glob_scores - log_total[..., None])
    d_probs = jnp.einsum("qhe,khe->hqk", d_attn, value_ext, preferred_element_type=jnp.float32)
    glob_d_probs = jnp.einsum(
        "qhe,ghe->hqg", d_attn, glob_value_own, preferred_element_type=jnp.float32
    )
    row_delta = jnp.sum(prob_full * d_probs, axis=-1) + jnp.sum(
        glob_prob_full * glob_d_probs, axis=-1
    )
    d_scores = (prob_full * (d_probs - row_delta[..., None])).astype(jnp.bfloat16)
    glob_d_scores = (glob_prob_full * (glob_d_probs - row_delta[..., None])).astype(jnp.bfloat16)
    query_rich_grad, key_rich_grad = rich_back(d_scores.astype(jnp.float32))
    query_grad = (
        jnp.einsum("hqk,khe->qhe", d_scores, key_win, preferred_element_type=jnp.float32)
        + jnp.einsum(
            "hqg,ghe->qhe", glob_d_scores, glob_key_own, preferred_element_type=jnp.float32
        )
    ) * score_scale + jnp.einsum("hqc,ehc->qhe", query_rich_grad, rich_q3_full, precision=PRECISE)
    key_win_grad = jnp.einsum(
        "hqk,qhe->khe", d_scores, q_part, preferred_element_type=jnp.float32
    ) * score_scale + jnp.einsum("hkc,ehc->khe", key_rich_grad, rich_k3_full, precision=PRECISE)
    value_win_grad = jnp.einsum(
        "hqk,qhe->khe", prob_full.astype(jnp.bfloat16), d_attn, preferred_element_type=jnp.float32
    )
    d_key_ext = d_key_ext.at[0:window].add(key_win_grad)
    d_value_ext = d_value_ext.at[0:window].add(value_win_grad)
    glob_key_grad = (
        jnp.einsum("hqg,qhe->ghe", glob_d_scores, q_part, preferred_element_type=jnp.float32)
        * score_scale
    )
    glob_value_grad = jnp.einsum(
        "hqg,qhe->ghe",
        glob_prob_full.astype(jnp.bfloat16),
        d_attn,
        preferred_element_type=jnp.float32,
    )
    grad_rich_q = jnp.einsum(
        "qhe,hqc->ehc", q_part.astype(jnp.float32), query_rich_grad, precision=PRECISE
    )
    grad_rich_k = jnp.einsum(
        "khe,hkc->ehc", key_win.astype(jnp.float32), key_rich_grad, precision=PRECISE
    )
    query_grads = query_grad.reshape(block_rows, D)
    glob_delta = jnp.sum(glob_d_attn.astype(jnp.float32) * glob_att_f, axis=-1)
    glob_delta_own = own_slot(glob_delta)
    glob_lse_own = own_slot(glob_lse)
    member_probs = jnp.where(
        member_mask[:, None, :], jnp.exp(member_scores - glob_lse_own[..., None]), 0.0
    )
    member_d_probs = jnp.einsum(
        "ghe,the->ght", glob_d_attn_own, value_heads, preferred_element_type=jnp.float32
    )
    member_d_scores = (member_probs * (member_d_probs - glob_delta_own[..., None])).astype(
        jnp.bfloat16
    )
    glob_query_part = (
        jnp.einsum("ght,the->ghe", member_d_scores, key_heads, preferred_element_type=jnp.float32)
        * score_scale
    )
    own_key_extra = (
        jnp.einsum(
            "ght,ghe->the", member_d_scores, glob_query_own, preferred_element_type=jnp.float32
        )
        * score_scale
    )
    own_value_extra = jnp.einsum(
        "ght,ghe->the", member_probs, glob_d_attn_own.astype(jnp.float32), precision=PRECISE
    )
    d_key_ext = d_key_ext.at[RADIUS : RADIUS + tok_count].add(own_key_extra)
    d_value_ext = d_value_ext.at[RADIUS : RADIUS + tok_count].add(own_value_extra)
    grad_rims = jnp.concatenate(
        [d_key_ext.reshape(ext_count, D), d_value_ext.reshape(ext_count, D)], axis=1
    )
    from_above = shifted(grad_rims[:RADIUS].astype(jnp.bfloat16), "seq", -1).astype(jnp.float32)
    from_below = shifted(grad_rims[tok_count + RADIUS :].astype(jnp.bfloat16), "seq", 1).astype(
        jnp.float32
    )
    kv_grad = grad_rims[RADIUS : RADIUS + tok_count]
    kv_grad = kv_grad.at[:RADIUS].add(from_below).at[tok_count - RADIUS :].add(from_above)
    summed_query, summed_key, summed_value = (
        lax.psum(to_slots(glob_query_part).astype(jnp.bfloat16), "seq").astype(jnp.float32),
        lax.psum(to_slots(glob_key_grad).astype(jnp.bfloat16), "seq").astype(jnp.float32),
        lax.psum(to_slots(glob_value_grad).astype(jnp.bfloat16), "seq").astype(jnp.float32),
    )
    self_probs = jnp.exp(self_scores - glob_lse[..., None])
    self_d_probs = jnp.einsum(
        "sghe,skhe->sghk", glob_d_attn, glob_value, preferred_element_type=jnp.float32
    )
    self_d_scores = (self_probs * (self_d_probs - glob_delta[..., None])).astype(jnp.bfloat16)
    glob_rows_total = group_seqs * GLOBALS
    glob_d_query = (
        (
            summed_query
            + jnp.einsum(
                "sghk,skhe->sghe", self_d_scores, glob_key, preferred_element_type=jnp.float32
            )
            * score_scale
        )
        .astype(jnp.bfloat16)
        .reshape(glob_rows_total, D)
    )
    glob_d_key = (
        (
            summed_key
            + jnp.einsum(
                "sghk,sghe->skhe", self_d_scores, glob_query, preferred_element_type=jnp.float32
            )
            * score_scale
        )
        .astype(jnp.bfloat16)
        .reshape(glob_rows_total, D)
    )
    glob_d_value = (
        (
            summed_value
            + jnp.einsum(
                "sghk,sghe->skhe", self_probs, glob_d_attn.astype(jnp.float32), precision=PRECISE
            )
        )
        .astype(jnp.bfloat16)
        .reshape(glob_rows_total, D)
    )
    d_query = query_grads.astype(jnp.bfloat16)
    d_key = kv_grad[:, :D].astype(jnp.bfloat16)
    d_value = kv_grad[:, D:].astype(jnp.bfloat16)
    grad_query = product_left(normed, d_query) + first_flag * product_left(
        glob_normed, glob_d_query
    )
    grad_key = product_left(normed, d_key) + first_flag * product_left(glob_normed, glob_d_key)
    grad_value = product_left(normed, d_value) + first_flag * product_left(
        glob_normed, glob_d_value
    )
    d_normed = (
        product_right(d_query, w_query)
        + product_right(d_key, w_key)
        + product_right(d_value, w_value)
    )
    glob_d_normed = (
        product_right(glob_d_query, w_query)
        + product_right(glob_d_key, w_key)
        + product_right(glob_d_value, w_value)
    )
    d_super_norm, grad_gain_one, grad_shift_one = norm_back(d_normed)
    d_super = d_y_one + d_super_norm
    glob_d_norm, glob_gain_one, glob_shift_one = glob_norm_back(glob_d_normed)
    grad_global = glob_d_y_one + glob_d_norm
    grad_gain_one = grad_gain_one + first_flag * glob_gain_one
    grad_shift_one = grad_shift_one + first_flag * glob_shift_one
    d_graph_pre = graph_back(d_super)[0].astype(jnp.bfloat16)
    grad_graph = product_left(agg_low, d_graph_pre)
    d_agg = product_right(d_graph_pre, w_graph) / NEIGH
    d_token_ext = (
        jnp.zeros((ext_count, D), jnp.float32).at[flat_index].add(jnp.repeat(d_agg, NEIGH, axis=0))
    )
    d_token_ext = jnp.where(key_valid[:, None], d_token_ext, 0.0)
    token_above = shifted(d_token_ext[:RADIUS].astype(jnp.bfloat16), "seq", -1).astype(jnp.float32)
    token_below = shifted(d_token_ext[tok_count + RADIUS :].astype(jnp.bfloat16), "seq", 1).astype(
        jnp.float32
    )
    own_grad = (
        d_token_ext[RADIUS : RADIUS + tok_count]
        .at[:RADIUS]
        .add(token_below)
        .at[tok_count - RADIUS :]
        .add(token_above)
    )
    grad_tokens = d_super + own_grad
    weight_grads = (
        grad_graph,
        grad_gain_one,
        grad_shift_one,
        grad_query,
        grad_key,
        grad_value,
        grad_rich_q.reshape(HEAD_DIM, 4 * HEADS),
        grad_rich_k.reshape(HEAD_DIM, 4 * HEADS),
        grad_out,
        mlp_grads[0],
        mlp_grads[1],
        mlp_grads[2],
        mlp_grads[3],
        mlp_grads[4],
        mlp_grads[5],
    )
    pieces = [weight_grad.reshape(seq_count, -1) for weight_grad in weight_grads]
    packed = jnp.concatenate(pieces, axis=1)
    group_count = lax.axis_size("grp")
    received = lax.all_to_all(
        packed.astype(jnp.bfloat16), "seq", split_axis=0, concat_axis=0, tiled=True
    ).astype(packed.dtype)
    group_total = jnp.sum(received, axis=0).reshape(group_count, -1)
    crossed = lax.all_to_all(
        group_total.astype(jnp.bfloat16), "grp", split_axis=0, concat_axis=0, tiled=True
    ).astype(group_total.dtype)
    final_part = jnp.sum(crossed, axis=0)
    flat_sum = lax.all_gather(final_part.astype(jnp.bfloat16), "grp", axis=0, tiled=True).astype(
        final_part.dtype
    )
    results = []
    offset = 0
    for weight_grad in weight_grads:
        part_len = weight_grad.size // seq_count
        results.append(
            flat_sum[offset : offset + part_len].reshape(
                (weight_grad.shape[0] // seq_count,) + weight_grad.shape[1:]
            )
        )
        offset = offset + part_len
    return (
        out_tokens,
        out_global,
        grad_tokens,
        grad_global,
        results[0],
        results[1],
        results[2],
        results[3],
        results[4],
        results[5],
        results[6],
        results[7],
        results[8],
        results[9],
        results[10],
        results[11],
        results[12],
        results[13],
        results[14],
    )


SEQ_WAYS = 4
GRP_WAYS = 8
OWN_HEADS = HEADS // SEQ_WAYS
OWN = D // SEQ_WAYS
FF = 3072
FF_OWN = FF // SEQ_WAYS
TOK = 128
ROWS = SEQ_WAYS * TOK
ALL = ROWS + GLOBALS
GLOB_OWN = GLOBALS // SEQ_WAYS
CHUNK = TOK + GLOB_OWN
PIECE = OWN // GRP_WAYS
BAND = SEQ_WAYS * PIECE
WIN = TOK + 2 * RADIUS
PAD = ROWS + 2 * RADIUS
BF = jnp.bfloat16
F32 = jnp.float32
GELU_SCALE = math.sqrt(2.0 / math.pi)
GELU_CUBE = 0.044715
LOG_NORM = math.log(1.0 + ROWS)
SCORE_SCALE = 1.0 / math.sqrt(HEAD_DIM)
CORE_SWAP = [(0, 1), (1, 0), (2, 3), (3, 2)]
Y_SWAP = [(0, 2), (2, 0), (1, 3), (3, 1)]
X_SWAP = [(g, g ^ 1) for g in range(GRP_WAYS)]
Z_NEAR = [(g, g ^ 2) for g in range(GRP_WAYS)]
Z_FAR = [(g, g ^ 4) for g in range(GRP_WAYS)]
HALF_TOK = ROWS // 2
HALF_GLOB = GLOBALS // 2
HALF = HALF_TOK + HALF_GLOB
SEND = CHUNK + 32
CODED = D + 128
WIDE = 640
GRAPH_ROWS = 32
X_PAIRS = ((0, 1), (2, 3), (4, 5), (6, 7))
KERNEL_COST = 60_000_000_000
RICH = OWN_HEADS * 2 * 4


def nn(left, right):
    return lax.dot_general(left, right, (((1,), (0,)), ((), ())), preferred_element_type=F32)


def nt(left, right):
    return lax.dot_general(left, right, (((1,), (1,)), ((), ())), preferred_element_type=F32)


def tn(left, right):
    return lax.dot_general(left, right, (((0,), (0,)), ((), ())), preferred_element_type=F32)


def load(source, target, sem):
    copy = pltpu.make_async_copy(source, target, sem)
    copy.start()
    return copy


def pick(stacked, index):
    return lax.dynamic_index_in_dim(stacked, index, 0, keepdims=False)


def tie(*values):
    return lax.optimization_barrier(values)


def reach_seq(block):
    return lax.ppermute(block, "seq", CORE_SWAP), lax.ppermute(block, "seq", Y_SWAP)


def gather_seq(block):
    beside, across = reach_seq(block)
    return [block, beside, across, lax.ppermute(across, "seq", CORE_SWAP)]


def turn_core(chunks):
    me = lax.axis_index("seq")
    return lax.ppermute(jnp.stack([pick(chunks, me ^ 1), pick(chunks, me ^ 3)]), "seq", CORE_SWAP)


def turn_y(chunks, came):
    return jnp.stack([pick(chunks, lax.axis_index("seq") ^ 2), came[1]])


def turned(chunks, came, far):
    mine = pick(chunks, lax.axis_index("seq"))
    return jnp.concatenate([mine, came[0], far[0], far[1]], axis=0)


def added(kept, came):
    return (kept.astype(F32) + came.astype(F32)).astype(BF)


def swap_x(sent):
    return lax.ppermute(sent, "grp", X_SWAP)


def swap_near(sent):
    return lax.ppermute(sent, "grp", Z_NEAR)


def swap_far(sent):
    return lax.ppermute(sent, "grp", Z_FAR)


def halves(kept, came, bit):
    grid = added(kept, came).reshape((-1, 2) + kept.shape[1:])
    mine = lax.dynamic_index_in_dim(grid, bit, 1, keepdims=False)
    return mine, lax.dynamic_index_in_dim(grid, 1 - bit, 1, keepdims=False)


def row_stats(rows_in):
    centred = rows_in - jnp.mean(rows_in, axis=-1, keepdims=True)
    scale = lax.rsqrt(jnp.mean(centred * centred, axis=-1, keepdims=True) + EPSILON)
    return centred * scale, scale


def norm_back(cotangent, gain, rows_in):
    hat, scale = row_stats(rows_in)
    scaled = cotangent * gain
    back = scale * (
        scaled
        - jnp.mean(scaled, axis=-1, keepdims=True)
        - hat * jnp.mean(scaled * hat, axis=-1, keepdims=True)
    )
    return (
        back,
        jnp.sum(cotangent * hat, axis=0, keepdims=True),
        jnp.sum(cotangent, axis=0, keepdims=True),
    )


def gelu_parts(pre):
    square = pre * pre
    bent = jnp.tanh(GELU_SCALE * pre * (1.0 + GELU_CUBE * square))
    half = 0.5 * (1.0 + bent)
    slope = half + 0.5 * pre * (1.0 - bent * bent) * (
        GELU_SCALE * (1.0 + 3.0 * GELU_CUBE * square)
    )
    return pre * half, slope


def counts_of(neigh, first, width):
    spots = (lax.broadcasted_iota(jnp.int32, (neigh.shape[0], width), 1) + first).astype(F32)
    total = jnp.zeros((neigh.shape[0], width), F32)
    for k in range(NEIGH):
        total = total + jnp.where(neigh[:, k : k + 1] == spots, 1.0, 0.0)
    return total.astype(BF)


def as_row(ref):
    return ref[...].reshape(1, ref.shape[0])


def own_window(me):
    return pl.ds(pl.multiple_of(lax.div(3 * me, 2) * 128, 128), 256)


def own_part(wide, me):
    return jnp.where(me % 2 == 0, wide[:, :OWN], wide[:, 256 - OWN :])


def rich_rows(rich, me, h):
    lane = lax.broadcasted_iota(jnp.int32, (8, 4 * HEADS), 1)
    term = lax.broadcasted_iota(jnp.int32, (8, 4 * HEADS), 0)
    chosen = (lane == 4 * (OWN_HEADS * me + h) + term) & (term < 4)
    return nn(jnp.where(chosen, 1.0, 0.0).astype(BF), rich)


def rich_columns(rich, me, h):
    row = lax.broadcasted_iota(jnp.int32, (4 * HEADS, 128), 0)
    term = lax.broadcasted_iota(jnp.int32, (4 * HEADS, 128), 1)
    chosen = (row == 4 * (OWN_HEADS * me + h) + term) & (term < 4)
    return tn(rich, jnp.where(chosen, 1.0, 0.0).astype(BF))


def code_kernel(
    tok_any, neigh_any, rank_any, member_any, out_ref, tok_ref, neigh_ref, rank_ref, member_ref, sems
):
    pairs = (tok_any, tok_ref), (neigh_any, neigh_ref), (rank_any, rank_ref), (member_any, member_ref)
    copies = [load(source, target, sems.at[i]) for i, (source, target) in enumerate(pairs)]
    for copy in copies:
        copy.wait()
    out_ref[:, :D] = tok_ref[...]
    ints = jnp.concatenate(
        [neigh_ref[...], rank_ref[...], member_ref[...], jnp.zeros((TOK - 11, TOK), jnp.int32)], axis=0
    )
    ints = ints.astype(F32).T
    high = jnp.floor(ints * (1.0 / 256.0))
    low = ints - 256.0 * high
    out_ref[:, D:] = jnp.concatenate([low[:, :16], high[:, :16], low[:, 32:]], axis=1).astype(BF)


def decoded(coded):
    coded = coded.astype(F32)
    return coded + 256.0 * jnp.concatenate([coded[:, 16:], coded[:, :16]], axis=1)


def share_out(chunk_of, bit, pairs, kept_ref, sent_ref):
    for i, pair in enumerate(pairs):
        first, second = (chunk_of(g) for g in pair)
        kept_ref[i] = jnp.where(bit == 0, first, second)
        sent_ref[i] = jnp.where(bit == 0, second, first)


def row_pieces(ref, g):
    return [ref[OWN * p + PIECE * g : OWN * p + PIECE * (g + 1)] for p in range(SEQ_WAYS)]


def pair_terms(meta_col, meta_row, before_ref, distance_ref):
    for c in range(2):
        gap = meta_col[:, 8 + c : 9 + c] - meta_row[8 + c : 9 + c]
        before_ref[c] = jnp.where(gap < 0.0, 1.0, -1.0)
        distance_ref[c] = jnp.log(1.0 + jnp.abs(gap)) * (1.0 / LOG_NORM)


def attend_kernel(
    tok_a, tok_b, tok_c, tok_d, glob_ref, gain_ref, shift_ref, rich_q_ref, rich_k_ref,
    w_graph_any, w_query_any, w_key_any, w_value_any,
    both_ref, member_ref, glob_att_ref, meta_row_ref,
    agg_any, pre_any, super_any, normed_any, qkv_any, prob_any,
    agg_ref, pre_ref, super_ref, normed_ref, qkv_ref, prob_ref,
    padded, w_graph_ref, w_project_ref, keys, values, key_rich, meta_pad, before_ref, distance_ref,
    rich_left, far_ref, heads_out, attn_ref, meta_col_ref, sems, prob_sems,
):
    me = lax.axis_index("seq")
    graph_copy = load(w_graph_any, w_graph_ref, sems.at[0])
    project_copies = [
        load(weight.at[:, own_window(me)], w_project_ref.at[i], sems.at[1 + i])
        for i, weight in enumerate((w_query_any, w_key_any, w_value_any))
    ]
    padded[:RADIUS] = jnp.zeros((RADIUS, D), BF)
    padded[RADIUS + ROWS :] = jnp.zeros((RADIUS, D), BF)
    starts = [pl.multiple_of((me ^ k) * TOK, TOK) for k in range(SEQ_WAYS)]
    for start, tok in zip(starts, (tok_a, tok_b, tok_c, tok_d)):
        padded[pl.ds(start + RADIUS, TOK)] = tok[:, :D]
    for start, tok in zip(starts, (tok_a, tok_b, tok_c, tok_d)):
        floats = decoded(tok[:, D:])
        meta_col_ref[pl.ds(start, TOK)] = floats
        meta_row_ref[:, pl.ds(start, TOK)] = floats.T[:16]
        counts = counts_of(floats, 0, WIN)
        mean = nn(counts, padded[pl.ds(start, WIN)]) * (1.0 / NEIGH)
        agg_ref[pl.ds(start, TOK)] = mean.astype(BF)
    gain, shift = as_row(gain_ref), as_row(shift_ref)
    graph_copy.wait()
    for low in range(0, ROWS, 256):
        rows = slice(low, low + 256)
        pre = nn(agg_ref[rows], w_graph_ref[...])
        pre_ref[rows] = pre
        tokens = padded[RADIUS + low : RADIUS + low + 256].astype(F32)
        super_rows = tokens + gelu_parts(pre)[0]
        super_ref[rows] = super_rows
        normed_ref[rows] = (row_stats(super_rows)[0] * gain + shift).astype(BF)
    glob_hat = row_stats(glob_ref[...].astype(F32))[0]
    normed_ref[ROWS:] = (glob_hat * gain + shift).astype(BF)
    kept = [
        load(source, target, sems.at[4 + i])
        for i, (source, target) in enumerate((
            (agg_ref.at[:, own_window(me)], agg_any), (pre_ref, pre_any), (super_ref, super_any), (normed_ref, normed_any),
        ))
    ]
    normed = normed_ref[...]
    for part in range(3):
        project_copies[part].wait()
        projected = nn(normed, own_part(w_project_ref[part], me)).astype(BF)
        for h in range(OWN_HEADS):
            qkv_ref[part * OWN_HEADS + h] = projected[:, h * HEAD_DIM : (h + 1) * HEAD_DIM]
    kept.append(load(qkv_ref, qkv_any, sems.at[8]))
    rich_q, rich_k = rich_q_ref[...], rich_k_ref[...]
    spread_keys(qkv_ref, keys, values)
    meta_pad[...] = jnp.zeros((16, PAD), F32)
    meta_pad[:, RADIUS : RADIUS + ROWS] = meta_row_ref[...]

    def prepare(h, carry):
        key_rich[h] = nt(rich_rows(rich_k, me, h).astype(BF), keys[h])
        rich_left[h] = rich_columns(rich_q, me, h).astype(BF)
        return carry

    lax.fori_loop(0, OWN_HEADS, prepare, 0)

    def prob_copy(b):
        rows = pl.ds(pl.multiple_of(b * TOK, TOK), TOK)
        return pltpu.make_async_copy(prob_ref.at[:, rows], prob_any.at[:, rows], prob_sems.at[b])

    def block(b, carry):
        start = pl.multiple_of(b * TOK, TOK)
        rows = pl.ds(start, TOK)
        window = pl.ds(start, WIN)
        pair_terms(meta_col_ref[rows], meta_pad[:, window], before_ref, distance_ref)
        q_spot = lax.broadcasted_iota(jnp.int32, (TOK, WIN), 0)
        k_spot = lax.broadcasted_iota(jnp.int32, (TOK, WIN), 1)
        ahead = k_spot - q_spot
        place = k_spot + (start - RADIUS)
        mask = (ahead >= 0) & (ahead <= 2 * RADIUS) & (place >= 0) & (place < ROWS)
        far_ref[...] = jnp.where(mask, 0.0, MASKED)

        def head(h, inner):
            query = qkv_ref[h, rows]
            query_rich = nn(query, rich_left[h])
            right = key_rich[h, :, window]
            scores = nt(query, keys[h, window]) * SCORE_SCALE + far_ref[...]
            spread = None
            for c in range(2):
                logit = (query_rich[:, c : c + 1] + right[c : c + 1]) * before_ref[c]
                off = distance_ref[c] - (query_rich[:, 2 + c : 3 + c] + right[2 + c : 3 + c])
                scores = scores + (jnp.minimum(logit, 0.0) - 0.5 * off * off)
                grown = 1.0 + jnp.exp(-jnp.abs(logit))
                spread = grown if spread is None else spread * grown
            scores = scores - jnp.log(spread)
            glob_scores = nt(query, qkv_ref[OWN_HEADS + h, ROWS:]) * SCORE_SCALE
            top = jnp.maximum(
                jnp.max(scores, axis=-1, keepdims=True), jnp.max(glob_scores, axis=-1, keepdims=True)
            )
            prob = jnp.exp(scores - top)
            glob_prob = jnp.exp(glob_scores - top)
            total = jnp.sum(prob, axis=-1, keepdims=True) + jnp.sum(
                glob_prob, axis=-1, keepdims=True
            )
            inverse = 1.0 / total
            prob = prob * inverse
            glob_prob = glob_prob * inverse
            prob_ref[h, rows, :WIN] = prob
            prob_ref[h, rows, WIN : WIN + GLOBALS] = glob_prob
            mixed = nn(prob.astype(BF), values[h, window]) + nn(
                glob_prob.astype(BF), qkv_ref[2 * OWN_HEADS + h, ROWS:]
            )
            heads_out[h, rows] = mixed.astype(BF)
            return inner

        lax.fori_loop(0, OWN_HEADS, head, 0, unroll=True)
        prob_copy(b).start()
        return carry

    lax.fori_loop(0, SEQ_WAYS, block, 0)
    slot = lax.broadcasted_iota(jnp.int32, (GLOBALS, ROWS), 0).astype(F32)
    member = meta_row_ref[10:11] == slot

    def glob_head(h, carry):
        query = qkv_ref[h, ROWS:]
        scores = nt(query, qkv_ref[OWN_HEADS + h, :ROWS]) * SCORE_SCALE
        scores = jnp.where(member, scores, MASKED)
        own = nt(query, qkv_ref[OWN_HEADS + h, ROWS:]) * SCORE_SCALE
        top = jnp.maximum(
            jnp.max(scores, axis=-1, keepdims=True), jnp.max(own, axis=-1, keepdims=True)
        )
        prob = jnp.exp(scores - top)
        own_prob = jnp.exp(own - top)
        total = jnp.sum(prob, axis=-1, keepdims=True) + jnp.sum(own_prob, axis=-1, keepdims=True)
        inverse = 1.0 / total
        prob = prob * inverse
        own_prob = own_prob * inverse
        member_ref[h, :, :ROWS] = prob
        member_ref[h, :, ROWS : ROWS + GLOBALS] = own_prob
        mixed = nn(prob.astype(BF), qkv_ref[2 * OWN_HEADS + h, :ROWS]) + nn(
            own_prob.astype(BF), qkv_ref[2 * OWN_HEADS + h, ROWS:]
        )
        glob_att_ref[h] = mixed
        heads_out[h, ROWS:] = mixed.astype(BF)
        return carry

    lax.fori_loop(0, OWN_HEADS, glob_head, 0)
    for h in range(OWN_HEADS):
        attn_ref[:, h * HEAD_DIM : (h + 1) * HEAD_DIM] = heads_out[h]
    for half in range(2):
        span = slice(OWN * half, OWN * (half + 1))
        low, glob_low = HALF_TOK * half, ROWS + HALF_GLOB * half
        both_ref[:HALF_TOK, span] = attn_ref[low : low + HALF_TOK]
        both_ref[HALF_TOK:, span] = attn_ref[glob_low : glob_low + HALF_GLOB]
    for copy in kept:
        copy.wait()
    for b in range(SEQ_WAYS):
        prob_copy(b).wait()


def meta_columns(meta_row):
    return jnp.concatenate([meta_row, jnp.zeros((TOK - 16, TOK), F32)], axis=0).T


def spread_keys(qkv_ref, keys, values):
    edge = jnp.zeros((OWN_HEADS, RADIUS, HEAD_DIM), BF)
    for held, first in ((keys, OWN_HEADS), (values, 2 * OWN_HEADS)):
        held[:, :RADIUS] = edge
        held[:, RADIUS + ROWS :] = edge
        held[:, RADIUS : RADIUS + ROWS] = qkv_ref[first : first + OWN_HEADS, :ROWS]


def own_feed_kernel(
    att_a, att_b, att_c, att_d, gain_ref, shift_ref, bias_up_ref, bias_down_ref, cot_ref,
    super_any, glob_any, cot_glob_any, w_out_any, w_up_any, w_down_any,
    out_ref, send_ref,
    att_refs, glob_att_refs, super_ref, glob_ref, cot_glob_ref, w_out_ref, w_up_ref, w_down_ref,
    bias_ref, out_sum, back_sum, sems,
):
    me = lax.axis_index("seq")
    half = lax.div(me, 2)
    inner = lax.rem(me, 2)
    tok_rows = pl.ds(pl.multiple_of(inner * TOK, TOK), TOK)
    glob_rows = pl.ds(pl.multiple_of(HALF_TOK + inner * GLOB_OWN, GLOB_OWN), GLOB_OWN)
    own_tok = pl.ds(pl.multiple_of(me * TOK, TOK), TOK)
    own_glob = pl.ds(pl.multiple_of(me * GLOB_OWN, GLOB_OWN), GLOB_OWN)
    first = []
    for k, att in enumerate((att_a, att_b, att_c, att_d)):
        first.append(load(att.at[tok_rows], att_refs.at[k], sems.at[k]))
        first.append(load(att.at[glob_rows], glob_att_refs.at[k], sems.at[4 + k]))
    first.append(load(super_any.at[own_tok], super_ref, sems.at[8]))
    first.append(load(glob_any.at[own_glob], glob_ref, sems.at[9]))
    first.append(load(cot_glob_any.at[own_glob], cot_glob_ref, sems.at[10]))
    first.append(load(w_out_any, w_out_ref, sems.at[11]))

    def up_copy(j):
        span = pl.ds(pl.multiple_of(j * FF_OWN, FF_OWN), FF_OWN)
        return pltpu.make_async_copy(w_up_any.at[:, span], w_up_ref.at[j], sems.at[12 + j])

    def down_copy(j):
        span = pl.ds(pl.multiple_of(j * FF_OWN, FF_OWN), FF_OWN)
        return pltpu.make_async_copy(w_down_any.at[span], w_down_ref.at[j], sems.at[16 + j])

    for j in range(SEQ_WAYS):
        up_copy(j).start()
        down_copy(j).start()
    for copy in first:
        copy.wait()
    y_rows = jnp.concatenate([super_ref[...], glob_ref[...].astype(F32)], axis=0)
    for k in range(SEQ_WAYS):
        wide = jnp.concatenate([att_refs[k], glob_att_refs[k]], axis=0)
        mixed = jnp.where(half == 0, wide[:, :OWN], wide[:, OWN:])
        y_rows = y_rows + nn(mixed, w_out_ref[pl.ds(pl.multiple_of((me ^ k) * OWN, OWN), OWN)])
    gain = as_row(gain_ref)
    hat, scale = row_stats(y_rows)
    normed = (hat * gain + as_row(shift_ref)).astype(BF)
    cot = jnp.concatenate([cot_ref[...], cot_glob_ref[...]], axis=0)
    bias = as_row(bias_up_ref)
    for j in range(SEQ_WAYS):
        bias_ref[j : j + 1] = bias[:, FF_OWN * j : FF_OWN * (j + 1)]
    out_sum[...] = y_rows + as_row(bias_down_ref)
    back_sum[...] = jnp.zeros((CHUNK, D), F32)

    def units(j, carry):
        up_copy(j).wait()
        hidden, slope = gelu_parts(nn(normed, w_up_ref[j]) + bias_ref[pl.ds(j, 1)])
        down_copy(j).wait()
        d_pre = (nt(cot, w_down_ref[j]) * slope).astype(BF)
        back_sum[...] += nt(d_pre, w_up_ref[j])
        out_sum[...] += nn(hidden.astype(BF), w_down_ref[j])
        return carry

    lax.fori_loop(0, SEQ_WAYS, units, 0)
    out, back = out_sum[...], back_sum[...]
    out_ref[...] = out[:TOK].astype(BF)
    scaled = back * gain
    cot = cot.astype(F32)
    d_rows = cot + scale * (
        scaled
        - jnp.mean(scaled, axis=-1, keepdims=True)
        - hat * jnp.mean(scaled * hat, axis=-1, keepdims=True)
    )
    sums = [back * hat, back, cot]
    sums = [jnp.sum(rows, axis=0, keepdims=True) for rows in sums]
    send_ref[:CHUNK] = d_rows.astype(BF)
    send_ref[CHUNK : CHUNK + GLOB_OWN] = out[TOK:].astype(BF)
    sums = jnp.concatenate(sums + [jnp.zeros((13, D), F32)], axis=0)
    send_ref[CHUNK + GLOB_OWN :] = sums.astype(BF)


def feed_rows_kernel(
    att_a, att_b, att_c, att_d, cot_a, cot_b, cot_c, cot_d, cot_glob_ref, glob_ref, gain_ref,
    shift_ref, bias_ref, super_any, w_out_any, w_up_any,
    kept_ref, sent_ref, normed_ref, slope_ref, cot_ref,
    super_ref, w_out_ref, w_up_ref, hidden_ref, grad, sems,
):
    me, x = lax.axis_index("seq"), lax.rem(lax.axis_index("grp"), 2)
    mine = pl.multiple_of(me * FF_OWN, FF_OWN)
    copies = [
        load(super_any, super_ref, sems.at[0]),
        load(w_out_any, w_out_ref, sems.at[1]),
        load(w_up_any.at[:, pl.ds(mine, FF_OWN)], w_up_ref, sems.at[2]),
    ]
    for k, cot in enumerate((cot_a, cot_b, cot_c, cot_d)):
        b = me ^ k
        at = lax.div(b, 2) * HALF + lax.rem(b, 2) * TOK
        cot_ref[pl.ds(pl.multiple_of(at, 32), TOK)] = cot[...]
    for half in range(2):
        cot_ref[HALF * half + HALF_TOK : HALF * (half + 1)] = cot_glob_ref[
            HALF_GLOB * half : HALF_GLOB * (half + 1)
        ]
    gain, shift = as_row(gain_ref), as_row(shift_ref)
    bias = as_row(bias_ref)
    bias = [bias[:, FF_OWN * j : FF_OWN * (j + 1)] for j in range(SEQ_WAYS)]
    bias = jnp.where(me < 2, jnp.where(me == 0, bias[0], bias[1]), jnp.where(me == 2, bias[2], bias[3]))
    for copy in copies:
        copy.wait()
    for half in range(2):
        rows = slice(HALF * half, HALF * (half + 1))
        glob_rows = glob_ref[HALF_GLOB * half : HALF_GLOB * (half + 1)].astype(F32)
        y_rows = jnp.concatenate([super_ref[HALF_TOK * half : HALF_TOK * (half + 1)], glob_rows], axis=0)
        for k, att in enumerate((att_a, att_b, att_c, att_d)):
            w_rows = w_out_ref[pl.ds(pl.multiple_of((me ^ k) * OWN, OWN), OWN)]
            y_rows = y_rows + nn(att[:, OWN * half : OWN * (half + 1)], w_rows)
        normed = (row_stats(y_rows)[0] * gain + shift).astype(BF)
        normed_ref[rows] = normed
        hidden, slope = gelu_parts(nn(normed, w_up_ref[...]) + bias)
        hidden_ref[rows] = hidden.astype(BF)
        slope_ref[rows] = slope
    grad[...] = tn(hidden_ref[...], cot_ref[...])
    share_out(lambda g: grad[BAND * g : BAND * (g + 1)].astype(BF), x, X_PAIRS, kept_ref, sent_ref)


def feed_back_kernel(
    normed_ref, slope_ref, cot_ref, w_down_any,
    kept_ref, sent_ref, d_bias_ref, w_down_ref, d_pre_ref, grad, sems,
):
    me = lax.axis_index("seq")
    x = lax.rem(lax.axis_index("grp"), 2)
    mine = pl.ds(pl.multiple_of(me * FF_OWN, FF_OWN), FF_OWN)
    load(w_down_any.at[mine], w_down_ref, sems.at[0]).wait()
    d_bias = jnp.zeros((1, FF_OWN), F32)
    for half in range(2):
        rows = slice(HALF * half, HALF * (half + 1))
        d_pre = (nt(cot_ref[rows], w_down_ref[...]) * slope_ref[rows]).astype(BF)
        d_pre_ref[rows] = d_pre
        d_bias = d_bias + jnp.sum(d_pre.astype(F32), axis=0, keepdims=True)
    d_bias_ref[...] = d_bias
    grad[...] = tn(normed_ref[...], d_pre_ref[...])
    share_out(
        lambda g: jnp.concatenate(row_pieces(grad, g), axis=0).astype(BF), x, X_PAIRS, kept_ref, sent_ref
    )


def project_grad_kernel(normed_ref, d_qkv_ref, attn_ref, d_proj_ref, kept_ref, sent_ref, grad, grad_out):
    x = lax.rem(lax.axis_index("grp"), 2)
    grad[...] = tn(normed_ref[...], d_qkv_ref[:, : 3 * OWN])
    total = None
    for half in range(2):
        columns = slice(OWN * half, OWN * (half + 1))
        first, glob_first = HALF_TOK * half, ROWS + HALF_GLOB * half
        term = tn(attn_ref[:HALF_TOK, columns], d_proj_ref[first : first + HALF_TOK])
        term = term + tn(attn_ref[HALF_TOK:, columns], d_proj_ref[glob_first : glob_first + HALF_GLOB])
        total = term if total is None else total + term
    grad_out[...] = total

    def chunk(g):
        out_rows = grad_out[PIECE * g : PIECE * (g + 1)]
        left = jnp.concatenate(row_pieces(grad, g), axis=0)
        right = [out_rows[:, OWN * p : OWN * (p + 1)] for p in range(SEQ_WAYS)]
        return jnp.concatenate([left, jnp.concatenate(right, axis=0)], axis=1).astype(BF)

    share_out(chunk, x, X_PAIRS, kept_ref, sent_ref)


def back_kernel(
    back_a, back_b, back_c, back_d, glob_att_ref, meta_row_ref, rich_q_ref,
    rich_k_ref, w_out_any, qkv_any, prob_any, member_any,
    d_proj_ref, d_qkv_ref, vec_ref, out_global_ref,
    w_out_ref, qkv_ref, prob_ref, member_ref, keys, values, key_rich, meta_pad, before_ref, distance_ref,
    rich_left, d_att, d_keys, d_values, d_key_rich, d_query_rich, rich_qt, rich_kt, d_glob, parts, rich,
    sems, prob_sems,
):
    me = lax.axis_index("seq")
    own_rows = pl.ds(pl.multiple_of(me * OWN, OWN), OWN)
    w_copy = load(w_out_any.at[own_rows], w_out_ref, sems.at[0])
    qkv_copy = load(qkv_any, qkv_ref, sems.at[1])

    def prob_copy(b):
        rows = pl.ds(pl.multiple_of(b * TOK, TOK), TOK)
        return pltpu.make_async_copy(prob_any.at[:, rows], prob_ref.at[:, rows], prob_sems.at[b])

    for b in range(SEQ_WAYS):
        prob_copy(b).start()
    member_copy = load(member_any, member_ref, sems.at[2])
    sums = None
    for k, back in enumerate((back_a, back_b, back_c, back_d)):
        at = me ^ k
        d_proj_ref[pl.ds(pl.multiple_of(at * TOK, TOK), TOK)] = back[:TOK]
        d_proj_ref[pl.ds(pl.multiple_of(ROWS + at * GLOB_OWN, GLOB_OWN), GLOB_OWN)] = back[TOK:CHUNK]
        out_global_ref[pl.ds(pl.multiple_of(at * GLOB_OWN, GLOB_OWN), GLOB_OWN)] = back[
            CHUNK : CHUNK + GLOB_OWN
        ]
        part = back[CHUNK + GLOB_OWN :].astype(F32)
        sums = part if sums is None else sums + part
    vec_ref[...] = sums[:8]
    w_copy.wait()
    projected = nt(d_proj_ref[...], w_out_ref[...]).astype(BF)
    for h in range(OWN_HEADS):
        d_att[h] = projected[:, h * HEAD_DIM : (h + 1) * HEAD_DIM]
    meta_pad[...] = jnp.zeros((16, PAD), F32)
    meta_pad[:, RADIUS : RADIUS + ROWS] = meta_row_ref[...]
    qkv_copy.wait()
    spread_keys(qkv_ref, keys, values)
    rich_q, rich_k = rich_q_ref[...], rich_k_ref[...]

    def prepare(h, carry):
        rich_left[h] = rich_columns(rich_q, me, h).astype(BF)
        rich_qt[h] = rich_rows(rich_q, me, h)
        rich_kt[h] = rich_rows(rich_k, me, h)
        key_rich[h] = nt(rich_kt[h].astype(BF), keys[h])
        return carry

    lax.fori_loop(0, OWN_HEADS, prepare, 0)
    d_keys[...] = jnp.zeros((OWN_HEADS, PAD, HEAD_DIM), F32)
    d_values[...] = jnp.zeros((OWN_HEADS, PAD, HEAD_DIM), F32)
    d_key_rich[...] = jnp.zeros((OWN_HEADS, 8, PAD), F32)
    d_glob[...] = jnp.zeros((2 * OWN_HEADS, GLOBALS, HEAD_DIM), F32)

    def block(b, carry):
        start = pl.multiple_of(b * TOK, TOK)
        rows = pl.ds(start, TOK)
        window = pl.ds(start, WIN)
        pair_terms(meta_columns(meta_row_ref[:, rows]), meta_pad[:, window], before_ref, distance_ref)
        prob_copy(b).wait()

        def head(h, inner):
            query = qkv_ref[h, rows]
            d_out = d_att[h, rows]
            prob = prob_ref[h, rows, :WIN]
            glob_prob = prob_ref[h, rows, WIN : WIN + GLOBALS]
            d_prob = nt(d_out, values[h, window])
            d_glob_prob = nt(d_out, qkv_ref[2 * OWN_HEADS + h, ROWS:])
            delta = jnp.sum(prob * d_prob, axis=-1, keepdims=True) + jnp.sum(
                glob_prob * d_glob_prob, axis=-1, keepdims=True
            )
            d_scores = prob * (d_prob - delta)
            d_low = d_scores.astype(BF)
            d_glob_low = (glob_prob * (d_glob_prob - delta)).astype(BF)
            query_rich = nn(query, rich_left[h])
            right = key_rich[h, :, window]
            lefts, belows = [None] * 4, [None] * 4
            for c in range(2):
                logit = query_rich[:, c : c + 1] + right[c : c + 1]
                pulled = d_scores * (0.5 * before_ref[c] - 0.5 * jnp.tanh(0.5 * logit))
                off = distance_ref[c] - (query_rich[:, 2 + c : 3 + c] + right[2 + c : 3 + c])
                off = d_scores * off
                lefts[c] = jnp.sum(pulled, axis=-1, keepdims=True)
                lefts[2 + c] = jnp.sum(off, axis=-1, keepdims=True)
                belows[c] = jnp.sum(pulled, axis=0, keepdims=True)
                belows[2 + c] = jnp.sum(off, axis=0, keepdims=True)
            d_key_rich[h, :, window] += jnp.concatenate(belows + [jnp.zeros((4, WIN), F32)], axis=0)
            lane = lax.broadcasted_iota(jnp.int32, (TOK, 8), 1)
            d_left = jnp.zeros((TOK, 8), F32)
            d_query = (
                nn(d_low, keys[h, window]) + nn(d_glob_low, qkv_ref[OWN_HEADS + h, ROWS:])
            ) * SCORE_SCALE
            for c, column in enumerate(lefts):
                d_left = jnp.where(lane == c, column, d_left)
                d_query = d_query + column * rich_qt[h, c : c + 1]
            d_query_rich[h, rows] = d_left
            parts[h, rows] = d_query.astype(BF)
            d_keys[h, window] += tn(d_low, query) * SCORE_SCALE
            d_values[h, window] += tn(prob.astype(BF), d_out)
            d_glob[h] += tn(d_glob_low, query) * SCORE_SCALE
            d_glob[OWN_HEADS + h] += tn(glob_prob.astype(BF), d_out)
            return inner

        lax.fori_loop(0, OWN_HEADS, head, 0, unroll=True)
        return carry

    lax.fori_loop(0, SEQ_WAYS, block, 0)
    member_copy.wait()

    def glob_head(h, carry):
        query = qkv_ref[h, ROWS:]
        key_rows = qkv_ref[OWN_HEADS + h, :ROWS]
        value_rows = qkv_ref[2 * OWN_HEADS + h, :ROWS]
        glob_key = qkv_ref[OWN_HEADS + h, ROWS:]
        glob_value = qkv_ref[2 * OWN_HEADS + h, ROWS:]
        d_out = d_att[h, ROWS:]
        delta = jnp.sum(d_out.astype(F32) * glob_att_ref[h], axis=-1, keepdims=True)
        prob = member_ref[h, :, :ROWS]
        own_prob = member_ref[h, :, ROWS : ROWS + GLOBALS]
        d_low = (prob * (nt(d_out, value_rows) - delta)).astype(BF)
        d_own = (own_prob * (nt(d_out, glob_value) - delta)).astype(BF)
        d_query = (nn(d_low, key_rows) + nn(d_own, glob_key)) * SCORE_SCALE
        parts[h, ROWS:] = d_query.astype(BF)
        parts[OWN_HEADS + h, ROWS:] = (d_glob[h] + tn(d_own, query) * SCORE_SCALE).astype(BF)
        parts[2 * OWN_HEADS + h, ROWS:] = (
            d_glob[OWN_HEADS + h] + tn(own_prob.astype(BF), d_out)
        ).astype(BF)
        d_right = d_key_rich[h, :, RADIUS : RADIUS + ROWS]
        d_key = d_keys[h, RADIUS : RADIUS + ROWS] + tn(d_low, query) * SCORE_SCALE
        d_key = d_key + lax.dot_general(
            d_right, rich_kt[h], (((0,), (0,)), ((), ())), precision=PRECISE,
            preferred_element_type=F32,
        )
        d_value = d_values[h, RADIUS : RADIUS + ROWS] + tn(prob.astype(BF), d_out)
        parts[OWN_HEADS + h, :ROWS] = d_key.astype(BF)
        parts[2 * OWN_HEADS + h, :ROWS] = d_value.astype(BF)
        rich[pl.ds(pl.multiple_of(8 * h, 8), 8)] = jnp.concatenate(
            [tn(d_query_rich[h].astype(BF), qkv_ref[h, :ROWS])[:4], nn(d_right.astype(BF), key_rows)[:4]],
            axis=0,
        )
        return carry

    lax.fori_loop(0, OWN_HEADS, glob_head, 0)
    for i in range(3 * OWN_HEADS):
        d_qkv_ref[:, i * HEAD_DIM : (i + 1) * HEAD_DIM] = parts[i]
    rich[RICH:] = jnp.zeros((32 - RICH, HEAD_DIM), F32)
    d_qkv_ref[:, 3 * OWN :] = jnp.zeros((ALL, WIDE - 3 * OWN), BF)
    d_qkv_ref[:32, 3 * OWN :] = rich[...].astype(BF)


def norm_kernel(
    dqkv_a, dqkv_b, dqkv_c, dqkv_d, glob_ref, d_proj_ref, gain_ref, vec_two_ref, d_bias_up_ref,
    w_query_any, w_key_any, w_value_any, super_any, pre_any, agg_any,
    grad_glob_ref, kept_ref, sent_ref, d_own_ref, d_pre,
    w_query_ref, w_key_ref, w_value_ref, super_ref, pre_ref, agg_ref, d_super, d_qkv, d_norm, rich, sems,
):
    me, x = lax.axis_index("seq"), lax.rem(lax.axis_index("grp"), 2)
    weight_copies = [
        load(source, target, sems.at[i])
        for i, (source, target) in enumerate((
            (w_query_any, w_query_ref), (w_key_any, w_key_ref), (w_value_any, w_value_ref),
        ))
    ]
    row_copies = [load(super_any, super_ref, sems.at[3]), load(pre_any, pre_ref, sems.at[4])]
    agg_copy = load(agg_any, agg_ref, sems.at[5])
    for k, part in enumerate((dqkv_a, dqkv_b, dqkv_c, dqkv_d)):
        d_qkv[me ^ k] = part[...]
        rich[me ^ k] = part[:32, 3 * OWN :].astype(F32)
    total = None
    for i, weight in enumerate((w_query_ref, w_key_ref, w_value_ref)):
        weight_copies[i].wait()
        for p in range(SEQ_WAYS):
            term = nt(d_qkv[p, :, OWN * i : OWN * (i + 1)], weight[:, OWN * p : OWN * (p + 1)])
            total = term if total is None else total + term
    d_norm[...] = total
    for copy in row_copies:
        copy.wait()
    gain = as_row(gain_ref)
    d_gain = jnp.zeros((1, D), F32)
    d_shift = jnp.zeros((1, D), F32)
    for low in range(0, ALL, 192):
        rows = slice(low, low + 192)
        inner = min(192, ROWS - low)
        if inner == 192:
            rows_in = super_ref[rows]
        else:
            rows_in = jnp.concatenate([super_ref[low:], glob_ref[...].astype(F32)], axis=0)
        back, gain_part, shift_part = norm_back(d_norm[rows], gain, rows_in)
        d_gain = d_gain + gain_part
        d_shift = d_shift + shift_part
        back = back + d_proj_ref[rows].astype(F32)
        d_super[rows] = back
        long = slice(low, low + inner)
        slope = gelu_parts(pre_ref[long])[1]
        d_pre[long] = (back[:inner] * slope).astype(BF)
    grad_glob_ref[...] = d_super[ROWS:]
    d_own_ref[...] = d_super[pl.ds(pl.multiple_of(me * TOK, TOK), TOK)]
    agg_copy.wait()
    grad = tn(own_part(agg_ref[...], me), d_pre[...])
    extra = jnp.concatenate(
        [vec_two_ref[0:3], d_bias_up_ref[...], d_gain, d_shift, jnp.zeros((1, D), F32)], axis=0
    )

    def chunk(g):
        pieces = [rich[g // 2, 12 * (g % 2) + i : 12 * (g % 2) + i + 1] for i in range(12)]
        rows = [grad[PIECE * g : PIECE * (g + 1)], jnp.concatenate(pieces, axis=1), extra]
        return jnp.concatenate(rows, axis=0).astype(BF)

    share_out(chunk, x, X_PAIRS, kept_ref, sent_ref)


def tokens_kernel(d_own_ref, d_pre, meta_row_ref, w_graph_any, grad_tok_ref, w_graph_ref, sems):
    me = lax.axis_index("seq")
    copy = load(w_graph_any, w_graph_ref, sems.at[0])
    counts = []
    for shift in (-1, 0, 1):
        rows = pl.ds(pl.multiple_of(jnp.clip(me - shift, 0, SEQ_WAYS - 1) * TOK, TOK), TOK)
        counts.append(counts_of(meta_columns(meta_row_ref[:, rows]), (shift + 1) * TOK, TOK))
    copy.wait()
    total = d_own_ref[...]
    for shift, count in zip((-1, 0, 1), counts):
        b = me - shift
        fits = (b >= 0) & (b < SEQ_WAYS)
        rows = pl.ds(pl.multiple_of(jnp.clip(b, 0, SEQ_WAYS - 1) * TOK, TOK), TOK)
        d_agg = (nt(d_pre[rows], w_graph_ref[...]) * (1.0 / NEIGH)).astype(BF)
        total = total + jnp.where(fits, tn(count, d_agg), 0.0)
    grad_tok_ref[...] = total


DISTANCES = (0, 4, 2, 6)


def down_out_kernel(held, came, out_ref):
    for i, distance in enumerate(DISTANCES):
        for flip, pieces in enumerate((held, came)):
            g = lax.axis_index("grp") ^ (distance + flip)
            out_ref[pl.ds(pl.multiple_of(BAND * g, BAND), BAND)] = pieces[i].astype(F32)


def up_out_kernel(held, came, out_ref):
    for i, distance in enumerate(DISTANCES):
        for flip, pieces in enumerate((held, came)):
            g = lax.axis_index("grp") ^ (distance + flip)
            piece = pieces[i].astype(F32)
            rows = pl.ds(pl.multiple_of(PIECE * g, 8), PIECE)
            for k in range(SEQ_WAYS):
                columns = pl.ds(pl.multiple_of((lax.axis_index("seq") ^ k) * D, D), D)
                out_ref[rows, columns] = piece[PIECE * k : PIECE * (k + 1)]


def project_out_kernel(held, came, query_ref, key_ref, value_ref, out_ref, pieces):
    for i, distance in enumerate(DISTANCES):
        for flip, blocks in enumerate((held, came)):
            g = lax.axis_index("grp") ^ (distance + flip)
            rows = pl.ds(pl.multiple_of(PIECE * g, 8), PIECE)
            piece = blocks[i].astype(F32)
            for k in range(SEQ_WAYS):
                pieces[lax.axis_index("seq") ^ k] = piece[PIECE * k : PIECE * (k + 1), : 3 * OWN]
            for j, ref in enumerate((query_ref, key_ref, value_ref)):
                parts = [pieces[p, :, OWN * j : OWN * (j + 1)] for p in range(SEQ_WAYS)]
                ref[rows] = jnp.concatenate(parts, axis=1)
            parts = [piece[PIECE * p : PIECE * (p + 1), 3 * OWN :] for p in range(SEQ_WAYS)]
            out_ref[rows] = jnp.concatenate(parts, axis=1)


def graph_out_kernel(
    held, came, graph_ref, gain_one_ref, shift_one_ref, gain_two_ref, shift_two_ref, bias_up_ref,
    bias_down_ref, rich_q_ref, rich_k_ref, vectors,
):
    me = lax.axis_index("seq")
    for i, distance in enumerate(DISTANCES):
        for flip, blocks in enumerate((held, came)):
            g = lax.axis_index("grp") ^ (distance + flip)
            rows = pl.ds(pl.multiple_of(PIECE * g, 8), PIECE)
            piece = blocks[i].astype(F32)
            graph_ref[rows] = piece[:PIECE]
            for j in range(12):
                vectors[g, j : j + 1] = piece[PIECE : PIECE + 1, HEAD_DIM * j : HEAD_DIM * (j + 1)]
            vectors[g, 12:16] = jnp.zeros((4, HEAD_DIM), F32)
    sums = held[0, PIECE : PIECE + 8].astype(F32)
    lane = lax.broadcasted_iota(jnp.int32, (D, 256), 0)
    spot = lax.broadcasted_iota(jnp.int32, (D, 256), 1)
    own = jnp.where((lane == OWN * me + spot) & (spot < OWN), 1.0, 0.0).astype(BF)
    own = nn(sums.astype(BF), own)[:, :OWN]
    for ref, row in (
        (gain_two_ref, 1), (shift_two_ref, 2), (bias_down_ref, 3), (gain_one_ref, 5), (shift_one_ref, 6),
    ):
        ref[...] = own[row : row + 1].reshape(OWN)
    bias_up_ref[...] = sums[4:5].reshape(FF_OWN)
    lane = lax.broadcasted_iota(jnp.int32, (HEAD_DIM, 128), 0)
    spot = lax.broadcasted_iota(jnp.int32, (HEAD_DIM, 128), 1)
    part = HEAD_DIM // SEQ_WAYS
    own = jnp.where((lane == part * me + spot) & (spot < part), 1.0, 0.0).astype(BF)
    own = nn(vectors[...].reshape(16 * GRP_WAYS, HEAD_DIM).astype(BF), own).astype(BF)
    row = lax.broadcasted_iota(jnp.int32, (16 * GRP_WAYS, 128), 0)
    place = 12 * lax.div(row, 16) + lax.rem(row, 16)
    column = lax.broadcasted_iota(jnp.int32, (16 * GRP_WAYS, 128), 1)
    for side, ref in enumerate((rich_q_ref, rich_k_ref)):
        wanted = 8 * lax.div(column, 4) + 4 * side + lax.rem(column, 4)
        chosen = (place == wanted) & (lax.rem(row, 16) < 12) & (column < 4 * HEADS)
        turned_rich = tn(own, jnp.where(chosen, 1.0, 0.0).astype(BF))
        ref[...] = turned_rich[:part, : 4 * HEADS]


def call(kernel, ins, outs, scratch=(), apart=0, outs_apart=0, room=50):
    vmem, any_space = pl.BlockSpec(memory_space=pltpu.VMEM), pl.BlockSpec(memory_space=pltpu.HBM)
    return pl.pallas_call(
        kernel,
        out_shape=[jax.ShapeDtypeStruct(shape, kind) for shape, kind in outs],
        in_specs=[vmem] * (len(ins) - apart) + [any_space] * apart,
        out_specs=[vmem] * (len(outs) - outs_apart) + [any_space] * outs_apart,
        scratch_shapes=[pltpu.VMEM(*s) if isinstance(s, tuple) else s for s in scratch],
        compiler_params=pltpu.CompilerParams(vmem_limit_bytes=room * 1024 * 1024),
        cost_estimate=pl.CostEstimate(flops=KERNEL_COST, bytes_accessed=0, transcendentals=0),
    )(*ins)


def split_heads(
    tokens, global_tokens, neighbours, token_ranks, membership, w_graph, gain_one, shift_one,
    w_query, w_key, w_value, rich_query, rich_key, w_out, gain_two, shift_two, w_up, bias_up,
    w_down, bias_down, cot_tokens, cot_global,
):
    me = lax.axis_index("seq")
    grp = lax.axis_index("grp")
    x, z_low, z_high = grp % 2, (grp // 2) % 2, grp // 4
    (coded,) = call(
        code_kernel,
        [tokens, neighbours.T, token_ranks, membership.reshape(1, TOK)],
        [((TOK, CODED), BF)],
        [((TOK, D), BF), ((NEIGH, TOK), jnp.int32), ((2, TOK), jnp.int32), ((1, TOK), jnp.int32),
         pltpu.SemaphoreType.DMA((4,))],
        apart=4, room=60,
    )
    beside, across = reach_seq(coded)
    cot_tokens, across = tie(cot_tokens, across)
    tok_blocks = [coded, beside, across, lax.ppermute(across, "seq", CORE_SWAP)]
    cot_beside, cot_across = reach_seq(cot_tokens)
    rich_query, rich_key = rich_query.T, rich_key.T

    weights_shape = (D, D), BF
    stored = [
        ((ROWS, D), BF), ((ROWS, D), F32), ((ROWS, D), F32), ((ALL, D), BF),
        ((3 * OWN_HEADS, ALL, HEAD_DIM), BF), ((OWN_HEADS, ROWS, 512), F32),
    ]
    kept_agg = (ROWS, 256), BF
    heads_scratch = [
        ((OWN_HEADS, PAD, HEAD_DIM), BF), ((OWN_HEADS, PAD, HEAD_DIM), BF),
        ((OWN_HEADS, 8, PAD), F32), ((16, PAD), F32), ((2, TOK, WIN), F32), ((2, TOK, WIN), F32),
        ((OWN_HEADS, HEAD_DIM, 128), BF),
    ]
    (
        both, member_prob, glob_att, meta_row, agg, graph_pre, super_rows, normed, qkv,
        prob,
    ) = call(
        attend_kernel,
        [*tok_blocks, global_tokens, gain_one, shift_one, rich_query, rich_key, w_graph, w_query,
         w_key, w_value],
        [((HALF, 2 * OWN), BF), ((OWN_HEADS, GLOBALS, 640), F32),
         ((OWN_HEADS, GLOBALS, HEAD_DIM), F32), ((16, ROWS), F32), kept_agg, *stored[1:]],
        [*stored, ((PAD, D), BF), weights_shape, ((3, D, 256), BF), *heads_scratch,
         ((TOK, WIN), F32), ((OWN_HEADS, ALL, HEAD_DIM), BF), ((ALL, OWN), BF),
         ((ROWS, 128), F32), pltpu.SemaphoreType.DMA((9,)), pltpu.SemaphoreType.DMA((SEQ_WAYS,))],
        apart=4, outs_apart=6,
    )
    both, cot_beside, cot_across = tie(both, cot_beside, cot_across)
    att_blocks = gather_seq(both)
    cot_blocks = [cot_tokens, cot_beside, cot_across, lax.ppermute(cot_across, "seq", CORE_SWAP)]
    out_tokens, back = call(
        own_feed_kernel,
        [*att_blocks, gain_two, shift_two, bias_up, bias_down, cot_tokens, super_rows,
         global_tokens, cot_global, w_out, w_up, w_down],
        [((TOK, D), BF), ((SEND, D), BF)],
        [((SEQ_WAYS, TOK, 2 * OWN), BF), ((SEQ_WAYS, GLOB_OWN, 2 * OWN), BF), ((TOK, D), F32),
         ((GLOB_OWN, D), BF), ((GLOB_OWN, D), BF), weights_shape, ((SEQ_WAYS, D, FF_OWN), BF),
         ((SEQ_WAYS, FF_OWN, D), BF), ((SEQ_WAYS, FF_OWN), F32), ((CHUNK, D), F32), ((CHUNK, D), F32),
         pltpu.SemaphoreType.DMA((20,))],
        apart=6,
    )
    beside, across = reach_seq(back)
    late_gain, back = tie(gain_two, back)
    down_kept, down_sent, normed_two, slope, cot_all = call(
        feed_rows_kernel,
        [*att_blocks, *cot_blocks, cot_global, global_tokens, late_gain, shift_two,
         bias_up, super_rows, w_out, w_up],
        [((4, BAND, D), BF), ((4, BAND, D), BF), ((ALL, D), BF), ((ALL, FF_OWN), F32), ((ALL, D), BF)],
        [((ROWS, D), F32), weights_shape, ((D, FF_OWN), BF), ((ALL, FF_OWN), BF), ((D, D), F32),
         pltpu.SemaphoreType.DMA((3,))],
        apart=3,
    )
    down_came = swap_x(down_sent)
    across, down_kept = tie(across, down_kept)
    diagonal = lax.ppermute(across, "seq", CORE_SWAP)
    normed_two, across = tie(normed_two, across)
    up_kept, up_sent, d_bias_up = call(
        feed_back_kernel,
        [normed_two, slope, cot_all, w_down],
        [((4, BAND, D), BF), ((4, BAND, D), BF), ((1, FF_OWN), F32)],
        [((FF_OWN, D), BF), ((ALL, FF_OWN), BF), ((D, D), F32), pltpu.SemaphoreType.DMA((1,))],
        apart=1,
    )
    up_came = swap_x(up_sent)
    late_row, up_kept = tie(meta_row, up_kept)

    d_proj, d_qkv, vec_two, out_global = call(
        back_kernel,
        [back, beside, across, diagonal, glob_att, late_row, rich_query, rich_key,
         w_out, qkv, prob, member_prob],
        [((ALL, D), BF), ((ALL, WIDE), BF), ((8, D), F32), ((GLOBALS, D), BF)],
        [((OWN, D), BF), stored[4], stored[5], ((OWN_HEADS, GLOBALS, 640), F32), *heads_scratch,
         ((OWN_HEADS, ALL, HEAD_DIM), BF), ((OWN_HEADS, PAD, HEAD_DIM), F32),
         ((OWN_HEADS, PAD, HEAD_DIM), F32), ((OWN_HEADS, 8, PAD), F32), ((OWN_HEADS, ROWS, 8), F32),
         ((OWN_HEADS, 8, HEAD_DIM), F32), ((OWN_HEADS, 8, HEAD_DIM), F32),
         ((2 * OWN_HEADS, GLOBALS, HEAD_DIM), F32), ((3 * OWN_HEADS, ALL, HEAD_DIM), BF),
         ((32, HEAD_DIM), F32), pltpu.SemaphoreType.DMA((3,)), pltpu.SemaphoreType.DMA((SEQ_WAYS,))],
        apart=4,
    )
    beside, across = reach_seq(d_qkv)
    held = {"d_qkv": d_qkv, "down": down_kept, "up": up_kept}
    latest = ["d_qkv"]

    def due(value):
        value, held[latest[0]] = tie(value, held[latest[0]])
        return value

    def hold(key, value):
        held[key] = value
        latest[0] = key
        return value

    def halve(key, came, bit):
        kept, sent = halves(held[key], due(came), bit)
        hold(key, kept)
        return sent

    def total(key, came):
        return hold(key, added(held[key], due(came)))

    def join(key, came):
        return hold(key, jnp.concatenate([held[key], due(came)], axis=0))

    down_came = swap_near(halve("down", down_came, z_low))
    proj_kept, proj_sent = call(
        project_grad_kernel,
        [due(normed), d_qkv, both, d_proj],
        [((4, BAND, D), BF)] * 2,
        [((D, 3 * OWN), F32), ((OWN, D), F32)],
    )
    hold("proj", proj_kept)
    proj_came = swap_x(proj_sent)
    down_came = swap_far(halve("down", down_came, z_high))
    up_came = swap_near(halve("up", up_came, z_low))
    across = hold("across", due(across))
    diagonal = lax.ppermute(across, "seq", CORE_SWAP)
    down_came = swap_far(total("down", down_came))
    up_came = swap_far(halve("up", up_came, z_high))
    proj_came = swap_near(halve("proj", proj_came, z_low))

    grad_global, graph_kept, graph_sent, d_own, d_pre = call(
        norm_kernel,
        [d_qkv, beside, held["across"], diagonal, global_tokens, d_proj, gain_one, due(vec_two), d_bias_up,
         w_query, w_key, w_value, super_rows, graph_pre, agg],
        [((GLOBALS, D), F32), ((4, GRAPH_ROWS, D), BF), ((4, GRAPH_ROWS, D), BF), ((TOK, D), F32),
         ((ROWS, D), BF)],
        [*[weights_shape] * 3, ((ROWS, D), F32), ((ROWS, D), F32), ((ROWS, 256), BF), ((ALL, D), F32),
         ((SEQ_WAYS, ALL, WIDE), BF), ((ALL, D), F32), ((SEQ_WAYS, 32, HEAD_DIM), F32),
         pltpu.SemaphoreType.DMA((6,))],
        apart=6,
    )
    hold("graph", graph_kept)
    graph_came = swap_x(graph_sent)
    up_mine = total("up", up_came).reshape(SEQ_WAYS, PIECE, D)
    up_core = turn_core(up_mine)
    proj_came = swap_far(halve("proj", proj_came, z_high))
    down_came = swap_near(join("down", down_came))
    up_core = due(up_core)
    up_far = lax.ppermute(turn_y(up_mine, up_core), "seq", Y_SWAP)
    hold("up_core", up_core)
    (grad_tokens,) = call(
        tokens_kernel, [due(d_own), d_pre, meta_row, w_graph], [((TOK, D), F32)],
        [weights_shape, pltpu.SemaphoreType.DMA((1,))], apart=1,
    )
    hold("tokens", grad_tokens)
    up_came = swap_far(hold("up", turned(up_mine, held["up_core"], due(up_far))[None]))
    proj_sum = total("proj", proj_came)
    proj_core = turn_core(proj_sum[0, :, : 3 * OWN].reshape(SEQ_WAYS, PIECE, 3 * OWN))
    down_came = swap_x(join("down", down_came))
    graph_came = swap_near(halve("graph", graph_came, z_low))
    proj_core = due(proj_core)
    proj_mine = held["proj"][0, :, : 3 * OWN].reshape(SEQ_WAYS, PIECE, 3 * OWN)
    proj_far = lax.ppermute(turn_y(proj_mine, proj_core), "seq", Y_SWAP)
    hold("proj_core", proj_core)
    up_came = swap_near(join("up", up_came))
    proj_turned = turned(proj_mine, held["proj_core"], due(proj_far))
    proj_turned = jnp.concatenate([proj_turned, held["proj"][0, :, 3 * OWN :]], axis=1)[None]
    proj_came = swap_far(hold("proj", proj_turned))
    up_came = swap_x(join("up", up_came))
    proj_came = swap_near(join("proj", proj_came))
    graph_came = swap_far(halve("graph", graph_came, z_high))
    graph_came = swap_far(total("graph", graph_came))
    (g_down,) = call(down_out_kernel, [held["down"], due(down_came)], [((FF_OWN, D), F32)])
    hold("g_down", g_down)
    graph_came = swap_near(join("graph", graph_came))
    proj_came = swap_x(join("proj", proj_came))
    (g_up,) = call(up_out_kernel, [held["up"], due(up_came)], [((OWN, FF), F32)])
    hold("g_up", g_up)
    graph_came = swap_x(join("graph", graph_came))
    g_query, g_key, g_value, g_out = call(
        project_out_kernel,
        [held["proj"], due(proj_came)],
        [((OWN, D), F32)] * 4,
        [((SEQ_WAYS, PIECE, 3 * OWN), F32)],
    )
    hold("g_query", g_query)
    (
        g_graph, g_gain_one, g_shift_one, g_gain_two, g_shift_two, g_bias_up, g_bias_down, g_rich_q,
        g_rich_k,
    ) = call(
        graph_out_kernel,
        [held["graph"], due(graph_came)],
        [((OWN, D), F32), *[((OWN,), F32)] * 4, ((FF_OWN,), F32), ((OWN,), F32),
         *[((HEAD_DIM // SEQ_WAYS, 4 * HEADS), F32)] * 2],
        [((GRP_WAYS, 16, HEAD_DIM), F32)],
    )
    grad_tokens, g_down, g_up, g_query = (held[key] for key in ("tokens", "g_down", "g_up", "g_query"))
    return (
        out_tokens, out_global, grad_tokens, grad_global,
        g_graph, g_gain_one, g_shift_one, g_query, g_key, g_value, g_rich_q, g_rich_k,
        g_out, g_gain_two, g_shift_two, g_up, g_bias_up, g_down, g_bias_down,
    )


def layer(*arrays):
    tokens, global_tokens = arrays[:2]
    ways = (lax.axis_size("seq"), lax.axis_size("grp"))
    if ways == (SEQ_WAYS, GRP_WAYS) and tokens.shape[0] == TOK and global_tokens.shape[0] == GLOBALS:
        return split_heads(*arrays)
    return local(*arrays)


def solution(mesh):
    return jax.shard_map(
        layer,
        mesh=mesh,
        in_specs=(
            P(("grp", "seq"), None),
            P("grp", None),
            P(("grp", "seq"), None),
            P(None, ("grp", "seq")),
            P(("grp", "seq")),
            P(),
            P(),
            P(),
            P(),
            P(),
            P(),
            P(),
            P(),
            P(),
            P(),
            P(),
            P(),
            P(),
            P(),
            P(),
            P(("grp", "seq"), None),
            P("grp", None),
        ),
        out_specs=(
            P(("grp", "seq"), None),
            P("grp", None),
            P(("grp", "seq"), None),
            P("grp", None),
            P("seq", None),
            P("seq"),
            P("seq"),
            P("seq", None),
            P("seq", None),
            P("seq", None),
            P("seq", None),
            P("seq", None),
            P("seq", None),
            P("seq"),
            P("seq"),
            P("seq", None),
            P("seq"),
            P("seq", None),
            P("seq"),
        ),
        check_vma=False,
    )
```

```python
import functools
import math

import jax
import jax.numpy as jnp
from jax import lax
from jax.experimental import pallas as pl
from jax.experimental.pallas import tpu as pltpu
from jax.sharding import PartitionSpec as P

D = 768
HEADS = 12
HEAD_DIM = 64
RADIUS = 128
GLOBALS = 64
NEIGH = 8
SEQ_TOKENS = 2048


EPSILON = 1e-05
PRECISE = lax.Precision.HIGHEST
MASKED = -1e30


def with_halo(cells, sides, width):
    for axis, dim in sides:
        count = lax.axis_size(axis)
        ends = count - 1
        head = lax.slice_in_dim(cells, 0, width, axis=dim)
        tail = lax.slice_in_dim(cells, cells.shape[dim] - width, cells.shape[dim], axis=dim)
        cells = jnp.concatenate(
            [
                lax.ppermute(tail, axis, [(i, (i + 1) % count) for i in range(ends)]),
                cells,
                lax.ppermute(head, axis, [((i + 1) % count, i) for i in range(ends)]),
            ],
            axis=dim,
        )
    return cells


def joined(array, axis, combine):
    everything = jax.tree.map(
        lambda part, kind: lax.all_gather(part.astype(kind), axis),
        array,
        (jnp.bfloat16, jnp.bfloat16, jnp.bfloat16),
    )

    def take(k):
        return jax.tree.map(lambda part, own: part[k].astype(own.dtype), everything, array)

    return lax.fori_loop(
        1, lax.axis_size(axis), lambda k, so_far: combine(so_far, take(k)), take(0)
    )


def shifted(block, axis, distance):
    devices = range(lax.axis_size(axis))
    route = [(i - distance, i) for i in devices if i - distance in devices]
    return lax.ppermute(block, axis, route)


def layer_norm(rows_in, gain_in, shift_in):
    row_mean = jnp.mean(rows_in, axis=-1, keepdims=True)
    centred = rows_in - row_mean
    variance = jnp.mean(centred * centred, axis=-1, keepdims=True)
    return centred * lax.rsqrt(variance + EPSILON) * gain_in + shift_in


def rich_part(a_block, b_window, rank_query, rank_key, log_norm):
    combined = None
    for coordinate in range(2):
        order_flag = (rank_query[coordinate][:, None] < rank_key[coordinate][None, :]).astype(
            jnp.float32
        )
        distance = (
            jnp.log1p(
                jnp.abs(rank_query[coordinate][:, None] - rank_key[coordinate][None, :]).astype(
                    jnp.float32
                )
            )
            / log_norm
        )
        order_logit = a_block[:, :, None, coordinate] + b_window[:, None, :, coordinate]
        centre = a_block[:, :, None, 2 + coordinate] + b_window[:, None, :, 2 + coordinate]
        pair_term = (
            order_flag * jax.nn.log_sigmoid(order_logit)
            + (1.0 - order_flag) * jax.nn.log_sigmoid(-order_logit)
            - 0.5 * (distance - centre) ** 2
        )
        combined = pair_term if combined is None else combined + pair_term
    return combined


def product(left, right):
    return jnp.dot(left, right, preferred_element_type=jnp.float32)


def product_left(left, right):
    return jnp.einsum("ta,tb->ab", left, right, preferred_element_type=jnp.float32)


def product_right(left, right):
    return jnp.einsum("tb,ab->ta", left, right, preferred_element_type=jnp.float32)


def local(
    tokens,
    global_tokens,
    neighbours,
    token_ranks,
    membership,
    w_graph,
    gain_one,
    shift_one,
    w_query,
    w_key,
    w_value,
    rich_query,
    rich_key,
    w_out,
    gain_two,
    shift_two,
    w_up,
    bias_up,
    w_down,
    bias_down,
    cot_tokens,
    cot_global,
):
    tok_count = tokens.shape[0]
    seq_count = lax.axis_size("seq")
    seq_index = lax.axis_index("seq")
    seq_len = min(SEQ_TOKENS, tok_count * seq_count)
    span = seq_len // tok_count
    group_seqs = global_tokens.shape[0] // GLOBALS
    seq_slot = seq_index // span
    seq_local = seq_index % span
    slot_flag = (jnp.arange(group_seqs, dtype=jnp.int32) == seq_slot).astype(jnp.float32)
    log_norm = math.log(1.0 + seq_len)
    score_scale = 1.0 / math.sqrt(HEAD_DIM)
    block_rows = min(512, tok_count)
    window = block_rows + 2 * RADIUS
    ext_count = tok_count + 2 * RADIUS
    first_flag = (seq_index == 0).astype(jnp.float32)
    own_pos = seq_local * tok_count + jnp.arange(tok_count, dtype=jnp.int32)
    ext_pos = seq_local * tok_count - RADIUS + jnp.arange(ext_count, dtype=jnp.int32)
    key_valid = (ext_pos >= 0) & (ext_pos < seq_len)

    def own_slot(array_in):
        return lax.dynamic_index_in_dim(array_in, seq_slot, 0, keepdims=False)

    def to_slots(array_in):
        return slot_flag.reshape((group_seqs,) + (1,) * array_in.ndim) * array_in[None]

    token_ext = with_halo(tokens, (("seq", 0),), RADIUS)
    token_ext = jnp.where(key_valid[:, None], token_ext, jnp.zeros_like(token_ext))
    flat_index = neighbours.reshape(-1)
    gathered = (
        jnp.take(token_ext, flat_index, axis=0).astype(jnp.float32).reshape(tok_count, NEIGH, D)
    )
    agg_low = jnp.mean(gathered, axis=1).astype(jnp.bfloat16)
    graph_pre = product(agg_low, w_graph)
    graph_out, graph_back = jax.vjp(jax.nn.gelu, graph_pre)
    super_rows = tokens.astype(jnp.float32) + graph_out
    normed_full, norm_back = jax.vjp(layer_norm, super_rows, gain_one, shift_one)
    normed = normed_full.astype(jnp.bfloat16)
    glob_in = global_tokens.astype(jnp.float32)
    glob_normed_full, glob_norm_back = jax.vjp(layer_norm, glob_in, gain_one, shift_one)
    glob_normed = glob_normed_full.astype(jnp.bfloat16)
    query = product(normed, w_query).astype(jnp.bfloat16)
    key_own = product(normed, w_key).astype(jnp.bfloat16)
    value_own = product(normed, w_value).astype(jnp.bfloat16)
    glob_query = (
        product(glob_normed, w_query)
        .astype(jnp.bfloat16)
        .reshape(group_seqs, GLOBALS, HEADS, HEAD_DIM)
    )
    glob_key = (
        product(glob_normed, w_key)
        .astype(jnp.bfloat16)
        .reshape(group_seqs, GLOBALS, HEADS, HEAD_DIM)
    )
    glob_value = (
        product(glob_normed, w_value)
        .astype(jnp.bfloat16)
        .reshape(group_seqs, GLOBALS, HEADS, HEAD_DIM)
    )
    glob_query_own = own_slot(glob_query)
    glob_key_own = own_slot(glob_key)
    glob_value_own = own_slot(glob_value)
    kv_ext = with_halo(jnp.concatenate([key_own, value_own], axis=1), (("seq", 0),), RADIUS)
    key_ext = kv_ext[:, :D].reshape(ext_count, HEADS, HEAD_DIM)
    value_ext = kv_ext[:, D:].reshape(ext_count, HEADS, HEAD_DIM)
    rank_ext = with_halo(token_ranks, (("seq", 1),), RADIUS)
    rich_q3 = rich_query.reshape(HEAD_DIM, HEADS, 4)
    rich_k3 = rich_key.reshape(HEAD_DIM, HEADS, 4)
    query_heads = query.reshape(tok_count, HEADS, HEAD_DIM)
    a_rows = jnp.einsum("the,ehc->htc", query_heads, rich_q3, preferred_element_type=jnp.float32)
    b_ext = jnp.einsum("the,ehc->htc", key_ext, rich_k3, preferred_element_type=jnp.float32)

    def block_scores():

        def rich_scores(left_rows, right_rows):
            return rich_part(left_rows, right_rows, token_ranks, rank_ext, log_norm)

        rich_vals, rich_back = jax.vjp(rich_scores, a_rows, b_ext)
        raw_scores = (
            jnp.einsum("qhe,khe->hqk", query_heads, key_ext, preferred_element_type=jnp.float32)
            * score_scale
        )
        pos_gap = own_pos[:, None] - ext_pos[None, :]
        key_mask = (jnp.abs(pos_gap) <= RADIUS) & key_valid[None, :]
        scores = jnp.where(key_mask[None], raw_scores + rich_vals, MASKED)
        glob_scores = (
            jnp.einsum(
                "qhe,ghe->hqg", query_heads, glob_key_own, preferred_element_type=jnp.float32
            )
            * score_scale
        )
        return (scores, glob_scores, rich_back, query_heads, key_ext)

    scored = block_scores()
    scores = scored[0]
    glob_scores = scored[1]
    row_top = jnp.maximum(jnp.max(scores, axis=-1), jnp.max(glob_scores, axis=-1))
    row_denom = jnp.sum(jnp.exp(scores - row_top[..., None]), axis=-1) + jnp.sum(
        jnp.exp(glob_scores - row_top[..., None]), axis=-1
    )
    log_total = row_top + jnp.log(row_denom)
    prob_rows = jnp.exp(scores - log_total[..., None]).astype(jnp.bfloat16)
    glob_probs = jnp.exp(glob_scores - log_total[..., None]).astype(jnp.bfloat16)
    attn_block = jnp.einsum(
        "hqk,khe->qhe", prob_rows, value_ext, preferred_element_type=jnp.float32
    ) + jnp.einsum("hqg,ghe->qhe", glob_probs, glob_value_own, preferred_element_type=jnp.float32)
    attn_parts = attn_block.reshape(block_rows, D)
    attn_rows = attn_parts.astype(jnp.bfloat16)
    member_mask = membership[None, :] == jnp.arange(GLOBALS, dtype=jnp.int32)[:, None]
    key_heads = key_ext[RADIUS : RADIUS + tok_count]
    value_heads = value_ext[RADIUS : RADIUS + tok_count]
    member_raw = (
        jnp.einsum("ghe,the->ght", glob_query_own, key_heads, preferred_element_type=jnp.float32)
        * score_scale
    )
    member_scores = jnp.where(member_mask[:, None, :], member_raw, MASKED)
    local_top = jnp.max(member_scores, axis=-1)
    member_exp = jnp.where(
        member_mask[:, None, :], jnp.exp(member_scores - local_top[..., None]), 0.0
    )
    local_sum = jnp.sum(member_exp, axis=-1)
    local_acc = jnp.einsum(
        "ght,the->ghe", member_exp, value_heads.astype(jnp.float32), precision=PRECISE
    )
    slot_top = jnp.where(slot_flag[:, None, None] > 0.5, local_top[None], MASKED)
    slot_sum = to_slots(local_sum)
    slot_acc = to_slots(local_acc)

    def combine_softmax(first_part, second_part):
        top_one, sum_one, acc_one = first_part
        top_two, sum_two, acc_two = second_part
        top_both = jnp.maximum(top_one, top_two)
        scale_one = jnp.exp(top_one - top_both)
        scale_two = jnp.exp(top_two - top_both)
        return (
            top_both,
            sum_one * scale_one + sum_two * scale_two,
            acc_one * scale_one[..., None] + acc_two * scale_two[..., None],
        )

    merged_top, merged_sum, merged_acc = joined(
        (slot_top, slot_sum, slot_acc), "seq", combine_softmax
    )
    self_scores = (
        jnp.einsum("sghe,skhe->sghk", glob_query, glob_key, preferred_element_type=jnp.float32)
        * score_scale
    )
    glob_top = jnp.maximum(merged_top, jnp.max(self_scores, axis=-1))
    self_exp = jnp.exp(self_scores - glob_top[..., None])
    merged_scale = jnp.exp(merged_top - glob_top)
    glob_denom = merged_sum * merged_scale + jnp.sum(self_exp, axis=-1)
    glob_lse = glob_top + jnp.log(glob_denom)
    glob_att_f = (
        merged_acc * merged_scale[..., None]
        + jnp.einsum("sghk,skhe->sghe", self_exp, glob_value.astype(jnp.float32), precision=PRECISE)
    ) / glob_denom[..., None]
    glob_attn = glob_att_f.reshape(group_seqs * GLOBALS, D).astype(jnp.bfloat16)
    y_one = super_rows + product(attn_rows, w_out)
    glob_y_one = glob_in + product(glob_attn, w_out)

    def feed_forward(rows_in):
        normed_two_full, back_two = jax.vjp(layer_norm, rows_in, gain_two, shift_two)
        normed_two = normed_two_full.astype(jnp.bfloat16)
        hidden_pre = product(normed_two, w_up) + bias_up
        hidden_full, gelu_back = jax.vjp(jax.nn.gelu, hidden_pre)
        hidden = hidden_full.astype(jnp.bfloat16)
        result = rows_in + product(hidden, w_down) + bias_down
        return (result, normed_two, hidden, back_two, gelu_back)

    def feed_back(cotangent, normed_two, hidden, back_two, gelu_back):
        cot_full = cotangent.astype(jnp.float32)
        grad_down = product_left(hidden, cotangent)
        grad_bias_d = jnp.sum(cot_full, axis=0)
        d_hidden = product_right(cotangent, w_down)
        d_pre = gelu_back(d_hidden)[0].astype(jnp.bfloat16)
        grad_up = product_left(normed_two, d_pre)
        grad_bias_u = jnp.sum(d_pre.astype(jnp.float32), axis=0)
        d_normed_two = product_right(d_pre, w_up)
        d_rows, grad_gain, grad_shift = back_two(d_normed_two)
        return (
            cot_full + d_rows,
            (grad_gain, grad_shift, grad_up, grad_bias_u, grad_down, grad_bias_d),
        )

    long_ff = feed_forward(y_one)
    glob_ff = feed_forward(glob_y_one)
    out_tokens = long_ff[0].astype(jnp.bfloat16)
    out_global = glob_ff[0].astype(jnp.bfloat16)
    d_y_one, long_mlp = feed_back(cot_tokens, long_ff[1], long_ff[2], long_ff[3], long_ff[4])
    glob_d_y_one, glob_mlp = feed_back(cot_global, glob_ff[1], glob_ff[2], glob_ff[3], glob_ff[4])
    mlp_grads = [
        local_part + first_flag * glob_part for local_part, glob_part in zip(long_mlp, glob_mlp)
    ]
    d_proj = d_y_one.astype(jnp.bfloat16)
    glob_d_proj = glob_d_y_one.astype(jnp.bfloat16)
    grad_out = product_left(attn_rows, d_proj) + first_flag * product_left(glob_attn, glob_d_proj)
    d_attn = product_right(d_proj, w_out).astype(jnp.bfloat16).reshape(tok_count, HEADS, HEAD_DIM)
    glob_d_attn = (
        product_right(glob_d_proj, w_out)
        .astype(jnp.bfloat16)
        .reshape(group_seqs, GLOBALS, HEADS, HEAD_DIM)
    )
    glob_d_attn_own = own_slot(glob_d_attn)
    rich_q3_full = rich_q3.astype(jnp.float32)
    rich_k3_full = rich_k3.astype(jnp.float32)
    d_key_ext = jnp.zeros((ext_count, HEADS, HEAD_DIM), jnp.float32)
    d_value_ext = jnp.zeros((ext_count, HEADS, HEAD_DIM), jnp.float32)
    scores, glob_scores, rich_back, q_part, key_win = block_scores()
    prob_full = jnp.exp(scores - log_total[..., None])
    glob_prob_full = jnp.exp(glob_scores - log_total[..., None])
    d_probs = jnp.einsum("qhe,khe->hqk", d_attn, value_ext, preferred_element_type=jnp.float32)
    glob_d_probs = jnp.einsum(
        "qhe,ghe->hqg", d_attn, glob_value_own, preferred_element_type=jnp.float32
    )
    row_delta = jnp.sum(prob_full * d_probs, axis=-1) + jnp.sum(
        glob_prob_full * glob_d_probs, axis=-1
    )
    d_scores = (prob_full * (d_probs - row_delta[..., None])).astype(jnp.bfloat16)
    glob_d_scores = (glob_prob_full * (glob_d_probs - row_delta[..., None])).astype(jnp.bfloat16)
    query_rich_grad, key_rich_grad = rich_back(d_scores.astype(jnp.float32))
    query_grad = (
        jnp.einsum("hqk,khe->qhe", d_scores, key_win, preferred_element_type=jnp.float32)
        + jnp.einsum(
            "hqg,ghe->qhe", glob_d_scores, glob_key_own, preferred_element_type=jnp.float32
        )
    ) * score_scale + jnp.einsum("hqc,ehc->qhe", query_rich_grad, rich_q3_full, precision=PRECISE)
    key_win_grad = jnp.einsum(
        "hqk,qhe->khe", d_scores, q_part, preferred_element_type=jnp.float32
    ) * score_scale + jnp.einsum("hkc,ehc->khe", key_rich_grad, rich_k3_full, precision=PRECISE)
    value_win_grad = jnp.einsum(
        "hqk,qhe->khe", prob_full.astype(jnp.bfloat16), d_attn, preferred_element_type=jnp.float32
    )
    d_key_ext = d_key_ext.at[0:window].add(key_win_grad)
    d_value_ext = d_value_ext.at[0:window].add(value_win_grad)
    glob_key_grad = (
        jnp.einsum("hqg,qhe->ghe", glob_d_scores, q_part, preferred_element_type=jnp.float32)
        * score_scale
    )
    glob_value_grad = jnp.einsum(
        "hqg,qhe->ghe",
        glob_prob_full.astype(jnp.bfloat16),
        d_attn,
        preferred_element_type=jnp.float32,
    )
    grad_rich_q = jnp.einsum(
        "qhe,hqc->ehc", q_part.astype(jnp.float32), query_rich_grad, precision=PRECISE
    )
    grad_rich_k = jnp.einsum(
        "khe,hkc->ehc", key_win.astype(jnp.float32), key_rich_grad, precision=PRECISE
    )
    query_grads = query_grad.reshape(block_rows, D)
    glob_delta = jnp.sum(glob_d_attn.astype(jnp.float32) * glob_att_f, axis=-1)
    glob_delta_own = own_slot(glob_delta)
    glob_lse_own = own_slot(glob_lse)
    member_probs = jnp.where(
        member_mask[:, None, :], jnp.exp(member_scores - glob_lse_own[..., None]), 0.0
    )
    member_d_probs = jnp.einsum(
        "ghe,the->ght", glob_d_attn_own, value_heads, preferred_element_type=jnp.float32
    )
    member_d_scores = (member_probs * (member_d_probs - glob_delta_own[..., None])).astype(
        jnp.bfloat16
    )
    glob_query_part = (
        jnp.einsum("ght,the->ghe", member_d_scores, key_heads, preferred_element_type=jnp.float32)
        * score_scale
    )
    own_key_extra = (
        jnp.einsum(
            "ght,ghe->the", member_d_scores, glob_query_own, preferred_element_type=jnp.float32
        )
        * score_scale
    )
    own_value_extra = jnp.einsum(
        "ght,ghe->the", member_probs, glob_d_attn_own.astype(jnp.float32), precision=PRECISE
    )
    d_key_ext = d_key_ext.at[RADIUS : RADIUS + tok_count].add(own_key_extra)
    d_value_ext = d_value_ext.at[RADIUS : RADIUS + tok_count].add(own_value_extra)
    grad_rims = jnp.concatenate(
        [d_key_ext.reshape(ext_count, D), d_value_ext.reshape(ext_count, D)], axis=1
    )
    from_above = shifted(grad_rims[:RADIUS].astype(jnp.bfloat16), "seq", -1).astype(jnp.float32)
    from_below = shifted(grad_rims[tok_count + RADIUS :].astype(jnp.bfloat16), "seq", 1).astype(
        jnp.float32
    )
    kv_grad = grad_rims[RADIUS : RADIUS + tok_count]
    kv_grad = kv_grad.at[:RADIUS].add(from_below).at[tok_count - RADIUS :].add(from_above)
    summed_query, summed_key, summed_value = (
        lax.psum(to_slots(glob_query_part).astype(jnp.bfloat16), "seq").astype(jnp.float32),
        lax.psum(to_slots(glob_key_grad).astype(jnp.bfloat16), "seq").astype(jnp.float32),
        lax.psum(to_slots(glob_value_grad).astype(jnp.bfloat16), "seq").astype(jnp.float32),
    )
    self_probs = jnp.exp(self_scores - glob_lse[..., None])
    self_d_probs = jnp.einsum(
        "sghe,skhe->sghk", glob_d_attn, glob_value, preferred_element_type=jnp.float32
    )
    self_d_scores = (self_probs * (self_d_probs - glob_delta[..., None])).astype(jnp.bfloat16)
    glob_rows_total = group_seqs * GLOBALS
    glob_d_query = (
        (
            summed_query
            + jnp.einsum(
                "sghk,skhe->sghe", self_d_scores, glob_key, preferred_element_type=jnp.float32
            )
            * score_scale
        )
        .astype(jnp.bfloat16)
        .reshape(glob_rows_total, D)
    )
    glob_d_key = (
        (
            summed_key
            + jnp.einsum(
                "sghk,sghe->skhe", self_d_scores, glob_query, preferred_element_type=jnp.float32
            )
            * score_scale
        )
        .astype(jnp.bfloat16)
        .reshape(glob_rows_total, D)
    )
    glob_d_value = (
        (
            summed_value
            + jnp.einsum(
                "sghk,sghe->skhe", self_probs, glob_d_attn.astype(jnp.float32), precision=PRECISE
            )
        )
        .astype(jnp.bfloat16)
        .reshape(glob_rows_total, D)
    )
    d_query = query_grads.astype(jnp.bfloat16)
    d_key = kv_grad[:, :D].astype(jnp.bfloat16)
    d_value = kv_grad[:, D:].astype(jnp.bfloat16)
    grad_query = product_left(normed, d_query) + first_flag * product_left(
        glob_normed, glob_d_query
    )
    grad_key = product_left(normed, d_key) + first_flag * product_left(glob_normed, glob_d_key)
    grad_value = product_left(normed, d_value) + first_flag * product_left(
        glob_normed, glob_d_value
    )
    d_normed = (
        product_right(d_query, w_query)
        + product_right(d_key, w_key)
        + product_right(d_value, w_value)
    )
    glob_d_normed = (
        product_right(glob_d_query, w_query)
        + product_right(glob_d_key, w_key)
        + product_right(glob_d_value, w_value)
    )
    d_super_norm, grad_gain_one, grad_shift_one = norm_back(d_normed)
    d_super = d_y_one + d_super_norm
    glob_d_norm, glob_gain_one, glob_shift_one = glob_norm_back(glob_d_normed)
    grad_global = glob_d_y_one + glob_d_norm
    grad_gain_one = grad_gain_one + first_flag * glob_gain_one
    grad_shift_one = grad_shift_one + first_flag * glob_shift_one
    d_graph_pre = graph_back(d_super)[0].astype(jnp.bfloat16)
    grad_graph = product_left(agg_low, d_graph_pre)
    d_agg = product_right(d_graph_pre, w_graph) / NEIGH
    d_token_ext = (
        jnp.zeros((ext_count, D), jnp.float32).at[flat_index].add(jnp.repeat(d_agg, NEIGH, axis=0))
    )
    d_token_ext = jnp.where(key_valid[:, None], d_token_ext, 0.0)
    token_above = shifted(d_token_ext[:RADIUS].astype(jnp.bfloat16), "seq", -1).astype(jnp.float32)
    token_below = shifted(d_token_ext[tok_count + RADIUS :].astype(jnp.bfloat16), "seq", 1).astype(
        jnp.float32
    )
    own_grad = (
        d_token_ext[RADIUS : RADIUS + tok_count]
        .at[:RADIUS]
        .add(token_below)
        .at[tok_count - RADIUS :]
        .add(token_above)
    )
    grad_tokens = d_super + own_grad
    weight_grads = (
        grad_graph,
        grad_gain_one,
        grad_shift_one,
        grad_query,
        grad_key,
        grad_value,
        grad_rich_q.reshape(HEAD_DIM, 4 * HEADS),
        grad_rich_k.reshape(HEAD_DIM, 4 * HEADS),
        grad_out,
        mlp_grads[0],
        mlp_grads[1],
        mlp_grads[2],
        mlp_grads[3],
        mlp_grads[4],
        mlp_grads[5],
    )
    pieces = [weight_grad.reshape(seq_count, -1) for weight_grad in weight_grads]
    packed = jnp.concatenate(pieces, axis=1)
    group_count = lax.axis_size("grp")
    received = lax.all_to_all(
        packed.astype(jnp.bfloat16), "seq", split_axis=0, concat_axis=0, tiled=True
    ).astype(packed.dtype)
    group_total = jnp.sum(received, axis=0).reshape(group_count, -1)
    crossed = lax.all_to_all(
        group_total.astype(jnp.bfloat16), "grp", split_axis=0, concat_axis=0, tiled=True
    ).astype(group_total.dtype)
    final_part = jnp.sum(crossed, axis=0)
    flat_sum = lax.all_gather(final_part.astype(jnp.bfloat16), "grp", axis=0, tiled=True).astype(
        final_part.dtype
    )
    results = []
    offset = 0
    for weight_grad in weight_grads:
        part_len = weight_grad.size // seq_count
        results.append(
            flat_sum[offset : offset + part_len].reshape(
                (weight_grad.shape[0] // seq_count,) + weight_grad.shape[1:]
            )
        )
        offset = offset + part_len
    return (
        out_tokens,
        out_global,
        grad_tokens,
        grad_global,
        results[0],
        results[1],
        results[2],
        results[3],
        results[4],
        results[5],
        results[6],
        results[7],
        results[8],
        results[9],
        results[10],
        results[11],
        results[12],
        results[13],
        results[14],
    )


SEQ_WAYS = 4
GRP_WAYS = 8
OWN_HEADS = HEADS // SEQ_WAYS
OWN = D // SEQ_WAYS
FF = 3072
FF_OWN = FF // SEQ_WAYS
TOK = 128
ROWS = SEQ_WAYS * TOK
ALL = ROWS + GLOBALS
GLOB_OWN = GLOBALS // SEQ_WAYS
CHUNK = TOK + GLOB_OWN
PIECE = OWN // GRP_WAYS
BAND = SEQ_WAYS * PIECE
WIN = TOK + 2 * RADIUS
PAD = ROWS + 2 * RADIUS
BF = jnp.bfloat16
F32 = jnp.float32
GELU_SCALE = math.sqrt(2.0 / math.pi)
GELU_CUBE = 0.044715
LOG_NORM = math.log(1.0 + ROWS)
SCORE_SCALE = 1.0 / math.sqrt(HEAD_DIM)
CORE_SWAP = [(0, 1), (1, 0), (2, 3), (3, 2)]
Y_SWAP = [(0, 2), (2, 0), (1, 3), (3, 1)]
X_SWAP = [(g, g ^ 1) for g in range(GRP_WAYS)]
Z_NEAR = [(g, g ^ 2) for g in range(GRP_WAYS)]
Z_FAR = [(g, g ^ 4) for g in range(GRP_WAYS)]
HALF_TOK = ROWS // 2
HALF_GLOB = GLOBALS // 2
HALF = HALF_TOK + HALF_GLOB
SEND = CHUNK + 32
WIDE = 640
GRAPH_ROWS = 32
X_PAIRS = ((0, 1), (2, 3), (4, 5), (6, 7))
KERNEL_COST = 60_000_000_000
RICH = OWN_HEADS * 2 * 4


def nn(left, right):
    return lax.dot_general(left, right, (((1,), (0,)), ((), ())), preferred_element_type=F32)


def nt(left, right):
    return lax.dot_general(left, right, (((1,), (1,)), ((), ())), preferred_element_type=F32)


def tn(left, right):
    return lax.dot_general(left, right, (((0,), (0,)), ((), ())), preferred_element_type=F32)


def load(source, target, sem):
    copy = pltpu.make_async_copy(source, target, sem)
    copy.start()
    return copy


def pick(stacked, index):
    return lax.dynamic_index_in_dim(stacked, index, 0, keepdims=False)


def tie(*values):
    return lax.optimization_barrier(values)


def reach_seq(block):
    return lax.ppermute(block, "seq", CORE_SWAP), lax.ppermute(block, "seq", Y_SWAP)


def gather_seq(block):
    beside, across = reach_seq(block)
    return [block, beside, across, lax.ppermute(across, "seq", CORE_SWAP)]


def turn_core(chunks):
    me = lax.axis_index("seq")
    return lax.ppermute(jnp.stack([pick(chunks, me ^ 1), pick(chunks, me ^ 3)]), "seq", CORE_SWAP)


def turn_y(chunks, came):
    return jnp.stack([pick(chunks, lax.axis_index("seq") ^ 2), came[1]])


def turned(chunks, came, far):
    mine = pick(chunks, lax.axis_index("seq"))
    return jnp.concatenate([mine, came[0], far[0], far[1]], axis=0)


def added(kept, came):
    return (kept.astype(F32) + came.astype(F32)).astype(BF)


def swap_x(sent):
    return lax.ppermute(sent, "grp", X_SWAP)


def swap_near(sent):
    return lax.ppermute(sent, "grp", Z_NEAR)


def swap_far(sent):
    return lax.ppermute(sent, "grp", Z_FAR)


def halves(kept, came, bit):
    grid = added(kept, came).reshape((-1, 2) + kept.shape[1:])
    mine = lax.dynamic_index_in_dim(grid, bit, 1, keepdims=False)
    return mine, lax.dynamic_index_in_dim(grid, 1 - bit, 1, keepdims=False)


def row_stats(rows_in):
    centred = rows_in - jnp.mean(rows_in, axis=-1, keepdims=True)
    scale = lax.rsqrt(jnp.mean(centred * centred, axis=-1, keepdims=True) + EPSILON)
    return centred * scale, scale


def norm_back(cotangent, gain, rows_in):
    hat, scale = row_stats(rows_in)
    scaled = cotangent * gain
    back = scale * (
        scaled
        - jnp.mean(scaled, axis=-1, keepdims=True)
        - hat * jnp.mean(scaled * hat, axis=-1, keepdims=True)
    )
    return (
        back,
        jnp.sum(cotangent * hat, axis=0, keepdims=True),
        jnp.sum(cotangent, axis=0, keepdims=True),
    )


def gelu_parts(pre):
    square = pre * pre
    bent = jnp.tanh(GELU_SCALE * pre * (1.0 + GELU_CUBE * square))
    half = 0.5 * (1.0 + bent)
    slope = half + 0.5 * pre * (1.0 - bent * bent) * (
        GELU_SCALE * (1.0 + 3.0 * GELU_CUBE * square)
    )
    return pre * half, slope


def ints_kernel(neigh_ref, rank_ref, member_ref, out_ref):
    out_ref[:NEIGH] = neigh_ref[...]
    out_ref[NEIGH:] = jnp.concatenate(
        [rank_ref[...], member_ref[...], jnp.zeros((16 - NEIGH - 3, TOK), jnp.int32)], axis=0
    )


def counts_of(neigh, first, width):
    spots = (lax.broadcasted_iota(jnp.int32, (neigh.shape[0], width), 1) + first).astype(F32)
    total = jnp.zeros((neigh.shape[0], width), F32)
    for k in range(NEIGH):
        total = total + jnp.where(neigh[:, k : k + 1] == spots, 1.0, 0.0)
    return total.astype(BF)


def as_row(ref):
    return ref[...].reshape(1, ref.shape[0])


def own_window(me):
    return pl.ds(pl.multiple_of(lax.div(3 * me, 2) * 128, 128), 256)


def own_part(wide, me):
    return jnp.where(me % 2 == 0, wide[:, :OWN], wide[:, 256 - OWN :])


def rich_rows(rich, me, h):
    lane = lax.broadcasted_iota(jnp.int32, (8, 4 * HEADS), 1)
    term = lax.broadcasted_iota(jnp.int32, (8, 4 * HEADS), 0)
    chosen = (lane == 4 * (OWN_HEADS * me + h) + term) & (term < 4)
    return nn(jnp.where(chosen, 1.0, 0.0).astype(BF), rich)


def rich_columns(rich, me, h):
    row = lax.broadcasted_iota(jnp.int32, (4 * HEADS, 128), 0)
    term = lax.broadcasted_iota(jnp.int32, (4 * HEADS, 128), 1)
    chosen = (row == 4 * (OWN_HEADS * me + h) + term) & (term < 4)
    return tn(rich, jnp.where(chosen, 1.0, 0.0).astype(BF))


def share_out(chunk_of, bit, pairs, kept_ref, sent_ref):
    for i, pair in enumerate(pairs):
        first, second = (chunk_of(g) for g in pair)
        kept_ref[i] = jnp.where(bit == 0, first, second)
        sent_ref[i] = jnp.where(bit == 0, second, first)


def row_pieces(ref, g):
    return [ref[OWN * p + PIECE * g : OWN * p + PIECE * (g + 1)] for p in range(SEQ_WAYS)]


def pair_terms(meta_col, meta_row, before_ref, distance_ref):
    for c in range(2):
        gap = meta_col[:, 8 + c : 9 + c] - meta_row[8 + c : 9 + c]
        before_ref[c] = jnp.where(gap < 0.0, 1.0, -1.0)
        distance_ref[c] = jnp.log(1.0 + jnp.abs(gap)) * (1.0 / LOG_NORM)


def attend_kernel(
    tok_a, tok_b, tok_c, tok_d, int_a, int_b, int_c, int_d, glob_ref, gain_ref, shift_ref, rich_q_ref,
    rich_k_ref,    w_graph_any, w_query_any, w_key_any, w_value_any,
    both_ref, member_ref, glob_att_ref, meta_row_ref,
    agg_any, pre_any, super_any, normed_any, qkv_any, prob_any,
    agg_ref, pre_ref, super_ref, normed_ref, qkv_ref, prob_ref,
    padded, w_graph_ref, w_project_ref, keys, values, key_rich, meta_pad, before_ref, distance_ref,
    rich_left, far_ref, heads_out, attn_ref, meta_col_ref, sems, prob_sems,
):
    me = lax.axis_index("seq")
    graph_copy = load(w_graph_any, w_graph_ref, sems.at[0])
    project_copies = [
        load(weight.at[:, own_window(me)], w_project_ref.at[i], sems.at[1 + i])
        for i, weight in enumerate((w_query_any, w_key_any, w_value_any))
    ]
    padded[:RADIUS] = jnp.zeros((RADIUS, D), BF)
    padded[RADIUS + ROWS :] = jnp.zeros((RADIUS, D), BF)
    starts = [pl.multiple_of((me ^ k) * TOK, TOK) for k in range(SEQ_WAYS)]
    for start, tok in zip(starts, (tok_a, tok_b, tok_c, tok_d)):
        padded[pl.ds(start + RADIUS, TOK)] = tok[...]
    for start, ints in zip(starts, (int_a, int_b, int_c, int_d)):
        rows = ints[...].astype(F32)
        meta_row_ref[:, pl.ds(start, TOK)] = rows
        floats = meta_columns(rows)
        meta_col_ref[pl.ds(start, TOK)] = floats
        counts = counts_of(floats, 0, WIN)
        mean = nn(counts, padded[pl.ds(start, WIN)]) * (1.0 / NEIGH)
        agg_ref[pl.ds(start, TOK)] = mean.astype(BF)
    gain, shift = as_row(gain_ref), as_row(shift_ref)
    graph_copy.wait()
    for low in range(0, ROWS, 256):
        rows = slice(low, low + 256)
        pre = nn(agg_ref[rows], w_graph_ref[...])
        pre_ref[rows] = pre
        tokens = padded[RADIUS + low : RADIUS + low + 256].astype(F32)
        super_rows = tokens + gelu_parts(pre)[0]
        super_ref[rows] = super_rows
        normed_ref[rows] = (row_stats(super_rows)[0] * gain + shift).astype(BF)
    glob_hat = row_stats(glob_ref[...].astype(F32))[0]
    normed_ref[ROWS:] = (glob_hat * gain + shift).astype(BF)
    kept = [
        load(source, target, sems.at[4 + i])
        for i, (source, target) in enumerate((
            (agg_ref.at[:, own_window(me)], agg_any), (pre_ref, pre_any), (super_ref, super_any), (normed_ref, normed_any),
        ))
    ]
    normed = normed_ref[...]
    for part in range(3):
        project_copies[part].wait()
        projected = nn(normed, own_part(w_project_ref[part], me)).astype(BF)
        for h in range(OWN_HEADS):
            qkv_ref[part * OWN_HEADS + h] = projected[:, h * HEAD_DIM : (h + 1) * HEAD_DIM]
    kept.append(load(qkv_ref, qkv_any, sems.at[8]))
    rich_q, rich_k = rich_q_ref[...], rich_k_ref[...]
    spread_keys(qkv_ref, keys, values)
    meta_pad[...] = jnp.zeros((16, PAD), F32)
    meta_pad[:, RADIUS : RADIUS + ROWS] = meta_row_ref[...]

    def prepare(h, carry):
        key_rich[h] = nt(rich_rows(rich_k, me, h).astype(BF), keys[h])
        rich_left[h] = rich_columns(rich_q, me, h).astype(BF)
        return carry

    lax.fori_loop(0, OWN_HEADS, prepare, 0)

    def prob_copy(b):
        rows = pl.ds(pl.multiple_of(b * TOK, TOK), TOK)
        return pltpu.make_async_copy(prob_ref.at[:, rows], prob_any.at[:, rows], prob_sems.at[b])

    def block(b, carry):
        start = pl.multiple_of(b * TOK, TOK)
        rows = pl.ds(start, TOK)
        window = pl.ds(start, WIN)
        pair_terms(meta_col_ref[rows], meta_pad[:, window], before_ref, distance_ref)
        q_spot = lax.broadcasted_iota(jnp.int32, (TOK, WIN), 0)
        k_spot = lax.broadcasted_iota(jnp.int32, (TOK, WIN), 1)
        ahead = k_spot - q_spot
        place = k_spot + (start - RADIUS)
        mask = (ahead >= 0) & (ahead <= 2 * RADIUS) & (place >= 0) & (place < ROWS)
        far_ref[...] = jnp.where(mask, 0.0, MASKED)

        def head(h, inner):
            query = qkv_ref[h, rows]
            query_rich = nn(query, rich_left[h])
            right = key_rich[h, :, window]
            scores = nt(query, keys[h, window]) * SCORE_SCALE + far_ref[...]
            spread = None
            for c in range(2):
                logit = (query_rich[:, c : c + 1] + right[c : c + 1]) * before_ref[c]
                off = distance_ref[c] - (query_rich[:, 2 + c : 3 + c] + right[2 + c : 3 + c])
                scores = scores + (jnp.minimum(logit, 0.0) - 0.5 * off * off)
                grown = 1.0 + jnp.exp(-jnp.abs(logit))
                spread = grown if spread is None else spread * grown
            scores = scores - jnp.log(spread)
            glob_scores = nt(query, qkv_ref[OWN_HEADS + h, ROWS:]) * SCORE_SCALE
            top = jnp.maximum(
                jnp.max(scores, axis=-1, keepdims=True), jnp.max(glob_scores, axis=-1, keepdims=True)
            )
            prob = jnp.exp(scores - top)
            glob_prob = jnp.exp(glob_scores - top)
            total = jnp.sum(prob, axis=-1, keepdims=True) + jnp.sum(
                glob_prob, axis=-1, keepdims=True
            )
            inverse = 1.0 / total
            prob = prob * inverse
            glob_prob = glob_prob * inverse
            prob_ref[h, rows, :WIN] = prob
            prob_ref[h, rows, WIN : WIN + GLOBALS] = glob_prob
            mixed = nn(prob.astype(BF), values[h, window]) + nn(
                glob_prob.astype(BF), qkv_ref[2 * OWN_HEADS + h, ROWS:]
            )
            heads_out[h, rows] = mixed.astype(BF)
            return inner

        lax.fori_loop(0, OWN_HEADS, head, 0, unroll=True)
        prob_copy(b).start()
        return carry

    lax.fori_loop(0, SEQ_WAYS, block, 0)
    slot = lax.broadcasted_iota(jnp.int32, (GLOBALS, ROWS), 0).astype(F32)
    member = meta_row_ref[10:11] == slot

    def glob_head(h, carry):
        query = qkv_ref[h, ROWS:]
        scores = nt(query, qkv_ref[OWN_HEADS + h, :ROWS]) * SCORE_SCALE
        scores = jnp.where(member, scores, MASKED)
        own = nt(query, qkv_ref[OWN_HEADS + h, ROWS:]) * SCORE_SCALE
        top = jnp.maximum(
            jnp.max(scores, axis=-1, keepdims=True), jnp.max(own, axis=-1, keepdims=True)
        )
        prob = jnp.exp(scores - top)
        own_prob = jnp.exp(own - top)
        total = jnp.sum(prob, axis=-1, keepdims=True) + jnp.sum(own_prob, axis=-1, keepdims=True)
        inverse = 1.0 / total
        prob = prob * inverse
        own_prob = own_prob * inverse
        member_ref[h, :, :ROWS] = prob
        member_ref[h, :, ROWS : ROWS + GLOBALS] = own_prob
        mixed = nn(prob.astype(BF), qkv_ref[2 * OWN_HEADS + h, :ROWS]) + nn(
            own_prob.astype(BF), qkv_ref[2 * OWN_HEADS + h, ROWS:]
        )
        glob_att_ref[h] = mixed
        heads_out[h, ROWS:] = mixed.astype(BF)
        return carry

    lax.fori_loop(0, OWN_HEADS, glob_head, 0)
    for h in range(OWN_HEADS):
        attn_ref[:, h * HEAD_DIM : (h + 1) * HEAD_DIM] = heads_out[h]
    for half in range(2):
        span = slice(OWN * half, OWN * (half + 1))
        low, glob_low = HALF_TOK * half, ROWS + HALF_GLOB * half
        both_ref[:HALF_TOK, span] = attn_ref[low : low + HALF_TOK]
        both_ref[HALF_TOK:, span] = attn_ref[glob_low : glob_low + HALF_GLOB]
    for copy in kept:
        copy.wait()
    for b in range(SEQ_WAYS):
        prob_copy(b).wait()


def meta_columns(meta_row):
    return jnp.concatenate([meta_row, jnp.zeros((TOK - 16, TOK), F32)], axis=0).T


def spread_keys(qkv_ref, keys, values):
    edge = jnp.zeros((OWN_HEADS, RADIUS, HEAD_DIM), BF)
    for held, first in ((keys, OWN_HEADS), (values, 2 * OWN_HEADS)):
        held[:, :RADIUS] = edge
        held[:, RADIUS + ROWS :] = edge
        held[:, RADIUS : RADIUS + ROWS] = qkv_ref[first : first + OWN_HEADS, :ROWS]


def own_feed_kernel(
    att_a, att_b, att_c, att_d, gain_ref, shift_ref, bias_up_ref, bias_down_ref, cot_ref,
    super_any, glob_any, cot_glob_any, w_out_any, w_up_any, w_down_any,
    out_ref, send_ref,
    att_refs, glob_att_refs, super_ref, glob_ref, cot_glob_ref, w_out_ref, w_up_ref, w_down_ref,
    bias_ref, out_sum, back_sum, sems,
):
    me = lax.axis_index("seq")
    half = lax.div(me, 2)
    inner = lax.rem(me, 2)
    tok_rows = pl.ds(pl.multiple_of(inner * TOK, TOK), TOK)
    glob_rows = pl.ds(pl.multiple_of(HALF_TOK + inner * GLOB_OWN, GLOB_OWN), GLOB_OWN)
    own_tok = pl.ds(pl.multiple_of(me * TOK, TOK), TOK)
    own_glob = pl.ds(pl.multiple_of(me * GLOB_OWN, GLOB_OWN), GLOB_OWN)
    first = []
    for k, att in enumerate((att_a, att_b, att_c, att_d)):
        first.append(load(att.at[tok_rows], att_refs.at[k], sems.at[k]))
        first.append(load(att.at[glob_rows], glob_att_refs.at[k], sems.at[4 + k]))
    first.append(load(super_any.at[own_tok], super_ref, sems.at[8]))
    first.append(load(glob_any.at[own_glob], glob_ref, sems.at[9]))
    first.append(load(cot_glob_any.at[own_glob], cot_glob_ref, sems.at[10]))
    first.append(load(w_out_any, w_out_ref, sems.at[11]))

    def up_copy(j):
        span = pl.ds(pl.multiple_of(j * FF_OWN, FF_OWN), FF_OWN)
        return pltpu.make_async_copy(w_up_any.at[:, span], w_up_ref.at[j], sems.at[12 + j])

    def down_copy(j):
        span = pl.ds(pl.multiple_of(j * FF_OWN, FF_OWN), FF_OWN)
        return pltpu.make_async_copy(w_down_any.at[span], w_down_ref.at[j], sems.at[16 + j])

    up_copy(0).start()
    down_copy(0).start()
    for copy in first:
        copy.wait()
    up_copy(1).start()
    down_copy(1).start()
    y_rows = jnp.concatenate([super_ref[...], glob_ref[...].astype(F32)], axis=0)
    for k in range(SEQ_WAYS):
        wide = jnp.concatenate([att_refs[k], glob_att_refs[k]], axis=0)
        mixed = jnp.where(half == 0, wide[:, :OWN], wide[:, OWN:])
        y_rows = y_rows + nn(mixed, w_out_ref[pl.ds(pl.multiple_of((me ^ k) * OWN, OWN), OWN)])
    gain = as_row(gain_ref)
    hat, scale = row_stats(y_rows)
    normed = (hat * gain + as_row(shift_ref)).astype(BF)
    cot = jnp.concatenate([cot_ref[...], cot_glob_ref[...]], axis=0)
    bias = as_row(bias_up_ref)
    for j in range(SEQ_WAYS):
        bias_ref[j : j + 1] = bias[:, FF_OWN * j : FF_OWN * (j + 1)]
    out_sum[...] = y_rows + as_row(bias_down_ref)
    back_sum[...] = jnp.zeros((CHUNK, D), F32)

    def units(j, carry):
        @pl.when(j + 2 < SEQ_WAYS)
        def _():
            up_copy(j + 2).start()
            down_copy(j + 2).start()

        up_copy(j).wait()
        hidden, slope = gelu_parts(nn(normed, w_up_ref[j]) + bias_ref[pl.ds(j, 1)])
        down_copy(j).wait()
        d_pre = (nt(cot, w_down_ref[j]) * slope).astype(BF)
        back_sum[...] += nt(d_pre, w_up_ref[j])
        out_sum[...] += nn(hidden.astype(BF), w_down_ref[j])
        return carry

    lax.fori_loop(0, SEQ_WAYS, units, 0)
    out, back = out_sum[...], back_sum[...]
    out_ref[...] = out[:TOK].astype(BF)
    scaled = back * gain
    cot = cot.astype(F32)
    d_rows = cot + scale * (
        scaled
        - jnp.mean(scaled, axis=-1, keepdims=True)
        - hat * jnp.mean(scaled * hat, axis=-1, keepdims=True)
    )
    sums = [back * hat, back, cot]
    sums = [jnp.sum(rows, axis=0, keepdims=True) for rows in sums]
    send_ref[:CHUNK] = d_rows.astype(BF)
    send_ref[CHUNK : CHUNK + GLOB_OWN] = out[TOK:].astype(BF)
    sums = jnp.concatenate(sums + [jnp.zeros((13, D), F32)], axis=0)
    send_ref[CHUNK + GLOB_OWN :] = sums.astype(BF)


def feed_rows_kernel(
    att_a, att_b, att_c, att_d, cot_a, cot_b, cot_c, cot_d, cot_glob_ref, glob_ref, gain_ref,
    shift_ref, bias_ref, super_any, w_out_any, w_up_any,
    kept_ref, sent_ref, normed_ref, slope_ref, cot_ref,
    super_ref, w_out_ref, w_up_ref, hidden_ref, grad, sems,
):
    me, x = lax.axis_index("seq"), lax.rem(lax.axis_index("grp"), 2)
    mine = pl.multiple_of(me * FF_OWN, FF_OWN)
    copies = [
        load(super_any, super_ref, sems.at[0]),
        load(w_out_any, w_out_ref, sems.at[1]),
        load(w_up_any.at[:, pl.ds(mine, FF_OWN)], w_up_ref, sems.at[2]),
    ]
    for k, cot in enumerate((cot_a, cot_b, cot_c, cot_d)):
        b = me ^ k
        at = lax.div(b, 2) * HALF + lax.rem(b, 2) * TOK
        cot_ref[pl.ds(pl.multiple_of(at, 32), TOK)] = cot[...]
    for half in range(2):
        cot_ref[HALF * half + HALF_TOK : HALF * (half + 1)] = cot_glob_ref[
            HALF_GLOB * half : HALF_GLOB * (half + 1)
        ]
    gain, shift = as_row(gain_ref), as_row(shift_ref)
    bias = as_row(bias_ref)
    bias = [bias[:, FF_OWN * j : FF_OWN * (j + 1)] for j in range(SEQ_WAYS)]
    bias = jnp.where(me < 2, jnp.where(me == 0, bias[0], bias[1]), jnp.where(me == 2, bias[2], bias[3]))
    for copy in copies:
        copy.wait()
    for half in range(2):
        rows = slice(HALF * half, HALF * (half + 1))
        glob_rows = glob_ref[HALF_GLOB * half : HALF_GLOB * (half + 1)].astype(F32)
        y_rows = jnp.concatenate([super_ref[HALF_TOK * half : HALF_TOK * (half + 1)], glob_rows], axis=0)
        for k, att in enumerate((att_a, att_b, att_c, att_d)):
            w_rows = w_out_ref[pl.ds(pl.multiple_of((me ^ k) * OWN, OWN), OWN)]
            y_rows = y_rows + nn(att[:, OWN * half : OWN * (half + 1)], w_rows)
        normed = (row_stats(y_rows)[0] * gain + shift).astype(BF)
        normed_ref[rows] = normed
        hidden, slope = gelu_parts(nn(normed, w_up_ref[...]) + bias)
        hidden_ref[rows] = hidden.astype(BF)
        slope_ref[rows] = slope
    grad[...] = tn(hidden_ref[...], cot_ref[...])
    share_out(lambda g: grad[BAND * g : BAND * (g + 1)].astype(BF), x, X_PAIRS, kept_ref, sent_ref)


def feed_back_kernel(
    normed_ref, slope_ref, cot_ref, w_down_any,
    kept_ref, sent_ref, d_bias_ref, w_down_ref, d_pre_ref, grad, sems,
):
    me = lax.axis_index("seq")
    x = lax.rem(lax.axis_index("grp"), 2)
    mine = pl.ds(pl.multiple_of(me * FF_OWN, FF_OWN), FF_OWN)
    load(w_down_any.at[mine], w_down_ref, sems.at[0]).wait()
    d_bias = jnp.zeros((1, FF_OWN), F32)
    for half in range(2):
        rows = slice(HALF * half, HALF * (half + 1))
        d_pre = (nt(cot_ref[rows], w_down_ref[...]) * slope_ref[rows]).astype(BF)
        d_pre_ref[rows] = d_pre
        d_bias = d_bias + jnp.sum(d_pre.astype(F32), axis=0, keepdims=True)
    d_bias_ref[...] = d_bias
    grad[...] = tn(normed_ref[...], d_pre_ref[...])
    share_out(
        lambda g: jnp.concatenate(row_pieces(grad, g), axis=0).astype(BF), x, X_PAIRS, kept_ref, sent_ref
    )


def project_grad_kernel(normed_ref, d_qkv_ref, attn_ref, d_proj_ref, kept_ref, sent_ref, grad, grad_out):
    x = lax.rem(lax.axis_index("grp"), 2)
    grad[...] = tn(normed_ref[...], d_qkv_ref[:, : 3 * OWN])
    total = None
    for half in range(2):
        columns = slice(OWN * half, OWN * (half + 1))
        first, glob_first = HALF_TOK * half, ROWS + HALF_GLOB * half
        term = tn(attn_ref[:HALF_TOK, columns], d_proj_ref[first : first + HALF_TOK])
        term = term + tn(attn_ref[HALF_TOK:, columns], d_proj_ref[glob_first : glob_first + HALF_GLOB])
        total = term if total is None else total + term
    grad_out[...] = total

    def chunk(g):
        out_rows = grad_out[PIECE * g : PIECE * (g + 1)]
        left = jnp.concatenate(row_pieces(grad, g), axis=0)
        right = [out_rows[:, OWN * p : OWN * (p + 1)] for p in range(SEQ_WAYS)]
        return jnp.concatenate([left, jnp.concatenate(right, axis=0)], axis=1).astype(BF)

    share_out(chunk, x, X_PAIRS, kept_ref, sent_ref)


def back_kernel(
    back_a, back_b, back_c, back_d, glob_att_ref, meta_row_ref, rich_q_ref,
    rich_k_ref, w_out_any, qkv_any, prob_any, member_any,
    d_proj_ref, d_qkv_ref, vec_ref, out_global_ref,
    w_out_ref, qkv_ref, prob_ref, member_ref, keys, values, key_rich, meta_pad, before_ref, distance_ref,
    rich_left, d_att, d_keys, d_values, d_key_rich, d_query_rich, rich_qt, rich_kt, d_glob, parts, rich,
    sems, prob_sems,
):
    me = lax.axis_index("seq")
    own_rows = pl.ds(pl.multiple_of(me * OWN, OWN), OWN)
    w_copy = load(w_out_any.at[own_rows], w_out_ref, sems.at[0])
    qkv_copy = load(qkv_any, qkv_ref, sems.at[1])

    def prob_copy(b):
        rows = pl.ds(pl.multiple_of(b * TOK, TOK), TOK)
        return pltpu.make_async_copy(prob_any.at[:, rows], prob_ref.at[:, rows], prob_sems.at[b])

    for b in range(SEQ_WAYS):
        prob_copy(b).start()
    member_copy = load(member_any, member_ref, sems.at[2])
    sums = None
    for k, back in enumerate((back_a, back_b, back_c, back_d)):
        at = me ^ k
        d_proj_ref[pl.ds(pl.multiple_of(at * TOK, TOK), TOK)] = back[:TOK]
        d_proj_ref[pl.ds(pl.multiple_of(ROWS + at * GLOB_OWN, GLOB_OWN), GLOB_OWN)] = back[TOK:CHUNK]
        out_global_ref[pl.ds(pl.multiple_of(at * GLOB_OWN, GLOB_OWN), GLOB_OWN)] = back[
            CHUNK : CHUNK + GLOB_OWN
        ]
        part = back[CHUNK + GLOB_OWN :].astype(F32)
        sums = part if sums is None else sums + part
    vec_ref[...] = sums[:8]
    w_copy.wait()
    projected = nt(d_proj_ref[...], w_out_ref[...]).astype(BF)
    for h in range(OWN_HEADS):
        d_att[h] = projected[:, h * HEAD_DIM : (h + 1) * HEAD_DIM]
    meta_pad[...] = jnp.zeros((16, PAD), F32)
    meta_pad[:, RADIUS : RADIUS + ROWS] = meta_row_ref[...]
    qkv_copy.wait()
    spread_keys(qkv_ref, keys, values)
    rich_q, rich_k = rich_q_ref[...], rich_k_ref[...]

    def prepare(h, carry):
        rich_left[h] = rich_columns(rich_q, me, h).astype(BF)
        rich_qt[h] = rich_rows(rich_q, me, h)
        rich_kt[h] = rich_rows(rich_k, me, h)
        key_rich[h] = nt(rich_kt[h].astype(BF), keys[h])
        return carry

    lax.fori_loop(0, OWN_HEADS, prepare, 0)
    d_keys[...] = jnp.zeros((OWN_HEADS, PAD, HEAD_DIM), F32)
    d_values[...] = jnp.zeros((OWN_HEADS, PAD, HEAD_DIM), F32)
    d_key_rich[...] = jnp.zeros((OWN_HEADS, 8, PAD), F32)
    d_glob[...] = jnp.zeros((2 * OWN_HEADS, GLOBALS, HEAD_DIM), F32)

    def block(b, carry):
        start = pl.multiple_of(b * TOK, TOK)
        rows = pl.ds(start, TOK)
        window = pl.ds(start, WIN)
        pair_terms(meta_columns(meta_row_ref[:, rows]), meta_pad[:, window], before_ref, distance_ref)
        prob_copy(b).wait()

        def head(h, inner):
            query = qkv_ref[h, rows]
            d_out = d_att[h, rows]
            prob = prob_ref[h, rows, :WIN]
            glob_prob = prob_ref[h, rows, WIN : WIN + GLOBALS]
            d_prob = nt(d_out, values[h, window])
            d_glob_prob = nt(d_out, qkv_ref[2 * OWN_HEADS + h, ROWS:])
            delta = jnp.sum(prob * d_prob, axis=-1, keepdims=True) + jnp.sum(
                glob_prob * d_glob_prob, axis=-1, keepdims=True
            )
            d_scores = prob * (d_prob - delta)
            d_low = d_scores.astype(BF)
            d_glob_low = (glob_prob * (d_glob_prob - delta)).astype(BF)
            query_rich = nn(query, rich_left[h])
            right = key_rich[h, :, window]
            lefts, belows = [None] * 4, [None] * 4
            for c in range(2):
                logit = query_rich[:, c : c + 1] + right[c : c + 1]
                pulled = d_scores * (0.5 * before_ref[c] - 0.5 * jnp.tanh(0.5 * logit))
                off = distance_ref[c] - (query_rich[:, 2 + c : 3 + c] + right[2 + c : 3 + c])
                off = d_scores * off
                lefts[c] = jnp.sum(pulled, axis=-1, keepdims=True)
                lefts[2 + c] = jnp.sum(off, axis=-1, keepdims=True)
                belows[c] = jnp.sum(pulled, axis=0, keepdims=True)
                belows[2 + c] = jnp.sum(off, axis=0, keepdims=True)
            d_key_rich[h, :, window] += jnp.concatenate(belows + [jnp.zeros((4, WIN), F32)], axis=0)
            lane = lax.broadcasted_iota(jnp.int32, (TOK, 8), 1)
            d_left = jnp.zeros((TOK, 8), F32)
            d_query = (
                nn(d_low, keys[h, window]) + nn(d_glob_low, qkv_ref[OWN_HEADS + h, ROWS:])
            ) * SCORE_SCALE
            for c, column in enumerate(lefts):
                d_left = jnp.where(lane == c, column, d_left)
                d_query = d_query + column * rich_qt[h, c : c + 1]
            d_query_rich[h, rows] = d_left
            parts[h, rows] = d_query.astype(BF)
            d_keys[h, window] += tn(d_low, query) * SCORE_SCALE
            d_values[h, window] += tn(prob.astype(BF), d_out)
            d_glob[h] += tn(d_glob_low, query) * SCORE_SCALE
            d_glob[OWN_HEADS + h] += tn(glob_prob.astype(BF), d_out)
            return inner

        lax.fori_loop(0, OWN_HEADS, head, 0, unroll=True)
        return carry

    lax.fori_loop(0, SEQ_WAYS, block, 0)
    member_copy.wait()

    def glob_head(h, carry):
        query = qkv_ref[h, ROWS:]
        key_rows = qkv_ref[OWN_HEADS + h, :ROWS]
        value_rows = qkv_ref[2 * OWN_HEADS + h, :ROWS]
        glob_key = qkv_ref[OWN_HEADS + h, ROWS:]
        glob_value = qkv_ref[2 * OWN_HEADS + h, ROWS:]
        d_out = d_att[h, ROWS:]
        delta = jnp.sum(d_out.astype(F32) * glob_att_ref[h], axis=-1, keepdims=True)
        prob = member_ref[h, :, :ROWS]
        own_prob = member_ref[h, :, ROWS : ROWS + GLOBALS]
        d_low = (prob * (nt(d_out, value_rows) - delta)).astype(BF)
        d_own = (own_prob * (nt(d_out, glob_value) - delta)).astype(BF)
        d_query = (nn(d_low, key_rows) + nn(d_own, glob_key)) * SCORE_SCALE
        parts[h, ROWS:] = d_query.astype(BF)
        parts[OWN_HEADS + h, ROWS:] = (d_glob[h] + tn(d_own, query) * SCORE_SCALE).astype(BF)
        parts[2 * OWN_HEADS + h, ROWS:] = (
            d_glob[OWN_HEADS + h] + tn(own_prob.astype(BF), d_out)
        ).astype(BF)
        d_right = d_key_rich[h, :, RADIUS : RADIUS + ROWS]
        d_key = d_keys[h, RADIUS : RADIUS + ROWS] + tn(d_low, query) * SCORE_SCALE
        d_key = d_key + lax.dot_general(
            d_right, rich_kt[h], (((0,), (0,)), ((), ())), precision=PRECISE,
            preferred_element_type=F32,
        )
        d_value = d_values[h, RADIUS : RADIUS + ROWS] + tn(prob.astype(BF), d_out)
        parts[OWN_HEADS + h, :ROWS] = d_key.astype(BF)
        parts[2 * OWN_HEADS + h, :ROWS] = d_value.astype(BF)
        rich[pl.ds(pl.multiple_of(8 * h, 8), 8)] = jnp.concatenate(
            [tn(d_query_rich[h].astype(BF), qkv_ref[h, :ROWS])[:4], nn(d_right.astype(BF), key_rows)[:4]],
            axis=0,
        )
        return carry

    lax.fori_loop(0, OWN_HEADS, glob_head, 0)
    for i in range(3 * OWN_HEADS):
        d_qkv_ref[:, i * HEAD_DIM : (i + 1) * HEAD_DIM] = parts[i]
    rich[RICH:] = jnp.zeros((32 - RICH, HEAD_DIM), F32)
    d_qkv_ref[:, 3 * OWN :] = jnp.zeros((ALL, WIDE - 3 * OWN), BF)
    d_qkv_ref[:32, 3 * OWN :] = rich[...].astype(BF)


def norm_kernel(
    dqkv_a, dqkv_b, dqkv_c, dqkv_d, glob_ref, d_proj_ref, gain_ref, vec_two_ref, d_bias_up_ref,
    w_query_any, w_key_any, w_value_any, super_any, pre_any, agg_any,
    grad_glob_ref, kept_ref, sent_ref, d_own_ref, d_pre,
    w_query_ref, w_key_ref, w_value_ref, super_ref, pre_ref, agg_ref, d_super, d_qkv, d_norm, rich, sems,
):
    me, x = lax.axis_index("seq"), lax.rem(lax.axis_index("grp"), 2)
    weight_copies = [
        load(source, target, sems.at[i])
        for i, (source, target) in enumerate((
            (w_query_any, w_query_ref), (w_key_any, w_key_ref), (w_value_any, w_value_ref),
        ))
    ]
    row_copies = [load(super_any, super_ref, sems.at[3]), load(pre_any, pre_ref, sems.at[4])]
    agg_copy = load(agg_any, agg_ref, sems.at[5])
    for k, part in enumerate((dqkv_a, dqkv_b, dqkv_c, dqkv_d)):
        d_qkv[me ^ k] = part[...]
        rich[me ^ k] = part[:32, 3 * OWN :].astype(F32)
    total = None
    for i, weight in enumerate((w_query_ref, w_key_ref, w_value_ref)):
        weight_copies[i].wait()
        for p in range(SEQ_WAYS):
            term = nt(d_qkv[p, :, OWN * i : OWN * (i + 1)], weight[:, OWN * p : OWN * (p + 1)])
            total = term if total is None else total + term
    d_norm[...] = total
    for copy in row_copies:
        copy.wait()
    gain = as_row(gain_ref)
    d_gain = jnp.zeros((1, D), F32)
    d_shift = jnp.zeros((1, D), F32)
    for low in range(0, ALL, 192):
        rows = slice(low, low + 192)
        inner = min(192, ROWS - low)
        if inner == 192:
            rows_in = super_ref[rows]
        else:
            rows_in = jnp.concatenate([super_ref[low:], glob_ref[...].astype(F32)], axis=0)
        back, gain_part, shift_part = norm_back(d_norm[rows], gain, rows_in)
        d_gain = d_gain + gain_part
        d_shift = d_shift + shift_part
        back = back + d_proj_ref[rows].astype(F32)
        d_super[rows] = back
        long = slice(low, low + inner)
        slope = gelu_parts(pre_ref[long])[1]
        d_pre[long] = (back[:inner] * slope).astype(BF)
    grad_glob_ref[...] = d_super[ROWS:]
    d_own_ref[...] = d_super[pl.ds(pl.multiple_of(me * TOK, TOK), TOK)]
    agg_copy.wait()
    grad = tn(own_part(agg_ref[...], me), d_pre[...])
    extra = jnp.concatenate(
        [vec_two_ref[0:3], d_bias_up_ref[...], d_gain, d_shift, jnp.zeros((1, D), F32)], axis=0
    )

    def chunk(g):
        pieces = [rich[g // 2, 12 * (g % 2) + i : 12 * (g % 2) + i + 1] for i in range(12)]
        rows = [grad[PIECE * g : PIECE * (g + 1)], jnp.concatenate(pieces, axis=1), extra]
        return jnp.concatenate(rows, axis=0).astype(BF)

    share_out(chunk, x, X_PAIRS, kept_ref, sent_ref)


def tokens_kernel(d_own_ref, d_pre, meta_row_ref, w_graph_any, grad_tok_ref, w_graph_ref, sems):
    me = lax.axis_index("seq")
    copy = load(w_graph_any, w_graph_ref, sems.at[0])
    counts = []
    for shift in (-1, 0, 1):
        rows = pl.ds(pl.multiple_of(jnp.clip(me - shift, 0, SEQ_WAYS - 1) * TOK, TOK), TOK)
        counts.append(counts_of(meta_columns(meta_row_ref[:, rows]), (shift + 1) * TOK, TOK))
    copy.wait()
    total = d_own_ref[...]
    for shift, count in zip((-1, 0, 1), counts):
        b = me - shift
        fits = (b >= 0) & (b < SEQ_WAYS)
        rows = pl.ds(pl.multiple_of(jnp.clip(b, 0, SEQ_WAYS - 1) * TOK, TOK), TOK)
        d_agg = (nt(d_pre[rows], w_graph_ref[...]) * (1.0 / NEIGH)).astype(BF)
        total = total + jnp.where(fits, tn(count, d_agg), 0.0)
    grad_tok_ref[...] = total


DISTANCES = (0, 4, 2, 6)


def down_out_kernel(held, came, out_ref):
    for i, distance in enumerate(DISTANCES):
        for flip, pieces in enumerate((held, came)):
            g = lax.axis_index("grp") ^ (distance + flip)
            out_ref[pl.ds(pl.multiple_of(BAND * g, BAND), BAND)] = pieces[i].astype(F32)


def up_out_kernel(held, came, out_ref):
    for i, distance in enumerate(DISTANCES):
        for flip, pieces in enumerate((held, came)):
            g = lax.axis_index("grp") ^ (distance + flip)
            piece = pieces[i].astype(F32)
            rows = pl.ds(pl.multiple_of(PIECE * g, 8), PIECE)
            for k in range(SEQ_WAYS):
                columns = pl.ds(pl.multiple_of((lax.axis_index("seq") ^ k) * D, D), D)
                out_ref[rows, columns] = piece[PIECE * k : PIECE * (k + 1)]


def project_out_kernel(held, came, query_ref, key_ref, value_ref, out_ref, pieces):
    for i, distance in enumerate(DISTANCES):
        for flip, blocks in enumerate((held, came)):
            g = lax.axis_index("grp") ^ (distance + flip)
            rows = pl.ds(pl.multiple_of(PIECE * g, 8), PIECE)
            piece = blocks[i].astype(F32)
            for k in range(SEQ_WAYS):
                pieces[lax.axis_index("seq") ^ k] = piece[PIECE * k : PIECE * (k + 1), : 3 * OWN]
            for j, ref in enumerate((query_ref, key_ref, value_ref)):
                parts = [pieces[p, :, OWN * j : OWN * (j + 1)] for p in range(SEQ_WAYS)]
                ref[rows] = jnp.concatenate(parts, axis=1)
            parts = [piece[PIECE * p : PIECE * (p + 1), 3 * OWN :] for p in range(SEQ_WAYS)]
            out_ref[rows] = jnp.concatenate(parts, axis=1)


def graph_out_kernel(
    held, came, graph_ref, gain_one_ref, shift_one_ref, gain_two_ref, shift_two_ref, bias_up_ref,
    bias_down_ref, rich_q_ref, rich_k_ref, vectors,
):
    me = lax.axis_index("seq")
    for i, distance in enumerate(DISTANCES):
        for flip, blocks in enumerate((held, came)):
            g = lax.axis_index("grp") ^ (distance + flip)
            rows = pl.ds(pl.multiple_of(PIECE * g, 8), PIECE)
            piece = blocks[i].astype(F32)
            graph_ref[rows] = piece[:PIECE]
            for j in range(12):
                vectors[g, j : j + 1] = piece[PIECE : PIECE + 1, HEAD_DIM * j : HEAD_DIM * (j + 1)]
            vectors[g, 12:16] = jnp.zeros((4, HEAD_DIM), F32)
    sums = held[0, PIECE : PIECE + 8].astype(F32)
    lane = lax.broadcasted_iota(jnp.int32, (D, 256), 0)
    spot = lax.broadcasted_iota(jnp.int32, (D, 256), 1)
    own = jnp.where((lane == OWN * me + spot) & (spot < OWN), 1.0, 0.0).astype(BF)
    own = nn(sums.astype(BF), own)[:, :OWN]
    for ref, row in (
        (gain_two_ref, 1), (shift_two_ref, 2), (bias_down_ref, 3), (gain_one_ref, 5), (shift_one_ref, 6),
    ):
        ref[...] = own[row : row + 1].reshape(OWN)
    bias_up_ref[...] = sums[4:5].reshape(FF_OWN)
    lane = lax.broadcasted_iota(jnp.int32, (HEAD_DIM, 128), 0)
    spot = lax.broadcasted_iota(jnp.int32, (HEAD_DIM, 128), 1)
    part = HEAD_DIM // SEQ_WAYS
    own = jnp.where((lane == part * me + spot) & (spot < part), 1.0, 0.0).astype(BF)
    own = nn(vectors[...].reshape(16 * GRP_WAYS, HEAD_DIM).astype(BF), own).astype(BF)
    row = lax.broadcasted_iota(jnp.int32, (16 * GRP_WAYS, 128), 0)
    place = 12 * lax.div(row, 16) + lax.rem(row, 16)
    column = lax.broadcasted_iota(jnp.int32, (16 * GRP_WAYS, 128), 1)
    for side, ref in enumerate((rich_q_ref, rich_k_ref)):
        wanted = 8 * lax.div(column, 4) + 4 * side + lax.rem(column, 4)
        chosen = (place == wanted) & (lax.rem(row, 16) < 12) & (column < 4 * HEADS)
        turned_rich = tn(own, jnp.where(chosen, 1.0, 0.0).astype(BF))
        ref[...] = turned_rich[:part, : 4 * HEADS]


def call(kernel, ins, outs, scratch=(), apart=0, outs_apart=0, room=50):
    vmem, any_space = pl.BlockSpec(memory_space=pltpu.VMEM), pl.BlockSpec(memory_space=pltpu.HBM)
    return pl.pallas_call(
        kernel,
        out_shape=[jax.ShapeDtypeStruct(shape, kind) for shape, kind in outs],
        in_specs=[vmem] * (len(ins) - apart) + [any_space] * apart,
        out_specs=[vmem] * (len(outs) - outs_apart) + [any_space] * outs_apart,
        scratch_shapes=[pltpu.VMEM(*s) if isinstance(s, tuple) else s for s in scratch],
        compiler_params=pltpu.CompilerParams(vmem_limit_bytes=room * 1024 * 1024),
        cost_estimate=pl.CostEstimate(flops=KERNEL_COST, bytes_accessed=0, transcendentals=0),
    )(*ins)


def split_heads(
    tokens, global_tokens, neighbours, token_ranks, membership, w_graph, gain_one, shift_one,
    w_query, w_key, w_value, rich_query, rich_key, w_out, gain_two, shift_two, w_up, bias_up,
    w_down, bias_down, cot_tokens, cot_global,
):
    me = lax.axis_index("seq")
    grp = lax.axis_index("grp")
    x, z_low, z_high = grp % 2, (grp // 2) % 2, grp // 4
    beside, across = reach_seq(tokens)
    (ints,) = call(
        ints_kernel, [neighbours.T, token_ranks, membership.reshape(1, TOK)], [((16, TOK), jnp.int32)],
        room=60,
    )
    int_beside, int_across = reach_seq(ints)
    int_blocks = [ints, int_beside, int_across, lax.ppermute(int_across, "seq", CORE_SWAP)]
    cot_tokens, across, int_blocks[3] = tie(cot_tokens, across, int_blocks[3])
    cot_across = lax.ppermute(cot_tokens, "seq", Y_SWAP)
    tok_blocks = [tokens, beside, across, lax.ppermute(across, "seq", CORE_SWAP)]
    rich_query, rich_key = rich_query.T, rich_key.T

    weights_shape = (D, D), BF
    stored = [
        ((ROWS, D), BF), ((ROWS, D), F32), ((ROWS, D), F32), ((ALL, D), BF),
        ((3 * OWN_HEADS, ALL, HEAD_DIM), BF), ((OWN_HEADS, ROWS, 512), F32),
    ]
    kept_agg = (ROWS, 256), BF
    heads_scratch = [
        ((OWN_HEADS, PAD, HEAD_DIM), BF), ((OWN_HEADS, PAD, HEAD_DIM), BF),
        ((OWN_HEADS, 8, PAD), F32), ((16, PAD), F32), ((2, TOK, WIN), F32), ((2, TOK, WIN), F32),
        ((OWN_HEADS, HEAD_DIM, 128), BF),
    ]
    (
        both, member_prob, glob_att, meta_row, agg, graph_pre, super_rows, normed, qkv,
        prob,
    ) = call(
        attend_kernel,
        [*tok_blocks, *int_blocks, global_tokens, gain_one, shift_one, rich_query, rich_key, w_graph, w_query,
         w_key, w_value],
        [((HALF, 2 * OWN), BF), ((OWN_HEADS, GLOBALS, 640), F32),
         ((OWN_HEADS, GLOBALS, HEAD_DIM), F32), ((16, ROWS), F32), kept_agg, *stored[1:]],
        [*stored, ((PAD, D), BF), weights_shape, ((3, D, 256), BF), *heads_scratch,
         ((TOK, WIN), F32), ((OWN_HEADS, ALL, HEAD_DIM), BF), ((ALL, OWN), BF),
         ((ROWS, 128), F32), pltpu.SemaphoreType.DMA((9,)), pltpu.SemaphoreType.DMA((SEQ_WAYS,))],
        apart=4, outs_apart=6, room=56,
    )
    both, cot_across, cot_tokens = tie(both, cot_across, cot_tokens)
    att_blocks = gather_seq(both)
    cot_beside = lax.ppermute(cot_tokens, "seq", CORE_SWAP)
    cot_blocks = [cot_tokens, cot_beside, cot_across, lax.ppermute(cot_across, "seq", CORE_SWAP)]
    out_tokens, back = call(
        own_feed_kernel,
        [*att_blocks, gain_two, shift_two, bias_up, bias_down, cot_tokens, super_rows,
         global_tokens, cot_global, w_out, w_up, w_down],
        [((TOK, D), BF), ((SEND, D), BF)],
        [((SEQ_WAYS, TOK, 2 * OWN), BF), ((SEQ_WAYS, GLOB_OWN, 2 * OWN), BF), ((TOK, D), F32),
         ((GLOB_OWN, D), BF), ((GLOB_OWN, D), BF), weights_shape, ((SEQ_WAYS, D, FF_OWN), BF),
         ((SEQ_WAYS, FF_OWN, D), BF), ((SEQ_WAYS, FF_OWN), F32), ((CHUNK, D), F32), ((CHUNK, D), F32),
         pltpu.SemaphoreType.DMA((20,))],
        apart=6,
    )
    beside, across = reach_seq(back)
    late_gain, back = tie(gain_two, back)
    down_kept, down_sent, normed_two, slope, cot_all = call(
        feed_rows_kernel,
        [*att_blocks, *cot_blocks, cot_global, global_tokens, late_gain, shift_two,
         bias_up, super_rows, w_out, w_up],
        [((4, BAND, D), BF), ((4, BAND, D), BF), ((ALL, D), BF), ((ALL, FF_OWN), F32), ((ALL, D), BF)],
        [((ROWS, D), F32), weights_shape, ((D, FF_OWN), BF), ((ALL, FF_OWN), BF), ((D, D), F32),
         pltpu.SemaphoreType.DMA((3,))],
        apart=3,
    )
    down_came = swap_x(down_sent)
    across, down_kept = tie(across, down_kept)
    diagonal = lax.ppermute(across, "seq", CORE_SWAP)
    normed_two, across = tie(normed_two, across)
    up_kept, up_sent, d_bias_up = call(
        feed_back_kernel,
        [normed_two, slope, cot_all, w_down],
        [((4, BAND, D), BF), ((4, BAND, D), BF), ((1, FF_OWN), F32)],
        [((FF_OWN, D), BF), ((ALL, FF_OWN), BF), ((D, D), F32), pltpu.SemaphoreType.DMA((1,))],
        apart=1,
    )
    up_came = swap_x(up_sent)
    late_row, up_kept = tie(meta_row, up_kept)

    d_proj, d_qkv, vec_two, out_global = call(
        back_kernel,
        [back, beside, across, diagonal, glob_att, late_row, rich_query, rich_key,
         w_out, qkv, prob, member_prob],
        [((ALL, D), BF), ((ALL, WIDE), BF), ((8, D), F32), ((GLOBALS, D), BF)],
        [((OWN, D), BF), stored[4], stored[5], ((OWN_HEADS, GLOBALS, 640), F32), *heads_scratch,
         ((OWN_HEADS, ALL, HEAD_DIM), BF), ((OWN_HEADS, PAD, HEAD_DIM), F32),
         ((OWN_HEADS, PAD, HEAD_DIM), F32), ((OWN_HEADS, 8, PAD), F32), ((OWN_HEADS, ROWS, 8), F32),
         ((OWN_HEADS, 8, HEAD_DIM), F32), ((OWN_HEADS, 8, HEAD_DIM), F32),
         ((2 * OWN_HEADS, GLOBALS, HEAD_DIM), F32), ((3 * OWN_HEADS, ALL, HEAD_DIM), BF),
         ((32, HEAD_DIM), F32), pltpu.SemaphoreType.DMA((3,)), pltpu.SemaphoreType.DMA((SEQ_WAYS,))],
        apart=4,
    )
    beside, across = reach_seq(d_qkv)
    held = {"d_qkv": d_qkv, "down": down_kept, "up": up_kept}
    latest = ["d_qkv"]

    def due(value):
        value, held[latest[0]] = tie(value, held[latest[0]])
        return value

    def hold(key, value):
        held[key] = value
        latest[0] = key
        return value

    def halve(key, came, bit):
        kept, sent = halves(held[key], due(came), bit)
        hold(key, kept)
        return sent

    def total(key, came):
        return hold(key, added(held[key], due(came)))

    def join(key, came):
        return hold(key, jnp.concatenate([held[key], due(came)], axis=0))

    down_came = swap_near(halve("down", down_came, z_low))
    proj_kept, proj_sent = call(
        project_grad_kernel,
        [due(normed), d_qkv, both, d_proj],
        [((4, BAND, D), BF)] * 2,
        [((D, 3 * OWN), F32), ((OWN, D), F32)],
    )
    hold("proj", proj_kept)
    proj_came = swap_x(proj_sent)
    up_came = swap_near(halve("up", up_came, z_low))
    down_came = swap_far(halve("down", down_came, z_high))
    across = hold("across", due(across))
    diagonal = lax.ppermute(across, "seq", CORE_SWAP)
    up_came = swap_far(halve("up", up_came, z_high))
    down_came = swap_far(total("down", down_came))
    proj_came = swap_near(halve("proj", proj_came, z_low))
    grad_global, graph_kept, graph_sent, d_own, d_pre = call(
        norm_kernel,
        [d_qkv, beside, held["across"], diagonal, global_tokens, d_proj, gain_one, due(vec_two), d_bias_up,
         w_query, w_key, w_value, super_rows, graph_pre, agg],
        [((GLOBALS, D), F32), ((4, GRAPH_ROWS, D), BF), ((4, GRAPH_ROWS, D), BF), ((TOK, D), F32),
         ((ROWS, D), BF)],
        [*[weights_shape] * 3, ((ROWS, D), F32), ((ROWS, D), F32), ((ROWS, 256), BF), ((ALL, D), F32),
         ((SEQ_WAYS, ALL, WIDE), BF), ((ALL, D), F32), ((SEQ_WAYS, 32, HEAD_DIM), F32),
         pltpu.SemaphoreType.DMA((6,))],
        apart=6,
    )
    hold("graph", graph_kept)
    graph_came = swap_x(graph_sent)
    up_mine = total("up", up_came).reshape(SEQ_WAYS, PIECE, D)
    up_core = turn_core(up_mine)
    proj_came = swap_far(halve("proj", proj_came, z_high))
    down_came = swap_near(join("down", down_came))
    up_core = due(up_core)
    up_far = lax.ppermute(turn_y(up_mine, up_core), "seq", Y_SWAP)
    hold("up_core", up_core)
    (grad_tokens,) = call(
        tokens_kernel, [due(d_own), d_pre, meta_row, w_graph], [((TOK, D), F32)],
        [weights_shape, pltpu.SemaphoreType.DMA((1,))], apart=1,
    )
    hold("tokens", grad_tokens)
    up_came = swap_far(hold("up", turned(up_mine, held["up_core"], due(up_far))[None]))
    proj_sum = total("proj", proj_came)
    proj_core = turn_core(proj_sum[0, :, : 3 * OWN].reshape(SEQ_WAYS, PIECE, 3 * OWN))
    down_came = swap_x(join("down", down_came))
    proj_core = due(proj_core)
    proj_mine = held["proj"][0, :, : 3 * OWN].reshape(SEQ_WAYS, PIECE, 3 * OWN)
    proj_far = lax.ppermute(turn_y(proj_mine, proj_core), "seq", Y_SWAP)
    hold("proj_core", proj_core)
    up_came = swap_near(join("up", up_came))
    graph_came = swap_near(halve("graph", graph_came, z_low))
    proj_turned = turned(proj_mine, held["proj_core"], due(proj_far))
    proj_turned = jnp.concatenate([proj_turned, held["proj"][0, :, 3 * OWN :]], axis=1)[None]
    proj_came = swap_far(hold("proj", proj_turned))
    up_came = swap_x(join("up", up_came))
    proj_came = swap_near(join("proj", proj_came))
    graph_came = swap_far(halve("graph", graph_came, z_high))
    graph_came = swap_far(total("graph", graph_came))
    (g_down,) = call(down_out_kernel, [held["down"], due(down_came)], [((FF_OWN, D), F32)])
    hold("g_down", g_down)
    graph_came = swap_near(join("graph", graph_came))
    proj_came = swap_x(join("proj", proj_came))
    graph_came = swap_x(join("graph", graph_came))
    (g_up,) = call(up_out_kernel, [held["up"], due(up_came)], [((OWN, FF), F32)])
    hold("g_up", g_up)
    g_query, g_key, g_value, g_out = call(
        project_out_kernel,
        [held["proj"], due(proj_came)],
        [((OWN, D), F32)] * 4,
        [((SEQ_WAYS, PIECE, 3 * OWN), F32)],
    )
    hold("g_query", g_query)
    (
        g_graph, g_gain_one, g_shift_one, g_gain_two, g_shift_two, g_bias_up, g_bias_down, g_rich_q,
        g_rich_k,
    ) = call(
        graph_out_kernel,
        [held["graph"], due(graph_came)],
        [((OWN, D), F32), *[((OWN,), F32)] * 4, ((FF_OWN,), F32), ((OWN,), F32),
         *[((HEAD_DIM // SEQ_WAYS, 4 * HEADS), F32)] * 2],
        [((GRP_WAYS, 16, HEAD_DIM), F32)],
    )
    hold("g_graph", g_graph)
    grad_tokens, g_down, g_up, g_query, g_graph = (
        held[key] for key in ("tokens", "g_down", "g_up", "g_query", "g_graph")
    )
    return (
        out_tokens, out_global, grad_tokens, grad_global,
        g_graph, g_gain_one, g_shift_one, g_query, g_key, g_value, g_rich_q, g_rich_k,
        g_out, g_gain_two, g_shift_two, g_up, g_bias_up, g_down, g_bias_down,
    )


def layer(*arrays):
    tokens, global_tokens = arrays[:2]
    ways = (lax.axis_size("seq"), lax.axis_size("grp"))
    if ways == (SEQ_WAYS, GRP_WAYS) and tokens.shape[0] == TOK and global_tokens.shape[0] == GLOBALS:
        return split_heads(*arrays)
    return local(*arrays)


def solution(mesh):
    return jax.shard_map(
        layer,
        mesh=mesh,
        in_specs=(
            P(("grp", "seq"), None),
            P("grp", None),
            P(("grp", "seq"), None),
            P(None, ("grp", "seq")),
            P(("grp", "seq")),
            P(),
            P(),
            P(),
            P(),
            P(),
            P(),
            P(),
            P(),
            P(),
            P(),
            P(),
            P(),
            P(),
            P(),
            P(),
            P(("grp", "seq"), None),
            P("grp", None),
        ),
        out_specs=(
            P(("grp", "seq"), None),
            P("grp", None),
            P(("grp", "seq"), None),
            P("grp", None),
            P("seq", None),
            P("seq"),
            P("seq"),
            P("seq", None),
            P("seq", None),
            P("seq", None),
            P("seq", None),
            P("seq", None),
            P("seq", None),
            P("seq"),
            P("seq"),
            P("seq", None),
            P("seq"),
            P("seq", None),
            P("seq"),
        ),
        check_vma=False,
    )
```

```python
import functools
import math

import jax
import jax.numpy as jnp
from jax import lax
from jax.experimental import pallas as pl
from jax.experimental.pallas import tpu as pltpu
from jax.sharding import PartitionSpec as P

D = 768
HEADS = 12
HEAD_DIM = 64
RADIUS = 128
GLOBALS = 64
NEIGH = 8
SEQ_TOKENS = 2048


EPSILON = 1e-05
PRECISE = lax.Precision.HIGHEST
MASKED = -1e30


def with_halo(cells, sides, width):
    for axis, dim in sides:
        count = lax.axis_size(axis)
        ends = count - 1
        head = lax.slice_in_dim(cells, 0, width, axis=dim)
        tail = lax.slice_in_dim(cells, cells.shape[dim] - width, cells.shape[dim], axis=dim)
        cells = jnp.concatenate(
            [
                lax.ppermute(tail, axis, [(i, (i + 1) % count) for i in range(ends)]),
                cells,
                lax.ppermute(head, axis, [((i + 1) % count, i) for i in range(ends)]),
            ],
            axis=dim,
        )
    return cells


def joined(array, axis, combine):
    everything = jax.tree.map(
        lambda part, kind: lax.all_gather(part.astype(kind), axis),
        array,
        (jnp.bfloat16, jnp.bfloat16, jnp.bfloat16),
    )

    def take(k):
        return jax.tree.map(lambda part, own: part[k].astype(own.dtype), everything, array)

    return lax.fori_loop(
        1, lax.axis_size(axis), lambda k, so_far: combine(so_far, take(k)), take(0)
    )


def shifted(block, axis, distance):
    devices = range(lax.axis_size(axis))
    route = [(i - distance, i) for i in devices if i - distance in devices]
    return lax.ppermute(block, axis, route)


def layer_norm(rows_in, gain_in, shift_in):
    row_mean = jnp.mean(rows_in, axis=-1, keepdims=True)
    centred = rows_in - row_mean
    variance = jnp.mean(centred * centred, axis=-1, keepdims=True)
    return centred * lax.rsqrt(variance + EPSILON) * gain_in + shift_in


def rich_part(a_block, b_window, rank_query, rank_key, log_norm):
    combined = None
    for coordinate in range(2):
        order_flag = (rank_query[coordinate][:, None] < rank_key[coordinate][None, :]).astype(
            jnp.float32
        )
        distance = (
            jnp.log1p(
                jnp.abs(rank_query[coordinate][:, None] - rank_key[coordinate][None, :]).astype(
                    jnp.float32
                )
            )
            / log_norm
        )
        order_logit = a_block[:, :, None, coordinate] + b_window[:, None, :, coordinate]
        centre = a_block[:, :, None, 2 + coordinate] + b_window[:, None, :, 2 + coordinate]
        pair_term = (
            order_flag * jax.nn.log_sigmoid(order_logit)
            + (1.0 - order_flag) * jax.nn.log_sigmoid(-order_logit)
            - 0.5 * (distance - centre) ** 2
        )
        combined = pair_term if combined is None else combined + pair_term
    return combined


def product(left, right):
    return jnp.dot(left, right, preferred_element_type=jnp.float32)


def product_left(left, right):
    return jnp.einsum("ta,tb->ab", left, right, preferred_element_type=jnp.float32)


def product_right(left, right):
    return jnp.einsum("tb,ab->ta", left, right, preferred_element_type=jnp.float32)


def local(
    tokens,
    global_tokens,
    neighbours,
    token_ranks,
    membership,
    w_graph,
    gain_one,
    shift_one,
    w_query,
    w_key,
    w_value,
    rich_query,
    rich_key,
    w_out,
    gain_two,
    shift_two,
    w_up,
    bias_up,
    w_down,
    bias_down,
    cot_tokens,
    cot_global,
):
    tok_count = tokens.shape[0]
    seq_count = lax.axis_size("seq")
    seq_index = lax.axis_index("seq")
    seq_len = min(SEQ_TOKENS, tok_count * seq_count)
    span = seq_len // tok_count
    group_seqs = global_tokens.shape[0] // GLOBALS
    seq_slot = seq_index // span
    seq_local = seq_index % span
    slot_flag = (jnp.arange(group_seqs, dtype=jnp.int32) == seq_slot).astype(jnp.float32)
    log_norm = math.log(1.0 + seq_len)
    score_scale = 1.0 / math.sqrt(HEAD_DIM)
    block_rows = min(512, tok_count)
    window = block_rows + 2 * RADIUS
    ext_count = tok_count + 2 * RADIUS
    first_flag = (seq_index == 0).astype(jnp.float32)
    own_pos = seq_local * tok_count + jnp.arange(tok_count, dtype=jnp.int32)
    ext_pos = seq_local * tok_count - RADIUS + jnp.arange(ext_count, dtype=jnp.int32)
    key_valid = (ext_pos >= 0) & (ext_pos < seq_len)

    def own_slot(array_in):
        return lax.dynamic_index_in_dim(array_in, seq_slot, 0, keepdims=False)

    def to_slots(array_in):
        return slot_flag.reshape((group_seqs,) + (1,) * array_in.ndim) * array_in[None]

    token_ext = with_halo(tokens, (("seq", 0),), RADIUS)
    token_ext = jnp.where(key_valid[:, None], token_ext, jnp.zeros_like(token_ext))
    flat_index = neighbours.reshape(-1)
    gathered = (
        jnp.take(token_ext, flat_index, axis=0).astype(jnp.float32).reshape(tok_count, NEIGH, D)
    )
    agg_low = jnp.mean(gathered, axis=1).astype(jnp.bfloat16)
    graph_pre = product(agg_low, w_graph)
    graph_out, graph_back = jax.vjp(jax.nn.gelu, graph_pre)
    super_rows = tokens.astype(jnp.float32) + graph_out
    normed_full, norm_back = jax.vjp(layer_norm, super_rows, gain_one, shift_one)
    normed = normed_full.astype(jnp.bfloat16)
    glob_in = global_tokens.astype(jnp.float32)
    glob_normed_full, glob_norm_back = jax.vjp(layer_norm, glob_in, gain_one, shift_one)
    glob_normed = glob_normed_full.astype(jnp.bfloat16)
    query = product(normed, w_query).astype(jnp.bfloat16)
    key_own = product(normed, w_key).astype(jnp.bfloat16)
    value_own = product(normed, w_value).astype(jnp.bfloat16)
    glob_query = (
        product(glob_normed, w_query)
        .astype(jnp.bfloat16)
        .reshape(group_seqs, GLOBALS, HEADS, HEAD_DIM)
    )
    glob_key = (
        product(glob_normed, w_key)
        .astype(jnp.bfloat16)
        .reshape(group_seqs, GLOBALS, HEADS, HEAD_DIM)
    )
    glob_value = (
        product(glob_normed, w_value)
        .astype(jnp.bfloat16)
        .reshape(group_seqs, GLOBALS, HEADS, HEAD_DIM)
    )
    glob_query_own = own_slot(glob_query)
    glob_key_own = own_slot(glob_key)
    glob_value_own = own_slot(glob_value)
    kv_ext = with_halo(jnp.concatenate([key_own, value_own], axis=1), (("seq", 0),), RADIUS)
    key_ext = kv_ext[:, :D].reshape(ext_count, HEADS, HEAD_DIM)
    value_ext = kv_ext[:, D:].reshape(ext_count, HEADS, HEAD_DIM)
    rank_ext = with_halo(token_ranks, (("seq", 1),), RADIUS)
    rich_q3 = rich_query.reshape(HEAD_DIM, HEADS, 4)
    rich_k3 = rich_key.reshape(HEAD_DIM, HEADS, 4)
    query_heads = query.reshape(tok_count, HEADS, HEAD_DIM)
    a_rows = jnp.einsum("the,ehc->htc", query_heads, rich_q3, preferred_element_type=jnp.float32)
    b_ext = jnp.einsum("the,ehc->htc", key_ext, rich_k3, preferred_element_type=jnp.float32)

    def block_scores():

        def rich_scores(left_rows, right_rows):
            return rich_part(left_rows, right_rows, token_ranks, rank_ext, log_norm)

        rich_vals, rich_back = jax.vjp(rich_scores, a_rows, b_ext)
        raw_scores = (
            jnp.einsum("qhe,khe->hqk", query_heads, key_ext, preferred_element_type=jnp.float32)
            * score_scale
        )
        pos_gap = own_pos[:, None] - ext_pos[None, :]
        key_mask = (jnp.abs(pos_gap) <= RADIUS) & key_valid[None, :]
        scores = jnp.where(key_mask[None], raw_scores + rich_vals, MASKED)
        glob_scores = (
            jnp.einsum(
                "qhe,ghe->hqg", query_heads, glob_key_own, preferred_element_type=jnp.float32
            )
            * score_scale
        )
        return (scores, glob_scores, rich_back, query_heads, key_ext)

    scored = block_scores()
    scores = scored[0]
    glob_scores = scored[1]
    row_top = jnp.maximum(jnp.max(scores, axis=-1), jnp.max(glob_scores, axis=-1))
    row_denom = jnp.sum(jnp.exp(scores - row_top[..., None]), axis=-1) + jnp.sum(
        jnp.exp(glob_scores - row_top[..., None]), axis=-1
    )
    log_total = row_top + jnp.log(row_denom)
    prob_rows = jnp.exp(scores - log_total[..., None]).astype(jnp.bfloat16)
    glob_probs = jnp.exp(glob_scores - log_total[..., None]).astype(jnp.bfloat16)
    attn_block = jnp.einsum(
        "hqk,khe->qhe", prob_rows, value_ext, preferred_element_type=jnp.float32
    ) + jnp.einsum("hqg,ghe->qhe", glob_probs, glob_value_own, preferred_element_type=jnp.float32)
    attn_parts = attn_block.reshape(block_rows, D)
    attn_rows = attn_parts.astype(jnp.bfloat16)
    member_mask = membership[None, :] == jnp.arange(GLOBALS, dtype=jnp.int32)[:, None]
    key_heads = key_ext[RADIUS : RADIUS + tok_count]
    value_heads = value_ext[RADIUS : RADIUS + tok_count]
    member_raw = (
        jnp.einsum("ghe,the->ght", glob_query_own, key_heads, preferred_element_type=jnp.float32)
        * score_scale
    )
    member_scores = jnp.where(member_mask[:, None, :], member_raw, MASKED)
    local_top = jnp.max(member_scores, axis=-1)
    member_exp = jnp.where(
        member_mask[:, None, :], jnp.exp(member_scores - local_top[..., None]), 0.0
    )
    local_sum = jnp.sum(member_exp, axis=-1)
    local_acc = jnp.einsum(
        "ght,the->ghe", member_exp, value_heads.astype(jnp.float32), precision=PRECISE
    )
    slot_top = jnp.where(slot_flag[:, None, None] > 0.5, local_top[None], MASKED)
    slot_sum = to_slots(local_sum)
    slot_acc = to_slots(local_acc)

    def combine_softmax(first_part, second_part):
        top_one, sum_one, acc_one = first_part
        top_two, sum_two, acc_two = second_part
        top_both = jnp.maximum(top_one, top_two)
        scale_one = jnp.exp(top_one - top_both)
        scale_two = jnp.exp(top_two - top_both)
        return (
            top_both,
            sum_one * scale_one + sum_two * scale_two,
            acc_one * scale_one[..., None] + acc_two * scale_two[..., None],
        )

    merged_top, merged_sum, merged_acc = joined(
        (slot_top, slot_sum, slot_acc), "seq", combine_softmax
    )
    self_scores = (
        jnp.einsum("sghe,skhe->sghk", glob_query, glob_key, preferred_element_type=jnp.float32)
        * score_scale
    )
    glob_top = jnp.maximum(merged_top, jnp.max(self_scores, axis=-1))
    self_exp = jnp.exp(self_scores - glob_top[..., None])
    merged_scale = jnp.exp(merged_top - glob_top)
    glob_denom = merged_sum * merged_scale + jnp.sum(self_exp, axis=-1)
    glob_lse = glob_top + jnp.log(glob_denom)
    glob_att_f = (
        merged_acc * merged_scale[..., None]
        + jnp.einsum("sghk,skhe->sghe", self_exp, glob_value.astype(jnp.float32), precision=PRECISE)
    ) / glob_denom[..., None]
    glob_attn = glob_att_f.reshape(group_seqs * GLOBALS, D).astype(jnp.bfloat16)
    y_one = super_rows + product(attn_rows, w_out)
    glob_y_one = glob_in + product(glob_attn, w_out)

    def feed_forward(rows_in):
        normed_two_full, back_two = jax.vjp(layer_norm, rows_in, gain_two, shift_two)
        normed_two = normed_two_full.astype(jnp.bfloat16)
        hidden_pre = product(normed_two, w_up) + bias_up
        hidden_full, gelu_back = jax.vjp(jax.nn.gelu, hidden_pre)
        hidden = hidden_full.astype(jnp.bfloat16)
        result = rows_in + product(hidden, w_down) + bias_down
        return (result, normed_two, hidden, back_two, gelu_back)

    def feed_back(cotangent, normed_two, hidden, back_two, gelu_back):
        cot_full = cotangent.astype(jnp.float32)
        grad_down = product_left(hidden, cotangent)
        grad_bias_d = jnp.sum(cot_full, axis=0)
        d_hidden = product_right(cotangent, w_down)
        d_pre = gelu_back(d_hidden)[0].astype(jnp.bfloat16)
        grad_up = product_left(normed_two, d_pre)
        grad_bias_u = jnp.sum(d_pre.astype(jnp.float32), axis=0)
        d_normed_two = product_right(d_pre, w_up)
        d_rows, grad_gain, grad_shift = back_two(d_normed_two)
        return (
            cot_full + d_rows,
            (grad_gain, grad_shift, grad_up, grad_bias_u, grad_down, grad_bias_d),
        )

    long_ff = feed_forward(y_one)
    glob_ff = feed_forward(glob_y_one)
    out_tokens = long_ff[0].astype(jnp.bfloat16)
    out_global = glob_ff[0].astype(jnp.bfloat16)
    d_y_one, long_mlp = feed_back(cot_tokens, long_ff[1], long_ff[2], long_ff[3], long_ff[4])
    glob_d_y_one, glob_mlp = feed_back(cot_global, glob_ff[1], glob_ff[2], glob_ff[3], glob_ff[4])
    mlp_grads = [
        local_part + first_flag * glob_part for local_part, glob_part in zip(long_mlp, glob_mlp)
    ]
    d_proj = d_y_one.astype(jnp.bfloat16)
    glob_d_proj = glob_d_y_one.astype(jnp.bfloat16)
    grad_out = product_left(attn_rows, d_proj) + first_flag * product_left(glob_attn, glob_d_proj)
    d_attn = product_right(d_proj, w_out).astype(jnp.bfloat16).reshape(tok_count, HEADS, HEAD_DIM)
    glob_d_attn = (
        product_right(glob_d_proj, w_out)
        .astype(jnp.bfloat16)
        .reshape(group_seqs, GLOBALS, HEADS, HEAD_DIM)
    )
    glob_d_attn_own = own_slot(glob_d_attn)
    rich_q3_full = rich_q3.astype(jnp.float32)
    rich_k3_full = rich_k3.astype(jnp.float32)
    d_key_ext = jnp.zeros((ext_count, HEADS, HEAD_DIM), jnp.float32)
    d_value_ext = jnp.zeros((ext_count, HEADS, HEAD_DIM), jnp.float32)
    scores, glob_scores, rich_back, q_part, key_win = block_scores()
    prob_full = jnp.exp(scores - log_total[..., None])
    glob_prob_full = jnp.exp(glob_scores - log_total[..., None])
    d_probs = jnp.einsum("qhe,khe->hqk", d_attn, value_ext, preferred_element_type=jnp.float32)
    glob_d_probs = jnp.einsum(
        "qhe,ghe->hqg", d_attn, glob_value_own, preferred_element_type=jnp.float32
    )
    row_delta = jnp.sum(prob_full * d_probs, axis=-1) + jnp.sum(
        glob_prob_full * glob_d_probs, axis=-1
    )
    d_scores = (prob_full * (d_probs - row_delta[..., None])).astype(jnp.bfloat16)
    glob_d_scores = (glob_prob_full * (glob_d_probs - row_delta[..., None])).astype(jnp.bfloat16)
    query_rich_grad, key_rich_grad = rich_back(d_scores.astype(jnp.float32))
    query_grad = (
        jnp.einsum("hqk,khe->qhe", d_scores, key_win, preferred_element_type=jnp.float32)
        + jnp.einsum(
            "hqg,ghe->qhe", glob_d_scores, glob_key_own, preferred_element_type=jnp.float32
        )
    ) * score_scale + jnp.einsum("hqc,ehc->qhe", query_rich_grad, rich_q3_full, precision=PRECISE)
    key_win_grad = jnp.einsum(
        "hqk,qhe->khe", d_scores, q_part, preferred_element_type=jnp.float32
    ) * score_scale + jnp.einsum("hkc,ehc->khe", key_rich_grad, rich_k3_full, precision=PRECISE)
    value_win_grad = jnp.einsum(
        "hqk,qhe->khe", prob_full.astype(jnp.bfloat16), d_attn, preferred_element_type=jnp.float32
    )
    d_key_ext = d_key_ext.at[0:window].add(key_win_grad)
    d_value_ext = d_value_ext.at[0:window].add(value_win_grad)
    glob_key_grad = (
        jnp.einsum("hqg,qhe->ghe", glob_d_scores, q_part, preferred_element_type=jnp.float32)
        * score_scale
    )
    glob_value_grad = jnp.einsum(
        "hqg,qhe->ghe",
        glob_prob_full.astype(jnp.bfloat16),
        d_attn,
        preferred_element_type=jnp.float32,
    )
    grad_rich_q = jnp.einsum(
        "qhe,hqc->ehc", q_part.astype(jnp.float32), query_rich_grad, precision=PRECISE
    )
    grad_rich_k = jnp.einsum(
        "khe,hkc->ehc", key_win.astype(jnp.float32), key_rich_grad, precision=PRECISE
    )
    query_grads = query_grad.reshape(block_rows, D)
    glob_delta = jnp.sum(glob_d_attn.astype(jnp.float32) * glob_att_f, axis=-1)
    glob_delta_own = own_slot(glob_delta)
    glob_lse_own = own_slot(glob_lse)
    member_probs = jnp.where(
        member_mask[:, None, :], jnp.exp(member_scores - glob_lse_own[..., None]), 0.0
    )
    member_d_probs = jnp.einsum(
        "ghe,the->ght", glob_d_attn_own, value_heads, preferred_element_type=jnp.float32
    )
    member_d_scores = (member_probs * (member_d_probs - glob_delta_own[..., None])).astype(
        jnp.bfloat16
    )
    glob_query_part = (
        jnp.einsum("ght,the->ghe", member_d_scores, key_heads, preferred_element_type=jnp.float32)
        * score_scale
    )
    own_key_extra = (
        jnp.einsum(
            "ght,ghe->the", member_d_scores, glob_query_own, preferred_element_type=jnp.float32
        )
        * score_scale
    )
    own_value_extra = jnp.einsum(
        "ght,ghe->the", member_probs, glob_d_attn_own.astype(jnp.float32), precision=PRECISE
    )
    d_key_ext = d_key_ext.at[RADIUS : RADIUS + tok_count].add(own_key_extra)
    d_value_ext = d_value_ext.at[RADIUS : RADIUS + tok_count].add(own_value_extra)
    grad_rims = jnp.concatenate(
        [d_key_ext.reshape(ext_count, D), d_value_ext.reshape(ext_count, D)], axis=1
    )
    from_above = shifted(grad_rims[:RADIUS].astype(jnp.bfloat16), "seq", -1).astype(jnp.float32)
    from_below = shifted(grad_rims[tok_count + RADIUS :].astype(jnp.bfloat16), "seq", 1).astype(
        jnp.float32
    )
    kv_grad = grad_rims[RADIUS : RADIUS + tok_count]
    kv_grad = kv_grad.at[:RADIUS].add(from_below).at[tok_count - RADIUS :].add(from_above)
    summed_query, summed_key, summed_value = (
        lax.psum(to_slots(glob_query_part).astype(jnp.bfloat16), "seq").astype(jnp.float32),
        lax.psum(to_slots(glob_key_grad).astype(jnp.bfloat16), "seq").astype(jnp.float32),
        lax.psum(to_slots(glob_value_grad).astype(jnp.bfloat16), "seq").astype(jnp.float32),
    )
    self_probs = jnp.exp(self_scores - glob_lse[..., None])
    self_d_probs = jnp.einsum(
        "sghe,skhe->sghk", glob_d_attn, glob_value, preferred_element_type=jnp.float32
    )
    self_d_scores = (self_probs * (self_d_probs - glob_delta[..., None])).astype(jnp.bfloat16)
    glob_rows_total = group_seqs * GLOBALS
    glob_d_query = (
        (
            summed_query
            + jnp.einsum(
                "sghk,skhe->sghe", self_d_scores, glob_key, preferred_element_type=jnp.float32
            )
            * score_scale
        )
        .astype(jnp.bfloat16)
        .reshape(glob_rows_total, D)
    )
    glob_d_key = (
        (
            summed_key
            + jnp.einsum(
                "sghk,sghe->skhe", self_d_scores, glob_query, preferred_element_type=jnp.float32
            )
            * score_scale
        )
        .astype(jnp.bfloat16)
        .reshape(glob_rows_total, D)
    )
    glob_d_value = (
        (
            summed_value
            + jnp.einsum(
                "sghk,sghe->skhe", self_probs, glob_d_attn.astype(jnp.float32), precision=PRECISE
            )
        )
        .astype(jnp.bfloat16)
        .reshape(glob_rows_total, D)
    )
    d_query = query_grads.astype(jnp.bfloat16)
    d_key = kv_grad[:, :D].astype(jnp.bfloat16)
    d_value = kv_grad[:, D:].astype(jnp.bfloat16)
    grad_query = product_left(normed, d_query) + first_flag * product_left(
        glob_normed, glob_d_query
    )
    grad_key = product_left(normed, d_key) + first_flag * product_left(glob_normed, glob_d_key)
    grad_value = product_left(normed, d_value) + first_flag * product_left(
        glob_normed, glob_d_value
    )
    d_normed = (
        product_right(d_query, w_query)
        + product_right(d_key, w_key)
        + product_right(d_value, w_value)
    )
    glob_d_normed = (
        product_right(glob_d_query, w_query)
        + product_right(glob_d_key, w_key)
        + product_right(glob_d_value, w_value)
    )
    d_super_norm, grad_gain_one, grad_shift_one = norm_back(d_normed)
    d_super = d_y_one + d_super_norm
    glob_d_norm, glob_gain_one, glob_shift_one = glob_norm_back(glob_d_normed)
    grad_global = glob_d_y_one + glob_d_norm
    grad_gain_one = grad_gain_one + first_flag * glob_gain_one
    grad_shift_one = grad_shift_one + first_flag * glob_shift_one
    d_graph_pre = graph_back(d_super)[0].astype(jnp.bfloat16)
    grad_graph = product_left(agg_low, d_graph_pre)
    d_agg = product_right(d_graph_pre, w_graph) / NEIGH
    d_token_ext = (
        jnp.zeros((ext_count, D), jnp.float32).at[flat_index].add(jnp.repeat(d_agg, NEIGH, axis=0))
    )
    d_token_ext = jnp.where(key_valid[:, None], d_token_ext, 0.0)
    token_above = shifted(d_token_ext[:RADIUS].astype(jnp.bfloat16), "seq", -1).astype(jnp.float32)
    token_below = shifted(d_token_ext[tok_count + RADIUS :].astype(jnp.bfloat16), "seq", 1).astype(
        jnp.float32
    )
    own_grad = (
        d_token_ext[RADIUS : RADIUS + tok_count]
        .at[:RADIUS]
        .add(token_below)
        .at[tok_count - RADIUS :]
        .add(token_above)
    )
    grad_tokens = d_super + own_grad
    weight_grads = (
        grad_graph,
        grad_gain_one,
        grad_shift_one,
        grad_query,
        grad_key,
        grad_value,
        grad_rich_q.reshape(HEAD_DIM, 4 * HEADS),
        grad_rich_k.reshape(HEAD_DIM, 4 * HEADS),
        grad_out,
        mlp_grads[0],
        mlp_grads[1],
        mlp_grads[2],
        mlp_grads[3],
        mlp_grads[4],
        mlp_grads[5],
    )
    pieces = [weight_grad.reshape(seq_count, -1) for weight_grad in weight_grads]
    packed = jnp.concatenate(pieces, axis=1)
    group_count = lax.axis_size("grp")
    received = lax.all_to_all(
        packed.astype(jnp.bfloat16), "seq", split_axis=0, concat_axis=0, tiled=True
    ).astype(packed.dtype)
    group_total = jnp.sum(received, axis=0).reshape(group_count, -1)
    crossed = lax.all_to_all(
        group_total.astype(jnp.bfloat16), "grp", split_axis=0, concat_axis=0, tiled=True
    ).astype(group_total.dtype)
    final_part = jnp.sum(crossed, axis=0)
    flat_sum = lax.all_gather(final_part.astype(jnp.bfloat16), "grp", axis=0, tiled=True).astype(
        final_part.dtype
    )
    results = []
    offset = 0
    for weight_grad in weight_grads:
        part_len = weight_grad.size // seq_count
        results.append(
            flat_sum[offset : offset + part_len].reshape(
                (weight_grad.shape[0] // seq_count,) + weight_grad.shape[1:]
            )
        )
        offset = offset + part_len
    return (
        out_tokens,
        out_global,
        grad_tokens,
        grad_global,
        results[0],
        results[1],
        results[2],
        results[3],
        results[4],
        results[5],
        results[6],
        results[7],
        results[8],
        results[9],
        results[10],
        results[11],
        results[12],
        results[13],
        results[14],
    )


SEQ_WAYS = 4
GRP_WAYS = 8
OWN_HEADS = HEADS // SEQ_WAYS
OWN = D // SEQ_WAYS
FF = 3072
FF_OWN = FF // SEQ_WAYS
TOK = 128
ROWS = SEQ_WAYS * TOK
ALL = ROWS + GLOBALS
GLOB_OWN = GLOBALS // SEQ_WAYS
CHUNK = TOK + GLOB_OWN
PIECE = OWN // GRP_WAYS
BAND = SEQ_WAYS * PIECE
WIN = TOK + 2 * RADIUS
PAD = ROWS + 2 * RADIUS
BF = jnp.bfloat16
F32 = jnp.float32
GELU_SCALE = math.sqrt(2.0 / math.pi)
GELU_CUBE = 0.044715
LOG_NORM = math.log(1.0 + ROWS)
SCORE_SCALE = 1.0 / math.sqrt(HEAD_DIM)
CORE_SWAP = [(0, 1), (1, 0), (2, 3), (3, 2)]
Y_SWAP = [(0, 2), (2, 0), (1, 3), (3, 1)]
X_SWAP = [(g, g ^ 1) for g in range(GRP_WAYS)]
Z_NEAR = [(g, g ^ 2) for g in range(GRP_WAYS)]
Z_FAR = [(g, g ^ 4) for g in range(GRP_WAYS)]
HALF_TOK = ROWS // 2
HALF_GLOB = GLOBALS // 2
HALF = HALF_TOK + HALF_GLOB
SEND = CHUNK + 32
WIDE = 640
GRAPH_ROWS = 32
X_PAIRS = ((0, 1), (2, 3), (4, 5), (6, 7))
KERNEL_COST = 60_000_000_000
RICH = OWN_HEADS * 2 * 4


def nn(left, right):
    return lax.dot_general(left, right, (((1,), (0,)), ((), ())), preferred_element_type=F32)


def nt(left, right):
    return lax.dot_general(left, right, (((1,), (1,)), ((), ())), preferred_element_type=F32)


def tn(left, right):
    return lax.dot_general(left, right, (((0,), (0,)), ((), ())), preferred_element_type=F32)


def load(source, target, sem):
    copy = pltpu.make_async_copy(source, target, sem)
    copy.start()
    return copy


def pick(stacked, index):
    return lax.dynamic_index_in_dim(stacked, index, 0, keepdims=False)


def tie(*values):
    return lax.optimization_barrier(values)


def reach_seq(block):
    return lax.ppermute(block, "seq", CORE_SWAP), lax.ppermute(block, "seq", Y_SWAP)


def gather_seq(block):
    beside, across = reach_seq(block)
    return [block, beside, across, lax.ppermute(across, "seq", CORE_SWAP)]


def turn_core(chunks):
    me = lax.axis_index("seq")
    return lax.ppermute(jnp.stack([pick(chunks, me ^ 1), pick(chunks, me ^ 3)]), "seq", CORE_SWAP)


def turn_y(chunks, came):
    return jnp.stack([pick(chunks, lax.axis_index("seq") ^ 2), came[1]])


def turned(chunks, came, far):
    mine = pick(chunks, lax.axis_index("seq"))
    return jnp.concatenate([mine, came[0], far[0], far[1]], axis=0)


def added(kept, came):
    return (kept.astype(F32) + came.astype(F32)).astype(BF)


def swap_x(sent):
    return lax.ppermute(sent, "grp", X_SWAP)


def swap_near(sent):
    return lax.ppermute(sent, "grp", Z_NEAR)


def swap_far(sent):
    return lax.ppermute(sent, "grp", Z_FAR)


def halves(kept, came, bit):
    grid = added(kept, came).reshape((-1, 2) + kept.shape[1:])
    mine = lax.dynamic_index_in_dim(grid, bit, 1, keepdims=False)
    return mine, lax.dynamic_index_in_dim(grid, 1 - bit, 1, keepdims=False)


def row_stats(rows_in):
    centred = rows_in - jnp.mean(rows_in, axis=-1, keepdims=True)
    scale = lax.rsqrt(jnp.mean(centred * centred, axis=-1, keepdims=True) + EPSILON)
    return centred * scale, scale


def norm_back(cotangent, gain, rows_in):
    hat, scale = row_stats(rows_in)
    scaled = cotangent * gain
    back = scale * (
        scaled
        - jnp.mean(scaled, axis=-1, keepdims=True)
        - hat * jnp.mean(scaled * hat, axis=-1, keepdims=True)
    )
    return (
        back,
        jnp.sum(cotangent * hat, axis=0, keepdims=True),
        jnp.sum(cotangent, axis=0, keepdims=True),
    )


def gelu_parts(pre):
    square = pre * pre
    bent = jnp.tanh(GELU_SCALE * pre * (1.0 + GELU_CUBE * square))
    half = 0.5 * (1.0 + bent)
    slope = half + 0.5 * pre * (1.0 - bent * bent) * (
        GELU_SCALE * (1.0 + 3.0 * GELU_CUBE * square)
    )
    return pre * half, slope


def ints_kernel(neigh_ref, rank_ref, member_ref, out_ref):
    out_ref[:NEIGH] = neigh_ref[...]
    out_ref[NEIGH:] = jnp.concatenate(
        [rank_ref[...], member_ref[...], jnp.zeros((16 - NEIGH - 3, TOK), jnp.int32)], axis=0
    )


def counts_of(neigh, first, width):
    spots = (lax.broadcasted_iota(jnp.int32, (neigh.shape[0], width), 1) + first).astype(F32)
    total = jnp.zeros((neigh.shape[0], width), F32)
    for k in range(NEIGH):
        total = total + jnp.where(neigh[:, k : k + 1] == spots, 1.0, 0.0)
    return total.astype(BF)


def as_row(ref):
    return ref[...].reshape(1, ref.shape[0])


def own_window(me):
    return pl.ds(pl.multiple_of(lax.div(3 * me, 2) * 128, 128), 256)


def own_part(wide, me):
    return jnp.where(me % 2 == 0, wide[:, :OWN], wide[:, 256 - OWN :])


def rich_rows(rich, me, h):
    lane = lax.broadcasted_iota(jnp.int32, (8, 4 * HEADS), 1)
    term = lax.broadcasted_iota(jnp.int32, (8, 4 * HEADS), 0)
    chosen = (lane == 4 * (OWN_HEADS * me + h) + term) & (term < 4)
    return nn(jnp.where(chosen, 1.0, 0.0).astype(BF), rich)


def rich_columns(rich, me, h):
    row = lax.broadcasted_iota(jnp.int32, (4 * HEADS, 128), 0)
    term = lax.broadcasted_iota(jnp.int32, (4 * HEADS, 128), 1)
    chosen = (row == 4 * (OWN_HEADS * me + h) + term) & (term < 4)
    return tn(rich, jnp.where(chosen, 1.0, 0.0).astype(BF))


def share_out(chunk_of, bit, pairs, kept_ref, sent_ref):
    for i, pair in enumerate(pairs):
        first, second = (chunk_of(g) for g in pair)
        kept_ref[i] = jnp.where(bit == 0, first, second)
        sent_ref[i] = jnp.where(bit == 0, second, first)


def row_pieces(ref, g):
    return [ref[OWN * p + PIECE * g : OWN * p + PIECE * (g + 1)] for p in range(SEQ_WAYS)]


def pair_terms(meta_col, meta_row, before_ref, distance_ref):
    for c in range(2):
        gap = meta_col[:, 8 + c : 9 + c] - meta_row[8 + c : 9 + c]
        before_ref[c] = jnp.where(gap < 0.0, 1.0, -1.0)
        distance_ref[c] = jnp.log(1.0 + jnp.abs(gap)) * (1.0 / LOG_NORM)


def attend_kernel(
    tok_a, tok_b, tok_c, tok_d, int_a, int_b, int_c, int_d, glob_ref, gain_ref, shift_ref, rich_q_ref,
    rich_k_ref,    w_graph_any, w_query_any, w_key_any, w_value_any,
    both_ref, member_ref, glob_att_ref, meta_row_ref,
    agg_any, pre_any, super_any, normed_any, qkv_any, prob_any,
    agg_ref, pre_ref, super_ref, normed_ref, qkv_ref, prob_ref,
    padded, w_graph_ref, w_project_ref, keys, values, key_rich, meta_pad, before_ref, distance_ref,
    rich_left, far_ref, heads_out, attn_ref, meta_col_ref, sems, prob_sems,
):
    me = lax.axis_index("seq")
    graph_copy = load(w_graph_any, w_graph_ref, sems.at[0])
    project_copies = [
        load(weight.at[:, own_window(me)], w_project_ref.at[i], sems.at[1 + i])
        for i, weight in enumerate((w_query_any, w_key_any, w_value_any))
    ]
    padded[:RADIUS] = jnp.zeros((RADIUS, D), BF)
    padded[RADIUS + ROWS :] = jnp.zeros((RADIUS, D), BF)
    starts = [pl.multiple_of((me ^ k) * TOK, TOK) for k in range(SEQ_WAYS)]
    for start, tok in zip(starts, (tok_a, tok_b, tok_c, tok_d)):
        padded[pl.ds(start + RADIUS, TOK)] = tok[...]
    for start, ints in zip(starts, (int_a, int_b, int_c, int_d)):
        rows = ints[...].astype(F32)
        meta_row_ref[:, pl.ds(start, TOK)] = rows
        floats = meta_columns(rows)
        meta_col_ref[pl.ds(start, TOK)] = floats
        counts = counts_of(floats, 0, WIN)
        mean = nn(counts, padded[pl.ds(start, WIN)]) * (1.0 / NEIGH)
        agg_ref[pl.ds(start, TOK)] = mean.astype(BF)
    gain, shift = as_row(gain_ref), as_row(shift_ref)
    graph_copy.wait()
    for low in range(0, ROWS, 256):
        rows = slice(low, low + 256)
        pre = nn(agg_ref[rows], w_graph_ref[...])
        pre_ref[rows] = pre
        tokens = padded[RADIUS + low : RADIUS + low + 256].astype(F32)
        super_rows = tokens + gelu_parts(pre)[0]
        super_ref[rows] = super_rows
        normed_ref[rows] = (row_stats(super_rows)[0] * gain + shift).astype(BF)
    glob_hat = row_stats(glob_ref[...].astype(F32))[0]
    normed_ref[ROWS:] = (glob_hat * gain + shift).astype(BF)
    kept = [
        load(source, target, sems.at[4 + i])
        for i, (source, target) in enumerate((
            (agg_ref.at[:, own_window(me)], agg_any), (pre_ref, pre_any), (super_ref, super_any), (normed_ref, normed_any),
        ))
    ]
    normed = normed_ref[...]
    for part in range(3):
        project_copies[part].wait()
        projected = nn(normed, own_part(w_project_ref[part], me)).astype(BF)
        for h in range(OWN_HEADS):
            qkv_ref[part * OWN_HEADS + h] = projected[:, h * HEAD_DIM : (h + 1) * HEAD_DIM]
    kept.append(load(qkv_ref, qkv_any, sems.at[8]))
    rich_q, rich_k = rich_q_ref[...], rich_k_ref[...]
    spread_keys(qkv_ref, keys, values)
    meta_pad[...] = jnp.zeros((16, PAD), F32)
    meta_pad[:, RADIUS : RADIUS + ROWS] = meta_row_ref[...]

    def prepare(h, carry):
        key_rich[h] = nt(rich_rows(rich_k, me, h).astype(BF), keys[h])
        rich_left[h] = rich_columns(rich_q, me, h).astype(BF)
        return carry

    lax.fori_loop(0, OWN_HEADS, prepare, 0, unroll=True)

    def prob_copy(b):
        rows = pl.ds(pl.multiple_of(b * TOK, TOK), TOK)
        return pltpu.make_async_copy(prob_ref.at[:, rows], prob_any.at[:, rows], prob_sems.at[b])

    def block(b, carry):
        start = pl.multiple_of(b * TOK, TOK)
        rows = pl.ds(start, TOK)
        window = pl.ds(start, WIN)
        pair_terms(meta_col_ref[rows], meta_pad[:, window], before_ref, distance_ref)
        q_spot = lax.broadcasted_iota(jnp.int32, (TOK, WIN), 0)
        k_spot = lax.broadcasted_iota(jnp.int32, (TOK, WIN), 1)
        ahead = k_spot - q_spot
        place = k_spot + (start - RADIUS)
        mask = (ahead >= 0) & (ahead <= 2 * RADIUS) & (place >= 0) & (place < ROWS)
        far_ref[...] = jnp.where(mask, 0.0, MASKED)

        def head(h, inner):
            query = qkv_ref[h, rows]
            query_rich = nn(query, rich_left[h])
            right = key_rich[h, :, window]
            scores = nt(query, keys[h, window]) * SCORE_SCALE + far_ref[...]
            spread = None
            for c in range(2):
                logit = (query_rich[:, c : c + 1] + right[c : c + 1]) * before_ref[c]
                off = distance_ref[c] - (query_rich[:, 2 + c : 3 + c] + right[2 + c : 3 + c])
                scores = scores + (jnp.minimum(logit, 0.0) - 0.5 * off * off)
                grown = 1.0 + jnp.exp(-jnp.abs(logit))
                spread = grown if spread is None else spread * grown
            scores = scores - jnp.log(spread)
            glob_scores = nt(query, qkv_ref[OWN_HEADS + h, ROWS:]) * SCORE_SCALE
            top = jnp.maximum(
                jnp.max(scores, axis=-1, keepdims=True), jnp.max(glob_scores, axis=-1, keepdims=True)
            )
            prob = jnp.exp(scores - top)
            glob_prob = jnp.exp(glob_scores - top)
            total = jnp.sum(prob, axis=-1, keepdims=True) + jnp.sum(
                glob_prob, axis=-1, keepdims=True
            )
            inverse = 1.0 / total
            prob = prob * inverse
            glob_prob = glob_prob * inverse
            prob_ref[h, rows, :WIN] = prob
            prob_ref[h, rows, WIN : WIN + GLOBALS] = glob_prob
            mixed = nn(prob.astype(BF), values[h, window]) + nn(
                glob_prob.astype(BF), qkv_ref[2 * OWN_HEADS + h, ROWS:]
            )
            heads_out[h, rows] = mixed.astype(BF)
            return inner

        lax.fori_loop(0, OWN_HEADS, head, 0, unroll=True)
        prob_copy(b).start()
        return carry

    lax.fori_loop(0, SEQ_WAYS, block, 0)
    slot = lax.broadcasted_iota(jnp.int32, (GLOBALS, ROWS), 0).astype(F32)
    member = meta_row_ref[10:11] == slot

    def glob_head(h, carry):
        query = qkv_ref[h, ROWS:]
        scores = nt(query, qkv_ref[OWN_HEADS + h, :ROWS]) * SCORE_SCALE
        scores = jnp.where(member, scores, MASKED)
        own = nt(query, qkv_ref[OWN_HEADS + h, ROWS:]) * SCORE_SCALE
        top = jnp.maximum(
            jnp.max(scores, axis=-1, keepdims=True), jnp.max(own, axis=-1, keepdims=True)
        )
        prob = jnp.exp(scores - top)
        own_prob = jnp.exp(own - top)
        total = jnp.sum(prob, axis=-1, keepdims=True) + jnp.sum(own_prob, axis=-1, keepdims=True)
        inverse = 1.0 / total
        prob = prob * inverse
        own_prob = own_prob * inverse
        member_ref[h, :, :ROWS] = prob
        member_ref[h, :, ROWS : ROWS + GLOBALS] = own_prob
        mixed = nn(prob.astype(BF), qkv_ref[2 * OWN_HEADS + h, :ROWS]) + nn(
            own_prob.astype(BF), qkv_ref[2 * OWN_HEADS + h, ROWS:]
        )
        glob_att_ref[h] = mixed
        heads_out[h, ROWS:] = mixed.astype(BF)
        return carry

    lax.fori_loop(0, OWN_HEADS, glob_head, 0, unroll=True)
    for h in range(OWN_HEADS):
        attn_ref[:, h * HEAD_DIM : (h + 1) * HEAD_DIM] = heads_out[h]
    for half in range(2):
        span = slice(OWN * half, OWN * (half + 1))
        low, glob_low = HALF_TOK * half, ROWS + HALF_GLOB * half
        both_ref[:HALF_TOK, span] = attn_ref[low : low + HALF_TOK]
        both_ref[HALF_TOK:, span] = attn_ref[glob_low : glob_low + HALF_GLOB]
    for copy in kept:
        copy.wait()
    for b in range(SEQ_WAYS):
        prob_copy(b).wait()


def meta_columns(meta_row):
    return jnp.concatenate([meta_row, jnp.zeros((TOK - 16, TOK), F32)], axis=0).T


def spread_keys(qkv_ref, keys, values):
    edge = jnp.zeros((OWN_HEADS, RADIUS, HEAD_DIM), BF)
    for held, first in ((keys, OWN_HEADS), (values, 2 * OWN_HEADS)):
        held[:, :RADIUS] = edge
        held[:, RADIUS + ROWS :] = edge
        held[:, RADIUS : RADIUS + ROWS] = qkv_ref[first : first + OWN_HEADS, :ROWS]


def own_feed_kernel(
    att_a, att_b, att_c, att_d, gain_ref, shift_ref, bias_up_ref, bias_down_ref, cot_ref,
    super_any, glob_any, cot_glob_any, w_out_any, w_up_any, w_down_any,
    out_ref, send_ref,
    att_refs, glob_att_refs, super_ref, glob_ref, cot_glob_ref, w_out_ref, w_up_ref, w_down_ref,
    bias_ref, out_sum, back_sum, sems,
):
    me = lax.axis_index("seq")
    half = lax.div(me, 2)
    inner = lax.rem(me, 2)
    tok_rows = pl.ds(pl.multiple_of(inner * TOK, TOK), TOK)
    glob_rows = pl.ds(pl.multiple_of(HALF_TOK + inner * GLOB_OWN, GLOB_OWN), GLOB_OWN)
    own_tok = pl.ds(pl.multiple_of(me * TOK, TOK), TOK)
    own_glob = pl.ds(pl.multiple_of(me * GLOB_OWN, GLOB_OWN), GLOB_OWN)
    first = []
    for k, att in enumerate((att_a, att_b, att_c, att_d)):
        first.append(load(att.at[tok_rows], att_refs.at[k], sems.at[k]))
        first.append(load(att.at[glob_rows], glob_att_refs.at[k], sems.at[4 + k]))
    first.append(load(super_any.at[own_tok], super_ref, sems.at[8]))
    first.append(load(glob_any.at[own_glob], glob_ref, sems.at[9]))
    first.append(load(cot_glob_any.at[own_glob], cot_glob_ref, sems.at[10]))
    first.append(load(w_out_any, w_out_ref, sems.at[11]))

    def up_copy(j):
        span = pl.ds(pl.multiple_of(j * FF_OWN, FF_OWN), FF_OWN)
        return pltpu.make_async_copy(w_up_any.at[:, span], w_up_ref.at[j], sems.at[12 + j])

    def down_copy(j):
        span = pl.ds(pl.multiple_of(j * FF_OWN, FF_OWN), FF_OWN)
        return pltpu.make_async_copy(w_down_any.at[span], w_down_ref.at[j], sems.at[16 + j])

    up_copy(0).start()
    down_copy(0).start()
    for copy in first:
        copy.wait()
    up_copy(1).start()
    down_copy(1).start()
    y_rows = jnp.concatenate([super_ref[...], glob_ref[...].astype(F32)], axis=0)
    for k in range(SEQ_WAYS):
        wide = jnp.concatenate([att_refs[k], glob_att_refs[k]], axis=0)
        mixed = jnp.where(half == 0, wide[:, :OWN], wide[:, OWN:])
        y_rows = y_rows + nn(mixed, w_out_ref[pl.ds(pl.multiple_of((me ^ k) * OWN, OWN), OWN)])
    gain = as_row(gain_ref)
    hat, scale = row_stats(y_rows)
    normed = (hat * gain + as_row(shift_ref)).astype(BF)
    cot = jnp.concatenate([cot_ref[...], cot_glob_ref[...]], axis=0)
    bias = as_row(bias_up_ref)
    for j in range(SEQ_WAYS):
        bias_ref[j : j + 1] = bias[:, FF_OWN * j : FF_OWN * (j + 1)]
    out_sum[...] = y_rows + as_row(bias_down_ref)
    back_sum[...] = jnp.zeros((CHUNK, D), F32)

    def units(j, carry):
        @pl.when(j + 2 < SEQ_WAYS)
        def _():
            up_copy(j + 2).start()
            down_copy(j + 2).start()

        up_copy(j).wait()
        hidden, slope = gelu_parts(nn(normed, w_up_ref[j]) + bias_ref[pl.ds(j, 1)])
        down_copy(j).wait()
        d_pre = (nt(cot, w_down_ref[j]) * slope).astype(BF)
        back_sum[...] += nt(d_pre, w_up_ref[j])
        out_sum[...] += nn(hidden.astype(BF), w_down_ref[j])
        return carry

    lax.fori_loop(0, SEQ_WAYS, units, 0)
    out, back = out_sum[...], back_sum[...]
    out_ref[...] = out[:TOK].astype(BF)
    scaled = back * gain
    cot = cot.astype(F32)
    d_rows = cot + scale * (
        scaled
        - jnp.mean(scaled, axis=-1, keepdims=True)
        - hat * jnp.mean(scaled * hat, axis=-1, keepdims=True)
    )
    sums = [back * hat, back, cot]
    sums = [jnp.sum(rows, axis=0, keepdims=True) for rows in sums]
    send_ref[:CHUNK] = d_rows.astype(BF)
    send_ref[CHUNK : CHUNK + GLOB_OWN] = out[TOK:].astype(BF)
    sums = jnp.concatenate(sums + [jnp.zeros((13, D), F32)], axis=0)
    send_ref[CHUNK + GLOB_OWN :] = sums.astype(BF)


def feed_rows_kernel(
    att_a, att_b, att_c, att_d, cot_a, cot_b, cot_c, cot_d, cot_glob_ref, glob_ref, gain_ref,
    shift_ref, bias_ref, super_any, w_out_any, w_up_any,
    kept_ref, sent_ref, normed_ref, slope_ref, cot_ref,
    super_ref, w_out_ref, w_up_ref, hidden_ref, grad, sems,
):
    me, x = lax.axis_index("seq"), lax.rem(lax.axis_index("grp"), 2)
    mine = pl.multiple_of(me * FF_OWN, FF_OWN)
    copies = [
        load(super_any, super_ref, sems.at[0]),
        load(w_out_any, w_out_ref, sems.at[1]),
        load(w_up_any.at[:, pl.ds(mine, FF_OWN)], w_up_ref, sems.at[2]),
    ]
    for k, cot in enumerate((cot_a, cot_b, cot_c, cot_d)):
        b = me ^ k
        at = lax.div(b, 2) * HALF + lax.rem(b, 2) * TOK
        cot_ref[pl.ds(pl.multiple_of(at, 32), TOK)] = cot[...]
    for half in range(2):
        cot_ref[HALF * half + HALF_TOK : HALF * (half + 1)] = cot_glob_ref[
            HALF_GLOB * half : HALF_GLOB * (half + 1)
        ]
    gain, shift = as_row(gain_ref), as_row(shift_ref)
    bias = as_row(bias_ref)
    bias = [bias[:, FF_OWN * j : FF_OWN * (j + 1)] for j in range(SEQ_WAYS)]
    bias = jnp.where(me < 2, jnp.where(me == 0, bias[0], bias[1]), jnp.where(me == 2, bias[2], bias[3]))
    for copy in copies:
        copy.wait()
    for half in range(2):
        rows = slice(HALF * half, HALF * (half + 1))
        glob_rows = glob_ref[HALF_GLOB * half : HALF_GLOB * (half + 1)].astype(F32)
        y_rows = jnp.concatenate([super_ref[HALF_TOK * half : HALF_TOK * (half + 1)], glob_rows], axis=0)
        for k, att in enumerate((att_a, att_b, att_c, att_d)):
            w_rows = w_out_ref[pl.ds(pl.multiple_of((me ^ k) * OWN, OWN), OWN)]
            y_rows = y_rows + nn(att[:, OWN * half : OWN * (half + 1)], w_rows)
        normed = (row_stats(y_rows)[0] * gain + shift).astype(BF)
        normed_ref[rows] = normed
        hidden, slope = gelu_parts(nn(normed, w_up_ref[...]) + bias)
        hidden_ref[rows] = hidden.astype(BF)
        slope_ref[rows] = slope
    grad[...] = tn(hidden_ref[...], cot_ref[...])
    share_out(lambda g: grad[BAND * g : BAND * (g + 1)].astype(BF), x, X_PAIRS, kept_ref, sent_ref)


def feed_back_kernel(
    normed_ref, slope_ref, cot_ref, w_down_any,
    kept_ref, sent_ref, d_bias_ref, w_down_ref, d_pre_ref, grad, sems,
):
    me = lax.axis_index("seq")
    x = lax.rem(lax.axis_index("grp"), 2)
    mine = pl.ds(pl.multiple_of(me * FF_OWN, FF_OWN), FF_OWN)
    load(w_down_any.at[mine], w_down_ref, sems.at[0]).wait()
    d_bias = jnp.zeros((1, FF_OWN), F32)
    for half in range(2):
        rows = slice(HALF * half, HALF * (half + 1))
        d_pre = (nt(cot_ref[rows], w_down_ref[...]) * slope_ref[rows]).astype(BF)
        d_pre_ref[rows] = d_pre
        d_bias = d_bias + jnp.sum(d_pre.astype(F32), axis=0, keepdims=True)
    d_bias_ref[...] = d_bias
    grad[...] = tn(normed_ref[...], d_pre_ref[...])
    share_out(
        lambda g: jnp.concatenate(row_pieces(grad, g), axis=0).astype(BF), x, X_PAIRS, kept_ref, sent_ref
    )


def project_grad_kernel(normed_ref, d_qkv_ref, attn_ref, d_proj_ref, kept_ref, sent_ref, grad, grad_out):
    x = lax.rem(lax.axis_index("grp"), 2)
    grad[...] = tn(normed_ref[...], d_qkv_ref[:, : 3 * OWN])
    total = None
    for half in range(2):
        columns = slice(OWN * half, OWN * (half + 1))
        first, glob_first = HALF_TOK * half, ROWS + HALF_GLOB * half
        term = tn(attn_ref[:HALF_TOK, columns], d_proj_ref[first : first + HALF_TOK])
        term = term + tn(attn_ref[HALF_TOK:, columns], d_proj_ref[glob_first : glob_first + HALF_GLOB])
        total = term if total is None else total + term
    grad_out[...] = total

    def chunk(g):
        out_rows = grad_out[PIECE * g : PIECE * (g + 1)]
        left = jnp.concatenate(row_pieces(grad, g), axis=0)
        right = [out_rows[:, OWN * p : OWN * (p + 1)] for p in range(SEQ_WAYS)]
        return jnp.concatenate([left, jnp.concatenate(right, axis=0)], axis=1).astype(BF)

    share_out(chunk, x, X_PAIRS, kept_ref, sent_ref)


def back_kernel(
    back_a, back_b, back_c, back_d, glob_att_ref, meta_row_ref, rich_q_ref,
    rich_k_ref, w_out_any, qkv_any, prob_any, member_any,
    d_proj_ref, d_qkv_ref, vec_ref, out_global_ref,
    w_out_ref, qkv_ref, prob_ref, member_ref, keys, values, key_rich, meta_pad, before_ref, distance_ref,
    rich_left, d_att, d_keys, d_values, d_key_rich, d_query_rich, rich_qt, rich_kt, d_glob, parts, rich,
    sems, prob_sems,
):
    me = lax.axis_index("seq")
    own_rows = pl.ds(pl.multiple_of(me * OWN, OWN), OWN)
    w_copy = load(w_out_any.at[own_rows], w_out_ref, sems.at[0])
    qkv_copy = load(qkv_any, qkv_ref, sems.at[1])

    def prob_copy(b):
        rows = pl.ds(pl.multiple_of(b * TOK, TOK), TOK)
        return pltpu.make_async_copy(prob_any.at[:, rows], prob_ref.at[:, rows], prob_sems.at[b])

    for b in range(SEQ_WAYS):
        prob_copy(b).start()
    member_copy = load(member_any, member_ref, sems.at[2])
    sums = None
    for k, back in enumerate((back_a, back_b, back_c, back_d)):
        at = me ^ k
        d_proj_ref[pl.ds(pl.multiple_of(at * TOK, TOK), TOK)] = back[:TOK]
        d_proj_ref[pl.ds(pl.multiple_of(ROWS + at * GLOB_OWN, GLOB_OWN), GLOB_OWN)] = back[TOK:CHUNK]
        out_global_ref[pl.ds(pl.multiple_of(at * GLOB_OWN, GLOB_OWN), GLOB_OWN)] = back[
            CHUNK : CHUNK + GLOB_OWN
        ]
        part = back[CHUNK + GLOB_OWN :].astype(F32)
        sums = part if sums is None else sums + part
    vec_ref[...] = sums[:8]
    w_copy.wait()
    projected = nt(d_proj_ref[...], w_out_ref[...]).astype(BF)
    for h in range(OWN_HEADS):
        d_att[h] = projected[:, h * HEAD_DIM : (h + 1) * HEAD_DIM]
    meta_pad[...] = jnp.zeros((16, PAD), F32)
    meta_pad[:, RADIUS : RADIUS + ROWS] = meta_row_ref[...]
    qkv_copy.wait()
    spread_keys(qkv_ref, keys, values)
    rich_q, rich_k = rich_q_ref[...], rich_k_ref[...]

    def prepare(h, carry):
        rich_left[h] = rich_columns(rich_q, me, h).astype(BF)
        rich_qt[h] = rich_rows(rich_q, me, h)
        rich_kt[h] = rich_rows(rich_k, me, h)
        key_rich[h] = nt(rich_kt[h].astype(BF), keys[h])
        return carry

    lax.fori_loop(0, OWN_HEADS, prepare, 0, unroll=True)
    d_keys[...] = jnp.zeros((OWN_HEADS, PAD, HEAD_DIM), F32)
    d_values[...] = jnp.zeros((OWN_HEADS, PAD, HEAD_DIM), F32)
    d_key_rich[...] = jnp.zeros((OWN_HEADS, 8, PAD), F32)
    d_glob[...] = jnp.zeros((2 * OWN_HEADS, GLOBALS, HEAD_DIM), F32)

    def block(b, carry):
        start = pl.multiple_of(b * TOK, TOK)
        rows = pl.ds(start, TOK)
        window = pl.ds(start, WIN)
        pair_terms(meta_columns(meta_row_ref[:, rows]), meta_pad[:, window], before_ref, distance_ref)
        prob_copy(b).wait()

        def head(h, inner):
            query = qkv_ref[h, rows]
            d_out = d_att[h, rows]
            prob = prob_ref[h, rows, :WIN]
            glob_prob = prob_ref[h, rows, WIN : WIN + GLOBALS]
            d_prob = nt(d_out, values[h, window])
            d_glob_prob = nt(d_out, qkv_ref[2 * OWN_HEADS + h, ROWS:])
            delta = jnp.sum(prob * d_prob, axis=-1, keepdims=True) + jnp.sum(
                glob_prob * d_glob_prob, axis=-1, keepdims=True
            )
            d_scores = prob * (d_prob - delta)
            d_low = d_scores.astype(BF)
            d_glob_low = (glob_prob * (d_glob_prob - delta)).astype(BF)
            query_rich = nn(query, rich_left[h])
            right = key_rich[h, :, window]
            lefts, belows = [None] * 4, [None] * 4
            for c in range(2):
                logit = query_rich[:, c : c + 1] + right[c : c + 1]
                pulled = d_scores * (0.5 * before_ref[c] - 0.5 * jnp.tanh(0.5 * logit))
                off = distance_ref[c] - (query_rich[:, 2 + c : 3 + c] + right[2 + c : 3 + c])
                off = d_scores * off
                lefts[c] = jnp.sum(pulled, axis=-1, keepdims=True)
                lefts[2 + c] = jnp.sum(off, axis=-1, keepdims=True)
                belows[c] = jnp.sum(pulled, axis=0, keepdims=True)
                belows[2 + c] = jnp.sum(off, axis=0, keepdims=True)
            d_key_rich[h, :, window] += jnp.concatenate(belows + [jnp.zeros((4, WIN), F32)], axis=0)
            lane = lax.broadcasted_iota(jnp.int32, (TOK, 8), 1)
            d_left = jnp.zeros((TOK, 8), F32)
            d_query = (
                nn(d_low, keys[h, window]) + nn(d_glob_low, qkv_ref[OWN_HEADS + h, ROWS:])
            ) * SCORE_SCALE
            for c, column in enumerate(lefts):
                d_left = jnp.where(lane == c, column, d_left)
                d_query = d_query + column * rich_qt[h, c : c + 1]
            d_query_rich[h, rows] = d_left
            parts[h, rows] = d_query.astype(BF)
            d_keys[h, window] += tn(d_low, query) * SCORE_SCALE
            d_values[h, window] += tn(prob.astype(BF), d_out)
            d_glob[h] += tn(d_glob_low, query) * SCORE_SCALE
            d_glob[OWN_HEADS + h] += tn(glob_prob.astype(BF), d_out)
            return inner

        lax.fori_loop(0, OWN_HEADS, head, 0, unroll=True)
        return carry

    lax.fori_loop(0, SEQ_WAYS, block, 0)
    member_copy.wait()

    def glob_head(h, carry):
        query = qkv_ref[h, ROWS:]
        key_rows = qkv_ref[OWN_HEADS + h, :ROWS]
        value_rows = qkv_ref[2 * OWN_HEADS + h, :ROWS]
        glob_key = qkv_ref[OWN_HEADS + h, ROWS:]
        glob_value = qkv_ref[2 * OWN_HEADS + h, ROWS:]
        d_out = d_att[h, ROWS:]
        delta = jnp.sum(d_out.astype(F32) * glob_att_ref[h], axis=-1, keepdims=True)
        prob = member_ref[h, :, :ROWS]
        own_prob = member_ref[h, :, ROWS : ROWS + GLOBALS]
        d_low = (prob * (nt(d_out, value_rows) - delta)).astype(BF)
        d_own = (own_prob * (nt(d_out, glob_value) - delta)).astype(BF)
        d_query = (nn(d_low, key_rows) + nn(d_own, glob_key)) * SCORE_SCALE
        parts[h, ROWS:] = d_query.astype(BF)
        parts[OWN_HEADS + h, ROWS:] = (d_glob[h] + tn(d_own, query) * SCORE_SCALE).astype(BF)
        parts[2 * OWN_HEADS + h, ROWS:] = (
            d_glob[OWN_HEADS + h] + tn(own_prob.astype(BF), d_out)
        ).astype(BF)
        d_right = d_key_rich[h, :, RADIUS : RADIUS + ROWS]
        d_key = d_keys[h, RADIUS : RADIUS + ROWS] + tn(d_low, query) * SCORE_SCALE
        d_key = d_key + lax.dot_general(
            d_right, rich_kt[h], (((0,), (0,)), ((), ())), precision=PRECISE,
            preferred_element_type=F32,
        )
        d_value = d_values[h, RADIUS : RADIUS + ROWS] + tn(prob.astype(BF), d_out)
        parts[OWN_HEADS + h, :ROWS] = d_key.astype(BF)
        parts[2 * OWN_HEADS + h, :ROWS] = d_value.astype(BF)
        rich[pl.ds(pl.multiple_of(8 * h, 8), 8)] = jnp.concatenate(
            [tn(d_query_rich[h].astype(BF), qkv_ref[h, :ROWS])[:4], nn(d_right.astype(BF), key_rows)[:4]],
            axis=0,
        )
        return carry

    lax.fori_loop(0, OWN_HEADS, glob_head, 0, unroll=True)
    for i in range(3 * OWN_HEADS):
        d_qkv_ref[:, i * HEAD_DIM : (i + 1) * HEAD_DIM] = parts[i]
    rich[RICH:] = jnp.zeros((32 - RICH, HEAD_DIM), F32)
    d_qkv_ref[:, 3 * OWN :] = jnp.zeros((ALL, WIDE - 3 * OWN), BF)
    d_qkv_ref[:32, 3 * OWN :] = rich[...].astype(BF)


def norm_kernel(
    dqkv_a, dqkv_b, dqkv_c, dqkv_d, glob_ref, d_proj_ref, gain_ref, vec_two_ref, d_bias_up_ref,
    w_query_any, w_key_any, w_value_any, super_any, pre_any, agg_any,
    grad_glob_ref, kept_ref, sent_ref, d_own_ref, d_pre,
    w_query_ref, w_key_ref, w_value_ref, super_ref, pre_ref, agg_ref, d_super, d_qkv, d_norm, rich, sems,
):
    me, x = lax.axis_index("seq"), lax.rem(lax.axis_index("grp"), 2)
    weight_copies = [
        load(source, target, sems.at[i])
        for i, (source, target) in enumerate((
            (w_query_any, w_query_ref), (w_key_any, w_key_ref), (w_value_any, w_value_ref),
        ))
    ]
    row_copies = [load(super_any, super_ref, sems.at[3]), load(pre_any, pre_ref, sems.at[4])]
    agg_copy = load(agg_any, agg_ref, sems.at[5])
    for k, part in enumerate((dqkv_a, dqkv_b, dqkv_c, dqkv_d)):
        d_qkv[me ^ k] = part[...]
        rich[me ^ k] = part[:32, 3 * OWN :].astype(F32)
    total = None
    for i, weight in enumerate((w_query_ref, w_key_ref, w_value_ref)):
        weight_copies[i].wait()
        columns = [d_qkv[p, :, OWN * i : OWN * (i + 1)] for p in range(SEQ_WAYS)]
        term = nt(jnp.concatenate(columns, axis=1), weight[...])
        total = term if total is None else total + term
    d_norm[...] = total
    for copy in row_copies:
        copy.wait()
    gain = as_row(gain_ref)
    d_gain = jnp.zeros((1, D), F32)
    d_shift = jnp.zeros((1, D), F32)
    for low in range(0, ALL, 192):
        rows = slice(low, low + 192)
        inner = min(192, ROWS - low)
        if inner == 192:
            rows_in = super_ref[rows]
        else:
            rows_in = jnp.concatenate([super_ref[low:], glob_ref[...].astype(F32)], axis=0)
        back, gain_part, shift_part = norm_back(d_norm[rows], gain, rows_in)
        d_gain = d_gain + gain_part
        d_shift = d_shift + shift_part
        back = back + d_proj_ref[rows].astype(F32)
        d_super[rows] = back
        long = slice(low, low + inner)
        slope = gelu_parts(pre_ref[long])[1]
        d_pre[long] = (back[:inner] * slope).astype(BF)
    grad_glob_ref[...] = d_super[ROWS:]
    d_own_ref[...] = d_super[pl.ds(pl.multiple_of(me * TOK, TOK), TOK)]
    agg_copy.wait()
    grad = tn(own_part(agg_ref[...], me), d_pre[...])
    extra = jnp.concatenate(
        [vec_two_ref[0:3], d_bias_up_ref[...], d_gain, d_shift, jnp.zeros((1, D), F32)], axis=0
    )

    def chunk(g):
        pieces = [rich[g // 2, 12 * (g % 2) + i : 12 * (g % 2) + i + 1] for i in range(12)]
        rows = [grad[PIECE * g : PIECE * (g + 1)], jnp.concatenate(pieces, axis=1), extra]
        return jnp.concatenate(rows, axis=0).astype(BF)

    share_out(chunk, x, X_PAIRS, kept_ref, sent_ref)


def tokens_kernel(d_own_ref, d_pre, meta_row_ref, w_graph_any, grad_tok_ref, w_graph_ref, sems):
    me = lax.axis_index("seq")
    copy = load(w_graph_any, w_graph_ref, sems.at[0])
    counts = []
    for shift in (-1, 0, 1):
        rows = pl.ds(pl.multiple_of(jnp.clip(me - shift, 0, SEQ_WAYS - 1) * TOK, TOK), TOK)
        counts.append(counts_of(meta_columns(meta_row_ref[:, rows]), (shift + 1) * TOK, TOK))
    copy.wait()
    total = d_own_ref[...]
    for shift, count in zip((-1, 0, 1), counts):
        b = me - shift
        fits = (b >= 0) & (b < SEQ_WAYS)
        rows = pl.ds(pl.multiple_of(jnp.clip(b, 0, SEQ_WAYS - 1) * TOK, TOK), TOK)
        d_agg = (nt(d_pre[rows], w_graph_ref[...]) * (1.0 / NEIGH)).astype(BF)
        total = total + jnp.where(fits, tn(count, d_agg), 0.0)
    grad_tok_ref[...] = total


DISTANCES = (0, 4, 2, 6)


def down_out_kernel(held, came, out_ref):
    for i, distance in enumerate(DISTANCES):
        for flip, pieces in enumerate((held, came)):
            g = lax.axis_index("grp") ^ (distance + flip)
            out_ref[pl.ds(pl.multiple_of(BAND * g, BAND), BAND)] = pieces[i].astype(F32)


def up_out_kernel(held, came, out_ref):
    for i, distance in enumerate(DISTANCES):
        for flip, pieces in enumerate((held, came)):
            g = lax.axis_index("grp") ^ (distance + flip)
            piece = pieces[i].astype(F32)
            rows = pl.ds(pl.multiple_of(PIECE * g, 8), PIECE)
            for k in range(SEQ_WAYS):
                columns = pl.ds(pl.multiple_of((lax.axis_index("seq") ^ k) * D, D), D)
                out_ref[rows, columns] = piece[PIECE * k : PIECE * (k + 1)]


def project_out_kernel(held, came, query_ref, key_ref, value_ref, out_ref, pieces):
    for i, distance in enumerate(DISTANCES):
        for flip, blocks in enumerate((held, came)):
            g = lax.axis_index("grp") ^ (distance + flip)
            rows = pl.ds(pl.multiple_of(PIECE * g, 8), PIECE)
            piece = blocks[i].astype(F32)
            for k in range(SEQ_WAYS):
                pieces[lax.axis_index("seq") ^ k] = piece[PIECE * k : PIECE * (k + 1), : 3 * OWN]
            for j, ref in enumerate((query_ref, key_ref, value_ref)):
                parts = [pieces[p, :, OWN * j : OWN * (j + 1)] for p in range(SEQ_WAYS)]
                ref[rows] = jnp.concatenate(parts, axis=1)
            parts = [piece[PIECE * p : PIECE * (p + 1), 3 * OWN :] for p in range(SEQ_WAYS)]
            out_ref[rows] = jnp.concatenate(parts, axis=1)


def graph_out_kernel(
    held, came, graph_ref, gain_one_ref, shift_one_ref, gain_two_ref, shift_two_ref, bias_up_ref,
    bias_down_ref, rich_q_ref, rich_k_ref, vectors,
):
    me = lax.axis_index("seq")
    for i, distance in enumerate(DISTANCES):
        for flip, blocks in enumerate((held, came)):
            g = lax.axis_index("grp") ^ (distance + flip)
            rows = pl.ds(pl.multiple_of(PIECE * g, 8), PIECE)
            piece = blocks[i].astype(F32)
            graph_ref[rows] = piece[:PIECE]
            for j in range(12):
                vectors[g, j : j + 1] = piece[PIECE : PIECE + 1, HEAD_DIM * j : HEAD_DIM * (j + 1)]
            vectors[g, 12:16] = jnp.zeros((4, HEAD_DIM), F32)
    sums = held[0, PIECE : PIECE + 8].astype(F32)
    lane = lax.broadcasted_iota(jnp.int32, (D, 256), 0)
    spot = lax.broadcasted_iota(jnp.int32, (D, 256), 1)
    own = jnp.where((lane == OWN * me + spot) & (spot < OWN), 1.0, 0.0).astype(BF)
    own = nn(sums.astype(BF), own)[:, :OWN]
    for ref, row in (
        (gain_two_ref, 1), (shift_two_ref, 2), (bias_down_ref, 3), (gain_one_ref, 5), (shift_one_ref, 6),
    ):
        ref[...] = own[row : row + 1].reshape(OWN)
    bias_up_ref[...] = sums[4:5].reshape(FF_OWN)
    lane = lax.broadcasted_iota(jnp.int32, (HEAD_DIM, 128), 0)
    spot = lax.broadcasted_iota(jnp.int32, (HEAD_DIM, 128), 1)
    part = HEAD_DIM // SEQ_WAYS
    own = jnp.where((lane == part * me + spot) & (spot < part), 1.0, 0.0).astype(BF)
    own = nn(vectors[...].reshape(16 * GRP_WAYS, HEAD_DIM).astype(BF), own).astype(BF)
    row = lax.broadcasted_iota(jnp.int32, (16 * GRP_WAYS, 128), 0)
    place = 12 * lax.div(row, 16) + lax.rem(row, 16)
    column = lax.broadcasted_iota(jnp.int32, (16 * GRP_WAYS, 128), 1)
    for side, ref in enumerate((rich_q_ref, rich_k_ref)):
        wanted = 8 * lax.div(column, 4) + 4 * side + lax.rem(column, 4)
        chosen = (place == wanted) & (lax.rem(row, 16) < 12) & (column < 4 * HEADS)
        turned_rich = tn(own, jnp.where(chosen, 1.0, 0.0).astype(BF))
        ref[...] = turned_rich[:part, : 4 * HEADS]


def call(kernel, ins, outs, scratch=(), apart=0, outs_apart=0, room=50):
    vmem, any_space = pl.BlockSpec(memory_space=pltpu.VMEM), pl.BlockSpec(memory_space=pltpu.HBM)
    return pl.pallas_call(
        kernel,
        out_shape=[jax.ShapeDtypeStruct(shape, kind) for shape, kind in outs],
        in_specs=[vmem] * (len(ins) - apart) + [any_space] * apart,
        out_specs=[vmem] * (len(outs) - outs_apart) + [any_space] * outs_apart,
        scratch_shapes=[pltpu.VMEM(*s) if isinstance(s, tuple) else s for s in scratch],
        compiler_params=pltpu.CompilerParams(vmem_limit_bytes=room * 1024 * 1024),
        cost_estimate=pl.CostEstimate(flops=KERNEL_COST, bytes_accessed=0, transcendentals=0),
    )(*ins)


def split_heads(
    tokens, global_tokens, neighbours, token_ranks, membership, w_graph, gain_one, shift_one,
    w_query, w_key, w_value, rich_query, rich_key, w_out, gain_two, shift_two, w_up, bias_up,
    w_down, bias_down, cot_tokens, cot_global,
):
    me = lax.axis_index("seq")
    grp = lax.axis_index("grp")
    x, z_low, z_high = grp % 2, (grp // 2) % 2, grp // 4
    beside, across = reach_seq(tokens)
    (ints,) = call(
        ints_kernel, [neighbours.T, token_ranks, membership.reshape(1, TOK)], [((16, TOK), jnp.int32)],
        room=60,
    )
    int_beside, int_across = reach_seq(ints)
    int_blocks = [ints, int_beside, int_across, lax.ppermute(int_across, "seq", CORE_SWAP)]
    cot_tokens, across, int_blocks[3] = tie(cot_tokens, across, int_blocks[3])
    cot_across = lax.ppermute(cot_tokens, "seq", Y_SWAP)
    tok_blocks = [tokens, beside, across, lax.ppermute(across, "seq", CORE_SWAP)]
    rich_query, rich_key = rich_query.T, rich_key.T

    weights_shape = (D, D), BF
    stored = [
        ((ROWS, D), BF), ((ROWS, D), F32), ((ROWS, D), F32), ((ALL, D), BF),
        ((3 * OWN_HEADS, ALL, HEAD_DIM), BF), ((OWN_HEADS, ROWS, 512), F32),
    ]
    kept_agg = (ROWS, 256), BF
    heads_scratch = [
        ((OWN_HEADS, PAD, HEAD_DIM), BF), ((OWN_HEADS, PAD, HEAD_DIM), BF),
        ((OWN_HEADS, 8, PAD), F32), ((16, PAD), F32), ((2, TOK, WIN), F32), ((2, TOK, WIN), F32),
        ((OWN_HEADS, HEAD_DIM, 128), BF),
    ]
    (
        both, member_prob, glob_att, meta_row, agg, graph_pre, super_rows, normed, qkv,
        prob,
    ) = call(
        attend_kernel,
        [*tok_blocks, *int_blocks, global_tokens, gain_one, shift_one, rich_query, rich_key, w_graph, w_query,
         w_key, w_value],
        [((HALF, 2 * OWN), BF), ((OWN_HEADS, GLOBALS, 640), F32),
         ((OWN_HEADS, GLOBALS, HEAD_DIM), F32), ((16, ROWS), F32), kept_agg, *stored[1:]],
        [*stored, ((PAD, D), BF), weights_shape, ((3, D, 256), BF), *heads_scratch,
         ((TOK, WIN), F32), ((OWN_HEADS, ALL, HEAD_DIM), BF), ((ALL, OWN), BF),
         ((ROWS, 128), F32), pltpu.SemaphoreType.DMA((9,)), pltpu.SemaphoreType.DMA((SEQ_WAYS,))],
        apart=4, outs_apart=6, room=56,
    )
    both, cot_across, cot_tokens = tie(both, cot_across, cot_tokens)
    att_blocks = gather_seq(both)
    cot_beside = lax.ppermute(cot_tokens, "seq", CORE_SWAP)
    cot_blocks = [cot_tokens, cot_beside, cot_across, lax.ppermute(cot_across, "seq", CORE_SWAP)]
    out_tokens, back = call(
        own_feed_kernel,
        [*att_blocks, gain_two, shift_two, bias_up, bias_down, cot_tokens, super_rows,
         global_tokens, cot_global, w_out, w_up, w_down],
        [((TOK, D), BF), ((SEND, D), BF)],
        [((SEQ_WAYS, TOK, 2 * OWN), BF), ((SEQ_WAYS, GLOB_OWN, 2 * OWN), BF), ((TOK, D), F32),
         ((GLOB_OWN, D), BF), ((GLOB_OWN, D), BF), weights_shape, ((SEQ_WAYS, D, FF_OWN), BF),
         ((SEQ_WAYS, FF_OWN, D), BF), ((SEQ_WAYS, FF_OWN), F32), ((CHUNK, D), F32), ((CHUNK, D), F32),
         pltpu.SemaphoreType.DMA((20,))],
        apart=6,
    )
    beside, across = reach_seq(back)
    late_gain, back = tie(gain_two, back)
    down_kept, down_sent, normed_two, slope, cot_all = call(
        feed_rows_kernel,
        [*att_blocks, *cot_blocks, cot_global, global_tokens, late_gain, shift_two,
         bias_up, super_rows, w_out, w_up],
        [((4, BAND, D), BF), ((4, BAND, D), BF), ((ALL, D), BF), ((ALL, FF_OWN), F32), ((ALL, D), BF)],
        [((ROWS, D), F32), weights_shape, ((D, FF_OWN), BF), ((ALL, FF_OWN), BF), ((D, D), F32),
         pltpu.SemaphoreType.DMA((3,))],
        apart=3,
    )
    down_came = swap_x(down_sent)
    across, down_kept = tie(across, down_kept)
    diagonal = lax.ppermute(across, "seq", CORE_SWAP)
    normed_two, across = tie(normed_two, across)
    up_kept, up_sent, d_bias_up = call(
        feed_back_kernel,
        [normed_two, slope, cot_all, w_down],
        [((4, BAND, D), BF), ((4, BAND, D), BF), ((1, FF_OWN), F32)],
        [((FF_OWN, D), BF), ((ALL, FF_OWN), BF), ((D, D), F32), pltpu.SemaphoreType.DMA((1,))],
        apart=1,
    )
    up_came = swap_x(up_sent)
    late_row, up_kept = tie(meta_row, up_kept)

    d_proj, d_qkv, vec_two, out_global = call(
        back_kernel,
        [back, beside, across, diagonal, glob_att, late_row, rich_query, rich_key,
         w_out, qkv, prob, member_prob],
        [((ALL, D), BF), ((ALL, WIDE), BF), ((8, D), F32), ((GLOBALS, D), BF)],
        [((OWN, D), BF), stored[4], stored[5], ((OWN_HEADS, GLOBALS, 640), F32), *heads_scratch,
         ((OWN_HEADS, ALL, HEAD_DIM), BF), ((OWN_HEADS, PAD, HEAD_DIM), F32),
         ((OWN_HEADS, PAD, HEAD_DIM), F32), ((OWN_HEADS, 8, PAD), F32), ((OWN_HEADS, ROWS, 8), F32),
         ((OWN_HEADS, 8, HEAD_DIM), F32), ((OWN_HEADS, 8, HEAD_DIM), F32),
         ((2 * OWN_HEADS, GLOBALS, HEAD_DIM), F32), ((3 * OWN_HEADS, ALL, HEAD_DIM), BF),
         ((32, HEAD_DIM), F32), pltpu.SemaphoreType.DMA((3,)), pltpu.SemaphoreType.DMA((SEQ_WAYS,))],
        apart=4,
    )
    beside, across = reach_seq(d_qkv)
    held = {"d_qkv": d_qkv, "down": down_kept, "up": up_kept}
    latest = ["d_qkv"]

    def due(value):
        value, held[latest[0]] = tie(value, held[latest[0]])
        return value

    def hold(key, value):
        held[key] = value
        latest[0] = key
        return value

    def halve(key, came, bit):
        kept, sent = halves(held[key], due(came), bit)
        hold(key, kept)
        return sent

    def total(key, came):
        return hold(key, added(held[key], due(came)))

    def join(key, came):
        return hold(key, jnp.concatenate([held[key], due(came)], axis=0))

    down_came = swap_near(halve("down", down_came, z_low))
    proj_kept, proj_sent = call(
        project_grad_kernel,
        [due(normed), d_qkv, both, d_proj],
        [((4, BAND, D), BF)] * 2,
        [((D, 3 * OWN), F32), ((OWN, D), F32)],
    )
    hold("proj", proj_kept)
    proj_came = swap_x(proj_sent)
    up_came = swap_near(halve("up", up_came, z_low))
    down_came = swap_far(halve("down", down_came, z_high))
    across = hold("across", due(across))
    diagonal = lax.ppermute(across, "seq", CORE_SWAP)
    up_came = swap_far(halve("up", up_came, z_high))
    down_came = swap_far(total("down", down_came))
    proj_came = swap_near(halve("proj", proj_came, z_low))
    grad_global, graph_kept, graph_sent, d_own, d_pre = call(
        norm_kernel,
        [d_qkv, beside, held["across"], diagonal, global_tokens, d_proj, gain_one, due(vec_two), d_bias_up,
         w_query, w_key, w_value, super_rows, graph_pre, agg],
        [((GLOBALS, D), F32), ((4, GRAPH_ROWS, D), BF), ((4, GRAPH_ROWS, D), BF), ((TOK, D), F32),
         ((ROWS, D), BF)],
        [*[weights_shape] * 3, ((ROWS, D), F32), ((ROWS, D), F32), ((ROWS, 256), BF), ((ALL, D), F32),
         ((SEQ_WAYS, ALL, WIDE), BF), ((ALL, D), F32), ((SEQ_WAYS, 32, HEAD_DIM), F32),
         pltpu.SemaphoreType.DMA((6,))],
        apart=6,
    )
    hold("graph", graph_kept)
    graph_came = swap_x(graph_sent)
    up_mine = total("up", up_came).reshape(SEQ_WAYS, PIECE, D)
    up_core = turn_core(up_mine)
    proj_came = swap_far(halve("proj", proj_came, z_high))
    down_came = swap_near(join("down", down_came))
    up_core = due(up_core)
    up_far = lax.ppermute(turn_y(up_mine, up_core), "seq", Y_SWAP)
    hold("up_core", up_core)
    (grad_tokens,) = call(
        tokens_kernel, [due(d_own), d_pre, meta_row, w_graph], [((TOK, D), F32)],
        [weights_shape, pltpu.SemaphoreType.DMA((1,))], apart=1,
    )
    hold("tokens", grad_tokens)
    up_came = swap_far(hold("up", turned(up_mine, held["up_core"], due(up_far))[None]))
    proj_sum = total("proj", proj_came)
    proj_core = turn_core(proj_sum[0, :, : 3 * OWN].reshape(SEQ_WAYS, PIECE, 3 * OWN))
    down_came = swap_x(join("down", down_came))
    proj_core = due(proj_core)
    proj_mine = held["proj"][0, :, : 3 * OWN].reshape(SEQ_WAYS, PIECE, 3 * OWN)
    proj_far = lax.ppermute(turn_y(proj_mine, proj_core), "seq", Y_SWAP)
    hold("proj_core", proj_core)
    up_came = swap_near(join("up", up_came))
    graph_came = swap_near(halve("graph", graph_came, z_low))
    proj_turned = turned(proj_mine, held["proj_core"], due(proj_far))
    proj_turned = jnp.concatenate([proj_turned, held["proj"][0, :, 3 * OWN :]], axis=1)[None]
    proj_came = swap_far(hold("proj", proj_turned))
    up_came = swap_x(join("up", up_came))
    proj_came = swap_near(join("proj", proj_came))
    graph_came = swap_far(halve("graph", graph_came, z_high))
    graph_came = swap_far(total("graph", graph_came))
    (g_down,) = call(down_out_kernel, [held["down"], due(down_came)], [((FF_OWN, D), F32)])
    hold("g_down", g_down)
    graph_came = swap_near(join("graph", graph_came))
    proj_came = swap_x(join("proj", proj_came))
    graph_came = swap_x(join("graph", graph_came))
    (g_up,) = call(up_out_kernel, [held["up"], due(up_came)], [((OWN, FF), F32)])
    hold("g_up", g_up)
    g_query, g_key, g_value, g_out = call(
        project_out_kernel,
        [held["proj"], due(proj_came)],
        [((OWN, D), F32)] * 4,
        [((SEQ_WAYS, PIECE, 3 * OWN), F32)],
    )
    hold("g_query", g_query)
    (
        g_graph, g_gain_one, g_shift_one, g_gain_two, g_shift_two, g_bias_up, g_bias_down, g_rich_q,
        g_rich_k,
    ) = call(
        graph_out_kernel,
        [held["graph"], due(graph_came)],
        [((OWN, D), F32), *[((OWN,), F32)] * 4, ((FF_OWN,), F32), ((OWN,), F32),
         *[((HEAD_DIM // SEQ_WAYS, 4 * HEADS), F32)] * 2],
        [((GRP_WAYS, 16, HEAD_DIM), F32)],
    )
    hold("g_graph", g_graph)
    grad_tokens, g_down, g_up, g_query, g_graph = (
        held[key] for key in ("tokens", "g_down", "g_up", "g_query", "g_graph")
    )
    return (
        out_tokens, out_global, grad_tokens, grad_global,
        g_graph, g_gain_one, g_shift_one, g_query, g_key, g_value, g_rich_q, g_rich_k,
        g_out, g_gain_two, g_shift_two, g_up, g_bias_up, g_down, g_bias_down,
    )


def layer(*arrays):
    tokens, global_tokens = arrays[:2]
    ways = (lax.axis_size("seq"), lax.axis_size("grp"))
    if ways == (SEQ_WAYS, GRP_WAYS) and tokens.shape[0] == TOK and global_tokens.shape[0] == GLOBALS:
        return split_heads(*arrays)
    return local(*arrays)


def solution(mesh):
    return jax.shard_map(
        layer,
        mesh=mesh,
        in_specs=(
            P(("grp", "seq"), None),
            P("grp", None),
            P(("grp", "seq"), None),
            P(None, ("grp", "seq")),
            P(("grp", "seq")),
            P(),
            P(),
            P(),
            P(),
            P(),
            P(),
            P(),
            P(),
            P(),
            P(),
            P(),
            P(),
            P(),
            P(),
            P(),
            P(("grp", "seq"), None),
            P("grp", None),
        ),
        out_specs=(
            P(("grp", "seq"), None),
            P("grp", None),
            P(("grp", "seq"), None),
            P("grp", None),
            P("seq", None),
            P("seq"),
            P("seq"),
            P("seq", None),
            P("seq", None),
            P("seq", None),
            P("seq", None),
            P("seq", None),
            P("seq", None),
            P("seq"),
            P("seq"),
            P("seq", None),
            P("seq"),
            P("seq", None),
            P("seq"),
        ),
        check_vma=False,
    )
```

```python
import functools
import math

import jax
import jax.numpy as jnp
from jax import lax
from jax.experimental import pallas as pl
from jax.experimental.pallas import tpu as pltpu
from jax.sharding import PartitionSpec as P

D = 768
HEADS = 12
HEAD_DIM = 64
RADIUS = 128
GLOBALS = 64
NEIGH = 8
SEQ_TOKENS = 2048


EPSILON = 1e-05
PRECISE = lax.Precision.HIGHEST
MASKED = -1e30


def with_halo(cells, sides, width):
    for axis, dim in sides:
        count = lax.axis_size(axis)
        ends = count - 1
        head = lax.slice_in_dim(cells, 0, width, axis=dim)
        tail = lax.slice_in_dim(cells, cells.shape[dim] - width, cells.shape[dim], axis=dim)
        cells = jnp.concatenate(
            [
                lax.ppermute(tail, axis, [(i, (i + 1) % count) for i in range(ends)]),
                cells,
                lax.ppermute(head, axis, [((i + 1) % count, i) for i in range(ends)]),
            ],
            axis=dim,
        )
    return cells


def joined(array, axis, combine):
    everything = jax.tree.map(
        lambda part, kind: lax.all_gather(part.astype(kind), axis),
        array,
        (jnp.bfloat16, jnp.bfloat16, jnp.bfloat16),
    )

    def take(k):
        return jax.tree.map(lambda part, own: part[k].astype(own.dtype), everything, array)

    return lax.fori_loop(
        1, lax.axis_size(axis), lambda k, so_far: combine(so_far, take(k)), take(0)
    )


def shifted(block, axis, distance):
    devices = range(lax.axis_size(axis))
    route = [(i - distance, i) for i in devices if i - distance in devices]
    return lax.ppermute(block, axis, route)


def layer_norm(rows_in, gain_in, shift_in):
    row_mean = jnp.mean(rows_in, axis=-1, keepdims=True)
    centred = rows_in - row_mean
    variance = jnp.mean(centred * centred, axis=-1, keepdims=True)
    return centred * lax.rsqrt(variance + EPSILON) * gain_in + shift_in


def rich_part(a_block, b_window, rank_query, rank_key, log_norm):
    combined = None
    for coordinate in range(2):
        order_flag = (rank_query[coordinate][:, None] < rank_key[coordinate][None, :]).astype(
            jnp.float32
        )
        distance = (
            jnp.log1p(
                jnp.abs(rank_query[coordinate][:, None] - rank_key[coordinate][None, :]).astype(
                    jnp.float32
                )
            )
            / log_norm
        )
        order_logit = a_block[:, :, None, coordinate] + b_window[:, None, :, coordinate]
        centre = a_block[:, :, None, 2 + coordinate] + b_window[:, None, :, 2 + coordinate]
        pair_term = (
            order_flag * jax.nn.log_sigmoid(order_logit)
            + (1.0 - order_flag) * jax.nn.log_sigmoid(-order_logit)
            - 0.5 * (distance - centre) ** 2
        )
        combined = pair_term if combined is None else combined + pair_term
    return combined


def product(left, right):
    return jnp.dot(left, right, preferred_element_type=jnp.float32)


def product_left(left, right):
    return jnp.einsum("ta,tb->ab", left, right, preferred_element_type=jnp.float32)


def product_right(left, right):
    return jnp.einsum("tb,ab->ta", left, right, preferred_element_type=jnp.float32)


def local(
    tokens,
    global_tokens,
    neighbours,
    token_ranks,
    membership,
    w_graph,
    gain_one,
    shift_one,
    w_query,
    w_key,
    w_value,
    rich_query,
    rich_key,
    w_out,
    gain_two,
    shift_two,
    w_up,
    bias_up,
    w_down,
    bias_down,
    cot_tokens,
    cot_global,
):
    tok_count = tokens.shape[0]
    seq_count = lax.axis_size("seq")
    seq_index = lax.axis_index("seq")
    seq_len = min(SEQ_TOKENS, tok_count * seq_count)
    span = seq_len // tok_count
    group_seqs = global_tokens.shape[0] // GLOBALS
    seq_slot = seq_index // span
    seq_local = seq_index % span
    slot_flag = (jnp.arange(group_seqs, dtype=jnp.int32) == seq_slot).astype(jnp.float32)
    log_norm = math.log(1.0 + seq_len)
    score_scale = 1.0 / math.sqrt(HEAD_DIM)
    block_rows = min(512, tok_count)
    window = block_rows + 2 * RADIUS
    ext_count = tok_count + 2 * RADIUS
    first_flag = (seq_index == 0).astype(jnp.float32)
    own_pos = seq_local * tok_count + jnp.arange(tok_count, dtype=jnp.int32)
    ext_pos = seq_local * tok_count - RADIUS + jnp.arange(ext_count, dtype=jnp.int32)
    key_valid = (ext_pos >= 0) & (ext_pos < seq_len)

    def own_slot(array_in):
        return lax.dynamic_index_in_dim(array_in, seq_slot, 0, keepdims=False)

    def to_slots(array_in):
        return slot_flag.reshape((group_seqs,) + (1,) * array_in.ndim) * array_in[None]

    token_ext = with_halo(tokens, (("seq", 0),), RADIUS)
    token_ext = jnp.where(key_valid[:, None], token_ext, jnp.zeros_like(token_ext))
    flat_index = neighbours.reshape(-1)
    gathered = (
        jnp.take(token_ext, flat_index, axis=0).astype(jnp.float32).reshape(tok_count, NEIGH, D)
    )
    agg_low = jnp.mean(gathered, axis=1).astype(jnp.bfloat16)
    graph_pre = product(agg_low, w_graph)
    graph_out, graph_back = jax.vjp(jax.nn.gelu, graph_pre)
    super_rows = tokens.astype(jnp.float32) + graph_out
    normed_full, norm_back = jax.vjp(layer_norm, super_rows, gain_one, shift_one)
    normed = normed_full.astype(jnp.bfloat16)
    glob_in = global_tokens.astype(jnp.float32)
    glob_normed_full, glob_norm_back = jax.vjp(layer_norm, glob_in, gain_one, shift_one)
    glob_normed = glob_normed_full.astype(jnp.bfloat16)
    query = product(normed, w_query).astype(jnp.bfloat16)
    key_own = product(normed, w_key).astype(jnp.bfloat16)
    value_own = product(normed, w_value).astype(jnp.bfloat16)
    glob_query = (
        product(glob_normed, w_query)
        .astype(jnp.bfloat16)
        .reshape(group_seqs, GLOBALS, HEADS, HEAD_DIM)
    )
    glob_key = (
        product(glob_normed, w_key)
        .astype(jnp.bfloat16)
        .reshape(group_seqs, GLOBALS, HEADS, HEAD_DIM)
    )
    glob_value = (
        product(glob_normed, w_value)
        .astype(jnp.bfloat16)
        .reshape(group_seqs, GLOBALS, HEADS, HEAD_DIM)
    )
    glob_query_own = own_slot(glob_query)
    glob_key_own = own_slot(glob_key)
    glob_value_own = own_slot(glob_value)
    kv_ext = with_halo(jnp.concatenate([key_own, value_own], axis=1), (("seq", 0),), RADIUS)
    key_ext = kv_ext[:, :D].reshape(ext_count, HEADS, HEAD_DIM)
    value_ext = kv_ext[:, D:].reshape(ext_count, HEADS, HEAD_DIM)
    rank_ext = with_halo(token_ranks, (("seq", 1),), RADIUS)
    rich_q3 = rich_query.reshape(HEAD_DIM, HEADS, 4)
    rich_k3 = rich_key.reshape(HEAD_DIM, HEADS, 4)
    query_heads = query.reshape(tok_count, HEADS, HEAD_DIM)
    a_rows = jnp.einsum("the,ehc->htc", query_heads, rich_q3, preferred_element_type=jnp.float32)
    b_ext = jnp.einsum("the,ehc->htc", key_ext, rich_k3, preferred_element_type=jnp.float32)

    def block_scores():

        def rich_scores(left_rows, right_rows):
            return rich_part(left_rows, right_rows, token_ranks, rank_ext, log_norm)

        rich_vals, rich_back = jax.vjp(rich_scores, a_rows, b_ext)
        raw_scores = (
            jnp.einsum("qhe,khe->hqk", query_heads, key_ext, preferred_element_type=jnp.float32)
            * score_scale
        )
        pos_gap = own_pos[:, None] - ext_pos[None, :]
        key_mask = (jnp.abs(pos_gap) <= RADIUS) & key_valid[None, :]
        scores = jnp.where(key_mask[None], raw_scores + rich_vals, MASKED)
        glob_scores = (
            jnp.einsum(
                "qhe,ghe->hqg", query_heads, glob_key_own, preferred_element_type=jnp.float32
            )
            * score_scale
        )
        return (scores, glob_scores, rich_back, query_heads, key_ext)

    scored = block_scores()
    scores = scored[0]
    glob_scores = scored[1]
    row_top = jnp.maximum(jnp.max(scores, axis=-1), jnp.max(glob_scores, axis=-1))
    row_denom = jnp.sum(jnp.exp(scores - row_top[..., None]), axis=-1) + jnp.sum(
        jnp.exp(glob_scores - row_top[..., None]), axis=-1
    )
    log_total = row_top + jnp.log(row_denom)
    prob_rows = jnp.exp(scores - log_total[..., None]).astype(jnp.bfloat16)
    glob_probs = jnp.exp(glob_scores - log_total[..., None]).astype(jnp.bfloat16)
    attn_block = jnp.einsum(
        "hqk,khe->qhe", prob_rows, value_ext, preferred_element_type=jnp.float32
    ) + jnp.einsum("hqg,ghe->qhe", glob_probs, glob_value_own, preferred_element_type=jnp.float32)
    attn_parts = attn_block.reshape(block_rows, D)
    attn_rows = attn_parts.astype(jnp.bfloat16)
    member_mask = membership[None, :] == jnp.arange(GLOBALS, dtype=jnp.int32)[:, None]
    key_heads = key_ext[RADIUS : RADIUS + tok_count]
    value_heads = value_ext[RADIUS : RADIUS + tok_count]
    member_raw = (
        jnp.einsum("ghe,the->ght", glob_query_own, key_heads, preferred_element_type=jnp.float32)
        * score_scale
    )
    member_scores = jnp.where(member_mask[:, None, :], member_raw, MASKED)
    local_top = jnp.max(member_scores, axis=-1)
    member_exp = jnp.where(
        member_mask[:, None, :], jnp.exp(member_scores - local_top[..., None]), 0.0
    )
    local_sum = jnp.sum(member_exp, axis=-1)
    local_acc = jnp.einsum(
        "ght,the->ghe", member_exp, value_heads.astype(jnp.float32), precision=PRECISE
    )
    slot_top = jnp.where(slot_flag[:, None, None] > 0.5, local_top[None], MASKED)
    slot_sum = to_slots(local_sum)
    slot_acc = to_slots(local_acc)

    def combine_softmax(first_part, second_part):
        top_one, sum_one, acc_one = first_part
        top_two, sum_two, acc_two = second_part
        top_both = jnp.maximum(top_one, top_two)
        scale_one = jnp.exp(top_one - top_both)
        scale_two = jnp.exp(top_two - top_both)
        return (
            top_both,
            sum_one * scale_one + sum_two * scale_two,
            acc_one * scale_one[..., None] + acc_two * scale_two[..., None],
        )

    merged_top, merged_sum, merged_acc = joined(
        (slot_top, slot_sum, slot_acc), "seq", combine_softmax
    )
    self_scores = (
        jnp.einsum("sghe,skhe->sghk", glob_query, glob_key, preferred_element_type=jnp.float32)
        * score_scale
    )
    glob_top = jnp.maximum(merged_top, jnp.max(self_scores, axis=-1))
    self_exp = jnp.exp(self_scores - glob_top[..., None])
    merged_scale = jnp.exp(merged_top - glob_top)
    glob_denom = merged_sum * merged_scale + jnp.sum(self_exp, axis=-1)
    glob_lse = glob_top + jnp.log(glob_denom)
    glob_att_f = (
        merged_acc * merged_scale[..., None]
        + jnp.einsum("sghk,skhe->sghe", self_exp, glob_value.astype(jnp.float32), precision=PRECISE)
    ) / glob_denom[..., None]
    glob_attn = glob_att_f.reshape(group_seqs * GLOBALS, D).astype(jnp.bfloat16)
    y_one = super_rows + product(attn_rows, w_out)
    glob_y_one = glob_in + product(glob_attn, w_out)

    def feed_forward(rows_in):
        normed_two_full, back_two = jax.vjp(layer_norm, rows_in, gain_two, shift_two)
        normed_two = normed_two_full.astype(jnp.bfloat16)
        hidden_pre = product(normed_two, w_up) + bias_up
        hidden_full, gelu_back = jax.vjp(jax.nn.gelu, hidden_pre)
        hidden = hidden_full.astype(jnp.bfloat16)
        result = rows_in + product(hidden, w_down) + bias_down
        return (result, normed_two, hidden, back_two, gelu_back)

    def feed_back(cotangent, normed_two, hidden, back_two, gelu_back):
        cot_full = cotangent.astype(jnp.float32)
        grad_down = product_left(hidden, cotangent)
        grad_bias_d = jnp.sum(cot_full, axis=0)
        d_hidden = product_right(cotangent, w_down)
        d_pre = gelu_back(d_hidden)[0].astype(jnp.bfloat16)
        grad_up = product_left(normed_two, d_pre)
        grad_bias_u = jnp.sum(d_pre.astype(jnp.float32), axis=0)
        d_normed_two = product_right(d_pre, w_up)
        d_rows, grad_gain, grad_shift = back_two(d_normed_two)
        return (
            cot_full + d_rows,
            (grad_gain, grad_shift, grad_up, grad_bias_u, grad_down, grad_bias_d),
        )

    long_ff = feed_forward(y_one)
    glob_ff = feed_forward(glob_y_one)
    out_tokens = long_ff[0].astype(jnp.bfloat16)
    out_global = glob_ff[0].astype(jnp.bfloat16)
    d_y_one, long_mlp = feed_back(cot_tokens, long_ff[1], long_ff[2], long_ff[3], long_ff[4])
    glob_d_y_one, glob_mlp = feed_back(cot_global, glob_ff[1], glob_ff[2], glob_ff[3], glob_ff[4])
    mlp_grads = [
        local_part + first_flag * glob_part for local_part, glob_part in zip(long_mlp, glob_mlp)
    ]
    d_proj = d_y_one.astype(jnp.bfloat16)
    glob_d_proj = glob_d_y_one.astype(jnp.bfloat16)
    grad_out = product_left(attn_rows, d_proj) + first_flag * product_left(glob_attn, glob_d_proj)
    d_attn = product_right(d_proj, w_out).astype(jnp.bfloat16).reshape(tok_count, HEADS, HEAD_DIM)
    glob_d_attn = (
        product_right(glob_d_proj, w_out)
        .astype(jnp.bfloat16)
        .reshape(group_seqs, GLOBALS, HEADS, HEAD_DIM)
    )
    glob_d_attn_own = own_slot(glob_d_attn)
    rich_q3_full = rich_q3.astype(jnp.float32)
    rich_k3_full = rich_k3.astype(jnp.float32)
    d_key_ext = jnp.zeros((ext_count, HEADS, HEAD_DIM), jnp.float32)
    d_value_ext = jnp.zeros((ext_count, HEADS, HEAD_DIM), jnp.float32)
    scores, glob_scores, rich_back, q_part, key_win = block_scores()
    prob_full = jnp.exp(scores - log_total[..., None])
    glob_prob_full = jnp.exp(glob_scores - log_total[..., None])
    d_probs = jnp.einsum("qhe,khe->hqk", d_attn, value_ext, preferred_element_type=jnp.float32)
    glob_d_probs = jnp.einsum(
        "qhe,ghe->hqg", d_attn, glob_value_own, preferred_element_type=jnp.float32
    )
    row_delta = jnp.sum(prob_full * d_probs, axis=-1) + jnp.sum(
        glob_prob_full * glob_d_probs, axis=-1
    )
    d_scores = (prob_full * (d_probs - row_delta[..., None])).astype(jnp.bfloat16)
    glob_d_scores = (glob_prob_full * (glob_d_probs - row_delta[..., None])).astype(jnp.bfloat16)
    query_rich_grad, key_rich_grad = rich_back(d_scores.astype(jnp.float32))
    query_grad = (
        jnp.einsum("hqk,khe->qhe", d_scores, key_win, preferred_element_type=jnp.float32)
        + jnp.einsum(
            "hqg,ghe->qhe", glob_d_scores, glob_key_own, preferred_element_type=jnp.float32
        )
    ) * score_scale + jnp.einsum("hqc,ehc->qhe", query_rich_grad, rich_q3_full, precision=PRECISE)
    key_win_grad = jnp.einsum(
        "hqk,qhe->khe", d_scores, q_part, preferred_element_type=jnp.float32
    ) * score_scale + jnp.einsum("hkc,ehc->khe", key_rich_grad, rich_k3_full, precision=PRECISE)
    value_win_grad = jnp.einsum(
        "hqk,qhe->khe", prob_full.astype(jnp.bfloat16), d_attn, preferred_element_type=jnp.float32
    )
    d_key_ext = d_key_ext.at[0:window].add(key_win_grad)
    d_value_ext = d_value_ext.at[0:window].add(value_win_grad)
    glob_key_grad = (
        jnp.einsum("hqg,qhe->ghe", glob_d_scores, q_part, preferred_element_type=jnp.float32)
        * score_scale
    )
    glob_value_grad = jnp.einsum(
        "hqg,qhe->ghe",
        glob_prob_full.astype(jnp.bfloat16),
        d_attn,
        preferred_element_type=jnp.float32,
    )
    grad_rich_q = jnp.einsum(
        "qhe,hqc->ehc", q_part.astype(jnp.float32), query_rich_grad, precision=PRECISE
    )
    grad_rich_k = jnp.einsum(
        "khe,hkc->ehc", key_win.astype(jnp.float32), key_rich_grad, precision=PRECISE
    )
    query_grads = query_grad.reshape(block_rows, D)
    glob_delta = jnp.sum(glob_d_attn.astype(jnp.float32) * glob_att_f, axis=-1)
    glob_delta_own = own_slot(glob_delta)
    glob_lse_own = own_slot(glob_lse)
    member_probs = jnp.where(
        member_mask[:, None, :], jnp.exp(member_scores - glob_lse_own[..., None]), 0.0
    )
    member_d_probs = jnp.einsum(
        "ghe,the->ght", glob_d_attn_own, value_heads, preferred_element_type=jnp.float32
    )
    member_d_scores = (member_probs * (member_d_probs - glob_delta_own[..., None])).astype(
        jnp.bfloat16
    )
    glob_query_part = (
        jnp.einsum("ght,the->ghe", member_d_scores, key_heads, preferred_element_type=jnp.float32)
        * score_scale
    )
    own_key_extra = (
        jnp.einsum(
            "ght,ghe->the", member_d_scores, glob_query_own, preferred_element_type=jnp.float32
        )
        * score_scale
    )
    own_value_extra = jnp.einsum(
        "ght,ghe->the", member_probs, glob_d_attn_own.astype(jnp.float32), precision=PRECISE
    )
    d_key_ext = d_key_ext.at[RADIUS : RADIUS + tok_count].add(own_key_extra)
    d_value_ext = d_value_ext.at[RADIUS : RADIUS + tok_count].add(own_value_extra)
    grad_rims = jnp.concatenate(
        [d_key_ext.reshape(ext_count, D), d_value_ext.reshape(ext_count, D)], axis=1
    )
    from_above = shifted(grad_rims[:RADIUS].astype(jnp.bfloat16), "seq", -1).astype(jnp.float32)
    from_below = shifted(grad_rims[tok_count + RADIUS :].astype(jnp.bfloat16), "seq", 1).astype(
        jnp.float32
    )
    kv_grad = grad_rims[RADIUS : RADIUS + tok_count]
    kv_grad = kv_grad.at[:RADIUS].add(from_below).at[tok_count - RADIUS :].add(from_above)
    summed_query, summed_key, summed_value = (
        lax.psum(to_slots(glob_query_part).astype(jnp.bfloat16), "seq").astype(jnp.float32),
        lax.psum(to_slots(glob_key_grad).astype(jnp.bfloat16), "seq").astype(jnp.float32),
        lax.psum(to_slots(glob_value_grad).astype(jnp.bfloat16), "seq").astype(jnp.float32),
    )
    self_probs = jnp.exp(self_scores - glob_lse[..., None])
    self_d_probs = jnp.einsum(
        "sghe,skhe->sghk", glob_d_attn, glob_value, preferred_element_type=jnp.float32
    )
    self_d_scores = (self_probs * (self_d_probs - glob_delta[..., None])).astype(jnp.bfloat16)
    glob_rows_total = group_seqs * GLOBALS
    glob_d_query = (
        (
            summed_query
            + jnp.einsum(
                "sghk,skhe->sghe", self_d_scores, glob_key, preferred_element_type=jnp.float32
            )
            * score_scale
        )
        .astype(jnp.bfloat16)
        .reshape(glob_rows_total, D)
    )
    glob_d_key = (
        (
            summed_key
            + jnp.einsum(
                "sghk,sghe->skhe", self_d_scores, glob_query, preferred_element_type=jnp.float32
            )
            * score_scale
        )
        .astype(jnp.bfloat16)
        .reshape(glob_rows_total, D)
    )
    glob_d_value = (
        (
            summed_value
            + jnp.einsum(
                "sghk,sghe->skhe", self_probs, glob_d_attn.astype(jnp.float32), precision=PRECISE
            )
        )
        .astype(jnp.bfloat16)
        .reshape(glob_rows_total, D)
    )
    d_query = query_grads.astype(jnp.bfloat16)
    d_key = kv_grad[:, :D].astype(jnp.bfloat16)
    d_value = kv_grad[:, D:].astype(jnp.bfloat16)
    grad_query = product_left(normed, d_query) + first_flag * product_left(
        glob_normed, glob_d_query
    )
    grad_key = product_left(normed, d_key) + first_flag * product_left(glob_normed, glob_d_key)
    grad_value = product_left(normed, d_value) + first_flag * product_left(
        glob_normed, glob_d_value
    )
    d_normed = (
        product_right(d_query, w_query)
        + product_right(d_key, w_key)
        + product_right(d_value, w_value)
    )
    glob_d_normed = (
        product_right(glob_d_query, w_query)
        + product_right(glob_d_key, w_key)
        + product_right(glob_d_value, w_value)
    )
    d_super_norm, grad_gain_one, grad_shift_one = norm_back(d_normed)
    d_super = d_y_one + d_super_norm
    glob_d_norm, glob_gain_one, glob_shift_one = glob_norm_back(glob_d_normed)
    grad_global = glob_d_y_one + glob_d_norm
    grad_gain_one = grad_gain_one + first_flag * glob_gain_one
    grad_shift_one = grad_shift_one + first_flag * glob_shift_one
    d_graph_pre = graph_back(d_super)[0].astype(jnp.bfloat16)
    grad_graph = product_left(agg_low, d_graph_pre)
    d_agg = product_right(d_graph_pre, w_graph) / NEIGH
    d_token_ext = (
        jnp.zeros((ext_count, D), jnp.float32).at[flat_index].add(jnp.repeat(d_agg, NEIGH, axis=0))
    )
    d_token_ext = jnp.where(key_valid[:, None], d_token_ext, 0.0)
    token_above = shifted(d_token_ext[:RADIUS].astype(jnp.bfloat16), "seq", -1).astype(jnp.float32)
    token_below = shifted(d_token_ext[tok_count + RADIUS :].astype(jnp.bfloat16), "seq", 1).astype(
        jnp.float32
    )
    own_grad = (
        d_token_ext[RADIUS : RADIUS + tok_count]
        .at[:RADIUS]
        .add(token_below)
        .at[tok_count - RADIUS :]
        .add(token_above)
    )
    grad_tokens = d_super + own_grad
    weight_grads = (
        grad_graph,
        grad_gain_one,
        grad_shift_one,
        grad_query,
        grad_key,
        grad_value,
        grad_rich_q.reshape(HEAD_DIM, 4 * HEADS),
        grad_rich_k.reshape(HEAD_DIM, 4 * HEADS),
        grad_out,
        mlp_grads[0],
        mlp_grads[1],
        mlp_grads[2],
        mlp_grads[3],
        mlp_grads[4],
        mlp_grads[5],
    )
    pieces = [weight_grad.reshape(seq_count, -1) for weight_grad in weight_grads]
    packed = jnp.concatenate(pieces, axis=1)
    group_count = lax.axis_size("grp")
    received = lax.all_to_all(
        packed.astype(jnp.bfloat16), "seq", split_axis=0, concat_axis=0, tiled=True
    ).astype(packed.dtype)
    group_total = jnp.sum(received, axis=0).reshape(group_count, -1)
    crossed = lax.all_to_all(
        group_total.astype(jnp.bfloat16), "grp", split_axis=0, concat_axis=0, tiled=True
    ).astype(group_total.dtype)
    final_part = jnp.sum(crossed, axis=0)
    flat_sum = lax.all_gather(final_part.astype(jnp.bfloat16), "grp", axis=0, tiled=True).astype(
        final_part.dtype
    )
    results = []
    offset = 0
    for weight_grad in weight_grads:
        part_len = weight_grad.size // seq_count
        results.append(
            flat_sum[offset : offset + part_len].reshape(
                (weight_grad.shape[0] // seq_count,) + weight_grad.shape[1:]
            )
        )
        offset = offset + part_len
    return (
        out_tokens,
        out_global,
        grad_tokens,
        grad_global,
        results[0],
        results[1],
        results[2],
        results[3],
        results[4],
        results[5],
        results[6],
        results[7],
        results[8],
        results[9],
        results[10],
        results[11],
        results[12],
        results[13],
        results[14],
    )


SEQ_WAYS = 4
GRP_WAYS = 8
OWN_HEADS = HEADS // SEQ_WAYS
OWN = D // SEQ_WAYS
FF = 3072
FF_OWN = FF // SEQ_WAYS
TOK = 128
ROWS = SEQ_WAYS * TOK
ALL = ROWS + GLOBALS
GLOB_OWN = GLOBALS // SEQ_WAYS
CHUNK = TOK + GLOB_OWN
PIECE = OWN // GRP_WAYS
BAND = SEQ_WAYS * PIECE
WIN = TOK + 2 * RADIUS
PAD = ROWS + 2 * RADIUS
BF = jnp.bfloat16
F32 = jnp.float32
GELU_SCALE = math.sqrt(2.0 / math.pi)
GELU_CUBE = 0.044715
LOG_NORM = math.log(1.0 + ROWS)
SCORE_SCALE = 1.0 / math.sqrt(HEAD_DIM)
CORE_SWAP = [(0, 1), (1, 0), (2, 3), (3, 2)]
Y_SWAP = [(0, 2), (2, 0), (1, 3), (3, 1)]
X_SWAP = [(g, g ^ 1) for g in range(GRP_WAYS)]
Z_NEAR = [(g, g ^ 2) for g in range(GRP_WAYS)]
Z_FAR = [(g, g ^ 4) for g in range(GRP_WAYS)]
HALF_TOK = ROWS // 2
HALF_GLOB = GLOBALS // 2
HALF = HALF_TOK + HALF_GLOB
SEND = CHUNK + 32
WIDE = 640
GRAPH_ROWS = 32
X_PAIRS = ((0, 1), (2, 3), (4, 5), (6, 7))
KERNEL_COST = 60_000_000_000
RICH = OWN_HEADS * 2 * 4


def nn(left, right):
    return lax.dot_general(left, right, (((1,), (0,)), ((), ())), preferred_element_type=F32)


def nt(left, right):
    return lax.dot_general(left, right, (((1,), (1,)), ((), ())), preferred_element_type=F32)


def tn(left, right):
    return lax.dot_general(left, right, (((0,), (0,)), ((), ())), preferred_element_type=F32)


def load(source, target, sem):
    copy = pltpu.make_async_copy(source, target, sem)
    copy.start()
    return copy


def pick(stacked, index):
    return lax.dynamic_index_in_dim(stacked, index, 0, keepdims=False)


def tie(*values):
    return lax.optimization_barrier(values)


def reach_seq(block):
    return lax.ppermute(block, "seq", CORE_SWAP), lax.ppermute(block, "seq", Y_SWAP)


def gather_seq(block):
    beside, across = reach_seq(block)
    return [block, beside, across, lax.ppermute(across, "seq", CORE_SWAP)]


def turn_core(chunks):
    me = lax.axis_index("seq")
    return lax.ppermute(jnp.stack([pick(chunks, me ^ 1), pick(chunks, me ^ 3)]), "seq", CORE_SWAP)


def turn_y(chunks, came):
    return jnp.stack([pick(chunks, lax.axis_index("seq") ^ 2), came[1]])


def turned(chunks, came, far):
    mine = pick(chunks, lax.axis_index("seq"))
    return jnp.concatenate([mine, came[0], far[0], far[1]], axis=0)


def added(kept, came):
    return (kept.astype(F32) + came.astype(F32)).astype(BF)


def swap_x(sent):
    return lax.ppermute(sent, "grp", X_SWAP)


def swap_near(sent):
    return lax.ppermute(sent, "grp", Z_NEAR)


def swap_far(sent):
    return lax.ppermute(sent, "grp", Z_FAR)


def halves(kept, came, bit):
    grid = added(kept, came).reshape((-1, 2) + kept.shape[1:])
    mine = lax.dynamic_index_in_dim(grid, bit, 1, keepdims=False)
    return mine, lax.dynamic_index_in_dim(grid, 1 - bit, 1, keepdims=False)


def row_stats(rows_in):
    centred = rows_in - jnp.mean(rows_in, axis=-1, keepdims=True)
    scale = lax.rsqrt(jnp.mean(centred * centred, axis=-1, keepdims=True) + EPSILON)
    return centred * scale, scale


def norm_back(cotangent, gain, rows_in):
    hat, scale = row_stats(rows_in)
    scaled = cotangent * gain
    back = scale * (
        scaled
        - jnp.mean(scaled, axis=-1, keepdims=True)
        - hat * jnp.mean(scaled * hat, axis=-1, keepdims=True)
    )
    return (
        back,
        jnp.sum(cotangent * hat, axis=0, keepdims=True),
        jnp.sum(cotangent, axis=0, keepdims=True),
    )


def gelu_parts(pre):
    square = pre * pre
    bent = jnp.tanh(GELU_SCALE * pre * (1.0 + GELU_CUBE * square))
    half = 0.5 * (1.0 + bent)
    slope = half + 0.5 * pre * (1.0 - bent * bent) * (
        GELU_SCALE * (1.0 + 3.0 * GELU_CUBE * square)
    )
    return pre * half, slope


def ints_kernel(neigh_ref, rank_ref, member_ref, out_ref):
    out_ref[:NEIGH] = neigh_ref[...]
    out_ref[NEIGH:] = jnp.concatenate(
        [rank_ref[...], member_ref[...], jnp.zeros((16 - NEIGH - 3, TOK), jnp.int32)], axis=0
    )


def counts_of(neigh, first, width):
    spots = (lax.broadcasted_iota(jnp.int32, (neigh.shape[0], width), 1) + first).astype(F32)
    total = jnp.zeros((neigh.shape[0], width), F32)
    for k in range(NEIGH):
        total = total + jnp.where(neigh[:, k : k + 1] == spots, 1.0, 0.0)
    return total.astype(BF)


def as_row(ref):
    return ref[...].reshape(1, ref.shape[0])


def own_window(me):
    return pl.ds(pl.multiple_of(lax.div(3 * me, 2) * 128, 128), 256)


def own_part(wide, me):
    return jnp.where(me % 2 == 0, wide[:, :OWN], wide[:, 256 - OWN :])


def rich_rows(rich, me, h):
    lane = lax.broadcasted_iota(jnp.int32, (8, 4 * HEADS), 1)
    term = lax.broadcasted_iota(jnp.int32, (8, 4 * HEADS), 0)
    chosen = (lane == 4 * (OWN_HEADS * me + h) + term) & (term < 4)
    return nn(jnp.where(chosen, 1.0, 0.0).astype(BF), rich)


def rich_columns(rich, me, h):
    row = lax.broadcasted_iota(jnp.int32, (4 * HEADS, 128), 0)
    term = lax.broadcasted_iota(jnp.int32, (4 * HEADS, 128), 1)
    chosen = (row == 4 * (OWN_HEADS * me + h) + term) & (term < 4)
    return tn(rich, jnp.where(chosen, 1.0, 0.0).astype(BF))


def share_out(chunk_of, bit, pairs, kept_ref, sent_ref):
    for i, pair in enumerate(pairs):
        first, second = (chunk_of(g) for g in pair)
        kept_ref[i] = jnp.where(bit == 0, first, second)
        sent_ref[i] = jnp.where(bit == 0, second, first)


def row_pieces(ref, g):
    return [ref[OWN * p + PIECE * g : OWN * p + PIECE * (g + 1)] for p in range(SEQ_WAYS)]


def pair_terms(meta_col, meta_row, before_ref, distance_ref):
    for c in range(2):
        gap = meta_col[:, 8 + c : 9 + c] - meta_row[8 + c : 9 + c]
        before_ref[c] = jnp.where(gap < 0.0, 1.0, -1.0)
        distance_ref[c] = jnp.log(1.0 + jnp.abs(gap)) * (1.0 / LOG_NORM)


def attend_kernel(
    tok_a, tok_b, tok_c, tok_d, int_a, int_b, int_c, int_d, glob_ref, gain_ref, shift_ref, rich_q_ref,
    rich_k_ref,    w_graph_any, w_query_any, w_key_any, w_value_any,
    both_ref, member_ref, glob_att_ref, meta_row_ref,
    agg_any, pre_any, super_any, normed_any, qkv_any, prob_any,
    agg_ref, pre_ref, super_ref, normed_ref, qkv_ref, prob_ref,
    padded, w_graph_ref, w_project_ref, keys, values, key_rich, meta_pad, before_ref, distance_ref,
    rich_left, far_ref, heads_out, attn_ref, meta_col_ref, sems, prob_sems,
):
    me = lax.axis_index("seq")
    graph_copy = load(w_graph_any, w_graph_ref, sems.at[0])
    project_copies = [
        load(weight.at[:, own_window(me)], w_project_ref.at[i], sems.at[1 + i])
        for i, weight in enumerate((w_query_any, w_key_any, w_value_any))
    ]
    padded[:RADIUS] = jnp.zeros((RADIUS, D), BF)
    padded[RADIUS + ROWS :] = jnp.zeros((RADIUS, D), BF)
    starts = [pl.multiple_of((me ^ k) * TOK, TOK) for k in range(SEQ_WAYS)]
    for start, tok in zip(starts, (tok_a, tok_b, tok_c, tok_d)):
        padded[pl.ds(start + RADIUS, TOK)] = tok[...]
    for start, ints in zip(starts, (int_a, int_b, int_c, int_d)):
        rows = ints[...].astype(F32)
        meta_row_ref[:, pl.ds(start, TOK)] = rows
        floats = meta_columns(rows)
        meta_col_ref[pl.ds(start, TOK)] = floats
        counts = counts_of(floats, 0, WIN)
        mean = nn(counts, padded[pl.ds(start, WIN)]) * (1.0 / NEIGH)
        agg_ref[pl.ds(start, TOK)] = mean.astype(BF)
    gain, shift = as_row(gain_ref), as_row(shift_ref)
    graph_copy.wait()
    for low in range(0, ROWS, 256):
        rows = slice(low, low + 256)
        pre = nn(agg_ref[rows], w_graph_ref[...])
        pre_ref[rows] = pre
        tokens = padded[RADIUS + low : RADIUS + low + 256].astype(F32)
        super_rows = tokens + gelu_parts(pre)[0]
        super_ref[rows] = super_rows
        normed_ref[rows] = (row_stats(super_rows)[0] * gain + shift).astype(BF)
    glob_hat = row_stats(glob_ref[...].astype(F32))[0]
    normed_ref[ROWS:] = (glob_hat * gain + shift).astype(BF)
    kept = [
        load(source, target, sems.at[4 + i])
        for i, (source, target) in enumerate((
            (agg_ref.at[:, own_window(me)], agg_any), (pre_ref, pre_any), (super_ref, super_any), (normed_ref, normed_any),
        ))
    ]
    normed = normed_ref[...]
    for part in range(3):
        project_copies[part].wait()
        projected = nn(normed, own_part(w_project_ref[part], me)).astype(BF)
        for h in range(OWN_HEADS):
            qkv_ref[part * OWN_HEADS + h] = projected[:, h * HEAD_DIM : (h + 1) * HEAD_DIM]
    kept.append(load(qkv_ref, qkv_any, sems.at[8]))
    rich_q, rich_k = rich_q_ref[...], rich_k_ref[...]
    spread_keys(qkv_ref, keys, values)
    meta_pad[...] = jnp.zeros((16, PAD), F32)
    meta_pad[:, RADIUS : RADIUS + ROWS] = meta_row_ref[...]

    def prepare(h, carry):
        key_rich[h] = nt(rich_rows(rich_k, me, h).astype(BF), keys[h])
        rich_left[h] = rich_columns(rich_q, me, h).astype(BF)
        return carry

    lax.fori_loop(0, OWN_HEADS, prepare, 0, unroll=True)

    def prob_copy(b):
        rows = pl.ds(pl.multiple_of(b * TOK, TOK), TOK)
        return pltpu.make_async_copy(prob_ref.at[:, rows], prob_any.at[:, rows], prob_sems.at[b])

    def block(b, carry):
        start = pl.multiple_of(b * TOK, TOK)
        rows = pl.ds(start, TOK)
        window = pl.ds(start, WIN)
        pair_terms(meta_col_ref[rows], meta_pad[:, window], before_ref, distance_ref)
        q_spot = lax.broadcasted_iota(jnp.int32, (TOK, WIN), 0)
        k_spot = lax.broadcasted_iota(jnp.int32, (TOK, WIN), 1)
        ahead = k_spot - q_spot
        place = k_spot + (start - RADIUS)
        mask = (ahead >= 0) & (ahead <= 2 * RADIUS) & (place >= 0) & (place < ROWS)
        far_ref[...] = jnp.where(mask, 0.0, MASKED)

        def head(h, inner):
            query = qkv_ref[h, rows]
            query_rich = nn(query, rich_left[h])
            right = key_rich[h, :, window]
            scores = nt(query, keys[h, window]) * SCORE_SCALE + far_ref[...]
            spread = None
            for c in range(2):
                logit = (query_rich[:, c : c + 1] + right[c : c + 1]) * before_ref[c]
                off = distance_ref[c] - (query_rich[:, 2 + c : 3 + c] + right[2 + c : 3 + c])
                scores = scores + (jnp.minimum(logit, 0.0) - 0.5 * off * off)
                grown = 1.0 + jnp.exp(-jnp.abs(logit))
                spread = grown if spread is None else spread * grown
            scores = scores - jnp.log(spread)
            glob_scores = nt(query, qkv_ref[OWN_HEADS + h, ROWS:]) * SCORE_SCALE
            top = jnp.maximum(
                jnp.max(scores, axis=-1, keepdims=True), jnp.max(glob_scores, axis=-1, keepdims=True)
            )
            prob = jnp.exp(scores - top)
            glob_prob = jnp.exp(glob_scores - top)
            total = jnp.sum(prob, axis=-1, keepdims=True) + jnp.sum(
                glob_prob, axis=-1, keepdims=True
            )
            inverse = 1.0 / total
            prob = prob * inverse
            glob_prob = glob_prob * inverse
            prob_ref[h, rows, :WIN] = prob
            prob_ref[h, rows, WIN : WIN + GLOBALS] = glob_prob
            mixed = nn(prob.astype(BF), values[h, window]) + nn(
                glob_prob.astype(BF), qkv_ref[2 * OWN_HEADS + h, ROWS:]
            )
            heads_out[h, rows] = mixed.astype(BF)
            return inner

        lax.fori_loop(0, OWN_HEADS, head, 0, unroll=True)
        prob_copy(b).start()
        return carry

    lax.fori_loop(0, SEQ_WAYS, block, 0)
    slot = lax.broadcasted_iota(jnp.int32, (GLOBALS, ROWS), 0).astype(F32)
    member = meta_row_ref[10:11] == slot

    def glob_head(h, carry):
        query = qkv_ref[h, ROWS:]
        scores = nt(query, qkv_ref[OWN_HEADS + h, :ROWS]) * SCORE_SCALE
        scores = jnp.where(member, scores, MASKED)
        own = nt(query, qkv_ref[OWN_HEADS + h, ROWS:]) * SCORE_SCALE
        top = jnp.maximum(
            jnp.max(scores, axis=-1, keepdims=True), jnp.max(own, axis=-1, keepdims=True)
        )
        prob = jnp.exp(scores - top)
        own_prob = jnp.exp(own - top)
        total = jnp.sum(prob, axis=-1, keepdims=True) + jnp.sum(own_prob, axis=-1, keepdims=True)
        inverse = 1.0 / total
        prob = prob * inverse
        own_prob = own_prob * inverse
        member_ref[h, :, :ROWS] = prob
        member_ref[h, :, ROWS : ROWS + GLOBALS] = own_prob
        mixed = nn(prob.astype(BF), qkv_ref[2 * OWN_HEADS + h, :ROWS]) + nn(
            own_prob.astype(BF), qkv_ref[2 * OWN_HEADS + h, ROWS:]
        )
        glob_att_ref[h] = mixed
        heads_out[h, ROWS:] = mixed.astype(BF)
        return carry

    lax.fori_loop(0, OWN_HEADS, glob_head, 0, unroll=True)
    for h in range(OWN_HEADS):
        attn_ref[:, h * HEAD_DIM : (h + 1) * HEAD_DIM] = heads_out[h]
    for half in range(2):
        span = slice(OWN * half, OWN * (half + 1))
        low, glob_low = HALF_TOK * half, ROWS + HALF_GLOB * half
        both_ref[:HALF_TOK, span] = attn_ref[low : low + HALF_TOK]
        both_ref[HALF_TOK:, span] = attn_ref[glob_low : glob_low + HALF_GLOB]
    for copy in kept:
        copy.wait()
    for b in range(SEQ_WAYS):
        prob_copy(b).wait()


def meta_columns(meta_row):
    return jnp.concatenate([meta_row, jnp.zeros((TOK - 16, TOK), F32)], axis=0).T


def spread_keys(qkv_ref, keys, values):
    edge = jnp.zeros((OWN_HEADS, RADIUS, HEAD_DIM), BF)
    for held, first in ((keys, OWN_HEADS), (values, 2 * OWN_HEADS)):
        held[:, :RADIUS] = edge
        held[:, RADIUS + ROWS :] = edge
        held[:, RADIUS : RADIUS + ROWS] = qkv_ref[first : first + OWN_HEADS, :ROWS]


def own_feed_kernel(
    att_a, att_b, att_c, att_d, gain_ref, shift_ref, bias_up_ref, bias_down_ref, cot_ref,
    super_any, glob_any, cot_glob_any, w_out_any, w_up_any, w_down_any,
    out_ref, send_ref,
    att_refs, glob_att_refs, super_ref, glob_ref, cot_glob_ref, w_out_ref, w_up_ref, w_down_ref,
    bias_ref, out_sum, back_sum, sems,
):
    me = lax.axis_index("seq")
    half = lax.div(me, 2)
    inner = lax.rem(me, 2)
    tok_rows = pl.ds(pl.multiple_of(inner * TOK, TOK), TOK)
    glob_rows = pl.ds(pl.multiple_of(HALF_TOK + inner * GLOB_OWN, GLOB_OWN), GLOB_OWN)
    own_tok = pl.ds(pl.multiple_of(me * TOK, TOK), TOK)
    own_glob = pl.ds(pl.multiple_of(me * GLOB_OWN, GLOB_OWN), GLOB_OWN)
    first = []
    for k, att in enumerate((att_a, att_b, att_c, att_d)):
        first.append(load(att.at[tok_rows], att_refs.at[k], sems.at[k]))
        first.append(load(att.at[glob_rows], glob_att_refs.at[k], sems.at[4 + k]))
    first.append(load(super_any.at[own_tok], super_ref, sems.at[8]))
    first.append(load(glob_any.at[own_glob], glob_ref, sems.at[9]))
    first.append(load(cot_glob_any.at[own_glob], cot_glob_ref, sems.at[10]))
    first.append(load(w_out_any, w_out_ref, sems.at[11]))

    def up_copy(j):
        span = pl.ds(pl.multiple_of(j * FF_OWN, FF_OWN), FF_OWN)
        return pltpu.make_async_copy(w_up_any.at[:, span], w_up_ref.at[j], sems.at[12 + j])

    def down_copy(j):
        span = pl.ds(pl.multiple_of(j * FF_OWN, FF_OWN), FF_OWN)
        return pltpu.make_async_copy(w_down_any.at[span], w_down_ref.at[j], sems.at[16 + j])

    up_copy(0).start()
    down_copy(0).start()
    for copy in first:
        copy.wait()
    up_copy(1).start()
    down_copy(1).start()
    y_rows = jnp.concatenate([super_ref[...], glob_ref[...].astype(F32)], axis=0)
    for k in range(SEQ_WAYS):
        wide = jnp.concatenate([att_refs[k], glob_att_refs[k]], axis=0)
        mixed = jnp.where(half == 0, wide[:, :OWN], wide[:, OWN:])
        y_rows = y_rows + nn(mixed, w_out_ref[pl.ds(pl.multiple_of((me ^ k) * OWN, OWN), OWN)])
    gain = as_row(gain_ref)
    hat, scale = row_stats(y_rows)
    normed = (hat * gain + as_row(shift_ref)).astype(BF)
    cot = jnp.concatenate([cot_ref[...], cot_glob_ref[...]], axis=0)
    bias = as_row(bias_up_ref)
    for j in range(SEQ_WAYS):
        bias_ref[j : j + 1] = bias[:, FF_OWN * j : FF_OWN * (j + 1)]
    out_sum[...] = y_rows + as_row(bias_down_ref)
    back_sum[...] = jnp.zeros((CHUNK, D), F32)

    def units(j, carry):
        @pl.when(j + 2 < SEQ_WAYS)
        def _():
            up_copy(j + 2).start()
            down_copy(j + 2).start()

        up_copy(j).wait()
        hidden, slope = gelu_parts(nn(normed, w_up_ref[j]) + bias_ref[pl.ds(j, 1)])
        down_copy(j).wait()
        d_pre = (nt(cot, w_down_ref[j]) * slope).astype(BF)
        back_sum[...] += nt(d_pre, w_up_ref[j])
        out_sum[...] += nn(hidden.astype(BF), w_down_ref[j])
        return carry

    lax.fori_loop(0, SEQ_WAYS, units, 0)
    out, back = out_sum[...], back_sum[...]
    out_ref[...] = out[:TOK].astype(BF)
    scaled = back * gain
    cot = cot.astype(F32)
    d_rows = cot + scale * (
        scaled
        - jnp.mean(scaled, axis=-1, keepdims=True)
        - hat * jnp.mean(scaled * hat, axis=-1, keepdims=True)
    )
    sums = [back * hat, back, cot]
    sums = [jnp.sum(rows, axis=0, keepdims=True) for rows in sums]
    send_ref[:CHUNK] = d_rows.astype(BF)
    send_ref[CHUNK : CHUNK + GLOB_OWN] = out[TOK:].astype(BF)
    sums = jnp.concatenate(sums + [jnp.zeros((13, D), F32)], axis=0)
    send_ref[CHUNK + GLOB_OWN :] = sums.astype(BF)


def feed_rows_kernel(
    att_a, att_b, att_c, att_d, cot_a, cot_b, cot_c, cot_d, cot_glob_ref, glob_ref, gain_ref,
    shift_ref, bias_ref, super_any, w_out_any, w_up_any,
    kept_ref, sent_ref, normed_ref, slope_ref, cot_ref,
    super_ref, w_out_ref, w_up_ref, hidden_ref, grad, sems,
):
    me, x = lax.axis_index("seq"), lax.rem(lax.axis_index("grp"), 2)
    mine = pl.multiple_of(me * FF_OWN, FF_OWN)
    copies = [
        load(super_any, super_ref, sems.at[0]),
        load(w_out_any, w_out_ref, sems.at[1]),
        load(w_up_any.at[:, pl.ds(mine, FF_OWN)], w_up_ref, sems.at[2]),
    ]
    for k, cot in enumerate((cot_a, cot_b, cot_c, cot_d)):
        b = me ^ k
        at = lax.div(b, 2) * HALF + lax.rem(b, 2) * TOK
        cot_ref[pl.ds(pl.multiple_of(at, 32), TOK)] = cot[...]
    for half in range(2):
        cot_ref[HALF * half + HALF_TOK : HALF * (half + 1)] = cot_glob_ref[
            HALF_GLOB * half : HALF_GLOB * (half + 1)
        ]
    gain, shift = as_row(gain_ref), as_row(shift_ref)
    bias = as_row(bias_ref)
    bias = [bias[:, FF_OWN * j : FF_OWN * (j + 1)] for j in range(SEQ_WAYS)]
    bias = jnp.where(me < 2, jnp.where(me == 0, bias[0], bias[1]), jnp.where(me == 2, bias[2], bias[3]))
    for copy in copies:
        copy.wait()
    for half in range(2):
        rows = slice(HALF * half, HALF * (half + 1))
        glob_rows = glob_ref[HALF_GLOB * half : HALF_GLOB * (half + 1)].astype(F32)
        y_rows = jnp.concatenate([super_ref[HALF_TOK * half : HALF_TOK * (half + 1)], glob_rows], axis=0)
        for k, att in enumerate((att_a, att_b, att_c, att_d)):
            w_rows = w_out_ref[pl.ds(pl.multiple_of((me ^ k) * OWN, OWN), OWN)]
            y_rows = y_rows + nn(att[:, OWN * half : OWN * (half + 1)], w_rows)
        normed = (row_stats(y_rows)[0] * gain + shift).astype(BF)
        normed_ref[rows] = normed
        hidden, slope = gelu_parts(nn(normed, w_up_ref[...]) + bias)
        hidden_ref[rows] = hidden.astype(BF)
        slope_ref[rows] = slope.astype(BF)
    grad[...] = tn(hidden_ref[...], cot_ref[...])
    share_out(lambda g: grad[BAND * g : BAND * (g + 1)].astype(BF), x, X_PAIRS, kept_ref, sent_ref)


def feed_back_kernel(
    normed_ref, slope_ref, cot_ref, w_down_any,
    kept_ref, sent_ref, d_bias_ref, w_down_ref, d_pre_ref, grad, sems,
):
    me = lax.axis_index("seq")
    x = lax.rem(lax.axis_index("grp"), 2)
    mine = pl.ds(pl.multiple_of(me * FF_OWN, FF_OWN), FF_OWN)
    load(w_down_any.at[mine], w_down_ref, sems.at[0]).wait()
    d_bias = jnp.zeros((1, FF_OWN), F32)
    for half in range(2):
        rows = slice(HALF * half, HALF * (half + 1))
        d_pre = (nt(cot_ref[rows], w_down_ref[...]) * slope_ref[rows].astype(F32)).astype(BF)
        d_pre_ref[rows] = d_pre
        d_bias = d_bias + jnp.sum(d_pre.astype(F32), axis=0, keepdims=True)
    d_bias_ref[...] = d_bias
    grad[...] = tn(normed_ref[...], d_pre_ref[...])
    share_out(
        lambda g: jnp.concatenate(row_pieces(grad, g), axis=0).astype(BF), x, X_PAIRS, kept_ref, sent_ref
    )


def project_grad_kernel(normed_ref, d_qkv_ref, attn_ref, d_proj_ref, kept_ref, sent_ref, grad, grad_out):
    x = lax.rem(lax.axis_index("grp"), 2)
    grad[...] = tn(normed_ref[...], d_qkv_ref[:, : 3 * OWN])
    total = None
    for half in range(2):
        columns = slice(OWN * half, OWN * (half + 1))
        first, glob_first = HALF_TOK * half, ROWS + HALF_GLOB * half
        term = tn(attn_ref[:HALF_TOK, columns], d_proj_ref[first : first + HALF_TOK])
        term = term + tn(attn_ref[HALF_TOK:, columns], d_proj_ref[glob_first : glob_first + HALF_GLOB])
        total = term if total is None else total + term
    grad_out[...] = total

    def chunk(g):
        out_rows = grad_out[PIECE * g : PIECE * (g + 1)]
        left = jnp.concatenate(row_pieces(grad, g), axis=0)
        right = [out_rows[:, OWN * p : OWN * (p + 1)] for p in range(SEQ_WAYS)]
        return jnp.concatenate([left, jnp.concatenate(right, axis=0)], axis=1).astype(BF)

    share_out(chunk, x, X_PAIRS, kept_ref, sent_ref)


def back_kernel(
    back_a, back_b, back_c, back_d, glob_att_ref, meta_row_ref, rich_q_ref,
    rich_k_ref, w_out_any, qkv_any, prob_any, member_any,
    d_proj_ref, d_qkv_ref, vec_ref, out_global_ref,
    w_out_ref, qkv_ref, prob_ref, member_ref, keys, values, key_rich, meta_pad, before_ref, distance_ref,
    rich_left, d_att, d_keys, d_values, d_key_rich, d_query_rich, rich_qt, rich_kt, d_glob, parts, rich,
    sems, prob_sems,
):
    me = lax.axis_index("seq")
    own_rows = pl.ds(pl.multiple_of(me * OWN, OWN), OWN)
    w_copy = load(w_out_any.at[own_rows], w_out_ref, sems.at[0])
    qkv_copy = load(qkv_any, qkv_ref, sems.at[1])

    def prob_copy(b):
        rows = pl.ds(pl.multiple_of(b * TOK, TOK), TOK)
        return pltpu.make_async_copy(prob_any.at[:, rows], prob_ref.at[:, rows], prob_sems.at[b])

    for b in range(SEQ_WAYS):
        prob_copy(b).start()
    member_copy = load(member_any, member_ref, sems.at[2])
    sums = None
    for k, back in enumerate((back_a, back_b, back_c, back_d)):
        at = me ^ k
        d_proj_ref[pl.ds(pl.multiple_of(at * TOK, TOK), TOK)] = back[:TOK]
        d_proj_ref[pl.ds(pl.multiple_of(ROWS + at * GLOB_OWN, GLOB_OWN), GLOB_OWN)] = back[TOK:CHUNK]
        out_global_ref[pl.ds(pl.multiple_of(at * GLOB_OWN, GLOB_OWN), GLOB_OWN)] = back[
            CHUNK : CHUNK + GLOB_OWN
        ]
        part = back[CHUNK + GLOB_OWN :].astype(F32)
        sums = part if sums is None else sums + part
    vec_ref[...] = sums[:8]
    w_copy.wait()
    projected = nt(d_proj_ref[...], w_out_ref[...]).astype(BF)
    for h in range(OWN_HEADS):
        d_att[h] = projected[:, h * HEAD_DIM : (h + 1) * HEAD_DIM]
    meta_pad[...] = jnp.zeros((16, PAD), F32)
    meta_pad[:, RADIUS : RADIUS + ROWS] = meta_row_ref[...]
    qkv_copy.wait()
    spread_keys(qkv_ref, keys, values)
    rich_q, rich_k = rich_q_ref[...], rich_k_ref[...]

    def prepare(h, carry):
        rich_left[h] = rich_columns(rich_q, me, h).astype(BF)
        rich_qt[h] = rich_rows(rich_q, me, h)
        rich_kt[h] = rich_rows(rich_k, me, h)
        key_rich[h] = nt(rich_kt[h].astype(BF), keys[h])
        return carry

    lax.fori_loop(0, OWN_HEADS, prepare, 0, unroll=True)
    d_keys[...] = jnp.zeros((OWN_HEADS, PAD, HEAD_DIM), F32)
    d_values[...] = jnp.zeros((OWN_HEADS, PAD, HEAD_DIM), F32)
    d_key_rich[...] = jnp.zeros((OWN_HEADS, 8, PAD), F32)
    d_glob[...] = jnp.zeros((2 * OWN_HEADS, GLOBALS, HEAD_DIM), F32)

    def block(b, carry):
        start = pl.multiple_of(b * TOK, TOK)
        rows = pl.ds(start, TOK)
        window = pl.ds(start, WIN)
        pair_terms(meta_columns(meta_row_ref[:, rows]), meta_pad[:, window], before_ref, distance_ref)
        prob_copy(b).wait()

        def head(h, inner):
            query = qkv_ref[h, rows]
            d_out = d_att[h, rows]
            prob = prob_ref[h, rows, :WIN]
            glob_prob = prob_ref[h, rows, WIN : WIN + GLOBALS]
            d_prob = nt(d_out, values[h, window])
            d_glob_prob = nt(d_out, qkv_ref[2 * OWN_HEADS + h, ROWS:])
            delta = jnp.sum(prob * d_prob, axis=-1, keepdims=True) + jnp.sum(
                glob_prob * d_glob_prob, axis=-1, keepdims=True
            )
            d_scores = prob * (d_prob - delta)
            d_low = d_scores.astype(BF)
            d_glob_low = (glob_prob * (d_glob_prob - delta)).astype(BF)
            query_rich = nn(query, rich_left[h])
            right = key_rich[h, :, window]
            lefts, belows = [None] * 4, [None] * 4
            for c in range(2):
                logit = query_rich[:, c : c + 1] + right[c : c + 1]
                pulled = d_scores * (0.5 * before_ref[c] - 0.5 * jnp.tanh(0.5 * logit))
                off = distance_ref[c] - (query_rich[:, 2 + c : 3 + c] + right[2 + c : 3 + c])
                off = d_scores * off
                lefts[c] = jnp.sum(pulled, axis=-1, keepdims=True)
                lefts[2 + c] = jnp.sum(off, axis=-1, keepdims=True)
                belows[c] = jnp.sum(pulled, axis=0, keepdims=True)
                belows[2 + c] = jnp.sum(off, axis=0, keepdims=True)
            d_key_rich[h, :, window] += jnp.concatenate(belows + [jnp.zeros((4, WIN), F32)], axis=0)
            lane = lax.broadcasted_iota(jnp.int32, (TOK, 8), 1)
            d_left = jnp.zeros((TOK, 8), F32)
            d_query = (
                nn(d_low, keys[h, window]) + nn(d_glob_low, qkv_ref[OWN_HEADS + h, ROWS:])
            ) * SCORE_SCALE
            for c, column in enumerate(lefts):
                d_left = jnp.where(lane == c, column, d_left)
                d_query = d_query + column * rich_qt[h, c : c + 1]
            d_query_rich[h, rows] = d_left
            parts[h, rows] = d_query.astype(BF)
            d_keys[h, window] += tn(d_low, query) * SCORE_SCALE
            d_values[h, window] += tn(prob.astype(BF), d_out)
            d_glob[h] += tn(d_glob_low, query) * SCORE_SCALE
            d_glob[OWN_HEADS + h] += tn(glob_prob.astype(BF), d_out)
            return inner

        lax.fori_loop(0, OWN_HEADS, head, 0, unroll=True)
        return carry

    lax.fori_loop(0, SEQ_WAYS, block, 0)
    member_copy.wait()

    def glob_head(h, carry):
        query = qkv_ref[h, ROWS:]
        key_rows = qkv_ref[OWN_HEADS + h, :ROWS]
        value_rows = qkv_ref[2 * OWN_HEADS + h, :ROWS]
        glob_key = qkv_ref[OWN_HEADS + h, ROWS:]
        glob_value = qkv_ref[2 * OWN_HEADS + h, ROWS:]
        d_out = d_att[h, ROWS:]
        delta = jnp.sum(d_out.astype(F32) * glob_att_ref[h], axis=-1, keepdims=True)
        prob = member_ref[h, :, :ROWS]
        own_prob = member_ref[h, :, ROWS : ROWS + GLOBALS]
        d_low = (prob * (nt(d_out, value_rows) - delta)).astype(BF)
        d_own = (own_prob * (nt(d_out, glob_value) - delta)).astype(BF)
        d_query = (nn(d_low, key_rows) + nn(d_own, glob_key)) * SCORE_SCALE
        parts[h, ROWS:] = d_query.astype(BF)
        parts[OWN_HEADS + h, ROWS:] = (d_glob[h] + tn(d_own, query) * SCORE_SCALE).astype(BF)
        parts[2 * OWN_HEADS + h, ROWS:] = (
            d_glob[OWN_HEADS + h] + tn(own_prob.astype(BF), d_out)
        ).astype(BF)
        d_right = d_key_rich[h, :, RADIUS : RADIUS + ROWS]
        d_key = d_keys[h, RADIUS : RADIUS + ROWS] + tn(d_low, query) * SCORE_SCALE
        d_key = d_key + lax.dot_general(
            d_right, rich_kt[h], (((0,), (0,)), ((), ())), precision=PRECISE,
            preferred_element_type=F32,
        )
        d_value = d_values[h, RADIUS : RADIUS + ROWS] + tn(prob.astype(BF), d_out)
        parts[OWN_HEADS + h, :ROWS] = d_key.astype(BF)
        parts[2 * OWN_HEADS + h, :ROWS] = d_value.astype(BF)
        rich[pl.ds(pl.multiple_of(8 * h, 8), 8)] = jnp.concatenate(
            [tn(d_query_rich[h].astype(BF), qkv_ref[h, :ROWS])[:4], nn(d_right.astype(BF), key_rows)[:4]],
            axis=0,
        )
        return carry

    lax.fori_loop(0, OWN_HEADS, glob_head, 0, unroll=True)
    for i in range(3 * OWN_HEADS):
        d_qkv_ref[:, i * HEAD_DIM : (i + 1) * HEAD_DIM] = parts[i]
    rich[RICH:] = jnp.zeros((32 - RICH, HEAD_DIM), F32)
    d_qkv_ref[:, 3 * OWN :] = jnp.zeros((ALL, WIDE - 3 * OWN), BF)
    d_qkv_ref[:32, 3 * OWN :] = rich[...].astype(BF)


def norm_kernel(
    dqkv_a, dqkv_b, dqkv_c, dqkv_d, glob_ref, d_proj_ref, gain_ref, vec_two_ref, d_bias_up_ref,
    w_query_any, w_key_any, w_value_any, super_any, pre_any, agg_any,
    grad_glob_ref, kept_ref, sent_ref, d_own_ref, d_pre,
    w_query_ref, w_key_ref, w_value_ref, super_ref, pre_ref, agg_ref, d_super, d_qkv, d_norm, rich, sems,
):
    me, x = lax.axis_index("seq"), lax.rem(lax.axis_index("grp"), 2)
    weight_copies = [
        load(source, target, sems.at[i])
        for i, (source, target) in enumerate((
            (w_query_any, w_query_ref), (w_key_any, w_key_ref), (w_value_any, w_value_ref),
        ))
    ]
    row_copies = [load(super_any, super_ref, sems.at[3]), load(pre_any, pre_ref, sems.at[4])]
    agg_copy = load(agg_any, agg_ref, sems.at[5])
    for k, part in enumerate((dqkv_a, dqkv_b, dqkv_c, dqkv_d)):
        d_qkv[me ^ k] = part[...]
        rich[me ^ k] = part[:32, 3 * OWN :].astype(F32)
    total = None
    for i, weight in enumerate((w_query_ref, w_key_ref, w_value_ref)):
        weight_copies[i].wait()
        columns = [d_qkv[p, :, OWN * i : OWN * (i + 1)] for p in range(SEQ_WAYS)]
        term = nt(jnp.concatenate(columns, axis=1), weight[...])
        total = term if total is None else total + term
    d_norm[...] = total
    for copy in row_copies:
        copy.wait()
    gain = as_row(gain_ref)
    d_gain = jnp.zeros((1, D), F32)
    d_shift = jnp.zeros((1, D), F32)
    for low in range(0, ALL, 192):
        rows = slice(low, low + 192)
        inner = min(192, ROWS - low)
        if inner == 192:
            rows_in = super_ref[rows]
        else:
            rows_in = jnp.concatenate([super_ref[low:], glob_ref[...].astype(F32)], axis=0)
        back, gain_part, shift_part = norm_back(d_norm[rows], gain, rows_in)
        d_gain = d_gain + gain_part
        d_shift = d_shift + shift_part
        back = back + d_proj_ref[rows].astype(F32)
        d_super[rows] = back
        long = slice(low, low + inner)
        slope = gelu_parts(pre_ref[long])[1]
        d_pre[long] = (back[:inner] * slope).astype(BF)
    grad_glob_ref[...] = d_super[ROWS:]
    d_own_ref[...] = d_super[pl.ds(pl.multiple_of(me * TOK, TOK), TOK)]
    agg_copy.wait()
    grad = tn(own_part(agg_ref[...], me), d_pre[...])
    extra = jnp.concatenate(
        [vec_two_ref[0:3], d_bias_up_ref[...], d_gain, d_shift, jnp.zeros((1, D), F32)], axis=0
    )

    def chunk(g):
        pieces = [rich[g // 2, 12 * (g % 2) + i : 12 * (g % 2) + i + 1] for i in range(12)]
        rows = [grad[PIECE * g : PIECE * (g + 1)], jnp.concatenate(pieces, axis=1), extra]
        return jnp.concatenate(rows, axis=0).astype(BF)

    share_out(chunk, x, X_PAIRS, kept_ref, sent_ref)


def tokens_kernel(d_own_ref, d_pre, meta_row_ref, w_graph_any, grad_tok_ref, w_graph_ref, sems):
    me = lax.axis_index("seq")
    copy = load(w_graph_any, w_graph_ref, sems.at[0])
    counts = []
    for shift in (-1, 0, 1):
        rows = pl.ds(pl.multiple_of(jnp.clip(me - shift, 0, SEQ_WAYS - 1) * TOK, TOK), TOK)
        counts.append(counts_of(meta_columns(meta_row_ref[:, rows]), (shift + 1) * TOK, TOK))
    copy.wait()
    total = d_own_ref[...]
    for shift, count in zip((-1, 0, 1), counts):
        b = me - shift
        fits = (b >= 0) & (b < SEQ_WAYS)
        rows = pl.ds(pl.multiple_of(jnp.clip(b, 0, SEQ_WAYS - 1) * TOK, TOK), TOK)
        d_agg = (nt(d_pre[rows], w_graph_ref[...]) * (1.0 / NEIGH)).astype(BF)
        total = total + jnp.where(fits, tn(count, d_agg), 0.0)
    grad_tok_ref[...] = total


DISTANCES = (0, 4, 2, 6)


def down_out_kernel(held, came, out_ref):
    for i, distance in enumerate(DISTANCES):
        for flip, pieces in enumerate((held, came)):
            g = lax.axis_index("grp") ^ (distance + flip)
            out_ref[pl.ds(pl.multiple_of(BAND * g, BAND), BAND)] = pieces[i].astype(F32)


def up_out_kernel(held, came, out_ref):
    for i, distance in enumerate(DISTANCES):
        for flip, pieces in enumerate((held, came)):
            g = lax.axis_index("grp") ^ (distance + flip)
            piece = pieces[i].astype(F32)
            rows = pl.ds(pl.multiple_of(PIECE * g, 8), PIECE)
            for k in range(SEQ_WAYS):
                columns = pl.ds(pl.multiple_of((lax.axis_index("seq") ^ k) * D, D), D)
                out_ref[rows, columns] = piece[PIECE * k : PIECE * (k + 1)]


def project_out_kernel(held, came, query_ref, key_ref, value_ref, out_ref, pieces):
    for i, distance in enumerate(DISTANCES):
        for flip, blocks in enumerate((held, came)):
            g = lax.axis_index("grp") ^ (distance + flip)
            rows = pl.ds(pl.multiple_of(PIECE * g, 8), PIECE)
            piece = blocks[i].astype(F32)
            for k in range(SEQ_WAYS):
                pieces[lax.axis_index("seq") ^ k] = piece[PIECE * k : PIECE * (k + 1), : 3 * OWN]
            for j, ref in enumerate((query_ref, key_ref, value_ref)):
                parts = [pieces[p, :, OWN * j : OWN * (j + 1)] for p in range(SEQ_WAYS)]
                ref[rows] = jnp.concatenate(parts, axis=1)
            parts = [piece[PIECE * p : PIECE * (p + 1), 3 * OWN :] for p in range(SEQ_WAYS)]
            out_ref[rows] = jnp.concatenate(parts, axis=1)


def graph_out_kernel(
    held, came, graph_ref, gain_one_ref, shift_one_ref, gain_two_ref, shift_two_ref, bias_up_ref,
    bias_down_ref, rich_q_ref, rich_k_ref, vectors,
):
    me = lax.axis_index("seq")
    for i, distance in enumerate(DISTANCES):
        for flip, blocks in enumerate((held, came)):
            g = lax.axis_index("grp") ^ (distance + flip)
            rows = pl.ds(pl.multiple_of(PIECE * g, 8), PIECE)
            piece = blocks[i].astype(F32)
            graph_ref[rows] = piece[:PIECE]
            for j in range(12):
                vectors[g, j : j + 1] = piece[PIECE : PIECE + 1, HEAD_DIM * j : HEAD_DIM * (j + 1)]
            vectors[g, 12:16] = jnp.zeros((4, HEAD_DIM), F32)
    sums = held[0, PIECE : PIECE + 8].astype(F32)
    lane = lax.broadcasted_iota(jnp.int32, (D, 256), 0)
    spot = lax.broadcasted_iota(jnp.int32, (D, 256), 1)
    own = jnp.where((lane == OWN * me + spot) & (spot < OWN), 1.0, 0.0).astype(BF)
    own = nn(sums.astype(BF), own)[:, :OWN]
    for ref, row in (
        (gain_two_ref, 1), (shift_two_ref, 2), (bias_down_ref, 3), (gain_one_ref, 5), (shift_one_ref, 6),
    ):
        ref[...] = own[row : row + 1].reshape(OWN)
    bias_up_ref[...] = sums[4:5].reshape(FF_OWN)
    lane = lax.broadcasted_iota(jnp.int32, (HEAD_DIM, 128), 0)
    spot = lax.broadcasted_iota(jnp.int32, (HEAD_DIM, 128), 1)
    part = HEAD_DIM // SEQ_WAYS
    own = jnp.where((lane == part * me + spot) & (spot < part), 1.0, 0.0).astype(BF)
    own = nn(vectors[...].reshape(16 * GRP_WAYS, HEAD_DIM).astype(BF), own).astype(BF)
    row = lax.broadcasted_iota(jnp.int32, (16 * GRP_WAYS, 128), 0)
    place = 12 * lax.div(row, 16) + lax.rem(row, 16)
    column = lax.broadcasted_iota(jnp.int32, (16 * GRP_WAYS, 128), 1)
    for side, ref in enumerate((rich_q_ref, rich_k_ref)):
        wanted = 8 * lax.div(column, 4) + 4 * side + lax.rem(column, 4)
        chosen = (place == wanted) & (lax.rem(row, 16) < 12) & (column < 4 * HEADS)
        turned_rich = tn(own, jnp.where(chosen, 1.0, 0.0).astype(BF))
        ref[...] = turned_rich[:part, : 4 * HEADS]


def call(kernel, ins, outs, scratch=(), apart=0, outs_apart=0, room=50):
    vmem, any_space = pl.BlockSpec(memory_space=pltpu.VMEM), pl.BlockSpec(memory_space=pltpu.HBM)
    return pl.pallas_call(
        kernel,
        out_shape=[jax.ShapeDtypeStruct(shape, kind) for shape, kind in outs],
        in_specs=[vmem] * (len(ins) - apart) + [any_space] * apart,
        out_specs=[vmem] * (len(outs) - outs_apart) + [any_space] * outs_apart,
        scratch_shapes=[pltpu.VMEM(*s) if isinstance(s, tuple) else s for s in scratch],
        compiler_params=pltpu.CompilerParams(vmem_limit_bytes=room * 1024 * 1024),
        cost_estimate=pl.CostEstimate(flops=KERNEL_COST, bytes_accessed=0, transcendentals=0),
    )(*ins)


def split_heads(
    tokens, global_tokens, neighbours, token_ranks, membership, w_graph, gain_one, shift_one,
    w_query, w_key, w_value, rich_query, rich_key, w_out, gain_two, shift_two, w_up, bias_up,
    w_down, bias_down, cot_tokens, cot_global,
):
    me = lax.axis_index("seq")
    grp = lax.axis_index("grp")
    x, z_low, z_high = grp % 2, (grp // 2) % 2, grp // 4
    beside, across = reach_seq(tokens)
    (ints,) = call(
        ints_kernel, [neighbours.T, token_ranks, membership.reshape(1, TOK)], [((16, TOK), jnp.int32)],
        room=60,
    )
    int_beside, int_across = reach_seq(ints)
    int_blocks = [ints, int_beside, int_across, lax.ppermute(int_across, "seq", CORE_SWAP)]
    cot_tokens, across, int_blocks[3] = tie(cot_tokens, across, int_blocks[3])
    cot_across = lax.ppermute(cot_tokens, "seq", Y_SWAP)
    tok_blocks = [tokens, beside, across, lax.ppermute(across, "seq", CORE_SWAP)]
    rich_query, rich_key = rich_query.T, rich_key.T

    weights_shape = (D, D), BF
    stored = [
        ((ROWS, D), BF), ((ROWS, D), F32), ((ROWS, D), F32), ((ALL, D), BF),
        ((3 * OWN_HEADS, ALL, HEAD_DIM), BF), ((OWN_HEADS, ROWS, 512), F32),
    ]
    kept_agg = (ROWS, 256), BF
    heads_scratch = [
        ((OWN_HEADS, PAD, HEAD_DIM), BF), ((OWN_HEADS, PAD, HEAD_DIM), BF),
        ((OWN_HEADS, 8, PAD), F32), ((16, PAD), F32), ((2, TOK, WIN), F32), ((2, TOK, WIN), F32),
        ((OWN_HEADS, HEAD_DIM, 128), BF),
    ]
    (
        both, member_prob, glob_att, meta_row, agg, graph_pre, super_rows, normed, qkv,
        prob,
    ) = call(
        attend_kernel,
        [*tok_blocks, *int_blocks, global_tokens, gain_one, shift_one, rich_query, rich_key, w_graph, w_query,
         w_key, w_value],
        [((HALF, 2 * OWN), BF), ((OWN_HEADS, GLOBALS, 640), F32),
         ((OWN_HEADS, GLOBALS, HEAD_DIM), F32), ((16, ROWS), F32), kept_agg, *stored[1:]],
        [*stored, ((PAD, D), BF), weights_shape, ((3, D, 256), BF), *heads_scratch,
         ((TOK, WIN), F32), ((OWN_HEADS, ALL, HEAD_DIM), BF), ((ALL, OWN), BF),
         ((ROWS, 128), F32), pltpu.SemaphoreType.DMA((9,)), pltpu.SemaphoreType.DMA((SEQ_WAYS,))],
        apart=4, outs_apart=6, room=56,
    )
    both, cot_across, cot_tokens = tie(both, cot_across, cot_tokens)
    att_blocks = gather_seq(both)
    cot_beside = lax.ppermute(cot_tokens, "seq", CORE_SWAP)
    cot_blocks = [cot_tokens, cot_beside, cot_across, lax.ppermute(cot_across, "seq", CORE_SWAP)]
    out_tokens, back = call(
        own_feed_kernel,
        [*att_blocks, gain_two, shift_two, bias_up, bias_down, cot_tokens, super_rows,
         global_tokens, cot_global, w_out, w_up, w_down],
        [((TOK, D), BF), ((SEND, D), BF)],
        [((SEQ_WAYS, TOK, 2 * OWN), BF), ((SEQ_WAYS, GLOB_OWN, 2 * OWN), BF), ((TOK, D), F32),
         ((GLOB_OWN, D), BF), ((GLOB_OWN, D), BF), weights_shape, ((SEQ_WAYS, D, FF_OWN), BF),
         ((SEQ_WAYS, FF_OWN, D), BF), ((SEQ_WAYS, FF_OWN), F32), ((CHUNK, D), F32), ((CHUNK, D), F32),
         pltpu.SemaphoreType.DMA((20,))],
        apart=6,
    )
    beside, across = reach_seq(back)
    late_gain, back = tie(gain_two, back)
    down_kept, down_sent, normed_two, slope, cot_all = call(
        feed_rows_kernel,
        [*att_blocks, *cot_blocks, cot_global, global_tokens, late_gain, shift_two,
         bias_up, super_rows, w_out, w_up],
        [((4, BAND, D), BF), ((4, BAND, D), BF), ((ALL, D), BF), ((ALL, FF_OWN), BF), ((ALL, D), BF)],
        [((ROWS, D), F32), weights_shape, ((D, FF_OWN), BF), ((ALL, FF_OWN), BF), ((D, D), F32),
         pltpu.SemaphoreType.DMA((3,))],
        apart=3,
    )
    down_came = swap_x(down_sent)
    across, down_kept = tie(across, down_kept)
    diagonal = lax.ppermute(across, "seq", CORE_SWAP)
    normed_two, across = tie(normed_two, across)
    up_kept, up_sent, d_bias_up = call(
        feed_back_kernel,
        [normed_two, slope, cot_all, w_down],
        [((4, BAND, D), BF), ((4, BAND, D), BF), ((1, FF_OWN), F32)],
        [((FF_OWN, D), BF), ((ALL, FF_OWN), BF), ((D, D), F32), pltpu.SemaphoreType.DMA((1,))],
        apart=1,
    )
    up_came = swap_x(up_sent)
    late_row, up_kept = tie(meta_row, up_kept)

    d_proj, d_qkv, vec_two, out_global = call(
        back_kernel,
        [back, beside, across, diagonal, glob_att, late_row, rich_query, rich_key,
         w_out, qkv, prob, member_prob],
        [((ALL, D), BF), ((ALL, WIDE), BF), ((8, D), F32), ((GLOBALS, D), BF)],
        [((OWN, D), BF), stored[4], stored[5], ((OWN_HEADS, GLOBALS, 640), F32), *heads_scratch,
         ((OWN_HEADS, ALL, HEAD_DIM), BF), ((OWN_HEADS, PAD, HEAD_DIM), F32),
         ((OWN_HEADS, PAD, HEAD_DIM), F32), ((OWN_HEADS, 8, PAD), F32), ((OWN_HEADS, ROWS, 8), F32),
         ((OWN_HEADS, 8, HEAD_DIM), F32), ((OWN_HEADS, 8, HEAD_DIM), F32),
         ((2 * OWN_HEADS, GLOBALS, HEAD_DIM), F32), ((3 * OWN_HEADS, ALL, HEAD_DIM), BF),
         ((32, HEAD_DIM), F32), pltpu.SemaphoreType.DMA((3,)), pltpu.SemaphoreType.DMA((SEQ_WAYS,))],
        apart=4,
    )
    beside, across = reach_seq(d_qkv)
    held = {"d_qkv": d_qkv, "down": down_kept, "up": up_kept}
    latest = ["d_qkv"]

    def due(value):
        value, held[latest[0]] = tie(value, held[latest[0]])
        return value

    def hold(key, value):
        held[key] = value
        latest[0] = key
        return value

    def halve(key, came, bit):
        kept, sent = halves(held[key], due(came), bit)
        hold(key, kept)
        return sent

    def total(key, came):
        return hold(key, added(held[key], due(came)))

    def join(key, came):
        return hold(key, jnp.concatenate([held[key], due(came)], axis=0))

    down_came = swap_near(halve("down", down_came, z_low))
    proj_kept, proj_sent = call(
        project_grad_kernel,
        [due(normed), d_qkv, both, d_proj],
        [((4, BAND, D), BF)] * 2,
        [((D, 3 * OWN), F32), ((OWN, D), F32)],
    )
    hold("proj", proj_kept)
    proj_came = swap_x(proj_sent)
    up_came = swap_near(halve("up", up_came, z_low))
    down_came = swap_far(halve("down", down_came, z_high))
    across = hold("across", due(across))
    diagonal = lax.ppermute(across, "seq", CORE_SWAP)
    up_came = swap_far(halve("up", up_came, z_high))
    down_came = swap_far(total("down", down_came))
    proj_came = swap_near(halve("proj", proj_came, z_low))
    grad_global, graph_kept, graph_sent, d_own, d_pre = call(
        norm_kernel,
        [d_qkv, beside, held["across"], diagonal, global_tokens, d_proj, gain_one, due(vec_two), d_bias_up,
         w_query, w_key, w_value, super_rows, graph_pre, agg],
        [((GLOBALS, D), F32), ((4, GRAPH_ROWS, D), BF), ((4, GRAPH_ROWS, D), BF), ((TOK, D), F32),
         ((ROWS, D), BF)],
        [*[weights_shape] * 3, ((ROWS, D), F32), ((ROWS, D), F32), ((ROWS, 256), BF), ((ALL, D), F32),
         ((SEQ_WAYS, ALL, WIDE), BF), ((ALL, D), F32), ((SEQ_WAYS, 32, HEAD_DIM), F32),
         pltpu.SemaphoreType.DMA((6,))],
        apart=6,
    )
    hold("graph", graph_kept)
    graph_came = swap_x(graph_sent)
    up_mine = total("up", up_came).reshape(SEQ_WAYS, PIECE, D)
    up_core = turn_core(up_mine)
    proj_came = swap_far(halve("proj", proj_came, z_high))
    down_came = swap_near(join("down", down_came))
    up_core = due(up_core)
    up_far = lax.ppermute(turn_y(up_mine, up_core), "seq", Y_SWAP)
    hold("up_core", up_core)
    (grad_tokens,) = call(
        tokens_kernel, [due(d_own), d_pre, meta_row, w_graph], [((TOK, D), F32)],
        [weights_shape, pltpu.SemaphoreType.DMA((1,))], apart=1,
    )
    hold("tokens", grad_tokens)
    up_came = swap_far(hold("up", turned(up_mine, held["up_core"], due(up_far))[None]))
    proj_sum = total("proj", proj_came)
    proj_core = turn_core(proj_sum[0, :, : 3 * OWN].reshape(SEQ_WAYS, PIECE, 3 * OWN))
    down_came = swap_x(join("down", down_came))
    proj_core = due(proj_core)
    proj_mine = held["proj"][0, :, : 3 * OWN].reshape(SEQ_WAYS, PIECE, 3 * OWN)
    proj_far = lax.ppermute(turn_y(proj_mine, proj_core), "seq", Y_SWAP)
    hold("proj_core", proj_core)
    up_came = swap_near(join("up", up_came))
    graph_came = swap_near(halve("graph", graph_came, z_low))
    proj_turned = turned(proj_mine, held["proj_core"], due(proj_far))
    proj_turned = jnp.concatenate([proj_turned, held["proj"][0, :, 3 * OWN :]], axis=1)[None]
    proj_came = swap_far(hold("proj", proj_turned))
    up_came = swap_x(join("up", up_came))
    proj_came = swap_near(join("proj", proj_came))
    graph_came = swap_far(halve("graph", graph_came, z_high))
    graph_came = swap_far(total("graph", graph_came))
    (g_down,) = call(down_out_kernel, [held["down"], due(down_came)], [((FF_OWN, D), F32)])
    hold("g_down", g_down)
    graph_came = swap_near(join("graph", graph_came))
    proj_came = swap_x(join("proj", proj_came))
    graph_came = swap_x(join("graph", graph_came))
    (g_up,) = call(up_out_kernel, [held["up"], due(up_came)], [((OWN, FF), F32)])
    hold("g_up", g_up)
    g_query, g_key, g_value, g_out = call(
        project_out_kernel,
        [held["proj"], due(proj_came)],
        [((OWN, D), F32)] * 4,
        [((SEQ_WAYS, PIECE, 3 * OWN), F32)],
    )
    hold("g_query", g_query)
    (
        g_graph, g_gain_one, g_shift_one, g_gain_two, g_shift_two, g_bias_up, g_bias_down, g_rich_q,
        g_rich_k,
    ) = call(
        graph_out_kernel,
        [held["graph"], due(graph_came)],
        [((OWN, D), F32), *[((OWN,), F32)] * 4, ((FF_OWN,), F32), ((OWN,), F32),
         *[((HEAD_DIM // SEQ_WAYS, 4 * HEADS), F32)] * 2],
        [((GRP_WAYS, 16, HEAD_DIM), F32)],
    )
    hold("g_graph", g_graph)
    grad_tokens, g_down, g_up, g_query, g_graph = (
        held[key] for key in ("tokens", "g_down", "g_up", "g_query", "g_graph")
    )
    return (
        out_tokens, out_global, grad_tokens, grad_global,
        g_graph, g_gain_one, g_shift_one, g_query, g_key, g_value, g_rich_q, g_rich_k,
        g_out, g_gain_two, g_shift_two, g_up, g_bias_up, g_down, g_bias_down,
    )


def layer(*arrays):
    tokens, global_tokens = arrays[:2]
    ways = (lax.axis_size("seq"), lax.axis_size("grp"))
    if ways == (SEQ_WAYS, GRP_WAYS) and tokens.shape[0] == TOK and global_tokens.shape[0] == GLOBALS:
        return split_heads(*arrays)
    return local(*arrays)


def solution(mesh):
    return jax.shard_map(
        layer,
        mesh=mesh,
        in_specs=(
            P(("grp", "seq"), None),
            P("grp", None),
            P(("grp", "seq"), None),
            P(None, ("grp", "seq")),
            P(("grp", "seq")),
            P(),
            P(),
            P(),
            P(),
            P(),
            P(),
            P(),
            P(),
            P(),
            P(),
            P(),
            P(),
            P(),
            P(),
            P(),
            P(("grp", "seq"), None),
            P("grp", None),
        ),
        out_specs=(
            P(("grp", "seq"), None),
            P("grp", None),
            P(("grp", "seq"), None),
            P("grp", None),
            P("seq", None),
            P("seq"),
            P("seq"),
            P("seq", None),
            P("seq", None),
            P("seq", None),
            P("seq", None),
            P("seq", None),
            P("seq", None),
            P("seq"),
            P("seq"),
            P("seq", None),
            P("seq"),
            P("seq", None),
            P("seq"),
        ),
        check_vma=False,
    )
```
